32 devices in a mesh: fsdp: 4 (over z), context: 2 (over y), tensor: 4 (over x, core).
Axes of the slice: x: 2, y: 2, z: 4, core: 2. Of those that a mesh axis runs over, the one named last changes fastest.
Arguments:
- tokens: bfloat16 [8, 4096, 768], P('fsdp', 'context'), may hold values from -6 to 6
- cotangent: bfloat16 [8, 4096, 768], P('fsdp', 'context'), may hold values from -6 to 6
- segments: int32 [8, 4096], P('fsdp'), may hold values from 0 to 4, as said below
- steps: int32 [8], P('fsdp'), may hold values from 0 to 255
- table: bfloat16 [256, 128], replicated, may hold values from -5 to 5
- ada_w: bfloat16 [128, 4608], replicated, may hold values from -0.5 to 0.5
- ada_b: bfloat16 [4608], replicated, may hold values from 0.099609375 to 1.8984375
- gain_one: bfloat16 [768], replicated, may hold values from 0.099609375 to 1.8984375
- w_qkv: bfloat16 [768, 2304], P('fsdp', 'tensor'), may hold values from -0.109375 to 0.109375
- w_out: bfloat16 [768, 768], P('tensor', 'fsdp'), may hold values from -3 to 3
- gain_two: bfloat16 [768], replicated, may hold values from 0.099609375 to 1.8984375
- w_up: bfloat16 [768, 3072], P('fsdp', 'tensor'), may hold values from -0.109375 to 0.109375
- b_up: bfloat16 [3072], replicated, may hold values from -3 to 3
- w_down: bfloat16 [3072, 768], P('tensor', 'fsdp'), may hold values from -0.15625 to 0.15625
- b_down: bfloat16 [768], replicated, may hold values from -3 to 3
Outputs:
- block_out: bfloat16 [8, 4096, 768], P('fsdp', 'context')
- grad_tokens: float32 [8, 4096, 768], P('fsdp', 'context', 'tensor')
- grad_table: float32 [256, 128], replicated
- grad_ada_w: float32 [128, 4608], replicated
- grad_ada_b: float32 [4608], replicated
- grad_gain_one: float32 [768], replicated
- grad_w_qkv: float32 [768, 2304], P('fsdp', 'tensor')
- grad_w_out: float32 [768, 768], P('tensor', 'fsdp')
- grad_gain_two: float32 [768], replicated
- grad_w_up: float32 [768, 3072], P('fsdp', 'tensor')
- grad_b_up: float32 [3072], replicated
- grad_w_down: float32 [3072, 768], P('tensor', 'fsdp')
- grad_b_down: float32 [768], replicated
The draws below stay inside these ranges and needn't reach their ends.
Inputs may be any that keep to these rules, and one draw needn't show every extreme that they name: `segments`: along each sequence segment numbers never fall; 1 to 4 are its documents in order, each present, and 0 marks the padding at its end, present in every sequence. No document has more than 2048 tokens, and in every sequence one document has exactly 2048.
All inputs are finite; a program needn't handle non-finite values.
Results may differ from the reference program's by a relative error of at most 0.02.
Values may be sent and summed in bfloat16 or wider, within the bound.
A program may use at most 768 MiB of HBM per device.

```python
from functools import partial
import jax
import jax.numpy as jnp
from jax import lax

D = 768
HEADS = 12
HDIM = 64
FF = 3072
COND = 128
STEPS = 256
NDOC = 4
SEQ_LEN = 4096
DOC_MOST = 2048
NSEQ = 8


def draw_segments(key, part):
    span = SEQ_LEN // NDOC
    reach = max(span // 8, 1)
    key_long, key_pad, key_cut = jax.random.split(jax.random.fold_in(key, 11), 3)
    long_doc = jax.random.randint(key_long, (NSEQ, 1), 1, NDOC + 1).astype(jnp.int32)
    padding = jax.random.randint(key_pad, (NSEQ, 1), 1, max(span // 4, 2)).astype(jnp.int32)
    rest = (SEQ_LEN - DOC_MOST - padding).astype(jnp.int32)
    jitter = jax.random.randint(key_cut, (NSEQ, NDOC - 2), -reach, reach + 1).astype(jnp.int32)
    inner = jnp.arange(1, NDOC - 1, dtype=jnp.int32)[None, :] * rest // (NDOC - 1) + jitter
    bounds = jnp.concatenate([jnp.zeros((NSEQ, 1), jnp.int32), inner, rest], axis=1)
    others = bounds[:, 1:] - bounds[:, :-1]
    documents = jnp.arange(1, NDOC + 1, dtype=jnp.int32)[None, :]
    place = documents - 1 - (documents > long_doc).astype(jnp.int32)
    place = jnp.clip(place, 0, NDOC - 2)
    picked = jnp.take_along_axis(others, place, axis=1)
    lengths = jnp.where(documents == long_doc, DOC_MOST, picked).astype(jnp.int32)
    ends = jnp.cumsum(lengths, axis=1).astype(jnp.int32)
    indices = jnp.arange(SEQ_LEN, dtype=jnp.int32)
    counted = jnp.sum((indices[None, :, None] >= ends[:, None, :NDOC - 1]).astype(jnp.int32), axis=2)
    live_end = ends[:, NDOC - 1:NDOC]
    return jnp.where(indices[None, :] < live_end, counted + 1, 0).astype(jnp.int32)


def place_ends(values, stream_key, least, high):
    dims = values.shape
    spot = [jax.random.randint(jax.random.fold_in(stream_key, axis), (), 0, dims[axis]) for axis in range(len(dims))]
    values = values.at[tuple(spot)].set(least)
    longest = dims.index(max(dims))
    spot[longest] = (spot[longest] + 1) % dims[longest]
    return values.at[tuple(spot)].set(high)


def block_levels(stream_key, shape, shards, low, high):
    def one(axis_at, blocks):
        draws = jax.random.uniform(jax.random.fold_in(jax.random.fold_in(stream_key, 6), axis_at), (blocks,), jnp.float32, low / len(shards), high / len(shards))
        return jnp.repeat(jnp.exp(draws), shape[axis_at] // blocks).reshape((-1,) + (1,) * (len(shape) - axis_at - 1))

    factor_of = one(*shards[0])
    for cut in shards[1:]:
        factor_of = factor_of * one(*cut)
    return factor_of


def bell_draw(stream_key, extent, deviation, limit, cuts=(), kind=jnp.bfloat16):
    values = deviation * jax.random.normal(stream_key, extent, jnp.float32)
    if cuts:
        values = values * block_levels(stream_key, extent, cuts, -0.22, 0.18)
    return jnp.clip(values, -limit, limit).astype(kind)


def setup_inputs(seed: int = 0) -> dict:
    keys = jax.random.split(jax.random.key(seed), 16)
    tokens = bell_draw(keys[0], (NSEQ, SEQ_LEN, D), 1.0, 6.0, ((0, 4), (1, 2)))
    cotangent = bell_draw(keys[1], (NSEQ, SEQ_LEN, D), 1.0, 6.0, ((0, 4), (1, 2)))
    segments = draw_segments(jax.random.fold_in(keys[15], 71), 0)
    steps = place_ends(jax.random.randint(keys[3], (NSEQ,), 0, STEPS), jax.random.fold_in(keys[3], 1), 0, STEPS - 1).astype(jnp.int32)
    table = bell_draw(keys[4], (STEPS, COND), 1.0, 5.0)
    ada_w = bell_draw(keys[5], (COND, 6 * D), COND ** -0.5, 0.5)
    ada_b = jnp.clip(1.0 + 0.18 * jax.random.normal(keys[6], (6 * D,), jnp.float32), 0.099609375, 1.8984375).astype(jnp.bfloat16)
    gain_one = jnp.clip(1.0 + 0.18 * jax.random.normal(keys[7], (D,), jnp.float32), 0.099609375, 1.8984375).astype(jnp.bfloat16)
    w_qkv = bell_draw(keys[8], (D, 3 * D), (4 * D) ** -0.5, 0.109375, ((0, 4), (1, 4)))
    w_out = bell_draw(keys[9], (D, D), 4 ** -0.5, 3.0, ((0, 4), (1, 4)))
    gain_two = jnp.clip(1.0 + 0.18 * jax.random.normal(keys[10], (D,), jnp.float32), 0.099609375, 1.8984375).astype(jnp.bfloat16)
    w_up = bell_draw(keys[11], (D, FF), (4 * D) ** -0.5, 0.109375, ((0, 4), (1, 4)))
    b_up = bell_draw(keys[12], (FF,), 0.5, 3.0)
    w_down = bell_draw(keys[13], (FF, D), (FF // 2) ** -0.5, 0.15625, ((0, 4), (1, 4)))
    b_down = bell_draw(keys[14], (D,), 0.5, 3.0)
    return dict(tokens=tokens, cotangent=cotangent, segments=segments, steps=steps, table=table, ada_w=ada_w, ada_b=ada_b, gain_one=gain_one, w_qkv=w_qkv, w_out=w_out, gain_two=gain_two, w_up=w_up, b_up=b_up, w_down=w_down, b_down=b_down)


@jax.custom_vjp
def low(v):
    return lax.optimization_barrier(v.astype(jnp.bfloat16)).astype(jnp.float32)

@jax.custom_vjp
def low_back(v):
    return v

def low_keep(v):
    return (low(v), None)

def low_pass(kept, grad):
    return (grad,)

def back_keep(v):
    return (v, None)

def back_low(kept, grad):
    return (low(grad),)
low.defvjp(low_keep, low_pass)
low_back.defvjp(back_keep, back_low)
precise = lax.Precision.HIGHEST

def matmul(left_side, right_side):
    return jnp.dot(left_side, right_side, precision=precise, preferred_element_type=jnp.float32)

def normalize(operand):
    center = operand - lax.optimization_barrier(jnp.mean(operand, axis=-1, keepdims=True))
    spread = lax.optimization_barrier(jnp.mean(center * center, axis=-1, keepdims=True))
    return center * lax.rsqrt(spread + 1e-05)

def positions(segment):
    indices = jnp.arange(segment.shape[0], dtype=jnp.int32)
    change = jnp.concatenate([jnp.ones((1,), jnp.bool_), segment[1:] != segment[:-1]])
    starts = lax.cummax(jnp.where(change, indices, 0).astype(jnp.int32), axis=0)
    return indices - starts

def rotate(operand, offsets):
    half_width = operand.shape[-1] // 2
    frequency = 10000.0 ** (-jnp.arange(half_width, dtype=jnp.float32) / half_width)
    angles = offsets.astype(jnp.float32)[:, None] * frequency[None, :]
    cosine = jnp.cos(angles)[:, None, :]
    sine_part = jnp.sin(angles)[:, None, :]
    front_half = operand[..., :half_width]
    second = operand[..., half_width:]
    return jnp.concatenate([front_half * cosine - second * sine_part, front_half * sine_part + second * cosine], axis=-1)

def attend_head(element, allowed):
    queries, key_rows, values = element
    scores = low_back(matmul(queries, key_rows.T) * 0.125)
    scores = jnp.where(allowed, scores, -1e+30)
    chances = jax.nn.softmax(scores, axis=-1)
    return matmul(low(chances), values)

def heads_first(operand):
    return jnp.transpose(operand, (1, 0, 2))

def one_sequence(weights, inputs_row, segment, step_index):
    table, ada_w, ada_b, gain_one, w_qkv, w_out, gain_two, w_up, b_up, w_down, b_down = weights
    length = inputs_row.shape[0]
    model_width = inputs_row.shape[1]
    embedding = jax.nn.silu(table[step_index])
    modulation = matmul(embedding[None, :], ada_w)[0] + ada_b
    shift_one, scale_one, gate_one, shift_two, scale_two, gate_two = jnp.split(modulation, 6)
    offsets = positions(segment)
    allowed = segment[:, None] == segment[None, :]
    entry_one = normalize(inputs_row) * gain_one * (1.0 + scale_one) + shift_one
    projected = low_back(matmul(low(entry_one), w_qkv)).reshape(length, HEADS, 3, HDIM)
    queries = low(rotate(projected[:, :, 0], offsets))
    key_rows = low(rotate(projected[:, :, 1], offsets))
    values = low(projected[:, :, 2])
    mixture = lax.map(jax.checkpoint(partial(attend_head, allowed=allowed)), (heads_first(queries), heads_first(key_rows), heads_first(values)))
    mixture = jnp.transpose(mixture, (1, 0, 2)).reshape(length, model_width)
    attended = low_back(matmul(low(low_back(mixture)), w_out))
    middle = inputs_row + gate_one * attended
    entry_two = normalize(middle) * gain_two * (1.0 + scale_two) + shift_two
    hidden = low_back(matmul(low(entry_two), w_up) + b_up)
    activated = jax.nn.gelu(hidden, approximate=True)
    output = low_back(matmul(low(activated), w_down) + b_down)
    return middle + gate_two * output

def reference(tokens, cotangent, segments, steps, table, ada_w, ada_b, gain_one, w_qkv, w_out, gain_two, w_up, b_up, w_down, b_down):
    weights = tuple((array.astype(jnp.float32) for array in (table, ada_w, ada_b, gain_one, w_qkv, w_out, gain_two, w_up, b_up, w_down, b_down)))
    inputs = tokens.astype(jnp.float32)

    def forward(weights, inputs):

        def advance(carried, element):
            inputs_row, segment, step_index = element
            return (carried, one_sequence(weights, inputs_row, segment, step_index))
        unused, results = lax.scan(jax.checkpoint(advance), jnp.zeros((), jnp.float32), (inputs, segments, steps))
        return results
    results, pullback = jax.vjp(forward, weights, inputs)
    valid = (segments != 0).astype(jnp.float32)[..., None]
    grad_weights, grad_inputs = pullback(cotangent.astype(jnp.float32) * valid)
    return (results.astype(jnp.bfloat16), grad_inputs, grad_weights[0], grad_weights[1], grad_weights[2], grad_weights[3], grad_weights[4], grad_weights[5], grad_weights[6], grad_weights[7], grad_weights[8], grad_weights[9], grad_weights[10])
```

```python
import math
from functools import partial

import jax
import jax.numpy as jnp
from jax import lax
from jax.experimental import pallas as pl
from jax.experimental.pallas import tpu as pltpu
from jax.sharding import PartitionSpec as P

HDIM = 64
HALF = HDIM // 2
SEGMENTS = 5
WIDE = 128
MASKED = 2.0**100
LOG2E = math.log2(math.e)
SAFE_EXPONENT = 60.0
EPSILON = 1e-05
VMEM = 56 * 2**20


precise = lax.Precision.HIGHEST
f32 = jnp.float32
bf16 = jnp.bfloat16


def product(left_side, right_side):
    return jnp.dot(left_side, right_side, preferred_element_type=jnp.float32)


def transposed(left_side, right_side):
    return lax.dot_general(
        left_side, right_side, (((0,), (0,)), ((), ())), preferred_element_type=jnp.float32
    )


def against(left_side, right_side):
    return lax.dot_general(
        left_side, right_side, (((1,), (1,)), ((), ())), preferred_element_type=jnp.float32
    )


def exact_product(left_side, right_side):
    return jnp.dot(left_side, right_side, precision=precise, preferred_element_type=jnp.float32)


def exact_transposed(left_side, right_side):
    return lax.dot_general(
        left_side,
        right_side,
        (((0,), (0,)), ((), ())),
        precision=precise,
        preferred_element_type=jnp.float32,
    )


def exact_against(left_side, right_side):
    return lax.dot_general(
        left_side,
        right_side,
        (((1,), (1,)), ((), ())),
        precision=precise,
        preferred_element_type=jnp.float32,
    )


def document_bounds(segment):
    indices = jnp.arange(segment.shape[-1], dtype=jnp.int32)
    same = segment[..., None, :] == jnp.arange(SEGMENTS, dtype=jnp.int32)[:, None]
    starts = jnp.min(jnp.where(same, indices, segment.shape[-1]), axis=-1)
    ends = jnp.max(jnp.where(same, indices + 1, 0), axis=-1)
    return same, starts, ends


def positions(segment):
    same, starts, _ = document_bounds(segment)
    first = jnp.sum(jnp.where(same, starts[..., :, None], 0), axis=-2)
    return jnp.arange(segment.shape[-1], dtype=jnp.int32) - first


def frequencies():
    return 10000.0 ** (-jnp.arange(HALF, dtype=jnp.float32) / HALF)


def entry_kernel(
    base_ref,
    rows_ref,
    gain_ref,
    shift_ref,
    weight_ref,
    cosine_ref,
    sine_ref,
    segment_ref,
    *refs,
    heads,
):
    del base_ref
    query_ref, key_ref, key_t_ref, value_ref, value_t_ref, hat_ref, scale_ref, norm_ref = refs[-8:]
    inputs = rows_ref[0].astype(f32).T
    center = inputs - jnp.mean(inputs, axis=0, keepdims=True)
    scaling = lax.rsqrt(jnp.mean(center * center, axis=0, keepdims=True) + EPSILON)
    hat = center * scaling
    hat_ref[...] = hat.astype(bf16)
    scale_ref[...] = scaling
    entry = (hat * gain_ref[...] + shift_ref[...]).astype(bf16)
    projected = product(weight_ref[...], entry)
    cosine = cosine_ref[...]
    sine = sine_ref[...]
    tokens = cosine.shape[1]
    group = heads * HDIM
    segment = segment_ref[...]
    number = lax.broadcasted_iota(jnp.int32, (WIDE - HDIM, tokens), 0)
    same = (number == segment).astype(f32)
    extra_query = same
    extra_key = jnp.where(
        number < SEGMENTS, (same - 1.0) * MASKED, jnp.where(number < SEGMENTS + 3, 1.0, 0.0)
    )
    extra_value = jnp.where(number < 3, 1.0, 0.0)
    norms = []
    for head in range(heads):

        def turned(kind, factor):
            at = kind * group + head * HDIM
            front = projected[at : at + HALF]
            back = projected[at + HALF : at + HDIM]
            return jnp.concatenate(
                [(front * cosine - back * sine) * factor, (front * sine + back * cosine) * factor],
                axis=0,
            )

        queries = turned(0, 0.125 * LOG2E)
        keys = turned(1, 1.0)
        values = projected[2 * group + head * HDIM : 2 * group + (head + 1) * HDIM]
        norms.append(jnp.sum(queries * queries, axis=0, keepdims=True))
        norms.append(jnp.sum(keys * keys, axis=0, keepdims=True))
        query_ref[head] = jnp.concatenate([queries, extra_query], axis=0).astype(bf16)
        key_ref[head] = jnp.concatenate([keys, extra_key], axis=0).T.astype(bf16)
        key_t_ref[head] = keys.astype(bf16)
        wide_values = jnp.concatenate([values, extra_value], axis=0)
        value_ref[head] = wide_values.T.astype(bf16)
        value_t_ref[head] = wide_values[: value_t_ref.shape[1]].astype(bf16)
    norms += [jnp.zeros_like(norms[0])] * (norm_ref.shape[0] - len(norms))
    norm_ref[...] = jnp.concatenate(norms, axis=0)


def entry_call(base, rows, row_index, gain, shift, weight, cosine, sine, segment, earlier, tile):
    length = cosine.shape[1]
    width, depth = weight.shape
    heads = width // (3 * HDIM)
    steps = rows.shape[1] // tile
    lanes = lambda i, base: (0, base[0] + i)
    heads_lanes = lambda i, base: (0, 0, base[0] + i)
    heads_rows = lambda i, base: (0, base[0] + i, 0)
    whole = lambda i, base: (0, 0)
    shapes = [
        jax.ShapeDtypeStruct((heads, WIDE, length), bf16),
        jax.ShapeDtypeStruct((heads, length, WIDE), bf16),
        jax.ShapeDtypeStruct((heads, HDIM, length), bf16),
        jax.ShapeDtypeStruct((heads, length, WIDE), bf16),
        jax.ShapeDtypeStruct((heads, HDIM + 16, length), bf16),
        jax.ShapeDtypeStruct((depth, length), bf16),
        jax.ShapeDtypeStruct((1, length), f32),
        jax.ShapeDtypeStruct((8, length), f32),
    ]
    out_specs = [
        pl.BlockSpec((heads, WIDE, tile), heads_lanes),
        pl.BlockSpec((heads, tile, WIDE), heads_rows),
        pl.BlockSpec((heads, HDIM, tile), heads_lanes),
        pl.BlockSpec((heads, tile, WIDE), heads_rows),
        pl.BlockSpec((heads, HDIM + 16, tile), heads_lanes),
        pl.BlockSpec((depth, tile), lanes),
        pl.BlockSpec((1, tile), lanes),
        pl.BlockSpec((8, tile), lanes),
    ]
    operands = [rows, gain, shift, weight, cosine, sine, segment]
    in_specs = [
        pl.BlockSpec((1, tile, depth), lambda i, base: (base[1], i, 0)),
        pl.BlockSpec((depth, 1), whole),
        pl.BlockSpec((depth, 1), whole),
        pl.BlockSpec((width, depth), whole),
        pl.BlockSpec((HALF, tile), lanes),
        pl.BlockSpec((HALF, tile), lanes),
        pl.BlockSpec((1, tile), lanes),
    ]
    aliases = {}
    if earlier is not None:
        aliases = {1 + len(operands) + k: k for k in range(len(shapes))}
        operands += list(earlier)
        in_specs += [pl.BlockSpec(memory_space=pl.ANY)] * len(shapes)
    return pl.pallas_call(
        partial(entry_kernel, heads=heads),
        grid_spec=pltpu.PrefetchScalarGridSpec(
            num_scalar_prefetch=1, grid=(steps,), in_specs=in_specs, out_specs=out_specs
        ),
        out_shape=shapes,
        input_output_aliases=aliases,
        compiler_params=pltpu.CompilerParams(vmem_limit_bytes=VMEM),
        name="entry",
    )(jnp.stack([base, row_index]).astype(jnp.int32), *operands)


def attend_kernel(range_ref, query_ref, key_ref, value_ref, out_ref, told_ref, total_ref, top_ref, *, block):
    step = pl.program_id(0)
    first, last = range_ref[0, step], range_ref[1, step]
    heads = query_ref.shape[0]
    total_ref[...] = jnp.zeros_like(total_ref)

    def scores(head, at):
        return product(key_ref[head, pl.ds(at, block), :], query_ref[head])

    def mix(head, at, weights):
        return product(value_ref[head, :, pl.ds(at, block)], weights)

    @pl.when(range_ref[2, 0] == 1)
    def _():
        top_ref[...] = jnp.zeros_like(top_ref)

        def body(number, carry):
            at = pl.multiple_of(number * block, block)
            raw = [scores(head, at) for head in range(heads)]
            weights = [jnp.exp2(one).astype(bf16) for one in raw]
            for head in range(heads):
                total_ref[head] += mix(head, at, weights[head])
            return carry

        lax.fori_loop(first, last, body, 0)

    @pl.when(range_ref[2, 0] != 1)
    def _():
        top_ref[...] = jnp.full_like(top_ref, -3e38)

        def body(number, carry):
            at = pl.multiple_of(number * block, block)
            for head in range(heads):
                raw = scores(head, at)
                before = top_ref[head]
                top = jnp.maximum(before, jnp.max(raw, axis=0, keepdims=True))
                weights = jnp.exp2(raw - top).astype(bf16)
                total_ref[head] = total_ref[head] * jnp.exp2(before - top) + mix(head, at, weights)
                top_ref[head] = top
            return carry

        lax.fori_loop(first, last, body, 0)

    tile = query_ref.shape[2]
    number = lax.broadcasted_iota(jnp.int32, (16, tile), 0)
    for head in range(heads):
        total = total_ref[head]
        mass = total[HDIM : HDIM + 1]
        out_ref[0, pl.ds(head * HDIM, HDIM), :] = (total[:HDIM] * (1.0 / mass)).astype(bf16)
        rows = split_rows(-(top_ref[head] + jnp.log2(mass)), number, SEGMENTS)
        told_ref[head, :HDIM, :] = query_ref[head, :HDIM, :]
        told_ref[head, HDIM : HDIM + 16, :] = jnp.where(
            number < SEGMENTS, query_ref[head, HDIM : HDIM + 16, :].astype(f32), rows
        ).astype(bf16)
        told_ref[head, HDIM + 16 :, :] = query_ref[head, HDIM + 16 :, :]


def split_rows(values, number, first):
    high = values.astype(bf16).astype(f32)
    rest = values - high
    middle = rest.astype(bf16).astype(f32)
    low = rest - middle
    return jnp.where(
        number == first,
        high,
        jnp.where(number == first + 1, middle, jnp.where(number == first + 2, low, 0.0)),
    )


def attend_call(ranges, queries, keys, values_t, tile, block):
    heads, _, length = queries.shape
    rows = values_t.shape[1]
    return pl.pallas_call(
        partial(attend_kernel, block=block),
        grid_spec=pltpu.PrefetchScalarGridSpec(
            num_scalar_prefetch=1,
            grid=(length // tile,),
            in_specs=[
                pl.BlockSpec((heads, WIDE, tile), lambda i, r: (0, 0, i)),
                pl.BlockSpec((heads, length, WIDE), lambda i, r: (0, 0, 0)),
                pl.BlockSpec((heads, rows, length), lambda i, r: (0, 0, 0)),
            ],
            out_specs=[
                pl.BlockSpec((1, heads * HDIM, tile), lambda i, r: (i, 0, 0)),
                pl.BlockSpec((heads, WIDE, tile), lambda i, r: (0, 0, i)),
            ],
            scratch_shapes=[
                pltpu.VMEM((heads, rows, tile), f32),
                pltpu.VMEM((heads, 1, tile), f32),
            ],
        ),
        out_shape=[
            jax.ShapeDtypeStruct((length // tile, heads * HDIM, tile), bf16),
            jax.ShapeDtypeStruct((heads, WIDE, length), bf16),
        ],
        compiler_params=pltpu.CompilerParams(vmem_limit_bytes=VMEM),
        name="attend",
    )(ranges, queries, keys, values_t)


def attend_back_kernel(
    range_ref,
    query_ref,
    key_ref,
    key_t_ref,
    value_ref,
    mixture_ref,
    grad_ref,
    cosine_ref,
    sine_ref,
    grad_query_ref,
    grad_key_ref,
    grad_value_ref,
    wide_ref,
    query_total,
    key_total,
    value_total,
    *,
    block,
):
    step = pl.program_id(0)
    first, last = range_ref[0, step], range_ref[1, step]
    heads, _, tile = query_ref.shape

    @pl.when(step == 0)
    def _():
        wide_ref[...] = jnp.zeros_like(wide_ref)
        key_total[...] = jnp.zeros_like(key_total)
        value_total[...] = jnp.zeros_like(value_total)

    number = lax.broadcasted_iota(jnp.int32, (16, tile), 0)
    query_total[...] = jnp.zeros_like(query_total)
    for head in range(heads):
        at = pl.ds(head * HDIM, HDIM)
        grad = grad_ref[0, at, :]
        delta = jnp.sum(grad.astype(f32) * mixture_ref[0, at, :].astype(f32), axis=0, keepdims=True)
        wide_ref[head, :HDIM, :] = grad
        wide_ref[head, HDIM : HDIM + 16, :] = split_rows(-delta, number, 0).astype(bf16)

    def body(number, carry):
        at = pl.multiple_of(number * block, block)
        rows = pl.ds(at, block)
        raw = [product(key_ref[head, rows, :], query_ref[head]) for head in range(heads)]
        slope = [product(value_ref[head, rows, :], wide_ref[head]) for head in range(heads)]
        for head in range(heads):
            weights = jnp.exp2(raw[head])
            grad_scores = (weights * slope[head]).astype(bf16)
            query_total[head] += product(key_t_ref[head, :, rows], grad_scores)
            key_total[head, :, rows] += against(query_ref[head, :HDIM, :], grad_scores)
            value_total[head, :, rows] += against(wide_ref[head, :HDIM, :], weights.astype(bf16))
        return carry

    lax.fori_loop(first, last, body, 0)

    def turned_back(grads, cosine, sine):
        front, back = grads[:HALF], grads[HALF:]
        return jnp.concatenate([front * cosine + back * sine, back * cosine - front * sine], axis=0)

    own = pl.ds(pl.multiple_of(step * tile, tile), tile)
    for head in range(heads):
        at = pl.ds(head * HDIM, HDIM)
        grad_query_ref[at, :] = turned_back(
            query_total[head] * 0.125, cosine_ref[:, own], sine_ref[:, own]
        ).astype(bf16)

    @pl.when(step == pl.num_programs(0) - 1)
    def _():
        for head in range(heads):
            at = pl.ds(head * HDIM, HDIM)
            grad_key_ref[at, :] = turned_back(
                key_total[head] * (1.0 / LOG2E), cosine_ref[...], sine_ref[...]
            ).astype(bf16)
            grad_value_ref[at, :] = value_total[head].astype(bf16)


def attend_back_call(
    ranges, queries, keys, keys_t, values, mixture, grad_mixture, cosine, sine, tile, block
):
    heads, _, length = queries.shape
    group = heads * HDIM
    whole2 = lambda i, r: (0, 0)
    whole3 = lambda i, r: (0, 0, 0)
    return pl.pallas_call(
        partial(attend_back_kernel, block=block),
        grid_spec=pltpu.PrefetchScalarGridSpec(
            num_scalar_prefetch=1,
            grid=(length // tile,),
            in_specs=[
                pl.BlockSpec((heads, WIDE, tile), lambda i, r: (0, 0, i)),
                pl.BlockSpec((heads, length, WIDE), whole3),
                pl.BlockSpec((heads, HDIM, length), whole3),
                pl.BlockSpec((heads, length, WIDE), whole3),
                pl.BlockSpec((1, group, tile), lambda i, r: (i, 0, 0)),
                pl.BlockSpec((1, group, tile), lambda i, r: (i, 0, 0)),
                pl.BlockSpec((HALF, length), whole2),
                pl.BlockSpec((HALF, length), whole2),
            ],
            out_specs=[
                pl.BlockSpec((group, tile), lambda i, r: (0, i)),
                pl.BlockSpec((group, length), whole2),
                pl.BlockSpec((group, length), whole2),
            ],
            scratch_shapes=[
                pltpu.VMEM((heads, WIDE, tile), bf16),
                pltpu.VMEM((heads, HDIM, tile), f32),
                pltpu.VMEM((heads, HDIM, length), f32),
                pltpu.VMEM((heads, HDIM, length), f32),
            ],
        ),
        out_shape=[jax.ShapeDtypeStruct((group, length), bf16)] * 3,
        compiler_params=pltpu.CompilerParams(vmem_limit_bytes=VMEM),
        name="attend_back",
    )(ranges, queries, keys, keys_t, values, mixture, grad_mixture, cosine, sine)


def middle_kernel(
    base_ref,
    mixture_ref,
    rows_ref,
    cotangent_ref,
    valid_ref,
    mod_ref,
    up_bias_ref,
    down_bias_ref,
    out_weight_ref,
    up_ref,
    down_ref,
    result_ref,
    grad_mixture_ref,
    grad_middle_ref,
    entry_ref,
    grad_output_ref,
    active_ref,
    grad_hidden_ref,
    grad_out_ref,
    sums_ref,
    bias_sums_ref,
):
    del base_ref
    sequence, step = pl.program_id(0), pl.program_id(1)
    mods = mod_ref[0]
    gate_one, shift_two, gain_two, gate_two = (mods[k : k + 1] for k in range(4))
    mixture_t = mixture_ref[0]
    inputs = rows_ref[0].astype(f32)
    attended = product(mixture_t.T, out_weight_ref[...])
    middle = inputs + gate_one * attended
    center = middle - jnp.mean(middle, axis=-1, keepdims=True)
    scaling = lax.rsqrt(jnp.mean(center * center, axis=-1, keepdims=True) + EPSILON)
    hat = center * scaling
    entry = (hat * gain_two + shift_two).astype(bf16)
    grad_result = cotangent_ref[0].astype(f32) * valid_ref[0]
    grad_output = (gate_two * grad_result).astype(bf16)
    entry_ref[...] = entry.T
    grad_output_ref[...] = grad_output.T

    @pl.when((sequence == 0) & (step == 0))
    def _():
        bias_sums_ref[...] = jnp.zeros_like(bias_sums_ref)
        grad_out_ref[...] = jnp.zeros_like(grad_out_ref)

    output = down_bias_ref[...]
    grad_entry = 0.0
    root = math.sqrt(2.0 / math.pi)
    for part in range(up_ref.shape[0]):
        hidden = product(entry, up_ref[part]) + up_bias_ref[part]
        square = hidden * hidden
        bent = jnp.tanh(root * hidden * (1.0 + 0.044715 * square))
        half = 0.5 * (1.0 + bent)
        active = (hidden * half).astype(bf16)
        slope = half + (0.5 * root) * hidden * (1.0 - bent * bent) * (1.0 + 0.134145 * square)
        grad_hidden_wide = product(grad_output, down_ref[part]) * slope
        grad_hidden = grad_hidden_wide.astype(bf16)
        output = output + against(active, down_ref[part])
        grad_entry = grad_entry + against(grad_hidden, up_ref[part])
        active_ref[part] = active
        grad_hidden_ref[part] = grad_hidden
        bias_sums_ref[part] += jnp.sum(grad_hidden.astype(f32), axis=0, keepdims=True)
    result_ref[0] = (middle + gate_two * output).astype(bf16)
    grad_lifted = grad_entry * gain_two
    grad_middle = grad_result + scaling * (
        grad_lifted
        - jnp.mean(grad_lifted, axis=-1, keepdims=True)
        - hat * jnp.mean(grad_lifted * hat, axis=-1, keepdims=True)
    )
    grad_attended = (gate_one * grad_middle).astype(bf16)
    grad_mixture_ref[0] = against(out_weight_ref[...], grad_attended).astype(bf16)
    grad_middle_ref[0] = grad_middle.T.astype(bf16)
    grad_out_ref[...] += product(mixture_t, grad_attended)

    @pl.when(step == 0)
    def _():
        sums_ref[...] = jnp.zeros_like(sums_ref)

    rows = [
        jnp.sum(grad_middle * attended, axis=0, keepdims=True),
        jnp.sum(grad_entry, axis=0, keepdims=True),
        jnp.sum(grad_entry * hat, axis=0, keepdims=True),
        jnp.sum(grad_result * output, axis=0, keepdims=True),
        jnp.sum(grad_output.astype(f32), axis=0, keepdims=True),
    ]
    rows += [jnp.zeros_like(rows[0])] * (sums_ref.shape[1] - len(rows))
    sums_ref[0] += jnp.concatenate(rows, axis=0)


def middle_call(
    base, mixture, rows, cotangent, valid, mods, up_bias, down_bias, out_weight, up, down, tile
):
    sequences, depth, own = mixture.shape
    parts, _, part_width = up.shape
    steps = own // tile
    tokens = sequences * own
    at_rows = lambda s, i, b: (s, b[0] * steps + i, 0)
    own_rows = lambda s, i, b: (s, i, 0)
    own_lanes = lambda s, i, b: (s, 0, i)
    whole2 = lambda s, i, b: (0, 0)
    whole3 = lambda s, i, b: (0, 0, 0)
    once = pl.Buffered(1)
    return pl.pallas_call(
        middle_kernel,
        grid_spec=pltpu.PrefetchScalarGridSpec(
            num_scalar_prefetch=1,
            grid=(sequences, steps),
            in_specs=[
                pl.BlockSpec((1, depth, tile), own_lanes),
                pl.BlockSpec((1, tile, depth), at_rows),
                pl.BlockSpec((1, tile, depth), at_rows),
                pl.BlockSpec((1, tile, 1), own_rows),
                pl.BlockSpec((1, 8, depth), lambda s, i, b: (s, 0, 0)),
                pl.BlockSpec((parts, 1, part_width), whole3, pipeline_mode=once),
                pl.BlockSpec((1, depth), whole2, pipeline_mode=once),
                pl.BlockSpec((depth, depth), whole2, pipeline_mode=once),
                pl.BlockSpec((parts, depth, part_width), whole3, pipeline_mode=once),
                pl.BlockSpec((parts, depth, part_width), whole3, pipeline_mode=once),
            ],
            out_specs=[
                pl.BlockSpec((1, tile, depth), own_rows),
                pl.BlockSpec((1, depth, tile), own_lanes),
                pl.BlockSpec((1, depth, tile), own_lanes),
                pl.BlockSpec((depth, tile), lambda s, i, b: (0, s * steps + i)),
                pl.BlockSpec((depth, tile), lambda s, i, b: (0, s * steps + i)),
                pl.BlockSpec((parts, tile, part_width), lambda s, i, b: (0, s * steps + i, 0)),
                pl.BlockSpec((parts, tile, part_width), lambda s, i, b: (0, s * steps + i, 0)),
                pl.BlockSpec((depth, depth), whole2),
                pl.BlockSpec((1, 8, depth), lambda s, i, b: (s, 0, 0)),
                pl.BlockSpec((parts, 1, part_width), whole3),
            ],
        ),
        out_shape=[
            jax.ShapeDtypeStruct((sequences, own, depth), bf16),
            jax.ShapeDtypeStruct((sequences, depth, own), bf16),
            jax.ShapeDtypeStruct((sequences, depth, own), bf16),
            jax.ShapeDtypeStruct((depth, tokens), bf16),
            jax.ShapeDtypeStruct((depth, tokens), bf16),
            jax.ShapeDtypeStruct((parts, tokens, part_width), bf16),
            jax.ShapeDtypeStruct((parts, tokens, part_width), bf16),
            jax.ShapeDtypeStruct((depth, depth), f32),
            jax.ShapeDtypeStruct((sequences, 8, depth), f32),
            jax.ShapeDtypeStruct((parts, 1, part_width), f32),
        ],
        compiler_params=pltpu.CompilerParams(vmem_limit_bytes=VMEM),
        name="middle",
    )(base, mixture, rows, cotangent, valid, mods, up_bias, down_bias, out_weight, up, down)


def weights_kernel(entry_ref, grad_output_ref, active_ref, grad_hidden_ref, grad_up_ref, grad_down_ref):
    grad_up_ref[0] = product(entry_ref[...], grad_hidden_ref[0]).astype(bf16)
    grad_down_ref[0] = product(grad_output_ref[...], active_ref[0]).astype(bf16)


def weights_call(entry_t, grad_output_t, active, grad_hidden):
    depth, tokens = entry_t.shape
    parts, _, part_width = active.shape
    part = lambda i: (i, 0, 0)
    return pl.pallas_call(
        weights_kernel,
        grid=(parts,),
        in_specs=[
            pl.BlockSpec((depth, tokens), lambda i: (0, 0)),
            pl.BlockSpec((depth, tokens), lambda i: (0, 0)),
            pl.BlockSpec((1, tokens, part_width), part),
            pl.BlockSpec((1, tokens, part_width), part),
        ],
        out_specs=[pl.BlockSpec((1, depth, part_width), part)] * 2,
        out_shape=[jax.ShapeDtypeStruct((parts, depth, part_width), bf16)] * 2,
        compiler_params=pltpu.CompilerParams(vmem_limit_bytes=VMEM),
        name="weights",
    )(entry_t, grad_output_t, active, grad_hidden)


def entry_back_kernel(
    grad_query_ref,
    grad_key_ref,
    grad_value_ref,
    hat_ref,
    scale_ref,
    gain_ref,
    shift_ref,
    weight_ref,
    part_ref,
    grad_weight_ref,
    sums_ref,
):
    @pl.when(pl.program_id(0) == 0)
    def _():
        grad_weight_ref[...] = jnp.zeros_like(grad_weight_ref)
        sums_ref[...] = jnp.zeros_like(sums_ref)

    grads = jnp.concatenate([grad_query_ref[...], grad_key_ref[...], grad_value_ref[...]], axis=0)
    grad_entry = product(weight_ref[...], grads)
    hat = hat_ref[...].astype(f32)
    gain = gain_ref[...]
    entry = (hat * gain + shift_ref[...]).astype(bf16)
    grad_weight_ref[...] += against(grads, entry)
    grad_lifted = grad_entry * gain
    part_ref[0] = (
        scale_ref[...]
        * (
            grad_lifted
            - jnp.mean(grad_lifted, axis=0, keepdims=True)
            - hat * jnp.mean(grad_lifted * hat, axis=0, keepdims=True)
        )
    ).astype(bf16)
    weighted = grad_entry * hat
    for lane in range(0, grad_entry.shape[1], WIDE):
        sums_ref[0] += grad_entry[:, lane : lane + WIDE]
        sums_ref[1] += weighted[:, lane : lane + WIDE]


def entry_back_call(grad_query, grad_key, grad_value, hat_t, scaling, gain, shift, weight, blocks, tile):
    group, length = grad_query.shape
    depth = hat_t.shape[0]
    steps = length // blocks // tile
    lanes = lambda i: (0, i)
    whole = lambda i: (0, 0)
    return pl.pallas_call(
        entry_back_kernel,
        grid=(length // tile,),
        in_specs=[
            pl.BlockSpec((group, tile), lanes),
            pl.BlockSpec((group, tile), lanes),
            pl.BlockSpec((group, tile), lanes),
            pl.BlockSpec((depth, tile), lanes),
            pl.BlockSpec((1, tile), lanes),
            pl.BlockSpec((depth, 1), whole),
            pl.BlockSpec((depth, 1), whole),
            pl.BlockSpec((depth, 3 * group), whole),
        ],
        out_specs=[
            pl.BlockSpec((1, depth, tile), lambda i: (i // steps, 0, i % steps)),
            pl.BlockSpec((3 * group, depth), whole),
            pl.BlockSpec((2, depth, WIDE), lambda i: (0, 0, 0)),
        ],
        out_shape=[
            jax.ShapeDtypeStruct((blocks, depth, length // blocks), bf16),
            jax.ShapeDtypeStruct((3 * group, depth), f32),
            jax.ShapeDtypeStruct((2, depth, WIDE), f32),
        ],
        compiler_params=pltpu.CompilerParams(vmem_limit_bytes=VMEM),
        name="entry_back",
    )(grad_query, grad_key, grad_value, hat_t, scaling, gain, shift, weight)


def by_sequence(
    tokens,
    cotangent,
    segments,
    steps,
    table,
    ada_w,
    ada_b,
    gain_one,
    w_qkv,
    w_out,
    gain_two,
    w_up,
    b_up,
    w_down,
    b_down,
):
    fsdp, tensor = lax.axis_size("fsdp"), lax.axis_size("tensor")
    context = lax.axis_size("context")
    tensor_rank = lax.axis_index("tensor")
    context_rank = lax.axis_index("context")
    fsdp_rank = lax.axis_index("fsdp")
    sequences, own_rows, depth = tokens.shape
    length = segments.shape[1]
    group = w_out.shape[0]
    part_width = w_up.shape[1]
    heads = group // HDIM
    quarter = own_rows // tensor

    mine = lax.dynamic_slice_in_dim(tokens, tensor_rank * quarter, quarter, axis=1)
    partner = [(k, (k + 1) % context) for k in range(context)]
    arrived = lax.ppermute(
        lax.dynamic_index_in_dim(mine, lax.rem(context_rank + 1, context), 0, keepdims=True),
        "context",
        partner,
    )
    other_rows = lax.all_gather(arrived, "tensor", axis=1, tiled=True)

    by_kind = w_qkv.reshape(-1, heads, 3, HDIM).transpose(0, 2, 1, 3).reshape(-1, 3 * group)
    qkv = lax.all_gather(by_kind, "fsdp", axis=0, tiled=True)
    both = ("tensor", "fsdp")
    up = lax.all_gather(w_up, both, axis=0, tiled=True).reshape(tensor, depth, part_width)
    down = lax.all_gather(w_down.T, both, axis=0, tiled=True).reshape(tensor, depth, part_width)
    out_weight = (
        lax.all_gather(w_out, both, axis=0, tiled=False)
        .reshape(tensor, fsdp, group, depth // fsdp)
        .transpose(0, 2, 1, 3)
        .reshape(depth, depth)
    )

    all_steps = lax.all_gather(steps, "fsdp", axis=0, tiled=True)
    ada_full = ada_w.astype(f32)
    choose = (all_steps[:, None] == jnp.arange(table.shape[0], dtype=jnp.int32)[None, :]).astype(f32)
    before = exact_product(choose, table.astype(f32))
    embedding, silu_back = jax.vjp(jax.nn.silu, before)
    modulation = exact_product(embedding, ada_full) + ada_b.astype(f32)
    local_mods = lax.dynamic_slice_in_dim(modulation, fsdp_rank * sequences, sequences, axis=0)
    local_mods = local_mods.reshape(sequences, 6, depth)
    gain_first, gain_second = gain_one.astype(f32), gain_two.astype(f32)
    own_mods = lax.dynamic_index_in_dim(local_mods, context_rank, 0, keepdims=False)
    gain_column = (gain_first * (1.0 + own_mods[1]))[:, None]
    shift_column = own_mods[0][:, None]
    mods = jnp.stack(
        [
            local_mods[:, 2],
            local_mods[:, 3],
            gain_second * (1.0 + local_mods[:, 4]),
            local_mods[:, 5],
        ]
        + [jnp.zeros((sequences, depth), f32)] * 4,
        axis=1,
    )

    segment = lax.dynamic_index_in_dim(segments, context_rank, 0, keepdims=False)
    same, starts, ends = document_bounds(segment)
    offsets = jnp.arange(length, dtype=jnp.int32) - jnp.sum(jnp.where(same, starts[:, None], 0), axis=0)
    angles = frequencies()[:, None] * offsets.astype(f32)[None, :]
    cosine, sine = jnp.cos(angles), jnp.sin(angles)
    tile = length // (context * tensor)
    block = tile
    first_key = jnp.sum(jnp.where(same, starts[:, None], 0), axis=0)[::tile]
    last_key = jnp.sum(jnp.where(same, ends[:, None], 0), axis=0)[tile - 1 :: tile]

    entry = partial(
        entry_call,
        gain=gain_column,
        shift=shift_column,
        weight=qkv.T,
        cosine=cosine,
        sine=sine,
        segment=segment[None, :],
        tile=tile,
    )
    per_block = own_rows // tile
    made = entry(context_rank * per_block, tokens, context_rank, earlier=None)
    other = lax.rem(context_rank + context - 1, context)
    made = entry(other * per_block, other_rows, jnp.zeros_like(other), earlier=made)
    queries, keys, keys_t, values, values_t, hat_t, scaling, norms = made
    largest = jnp.max(norms, axis=1)[: 2 * heads].reshape(heads, 2)
    safe = jnp.max(largest[:, 0] * largest[:, 1]) <= SAFE_EXPONENT**2
    ranges = jnp.stack(
        [
            first_key // block,
            (last_key + block - 1) // block,
            jnp.broadcast_to(safe.astype(jnp.int32), first_key.shape),
        ]
    ).astype(jnp.int32)
    mixture, told = attend_call(ranges, queries, keys, values_t, tile, block)

    everyone = ("context", "tensor")
    own_mixture = lax.all_to_all(mixture, everyone, 0, 0, tiled=True).reshape(
        context, tensor * group, tile
    )
    own_segments = lax.dynamic_slice_in_dim(
        segments, context_rank * own_rows + tensor_rank * quarter, quarter, axis=1
    )
    valid = (own_segments != 0).astype(f32)[:, :, None]
    (
        result,
        grad_mixture,
        grad_middle,
        entry_t,
        grad_output_t,
        active,
        grad_hidden,
        grad_out,
        sums,
        bias_sums,
    ) = middle_call(
        tensor_rank[None].astype(jnp.int32),
        own_mixture,
        tokens,
        cotangent,
        valid,
        mods,
        b_up.astype(f32).reshape(tensor, 1, part_width),
        b_down.astype(f32)[None, :],
        out_weight,
        up,
        down,
        tile=min(tile, 256),
    )
    block_out = lax.all_gather(result, "tensor", axis=1, tiled=True)
    grad_mixture = lax.all_to_all(
        grad_mixture.reshape(context * tensor, group, tile), everyone, 0, 0, tiled=True
    )
    middle_slice = lax.all_to_all(grad_middle, "tensor", 1, 2, tiled=True)
    grad_up, grad_down = weights_call(entry_t, grad_output_t, active, grad_hidden)
    grad_out = (
        grad_out.astype(bf16)
        .reshape(tensor, group, fsdp, depth // fsdp)
        .transpose(0, 2, 1, 3)
        .reshape(tensor * fsdp, group * (depth // fsdp) // part_width, part_width)
    )
    pieces = jnp.concatenate(
        [
            grad_up.reshape(tensor * fsdp, -1, part_width),
            grad_down.reshape(tensor * fsdp, -1, part_width),
            grad_out,
        ],
        axis=1,
    )
    pieces = lax.psum_scatter(pieces, both, scatter_dimension=0, tiled=True)[0]
    pieces = lax.psum(pieces, "context").astype(f32)
    rows = depth // fsdp
    grad_w_up = pieces[:rows]
    grad_w_down = pieces[rows : 2 * rows].T
    grad_w_out = pieces[2 * rows :].reshape(group, depth // fsdp)

    grad_query, grad_key, grad_value = attend_back_call(
        ranges, told, keys, keys_t, values, mixture, grad_mixture, cosine, sine, tile, block
    )
    part, grad_qkv, entry_sums = entry_back_call(
        grad_query, grad_key, grad_value, hat_t, scaling, gain_column, shift_column, qkv, context, tile
    )
    part = lax.psum_scatter(part, "tensor", scatter_dimension=1, tiled=True)
    part = lax.all_to_all(part, "context", 0, 0, tiled=True)
    grad_tokens = jnp.swapaxes(part.astype(f32) + middle_slice.astype(f32), 1, 2)

    grad_qkv = (
        grad_qkv.astype(bf16).reshape(3 * group, fsdp, depth // fsdp).transpose(1, 0, 2)
    )
    grad_qkv = lax.psum_scatter(grad_qkv, "fsdp", scatter_dimension=0, tiled=True)[0]
    grad_qkv = lax.psum(grad_qkv, "context").astype(f32)
    grad_w_qkv = (
        grad_qkv.reshape(3, heads, HDIM, depth // fsdp).transpose(3, 1, 0, 2).reshape(-1, 3 * group)
    )

    entry_sums = jnp.sum(entry_sums, axis=2)
    is_own = (jnp.arange(sequences) == context_rank).astype(f32)[:, None]
    grad_mod = jnp.concatenate(
        [
            is_own * entry_sums[0],
            is_own * (entry_sums[1] * gain_first),
            sums[:, 0],
            sums[:, 1],
            sums[:, 2] * gain_second,
            sums[:, 3],
        ],
        axis=1,
    )
    grad_mod = lax.dynamic_update_slice_in_dim(
        jnp.zeros((fsdp * sequences, 6 * depth), f32), grad_mod, fsdp_rank * sequences, 0
    )
    (grad_mod, grad_gain_one, grad_gain_two, grad_b_up, grad_b_down) = lax.psum(
        (
            grad_mod,
            entry_sums[1] * (1.0 + own_mods[1]),
            jnp.sum(sums[:, 2] * (1.0 + local_mods[:, 4]), axis=0),
            bias_sums.reshape(-1),
            jnp.sum(sums[:, 4], axis=0),
        ),
        ("fsdp", "context", "tensor"),
    )
    grad_ada_b = jnp.sum(grad_mod, axis=0)
    grad_ada_w = exact_transposed(embedding, grad_mod)
    grad_before = silu_back(exact_against(grad_mod, ada_full))[0]
    grad_table = exact_transposed(choose, grad_before)
    return (
        block_out,
        grad_tokens,
        grad_table,
        grad_ada_w,
        grad_ada_b,
        grad_gain_one,
        grad_w_qkv,
        grad_w_out,
        grad_gain_two,
        grad_w_up,
        grad_b_up,
        grad_w_down,
        grad_b_down,
    )


def normalize(operand):
    center = operand - jnp.mean(operand, axis=-1, keepdims=True)
    scaling = lax.rsqrt(jnp.mean(center * center, axis=-1, keepdims=True) + 1e-05)
    return (center * scaling, scaling)


def norm_back(grad_hat, hatted, scaling):
    return scaling * (
        grad_hat
        - jnp.mean(grad_hat, axis=-1, keepdims=True)
        - hatted * jnp.mean(grad_hat * hatted, axis=-1, keepdims=True)
    )


def angles_of(offsets, half_width):
    frequency = 10000.0 ** (-jnp.arange(half_width, dtype=jnp.float32) / half_width)
    angles = offsets.astype(jnp.float32)[:, None] * frequency[None, :]
    return (jnp.cos(angles)[:, None, :], jnp.sin(angles)[:, None, :])


def rotate(operand, cosine, sine_part, direction):
    half_width = operand.shape[-1] // 2
    front_half = operand[..., :half_width]
    second = operand[..., half_width:]
    return jnp.concatenate(
        [
            front_half * cosine - direction * second * sine_part,
            direction * front_half * sine_part + second * cosine,
        ],
        axis=-1,
    )


def scores_of(queries, key_rows, allowed):
    raw_scores = (
        jnp.einsum("qhd,khd->hqk", queries, key_rows, preferred_element_type=jnp.float32) * 0.125
    )
    return jnp.where(allowed[None], raw_scores, -1e30)


def attend(queries, key_rows, values, allowed):
    scores = scores_of(queries, key_rows, allowed)
    row_max = jnp.max(scores, axis=-1, keepdims=True)
    weights_raw = jnp.exp(scores - row_max)
    row_total = jnp.sum(weights_raw, axis=-1, keepdims=True)
    weights_low = (weights_raw / row_total).astype(jnp.bfloat16)
    mixture = jnp.einsum("hqk,khd->qhd", weights_low, values, preferred_element_type=jnp.float32)
    return (mixture, row_max + jnp.log(row_total))


def attend_back(queries, key_rows, values, grad_mixture, logsum, allowed, row_delta):
    scores = scores_of(queries, key_rows, allowed)
    chances = jnp.exp(scores - logsum)
    grad_chances = jnp.einsum(
        "qhd,khd->hqk", grad_mixture, values, preferred_element_type=jnp.float32
    )
    row_delta = jnp.sum(chances * grad_chances, axis=-1, keepdims=True)
    grad_scores = (chances * (grad_chances - row_delta)).astype(jnp.bfloat16)
    return (chances.astype(jnp.bfloat16), grad_scores, row_delta)


def by_block(
    tokens,
    cotangent,
    segments,
    steps,
    table,
    ada_w,
    ada_b,
    gain_one,
    w_qkv,
    w_out,
    gain_two,
    w_up,
    b_up,
    w_down,
    b_down,
):
    w_qkv, w_up, w_out, w_down = (
        lax.all_gather(w_qkv, "fsdp", axis=0, tiled=True),
        lax.all_gather(w_up, "fsdp", axis=0, tiled=True),
        lax.all_gather(w_out, "fsdp", axis=1, tiled=True),
        lax.all_gather(w_down, "fsdp", axis=1, tiled=True),
    )
    tensor_rank = lax.axis_index("tensor")
    context_rank = lax.axis_index("context")
    sequences, own_rows, model_width = tokens.shape
    length = segments.shape[1]
    local_heads = w_out.shape[0] // HDIM
    hidden_width = w_up.shape[1]
    up_bias = lax.dynamic_slice_in_dim(b_up, tensor_rank * hidden_width, hidden_width).astype(
        jnp.float32
    )
    down_bias = b_down.astype(jnp.float32)
    gain_first = gain_one.astype(jnp.float32)
    gain_second = gain_two.astype(jnp.float32)
    leader = (tensor_rank == 0).astype(jnp.float32)
    ada_full = ada_w.astype(jnp.float32)
    choose = (steps[:, None] == jnp.arange(table.shape[0], dtype=jnp.int32)[None, :]).astype(
        jnp.float32
    )
    before = exact_product(choose, table.astype(jnp.float32))
    embedding, silu_back = jax.vjp(jax.nn.silu, before)
    modulation = exact_product(embedding, ada_full) + ada_b.astype(jnp.float32)
    grad_qkv = jnp.zeros(w_qkv.shape, jnp.float32)
    grad_out_w = jnp.zeros(w_out.shape, jnp.float32)
    grad_up = jnp.zeros(w_up.shape, jnp.float32)
    grad_down = jnp.zeros(w_down.shape, jnp.float32)
    grad_bias_up = jnp.zeros((hidden_width,), jnp.float32)
    grad_bias_down = jnp.zeros((model_width,), jnp.float32)
    grad_gain_first = jnp.zeros((model_width,), jnp.float32)
    grad_gain_second = jnp.zeros((model_width,), jnp.float32)
    results = []
    partial_inputs = []
    carried = []
    grad_mods = []
    for number in range(sequences):
        shift_one, scale_one, gate_one, shift_two, scale_two, gate_two = jnp.split(
            modulation[number], 6
        )
        segment = segments[number]
        offsets = positions(segment)
        own_segment = lax.dynamic_slice_in_dim(segment, context_rank * own_rows, own_rows)
        own_offsets = lax.dynamic_slice_in_dim(offsets, context_rank * own_rows, own_rows)
        cosine, sine_part = angles_of(own_offsets, HDIM // 2)
        allowed = own_segment[:, None] == segment[None, :]
        inputs_row = tokens[number].astype(jnp.float32)
        hat_one, scaling_one = normalize(inputs_row)
        lifted_one = hat_one * gain_first
        entry_one = (lifted_one * (1.0 + scale_one) + shift_one).astype(jnp.bfloat16)
        projected = product(entry_one, w_qkv).reshape(own_rows, local_heads, 3, HDIM)
        queries = rotate(projected[:, :, 0], cosine, sine_part, 1.0).astype(jnp.bfloat16)
        key_rows = rotate(projected[:, :, 1], cosine, sine_part, 1.0).astype(jnp.bfloat16)
        values = projected[:, :, 2].astype(jnp.bfloat16)
        key_value = jnp.stack([key_rows, values], axis=1).reshape(own_rows, 2 * local_heads * HDIM)
        gathered = lax.all_gather(key_value, "context", axis=0, tiled=True).reshape(
            length, 2, local_heads, HDIM
        )
        all_keys = gathered[:, 0]
        all_values = gathered[:, 1]
        mixture, logsum = attend(queries, all_keys, all_values, allowed)
        mixture_low = mixture.reshape(own_rows, local_heads * HDIM).astype(jnp.bfloat16)
        attended = lax.psum(product(mixture_low, w_out).astype(jnp.bfloat16), "tensor").astype(
            jnp.float32
        )
        middle = inputs_row + gate_one * attended
        hat_two, scaling_two = normalize(middle)
        lifted_two = hat_two * gain_second
        entry_two = (lifted_two * (1.0 + scale_two) + shift_two).astype(jnp.bfloat16)
        hidden = product(entry_two, w_up) + up_bias
        activated, gelu_back = jax.vjp(partial(jax.nn.gelu, approximate=True), hidden)
        activated_low = activated.astype(jnp.bfloat16)
        output = (
            lax.psum(product(activated_low, w_down).astype(jnp.bfloat16), "tensor").astype(
                jnp.float32
            )
            + down_bias
        )
        results.append((middle + gate_two * output).astype(jnp.bfloat16))
        valid = (own_segment != 0).astype(jnp.float32)[:, None]
        grad_result = cotangent[number].astype(jnp.float32) * valid
        grad_output = (gate_two * grad_result).astype(jnp.bfloat16)
        grad_gate_two = jnp.sum(grad_result * output, axis=0)
        grad_bias_down = grad_bias_down + jnp.sum(grad_output.astype(jnp.float32), axis=0)
        grad_down = grad_down + transposed(activated_low, grad_output)
        grad_active = against(grad_output, w_down)
        grad_hidden = gelu_back(grad_active)[0].astype(jnp.bfloat16)
        grad_bias_up = grad_bias_up + jnp.sum(grad_hidden.astype(jnp.float32), axis=0)
        grad_up = grad_up + transposed(entry_two, grad_hidden)
        grad_entry_two = against(grad_hidden, w_up)
        grad_shift_two = jnp.sum(grad_entry_two, axis=0)
        grad_scale_two = jnp.sum(grad_entry_two * lifted_two, axis=0)
        grad_lifted_two = grad_entry_two * (1.0 + scale_two)
        grad_gain_second = grad_gain_second + jnp.sum(grad_lifted_two * hat_two, axis=0)
        part_two = norm_back(grad_lifted_two * gain_second, hat_two, scaling_two)
        grad_middle = grad_result + lax.psum(part_two.astype(jnp.bfloat16), "tensor").astype(
            jnp.float32
        )
        grad_attended = (gate_one * grad_middle).astype(jnp.bfloat16)
        grad_gate_one = jnp.sum(grad_middle * attended, axis=0)
        grad_out_w = grad_out_w + transposed(mixture_low, grad_attended)
        grad_mixture = (
            against(grad_attended, w_out).astype(jnp.bfloat16).reshape(own_rows, local_heads, HDIM)
        )
        chances_low, grad_scores, row_delta = attend_back(
            queries, all_keys, all_values, grad_mixture, logsum, allowed, None
        )
        grad_queries = (
            jnp.einsum("hqk,khd->qhd", grad_scores, all_keys, preferred_element_type=jnp.float32)
            * 0.125
        )
        grad_all_keys = (
            jnp.einsum("hqk,qhd->khd", grad_scores, queries, preferred_element_type=jnp.float32)
            * 0.125
        )
        grad_all_values = jnp.einsum(
            "hqk,qhd->khd", chances_low, grad_mixture, preferred_element_type=jnp.float32
        )
        both_grads = jnp.stack([grad_all_keys, grad_all_values], axis=1).reshape(
            length, 2 * local_heads * HDIM
        )
        own_grads = (
            lax.psum_scatter(
                both_grads.astype(jnp.bfloat16), "context", scatter_dimension=0, tiled=True
            )
            .astype(jnp.float32)
            .reshape(own_rows, 2, local_heads, HDIM)
        )
        grad_keys = own_grads[:, 0]
        grad_values = own_grads[:, 1]
        grad_queries = rotate(grad_queries, cosine, sine_part, -1.0)
        grad_keys = rotate(grad_keys, cosine, sine_part, -1.0)
        grad_projected = (
            jnp.stack([grad_queries, grad_keys, grad_values], axis=2)
            .reshape(own_rows, local_heads * 3 * HDIM)
            .astype(jnp.bfloat16)
        )
        grad_qkv = grad_qkv + transposed(entry_one, grad_projected)
        grad_entry_one = against(grad_projected, w_qkv)
        grad_shift_one = jnp.sum(grad_entry_one, axis=0)
        grad_scale_one = jnp.sum(grad_entry_one * lifted_one, axis=0)
        grad_lifted_one = grad_entry_one * (1.0 + scale_one)
        grad_gain_first = grad_gain_first + jnp.sum(grad_lifted_one * hat_one, axis=0)
        partial_inputs.append(norm_back(grad_lifted_one * gain_first, hat_one, scaling_one))
        carried.append(grad_middle)
        grad_mods.append(
            jnp.concatenate(
                [
                    grad_shift_one,
                    grad_scale_one,
                    grad_gate_one * leader,
                    grad_shift_two,
                    grad_scale_two,
                    grad_gate_two * leader,
                ]
            )
        )
    summed_inputs = lax.psum_scatter(
        jnp.stack(partial_inputs).astype(jnp.bfloat16), "tensor", scatter_dimension=2, tiled=True
    ).astype(jnp.float32)
    slice_width = model_width // lax.axis_size("tensor")
    own_middle = lax.dynamic_slice_in_dim(
        jnp.stack(carried), tensor_rank * slice_width, slice_width, axis=2
    )
    grad_tokens = summed_inputs + own_middle
    grad_mod = jnp.stack(grad_mods)
    bias_up_full = lax.dynamic_update_slice_in_dim(
        jnp.zeros((b_up.shape[0],), jnp.float32), grad_bias_up, tensor_rank * hidden_width, 0
    )
    grad_qkv, grad_up, grad_out_w, grad_down = (
        lax.psum_scatter(
            grad_qkv.astype(jnp.bfloat16), "fsdp", scatter_dimension=0, tiled=True
        ).astype(jnp.float32),
        lax.psum_scatter(
            grad_up.astype(jnp.bfloat16), "fsdp", scatter_dimension=0, tiled=True
        ).astype(jnp.float32),
        lax.psum_scatter(
            grad_out_w.astype(jnp.bfloat16), "fsdp", scatter_dimension=1, tiled=True
        ).astype(jnp.float32),
        lax.psum_scatter(
            grad_down.astype(jnp.bfloat16), "fsdp", scatter_dimension=1, tiled=True
        ).astype(jnp.float32),
    )
    grad_qkv, grad_up, grad_out_w, grad_down = (
        lax.psum(grad_qkv.astype(jnp.bfloat16), "context").astype(jnp.float32),
        lax.psum(grad_up.astype(jnp.bfloat16), "context").astype(jnp.float32),
        lax.psum(grad_out_w.astype(jnp.bfloat16), "context").astype(jnp.float32),
        lax.psum(grad_down.astype(jnp.bfloat16), "context").astype(jnp.float32),
    )
    grad_ada_b = jnp.sum(grad_mod, axis=0)
    grad_ada_w = exact_transposed(embedding, grad_mod)
    grad_embedding = exact_against(grad_mod, ada_full)
    grad_before = silu_back(grad_embedding)[0]
    grad_table = exact_transposed(choose, grad_before)
    (
        grad_table,
        grad_ada_w,
        grad_ada_b,
        grad_gain_first,
        grad_gain_second,
        bias_up_full,
        grad_bias_down,
    ) = lax.psum(
        (
            grad_table,
            grad_ada_w,
            grad_ada_b,
            grad_gain_first,
            grad_gain_second,
            bias_up_full,
            grad_bias_down * leader,
        ),
        ("fsdp", "context", "tensor"),
    )
    return (
        jnp.stack(results),
        grad_tokens,
        grad_table,
        grad_ada_w,
        grad_ada_b,
        grad_gain_first,
        grad_qkv,
        grad_out_w,
        grad_gain_second,
        grad_up,
        bias_up_full,
        grad_down,
        grad_bias_down,
    )


def solution(mesh):
    axes = dict(zip(mesh.axis_names, mesh.devices.shape))

    def whole(tokens, *others):
        sequences = tokens.shape[0] // axes["fsdp"]
        local = by_sequence if sequences == axes["context"] == 2 else by_block
        return mapped(local, mesh)(tokens, *others)

    return whole


def mapped(local, mesh):
    return jax.shard_map(
        local,
        mesh=mesh,
        in_specs=(
            P("fsdp", "context", None),
            P("fsdp", "context", None),
            P("fsdp", None),
            P("fsdp"),
            P(),
            P(),
            P(),
            P(),
            P("fsdp", "tensor"),
            P("tensor", "fsdp"),
            P(),
            P("fsdp", "tensor"),
            P(),
            P("tensor", "fsdp"),
            P(),
        ),
        out_specs=(
            P("fsdp", "context", None),
            P("fsdp", "context", "tensor"),
            P(),
            P(),
            P(),
            P(),
            P("fsdp", "tensor"),
            P("tensor", "fsdp"),
            P(),
            P("fsdp", "tensor"),
            P(),
            P("tensor", "fsdp"),
            P(),
        ),
        check_vma=False,
    )
```

```python
import math
from functools import partial

import jax
import jax.numpy as jnp
from jax import lax
from jax.experimental import pallas as pl
from jax.experimental.pallas import tpu as pltpu
from jax.sharding import PartitionSpec as P

HDIM = 64
HALF = HDIM // 2
SEGMENTS = 5
WIDE = 128
MASKED = 2.0**100
LOG2E = math.log2(math.e)
SAFE_EXPONENT = 60.0
EPSILON = 1e-05
VMEM = 56 * 2**20
VMEM_MOST = 60 * 2**20


def cost(flops, *arrays):
    size = sum(math.prod(one.shape) * one.dtype.itemsize for one in arrays)
    return pl.CostEstimate(flops=int(flops), bytes_accessed=int(size), transcendentals=0)


precise = lax.Precision.HIGHEST
f32 = jnp.float32
bf16 = jnp.bfloat16


def product(left_side, right_side):
    return jnp.dot(left_side, right_side, preferred_element_type=jnp.float32)


def transposed(left_side, right_side):
    return lax.dot_general(
        left_side, right_side, (((0,), (0,)), ((), ())), preferred_element_type=jnp.float32
    )


def against(left_side, right_side):
    return lax.dot_general(
        left_side, right_side, (((1,), (1,)), ((), ())), preferred_element_type=jnp.float32
    )


def exact_product(left_side, right_side):
    return jnp.dot(left_side, right_side, precision=precise, preferred_element_type=jnp.float32)


def exact_transposed(left_side, right_side):
    return lax.dot_general(
        left_side,
        right_side,
        (((0,), (0,)), ((), ())),
        precision=precise,
        preferred_element_type=jnp.float32,
    )


def exact_against(left_side, right_side):
    return lax.dot_general(
        left_side,
        right_side,
        (((1,), (1,)), ((), ())),
        precision=precise,
        preferred_element_type=jnp.float32,
    )


def document_bounds(segment):
    indices = jnp.arange(segment.shape[-1], dtype=jnp.int32)
    same = segment[..., None, :] == jnp.arange(SEGMENTS, dtype=jnp.int32)[:, None]
    starts = jnp.min(jnp.where(same, indices, segment.shape[-1]), axis=-1)
    ends = jnp.max(jnp.where(same, indices + 1, 0), axis=-1)
    return same, starts, ends


def positions(segment):
    same, starts, _ = document_bounds(segment)
    first = jnp.sum(jnp.where(same, starts[..., :, None], 0), axis=-2)
    return jnp.arange(segment.shape[-1], dtype=jnp.int32) - first


def frequencies():
    return 10000.0 ** (-jnp.arange(HALF, dtype=jnp.float32) / HALF)


def entry_kernel(
    base_ref,
    rows_ref,
    gain_ref,
    shift_ref,
    weight_ref,
    cosine_ref,
    sine_ref,
    segment_ref,
    *refs,
    heads,
):
    del base_ref
    query_ref, key_ref, key_t_ref, value_ref, value_t_ref, hat_ref, scale_ref, norm_ref = refs[-8:]
    inputs = rows_ref[0].astype(f32).T
    center = inputs - jnp.mean(inputs, axis=0, keepdims=True)
    scaling = lax.rsqrt(jnp.mean(center * center, axis=0, keepdims=True) + EPSILON)
    hat = center * scaling
    hat_ref[...] = hat.astype(bf16)
    scale_ref[...] = scaling
    entry = (hat * gain_ref[...] + shift_ref[...]).astype(bf16)
    projected = product(weight_ref[...], entry)
    cosine = cosine_ref[...]
    sine = sine_ref[...]
    tokens = cosine.shape[1]
    group = heads * HDIM
    segment = segment_ref[...]
    number = lax.broadcasted_iota(jnp.int32, (WIDE - HDIM, tokens), 0)
    same = (number == segment).astype(f32)
    extra_query = same
    extra_key = jnp.where(
        number < SEGMENTS, (same - 1.0) * MASKED, jnp.where(number < SEGMENTS + 3, 1.0, 0.0)
    )
    extra_value = jnp.where(number < 3, 1.0, 0.0)
    norms = []
    for head in range(heads):

        def turned(kind, factor):
            at = kind * group + head * HDIM
            front = projected[at : at + HALF]
            back = projected[at + HALF : at + HDIM]
            return jnp.concatenate(
                [(front * cosine - back * sine) * factor, (front * sine + back * cosine) * factor],
                axis=0,
            )

        queries = turned(0, 0.125 * LOG2E)
        keys = turned(1, 1.0)
        values = projected[2 * group + head * HDIM : 2 * group + (head + 1) * HDIM]
        norms.append(jnp.sum(queries * queries, axis=0, keepdims=True))
        norms.append(jnp.sum(keys * keys, axis=0, keepdims=True))
        query_ref[head] = jnp.concatenate([queries, extra_query], axis=0).astype(bf16)
        key_ref[head] = jnp.concatenate([keys, extra_key], axis=0).T.astype(bf16)
        key_t_ref[head] = keys.astype(bf16)
        wide_values = jnp.concatenate([values, extra_value], axis=0)
        value_ref[head] = wide_values.T.astype(bf16)
        value_t_ref[head] = wide_values[: value_t_ref.shape[1]].astype(bf16)
    norms += [jnp.zeros_like(norms[0])] * (norm_ref.shape[0] - len(norms))
    norm_ref[...] = jnp.concatenate(norms, axis=0)


def entry_call(base, rows, row_index, gain, shift, weight, cosine, sine, segment, earlier, tile):
    length = cosine.shape[1]
    width, depth = weight.shape
    heads = width // (3 * HDIM)
    steps = rows.shape[1] // tile
    lanes = lambda i, base: (0, base[0] + i)
    heads_lanes = lambda i, base: (0, 0, base[0] + i)
    heads_rows = lambda i, base: (0, base[0] + i, 0)
    whole = lambda i, base: (0, 0)
    shapes = [
        jax.ShapeDtypeStruct((heads, WIDE, length), bf16),
        jax.ShapeDtypeStruct((heads, length, WIDE), bf16),
        jax.ShapeDtypeStruct((heads, HDIM, length), bf16),
        jax.ShapeDtypeStruct((heads, length, WIDE), bf16),
        jax.ShapeDtypeStruct((heads, HDIM + 16, length), bf16),
        jax.ShapeDtypeStruct((depth, length), bf16),
        jax.ShapeDtypeStruct((1, length), f32),
        jax.ShapeDtypeStruct((8, length), f32),
    ]
    out_specs = [
        pl.BlockSpec((heads, WIDE, tile), heads_lanes),
        pl.BlockSpec((heads, tile, WIDE), heads_rows),
        pl.BlockSpec((heads, HDIM, tile), heads_lanes),
        pl.BlockSpec((heads, tile, WIDE), heads_rows),
        pl.BlockSpec((heads, HDIM + 16, tile), heads_lanes),
        pl.BlockSpec((depth, tile), lanes),
        pl.BlockSpec((1, tile), lanes),
        pl.BlockSpec((8, tile), lanes),
    ]
    operands = [rows, gain, shift, weight, cosine, sine, segment]
    in_specs = [
        pl.BlockSpec((1, tile, depth), lambda i, base: (base[1], i, 0)),
        pl.BlockSpec((depth, 1), whole),
        pl.BlockSpec((depth, 1), whole),
        pl.BlockSpec((width, depth), whole),
        pl.BlockSpec((HALF, tile), lanes),
        pl.BlockSpec((HALF, tile), lanes),
        pl.BlockSpec((1, tile), lanes),
    ]
    aliases = {}
    if earlier is not None:
        aliases = {1 + len(operands) + k: k for k in range(len(shapes))}
        operands += list(earlier)
        in_specs += [pl.BlockSpec(memory_space=pl.ANY)] * len(shapes)
    return pl.pallas_call(
        partial(entry_kernel, heads=heads),
        grid_spec=pltpu.PrefetchScalarGridSpec(
            num_scalar_prefetch=1, grid=(steps,), in_specs=in_specs, out_specs=out_specs
        ),
        out_shape=shapes,
        input_output_aliases=aliases,
        compiler_params=pltpu.CompilerParams(vmem_limit_bytes=VMEM),
        cost_estimate=cost(2 * rows.shape[1] * depth * width, rows, weight, *shapes),
        name="entry",
    )(jnp.stack([base, row_index]).astype(jnp.int32), *operands)


def attend_kernel(range_ref, query_ref, key_ref, value_ref, out_ref, told_ref, total_ref, top_ref, *, block):
    step = pl.program_id(0)
    first, last = range_ref[0, step], range_ref[1, step]
    heads = query_ref.shape[0]
    total_ref[...] = jnp.zeros_like(total_ref)

    def scores(head, at):
        return product(key_ref[head, pl.ds(at, block), :], query_ref[head])

    def mix(head, at, weights):
        return product(value_ref[head, :, pl.ds(at, block)], weights)

    @pl.when(range_ref[2, 0] == 1)
    def _():
        top_ref[...] = jnp.zeros_like(top_ref)

        def body(number, carry):
            at = pl.multiple_of(number * block, block)
            raw = [scores(head, at) for head in range(heads)]
            weights = [jnp.exp2(one).astype(bf16) for one in raw]
            for head in range(heads):
                total_ref[head] += mix(head, at, weights[head])
            return carry

        lax.fori_loop(first, last, body, 0)

    @pl.when(range_ref[2, 0] != 1)
    def _():
        top_ref[...] = jnp.full_like(top_ref, -3e38)

        def body(number, carry):
            at = pl.multiple_of(number * block, block)
            for head in range(heads):
                raw = scores(head, at)
                before = top_ref[head]
                top = jnp.maximum(before, jnp.max(raw, axis=0, keepdims=True))
                weights = jnp.exp2(raw - top).astype(bf16)
                total_ref[head] = total_ref[head] * jnp.exp2(before - top) + mix(head, at, weights)
                top_ref[head] = top
            return carry

        lax.fori_loop(first, last, body, 0)

    tile = query_ref.shape[2]
    number = lax.broadcasted_iota(jnp.int32, (16, tile), 0)
    for head in range(heads):
        total = total_ref[head]
        mass = total[HDIM : HDIM + 1]
        out_ref[0, pl.ds(head * HDIM, HDIM), :] = (total[:HDIM] * (1.0 / mass)).astype(bf16)
        rows = split_rows(-(top_ref[head] + jnp.log2(mass)), number, SEGMENTS)
        told_ref[head, :HDIM, :] = query_ref[head, :HDIM, :]
        told_ref[head, HDIM : HDIM + 16, :] = jnp.where(
            number < SEGMENTS, query_ref[head, HDIM : HDIM + 16, :].astype(f32), rows
        ).astype(bf16)
        told_ref[head, HDIM + 16 :, :] = query_ref[head, HDIM + 16 :, :]


def split_rows(values, number, first):
    high = values.astype(bf16).astype(f32)
    rest = values - high
    middle = rest.astype(bf16).astype(f32)
    low = rest - middle
    return jnp.where(
        number == first,
        high,
        jnp.where(number == first + 1, middle, jnp.where(number == first + 2, low, 0.0)),
    )


def attend_call(ranges, queries, keys, values_t, tile, block):
    heads, _, length = queries.shape
    rows = values_t.shape[1]
    return pl.pallas_call(
        partial(attend_kernel, block=block),
        grid_spec=pltpu.PrefetchScalarGridSpec(
            num_scalar_prefetch=1,
            grid=(length // tile,),
            in_specs=[
                pl.BlockSpec((heads, WIDE, tile), lambda i, r: (0, 0, i)),
                pl.BlockSpec((heads, length, WIDE), lambda i, r: (0, 0, 0)),
                pl.BlockSpec((heads, rows, length), lambda i, r: (0, 0, 0)),
            ],
            out_specs=[
                pl.BlockSpec((1, heads * HDIM, tile), lambda i, r: (i, 0, 0)),
                pl.BlockSpec((heads, WIDE, tile), lambda i, r: (0, 0, i)),
            ],
            scratch_shapes=[
                pltpu.VMEM((heads, rows, tile), f32),
                pltpu.VMEM((heads, 1, tile), f32),
            ],
        ),
        out_shape=[
            jax.ShapeDtypeStruct((length // tile, heads * HDIM, tile), bf16),
            jax.ShapeDtypeStruct((heads, WIDE, length), bf16),
        ],
        compiler_params=pltpu.CompilerParams(vmem_limit_bytes=VMEM),
        cost_estimate=cost(4 * heads * length * length * WIDE, queries, keys, values_t),
        name="attend",
    )(ranges, queries, keys, values_t)


def attend_back_kernel(
    range_ref,
    query_ref,
    key_ref,
    key_t_ref,
    value_ref,
    mixture_ref,
    grad_ref,
    cosine_ref,
    sine_ref,
    grad_query_ref,
    grad_key_ref,
    grad_value_ref,
    wide_ref,
    query_total,
    key_total,
    value_total,
    *,
    block,
):
    step = pl.program_id(0)
    first, last = range_ref[0, step], range_ref[1, step]
    heads, _, tile = query_ref.shape

    @pl.when(step == 0)
    def _():
        wide_ref[...] = jnp.zeros_like(wide_ref)
        key_total[...] = jnp.zeros_like(key_total)
        value_total[...] = jnp.zeros_like(value_total)

    number = lax.broadcasted_iota(jnp.int32, (16, tile), 0)
    query_total[...] = jnp.zeros_like(query_total)
    for head in range(heads):
        at = pl.ds(head * HDIM, HDIM)
        grad = grad_ref[0, at, :]
        delta = jnp.sum(grad.astype(f32) * mixture_ref[0, at, :].astype(f32), axis=0, keepdims=True)
        wide_ref[head, :HDIM, :] = grad
        wide_ref[head, HDIM : HDIM + 16, :] = split_rows(-delta, number, 0).astype(bf16)

    def body(number, carry):
        at = pl.multiple_of(number * block, block)
        rows = pl.ds(at, block)
        raw = [product(key_ref[head, rows, :], query_ref[head]) for head in range(heads)]
        slope = [product(value_ref[head, rows, :], wide_ref[head]) for head in range(heads)]
        for head in range(heads):
            weights = jnp.exp2(raw[head])
            grad_scores = (weights * slope[head]).astype(bf16)
            query_total[head] += product(key_t_ref[head, :, rows], grad_scores)
            key_total[head, :, rows] += against(query_ref[head, :HDIM, :], grad_scores)
            value_total[head, :, rows] += against(wide_ref[head, :HDIM, :], weights.astype(bf16))
        return carry

    lax.fori_loop(first, last, body, 0)

    def turned_back(grads, cosine, sine):
        front, back = grads[:HALF], grads[HALF:]
        return jnp.concatenate([front * cosine + back * sine, back * cosine - front * sine], axis=0)

    own = pl.ds(pl.multiple_of(step * tile, tile), tile)
    for head in range(heads):
        at = pl.ds(head * HDIM, HDIM)
        grad_query_ref[at, :] = turned_back(
            query_total[head] * 0.125, cosine_ref[:, own], sine_ref[:, own]
        ).astype(bf16)

    @pl.when(step == pl.num_programs(0) - 1)
    def _():
        for head in range(heads):
            at = pl.ds(head * HDIM, HDIM)
            grad_key_ref[at, :] = turned_back(
                key_total[head] * (1.0 / LOG2E), cosine_ref[...], sine_ref[...]
            ).astype(bf16)
            grad_value_ref[at, :] = value_total[head].astype(bf16)


def attend_back_call(
    ranges, queries, keys, keys_t, values, mixture, grad_mixture, cosine, sine, tile, block
):
    heads, _, length = queries.shape
    group = heads * HDIM
    whole2 = lambda i, r: (0, 0)
    whole3 = lambda i, r: (0, 0, 0)
    return pl.pallas_call(
        partial(attend_back_kernel, block=block),
        grid_spec=pltpu.PrefetchScalarGridSpec(
            num_scalar_prefetch=1,
            grid=(length // tile,),
            in_specs=[
                pl.BlockSpec((heads, WIDE, tile), lambda i, r: (0, 0, i)),
                pl.BlockSpec((heads, length, WIDE), whole3),
                pl.BlockSpec((heads, HDIM, length), whole3),
                pl.BlockSpec((heads, length, WIDE), whole3),
                pl.BlockSpec((1, group, tile), lambda i, r: (i, 0, 0)),
                pl.BlockSpec((1, group, tile), lambda i, r: (i, 0, 0)),
                pl.BlockSpec((HALF, length), whole2),
                pl.BlockSpec((HALF, length), whole2),
            ],
            out_specs=[
                pl.BlockSpec((group, tile), lambda i, r: (0, i)),
                pl.BlockSpec((group, length), whole2),
                pl.BlockSpec((group, length), whole2),
            ],
            scratch_shapes=[
                pltpu.VMEM((heads, WIDE, tile), bf16),
                pltpu.VMEM((heads, HDIM, tile), f32),
                pltpu.VMEM((heads, HDIM, length), f32),
                pltpu.VMEM((heads, HDIM, length), f32),
            ],
        ),
        out_shape=[jax.ShapeDtypeStruct((group, length), bf16)] * 3,
        compiler_params=pltpu.CompilerParams(vmem_limit_bytes=VMEM),
        cost_estimate=cost(10 * heads * length * length * WIDE, queries, keys, values),
        name="attend_back",
    )(ranges, queries, keys, keys_t, values, mixture, grad_mixture, cosine, sine)


def copy_to(source, target, sent, arrived, **device):
    return pltpu.make_async_remote_copy(
        src_ref=source,
        dst_ref=target,
        send_sem=sent,
        recv_sem=arrived,
        device_id=device,
        device_id_type=pl.DeviceIdType.MESH,
    )


def greet(devices):
    barrier = pltpu.get_barrier_semaphore()
    for device in devices:
        pl.semaphore_signal(barrier, inc=1, device_id=device, device_id_type=pl.DeviceIdType.MESH)
    pl.semaphore_wait(barrier, len(devices))


def middle_kernel(
    mixture_ref,
    rows_ref,
    cotangent_ref,
    valid_ref,
    mod_ref,
    up_bias_ref,
    down_bias_ref,
    out_weight_ref,
    up_ref,
    down_ref,
    result_ref,
    grad_mixture_ref,
    grad_middle_ref,
    grad_out_ref,
    sums_ref,
    bias_sums_ref,
    up_keep_ref,
    up_send_ref,
    down_keep_ref,
    down_send_ref,
    own_mixture,
    entry_rows,
    entry_columns,
    grad_output_rows,
    grad_output_columns,
    attended_rows,
    output_rows,
    grad_entry_rows,
    active,
    grad_hidden,
    grad_staged,
    to_sibling,
    from_sibling,
    staged_up,
    staged_down,
    sent_mixture,
    got_mixture,
    own_copied,
    sent_grad,
    got_grad,
    grad_copied,
    sent_part,
    got_part,
    kept,
    *,
    tile,
    tiles,
    parts,
):
    step = pl.program_id(0)
    context, tensor = lax.axis_index("context"), lax.axis_index("tensor")
    ranks = 4
    everyone = 2 * ranks
    place = context * ranks + tensor
    core = lax.rem(tensor, 2)
    sibling = tensor + 1 - 2 * core
    depth = rows_ref.shape[1]
    group = depth // ranks
    per_sequence = tiles // 2
    per_part = tiles + 1
    back_from = tiles + parts * per_part
    root = math.sqrt(2.0 / math.pi)

    def member(away):
        other = lax.rem(place + away, everyone)
        return other, {"context": other // ranks, "tensor": lax.rem(other, ranks)}

    def mixture_copy(away):
        other, device = member(away)
        return copy_to(
            mixture_ref.at[other],
            own_mixture.at[place],
            sent_mixture.at[away - 1],
            got_mixture.at[lax.rem(place + everyone, everyone)],
            **device,
        )

    def mixture_arrival(source):
        return pltpu.make_async_remote_copy(
            src_ref=mixture_ref.at[source],
            dst_ref=own_mixture.at[source],
            send_sem=sent_mixture.at[0],
            recv_sem=got_mixture.at[source],
            device_id={"tensor": sibling},
            device_id_type=pl.DeviceIdType.MESH,
        )

    def own_copy():
        return pltpu.make_async_copy(mixture_ref.at[place], own_mixture.at[place], own_copied)

    def part_copy(slot):
        return copy_to(
            to_sibling, from_sibling.at[slot], sent_part.at[slot], got_part.at[slot], tensor=sibling
        )

    def gradient_lanes(at):
        return pl.ds(pl.multiple_of(lax.rem(at, per_sequence) * tile, tile), tile)

    def gradient_copy(at, rank):
        return copy_to(
            grad_staged.at[at, rank],
            grad_mixture_ref.at[place, :, gradient_lanes(at)],
            sent_grad.at[at, rank],
            got_grad.at[place, lax.rem(at, per_sequence)],
            context=at // per_sequence,
            tensor=rank,
        )

    def gradient_own(at):
        return pltpu.make_async_copy(
            grad_staged.at[at, tensor],
            grad_mixture_ref.at[place, :, gradient_lanes(at)],
            grad_copied.at[lax.rem(at, per_sequence)],
        )

    def gradient_arrival(source, number):
        return pltpu.make_async_remote_copy(
            src_ref=grad_staged.at[0, 0],
            dst_ref=grad_mixture_ref.at[source, :, pl.ds(number * tile, tile)],
            send_sem=sent_grad.at[0, 0],
            recv_sem=got_grad.at[source, number],
            device_id={"tensor": sibling},
            device_id_type=pl.DeviceIdType.MESH,
        )

    def kept_copies(slot):
        if slot == 0:
            return [
                pltpu.make_async_copy(staged_up, up_send_ref, kept.at[0]),
                pltpu.make_async_copy(staged_down.at[0], down_keep_ref.at[0], kept.at[1]),
                pltpu.make_async_copy(staged_down.at[1], down_send_ref.at[0], kept.at[2]),
            ]
        return [
            pltpu.make_async_copy(staged_up, up_keep_ref, kept.at[3]),
            pltpu.make_async_copy(staged_down.at[0], down_keep_ref.at[1], kept.at[4]),
            pltpu.make_async_copy(staged_down.at[1], down_send_ref.at[1], kept.at[5]),
        ]

    def tile_of(at):
        sequence = at // per_sequence
        rows = pl.ds(pl.multiple_of(at * tile, tile), tile)
        mods = mod_ref[sequence]
        lanes = gradient_lanes(at)
        mixture_t = jnp.concatenate(
            [own_mixture[sequence * ranks + rank, :, lanes] for rank in range(ranks)], axis=0
        )
        return rows, mixture_t, tuple(mods[k : k + 1] for k in range(4))

    def normal(attended, gate_one):
        middle = rows_ref[...].astype(f32) + gate_one * attended
        center = middle - jnp.mean(middle, axis=-1, keepdims=True)
        scaling = lax.rsqrt(jnp.mean(center * center, axis=-1, keepdims=True) + EPSILON)
        return middle, center * scaling, scaling

    @pl.when(step == 0)
    def _():
        own_copy().start()
        greet([member(away)[1] for away in range(1, everyone)])
        for away in range(1, everyone):
            mixture_copy(away).start()
        sums_ref[...] = jnp.zeros_like(sums_ref)
        bias_sums_ref[...] = jnp.zeros_like(bias_sums_ref)
        grad_out_ref[...] = jnp.zeros_like(grad_out_ref)

    for sequence in range(2):

        @pl.when(step == sequence * per_sequence)
        def _():
            for rank in range(ranks):
                source = sequence * ranks + rank

                @pl.when(place == source)
                def _():
                    own_copy().wait()

                @pl.when(place != source)
                def _():
                    mixture_arrival(source).wait_recv()

    @pl.when(step < tiles)
    def _():
        rows, mixture_t, (gate_one, shift_two, gain_two, gate_two) = tile_of(step)
        attended = product(mixture_t.T, out_weight_ref[...])
        attended_rows[rows, :] = attended
        _, hat, _ = normal(attended, gate_one)
        entry = (hat * gain_two + shift_two).astype(bf16)
        grad_output = (gate_two * (cotangent_ref[...].astype(f32) * valid_ref[rows, :])).astype(bf16)
        entry_rows[rows, :] = entry
        entry_columns[:, rows] = entry.T
        grad_output_rows[rows, :] = grad_output
        grad_output_columns[:, rows] = grad_output.T
        output_rows[rows, :] = jnp.broadcast_to(down_bias_ref[...], (tile, depth))
        grad_entry_rows[rows, :] = jnp.zeros((tile, depth), f32)

    inner = lax.rem(step - tiles, per_part)
    position = (step - tiles) // per_part
    in_parts = (step >= tiles) & (step < back_from)

    @pl.when(in_parts & (inner < tiles))
    def _():
        rows = pl.ds(pl.multiple_of(inner * tile, tile), tile)
        number = part_at(position, tensor)
        hidden = product(entry_rows[rows, :], up_ref[0]) + up_bias_ref[0]
        square = hidden * hidden
        bent = jnp.tanh(root * hidden * (1.0 + 0.044715 * square))
        half = 0.5 * (1.0 + bent)
        activated = (hidden * half).astype(bf16)
        slope = half + (0.5 * root) * hidden * (1.0 - bent * bent) * (1.0 + 0.134145 * square)
        grads = (product(grad_output_rows[rows, :], down_ref[0]) * slope).astype(bf16)
        output_rows[rows, :] += against(activated, down_ref[0])
        grad_entry_rows[rows, :] += against(grads, up_ref[0])
        active[rows, :] = activated
        grad_hidden[rows, :] = grads
        bias_sums_ref[number] += jnp.sum(grads.astype(f32), axis=0, keepdims=True)

    for turn in range(parts):

        @pl.when(step == tiles + turn * per_part + tiles)
        def _():
            slot = turn // 2
            if turn % 2 == 0:
                if slot:
                    part_copy(0).wait_send()
            else:
                part_copy(slot).wait_recv()
                if slot:
                    for one in kept_copies(0):
                        one.wait()
            groups = up_keep_ref.shape[1]
            height = depth // groups
            for other in range(groups):
                at = pl.ds(other * height, height)
                up = product(entry_columns[at, :], grad_hidden[...])
                down = product(grad_output_columns[at, :], active[...])
                if turn % 2 == 0:
                    to_sibling[0, at, :] = up.astype(bf16)
                    to_sibling[1, at, :] = down.astype(bf16)
                else:
                    up = (up + from_sibling[slot, 0, at, :].astype(f32)).astype(bf16)
                    down = (down + from_sibling[slot, 1, at, :].astype(f32)).astype(bf16)
                    staged_up[context, other] = up[: height // 2]
                    staged_up[1 - context, other] = up[height // 2 :]
                    staged_down[context, other] = down[: height // 2]
                    staged_down[1 - context, other] = down[height // 2 :]
            if turn % 2 == 0:
                part_copy(slot).start()
            else:
                for one in kept_copies(slot):
                    one.start()

    @pl.when(step >= back_from)
    def _():
        at = step - back_from
        sequence = at // per_sequence
        rows, mixture_t, (gate_one, _, gain_two, gate_two) = tile_of(at)
        attended = attended_rows[rows, :]
        middle, hat, scaling = normal(attended, gate_one)
        output = output_rows[rows, :]
        grad_entry = grad_entry_rows[rows, :]
        grad_result = cotangent_ref[...].astype(f32) * valid_ref[rows, :]
        result_ref[...] = (middle + gate_two * output).astype(bf16)
        grad_lifted = grad_entry * gain_two
        grad_middle = grad_result + scaling * (
            grad_lifted
            - jnp.mean(grad_lifted, axis=-1, keepdims=True)
            - hat * jnp.mean(grad_lifted * hat, axis=-1, keepdims=True)
        )
        grad_attended = (gate_one * grad_middle).astype(bf16)
        grad_mixture = against(out_weight_ref[...], grad_attended).astype(bf16)
        for rank in range(ranks):
            grad_staged[at, rank] = grad_mixture[rank * group : (rank + 1) * group]
        for rank in range(ranks):
            own = (sequence == context) & (tensor == rank)

            @pl.when(own)
            def _():
                gradient_own(at).start()

            @pl.when(jnp.logical_not(own))
            def _():
                gradient_copy(at, rank).start()

        grad_middle_ref[0] = grad_middle.T.astype(bf16)
        grad_out_ref[...] += product(mixture_t, grad_attended)
        lines = [
            jnp.sum(grad_middle * attended, axis=0, keepdims=True),
            jnp.sum(grad_entry, axis=0, keepdims=True),
            jnp.sum(grad_entry * hat, axis=0, keepdims=True),
            jnp.sum(grad_result * output, axis=0, keepdims=True),
            jnp.sum(grad_output_rows[rows, :].astype(f32), axis=0, keepdims=True),
        ]
        lines += [jnp.zeros_like(lines[0])] * (sums_ref.shape[1] - len(lines))
        sums_ref[sequence] += jnp.concatenate(lines, axis=0)

    @pl.when(step == back_from + tiles - 1)
    def _():
        for source in range(everyone):
            for number in range(per_sequence):

                @pl.when(place != source)
                def _():
                    gradient_arrival(source, number).wait_recv()

        for at in range(tiles):
            for rank in range(ranks):
                own = (at // per_sequence == context) & (tensor == rank)

                @pl.when(own)
                def _():
                    gradient_own(at).wait()

                @pl.when(jnp.logical_not(own))
                def _():
                    gradient_copy(at, rank).wait_send()

        for away in range(1, everyone):
            mixture_copy(away).wait_send()
        part_copy(1).wait_send()
        for one in kept_copies(1):
            one.wait()


def part_at(position, tensor):
    core = lax.rem(tensor, 2)
    chip = tensor // 2
    away = jnp.where(position < 2, 1 - chip, chip)
    other = jnp.where(lax.rem(position, 2) == 0, 1 - core, core)
    return away * 2 + other


def middle_call(
    mixture, rows, cotangent, valid, mods, up_bias, down_bias, out_weight, up, down, groups, tile
):
    pieces, group, own = mixture.shape
    tokens, depth = rows.shape
    parts, _, part_width = up.shape
    tiles = tokens // tile
    per_sequence = tiles // 2
    per_part = tiles + 1
    back_from = tiles + parts * per_part
    half = depth // groups // 2

    def token_tile(i):
        return jnp.where(i < tiles, i, jnp.where(i < back_from, 0, i - back_from)), 0

    def part_block(i):
        position = jnp.clip((i - tiles) // per_part, 0, parts - 1)
        return part_at(position, lax.axis_index("tensor")), 0, 0

    def back_tile(i):
        return jnp.maximum(i - back_from, 0)

    whole2 = lambda i: (0, 0)
    whole3 = lambda i: (0, 0, 0)
    once = pl.Buffered(1)
    hbm = pl.BlockSpec(memory_space=pl.ANY)
    kept = jax.ShapeDtypeStruct((2, groups, half, part_width), bf16)
    wide = (tokens, depth)
    return pl.pallas_call(
        partial(middle_kernel, tile=tile, tiles=tiles, parts=parts),
        grid=(back_from + tiles,),
        in_specs=[
            hbm,
            pl.BlockSpec((tile, depth), token_tile),
            pl.BlockSpec((tile, depth), token_tile),
            pl.BlockSpec((tokens, 1), whole2, pipeline_mode=once),
            pl.BlockSpec(mods.shape, whole3, pipeline_mode=once),
            pl.BlockSpec((1, 1, part_width), part_block),
            pl.BlockSpec((1, depth), whole2, pipeline_mode=once),
            pl.BlockSpec((depth, depth), whole2, pipeline_mode=once),
            pl.BlockSpec((1, depth, part_width), part_block),
            pl.BlockSpec((1, depth, part_width), part_block),
        ],
        out_specs=[
            pl.BlockSpec((tile, depth), lambda i: (back_tile(i), 0)),
            hbm,
            pl.BlockSpec(
                (1, depth, tile),
                lambda i: (back_tile(i) // per_sequence, 0, lax.rem(back_tile(i), per_sequence)),
            ),
            pl.BlockSpec((depth, depth), whole2),
            pl.BlockSpec((2, 8, depth), whole3),
            pl.BlockSpec((parts, 1, part_width), whole3),
            hbm,
            hbm,
            hbm,
            hbm,
        ],
        out_shape=[
            jax.ShapeDtypeStruct((tokens, depth), bf16),
            jax.ShapeDtypeStruct(mixture.shape, bf16),
            jax.ShapeDtypeStruct((2, depth, own), bf16),
            jax.ShapeDtypeStruct((depth, depth), f32),
            jax.ShapeDtypeStruct((2, 8, depth), f32),
            jax.ShapeDtypeStruct((parts, 1, part_width), f32),
            kept,
            kept,
            kept,
            kept,
        ],
        scratch_shapes=[
            pltpu.VMEM(mixture.shape, bf16),
            pltpu.VMEM(wide, bf16),
            pltpu.VMEM((depth, tokens), bf16),
            pltpu.VMEM(wide, bf16),
            pltpu.VMEM((depth, tokens), bf16),
            pltpu.VMEM(wide, f32),
            pltpu.VMEM(wide, f32),
            pltpu.VMEM(wide, f32),
            pltpu.VMEM((tokens, part_width), bf16),
            pltpu.VMEM((tokens, part_width), bf16),
            pltpu.VMEM((tiles, 4, group, tile), bf16),
            pltpu.VMEM((2, depth, part_width), bf16),
            pltpu.VMEM((2, 2, depth, part_width), bf16),
            pltpu.VMEM((2, groups, half, part_width), bf16),
            pltpu.VMEM((2, groups, half, part_width), bf16),
            pltpu.SemaphoreType.DMA((pieces - 1,)),
            pltpu.SemaphoreType.DMA((pieces,)),
            pltpu.SemaphoreType.DMA,
            pltpu.SemaphoreType.DMA((tiles, 4)),
            pltpu.SemaphoreType.DMA((pieces, per_sequence)),
            pltpu.SemaphoreType.DMA((per_sequence,)),
            pltpu.SemaphoreType.DMA((2,)),
            pltpu.SemaphoreType.DMA((2,)),
            pltpu.SemaphoreType.DMA((6,)),
        ],
        compiler_params=pltpu.CompilerParams(
            vmem_limit_bytes=VMEM_MOST, collective_id=2, has_side_effects=True
        ),
        cost_estimate=cost(6 * tokens * depth * (depth + 3 * parts * part_width), rows, up, down),
        name="middle",
    )(mixture, rows, cotangent, valid, mods, up_bias, down_bias, out_weight, up, down)


def entry_back_kernel(
    grad_query_ref,
    grad_key_ref,
    grad_value_ref,
    hat_ref,
    scale_ref,
    gain_ref,
    shift_ref,
    weight_ref,
    middle_ref,
    middle_in_ref,
    small_ref,
    up_ref,
    down_ref,
    grad_out_ref,
    result_ref,
    result_in_ref,
    out_ref,
    grad_weight_ref,
    all_sums_ref,
    all_small_ref,
    pieces_ref,
    grad_out_sum_ref,
    block_ref,
    up_own,
    up_in,
    down_own,
    down_in,
    slices,
    slices_in,
    context_slice,
    context_in,
    small_in,
    small_sum,
    small_groups,
    out_in,
    loaded,
    sent_up,
    got_up,
    sent_down,
    got_down,
    sent_slice,
    got_slice,
    sent_context,
    got_context,
    sent_small,
    got_small,
    sent_sum,
    got_sum,
    sent_out,
    got_out,
    sent_result,
    got_result,
    moved,
    weight_total,
    sums,
    part,
    part_in,
    pair,
    pair_in,
    chip,
    chip_in,
    piece,
    piece_in,
    block_piece,
    block_in,
    rank_sums,
    rank_in,
    group_sums,
    group_in,
    sent_part,
    got_part,
    sent_pair,
    got_pair,
    sent_chip,
    got_chip,
    sent_piece,
    got_piece,
    sent_block,
    got_block,
    sent_rank,
    got_rank,
    sent_group,
    got_group,
    *,
    tiles,
    groups,
):
    step = pl.program_id(0)
    fsdp, context, tensor = (lax.axis_index(name) for name in ("fsdp", "context", "tensor"))
    ranks = 4
    half = tiles // 2
    core = lax.rem(tensor, 2)
    chip_x = tensor // 2
    sibling = tensor + 1 - 2 * core
    across = lax.rem(tensor + 2, ranks)
    place = fsdp * 2 + context
    depth = hat_ref.shape[0]
    slice_rows = depth // ranks
    weight_rows = depth // groups
    everyone = groups * 2

    def group_member(away):
        other = lax.rem(place + away, everyone)
        return {"fsdp": other // 2, "context": lax.rem(other, 2)}

    def group_away(number):
        return {"fsdp": lax.rem(fsdp + number // 2, groups), "context": number % 2}

    plane = context * ranks + tensor
    in_plane = 2 * ranks

    def plane_member(away):
        other = lax.rem(plane + away, in_plane)
        return {"context": other // ranks, "tensor": lax.rem(other, ranks)}

    def up_copy():
        return copy_to(up_ref.at[1], up_in, sent_up, got_up, context=1 - context)

    def down_copy():
        return copy_to(down_ref.at[0], down_in, sent_down, got_down, tensor=across)

    def loads():
        return [
            pltpu.make_async_copy(up_ref.at[0], up_own, loaded.at[0]),
            pltpu.make_async_copy(down_ref.at[1], down_own, loaded.at[1]),
        ]

    def slice_copy(away):
        other = lax.rem(fsdp + away, groups)
        return copy_to(
            slices.at[other],
            slices_in.at[away - 1],
            sent_slice.at[away - 1],
            got_slice.at[away - 1],
            fsdp=other,
        )

    def context_copy():
        return copy_to(context_slice, context_in, sent_context, got_context, context=1 - context)

    def small_copy(away):
        return copy_to(
            small_ref,
            small_in.at[away - 1],
            sent_small.at[away - 1],
            got_small.at[away - 1],
            **plane_member(away),
        )

    def sum_copy(away):
        return copy_to(
            small_sum,
            small_groups.at[away - 1],
            sent_sum.at[away - 1],
            got_sum.at[away - 1],
            fsdp=lax.rem(fsdp + away, groups),
        )

    def out_copy():
        return copy_to(grad_out_ref, out_in, sent_out, got_out, context=1 - context)

    quarter = result_ref.shape[1]

    def result_places():
        for number, (source, rank) in enumerate([(result_ref, tensor), (result_in_ref, across)]):
            rows = pl.ds(pl.multiple_of(rank * quarter, quarter), quarter)
            for sequence in range(2):
                yield number * 2 + sequence, source.at[sequence], block_ref.at[sequence, rows, :]

    def result_copies():
        return [
            copy_to(source, target, sent_result.at[k], got_result.at[k], tensor=sibling)
            for k, source, target in result_places()
        ]

    def result_moves():
        return [
            pltpu.make_async_copy(source, target, moved.at[k]) for k, source, target in result_places()
        ]

    def part_copy(tile):
        return copy_to(
            part.at[tile, 1 - core], part_in.at[tile], sent_part.at[tile], got_part.at[tile], tensor=sibling
        )

    def pair_copy(tile):
        return copy_to(
            pair.at[tile, 1 - chip_x], pair_in.at[tile], sent_pair.at[tile], got_pair.at[tile], tensor=across
        )

    def chip_copy(tile):
        return copy_to(
            chip.at[tile], chip_in.at[tile], sent_chip.at[tile], got_chip.at[tile], context=1 - context
        )

    def piece_copy(away):
        other = lax.rem(fsdp + away, groups)
        return copy_to(
            piece.at[other],
            piece_in.at[away - 1],
            sent_piece.at[away - 1],
            got_piece.at[away - 1],
            fsdp=other,
        )

    def block_copy():
        return copy_to(block_piece, block_in, sent_block, got_block, context=1 - context)

    def rank_copy(away):
        return copy_to(
            rank_sums,
            rank_in.at[away - 1],
            sent_rank.at[away - 1],
            got_rank.at[away - 1],
            tensor=lax.rem(tensor + away, ranks),
        )

    def group_copy(away):
        return copy_to(
            group_sums,
            group_in.at[away - 1],
            sent_group.at[away - 1],
            got_group.at[away - 1],
            **group_member(away),
        )

    @pl.when(step == 0)
    def _():
        greet(
            [plane_member(away) for away in range(1, in_plane)]
            + [group_away(away) for away in range(2, everyone)]
        )
        up_copy().start()
        down_copy().start()
        out_copy().start()
        for away in range(1, in_plane):
            small_copy(away).start()
        for one in result_copies() + result_moves() + loads():
            one.start()
        weight_total[...] = jnp.zeros_like(weight_total)
        sums[...] = jnp.zeros_like(sums)

    def grads():
        return jnp.concatenate([grad_query_ref[...], grad_key_ref[...], grad_value_ref[...]], axis=0)

    @pl.when(step < tiles)
    def _():
        entry = (hat_ref[...].astype(f32) * gain_ref[...] + shift_ref[...]).astype(bf16)
        weight_total[...] += against(entry, grads())

    @pl.when(step == tiles - 1)
    def _():
        for other in range(groups):
            piece[other] = weight_total[other * weight_rows : (other + 1) * weight_rows].astype(bf16)
        for away in range(1, groups):
            piece_copy(away).start()

    @pl.when((step >= tiles) & (step < 2 * tiles))
    def _():
        tile = step - tiles
        grad_entry = product(weight_ref[...], grads())
        hat = hat_ref[...].astype(f32)
        grad_lifted = grad_entry * gain_ref[...]
        term = scale_ref[...] * (
            grad_lifted
            - jnp.mean(grad_lifted, axis=0, keepdims=True)
            - hat * jnp.mean(grad_lifted * hat, axis=0, keepdims=True)
        )
        extra = jnp.where(tile < half, middle_in_ref[...], middle_ref[0]).astype(f32)
        term = (term + jnp.where(lax.rem(tile, half) == tensor, extra, 0.0)).astype(bf16)
        for rank in range(ranks):
            part[tile, rank % 2, rank // 2] = term[rank * slice_rows : (rank + 1) * slice_rows]
        part_copy(tile).start()
        weighted = grad_entry * hat
        for lane in range(0, grad_entry.shape[1], WIDE):
            sums[0] += grad_entry[:, lane : lane + WIDE]
            sums[1] += weighted[:, lane : lane + WIDE]

    @pl.when((step >= tiles + 1) & (step < 2 * tiles + 1))
    def _():
        tile = step - tiles - 1
        part_copy(tile).wait_recv()
        pair[tile] = (part[tile, core].astype(f32) + part_in[tile].astype(f32)).astype(bf16)
        pair_copy(tile).start()

    @pl.when((step >= tiles + 2) & (step < 2 * tiles + 2))
    def _():
        tile = step - tiles - 2
        pair_copy(tile).wait_recv()
        total = (pair[tile, chip_x].astype(f32) + pair_in[tile].astype(f32)).astype(bf16)

        @pl.when(tile < half)
        def _():
            chip[tile] = total
            chip_copy(tile).start()

        @pl.when(tile >= half)
        def _():
            out_ref[context, tile - half] = total

    @pl.when((step >= tiles + 5) & (step < tiles + 5 + half))
    def _():
        tile = step - tiles - 5
        chip_copy(tile).wait_recv()
        out_ref[1 - context, tile] = chip_in[tile]

    @pl.when(step == tiles)
    def _():
        for away in range(1, in_plane):
            small_copy(away).wait_recv()
        small_sum[...] = ordered_sum(small_ref[...], [small_in[k] for k in range(in_plane - 1)], plane)
        for away in range(1, groups):
            sum_copy(away).start()

    @pl.when(step == tiles + 2)
    def _():
        for one in loads():
            one.wait()
        up_copy().wait_recv()
        down_copy().wait_recv()
        for other in range(groups):
            slices[other, 0] = (up_own[other].astype(f32) + up_in[other].astype(f32)).astype(bf16)
            slices[other, 1] = (down_own[other].astype(f32) + down_in[other].astype(f32)).astype(bf16)
        for away in range(1, groups):
            slice_copy(away).start()

    @pl.when(step == tiles + 6)
    def _():
        total = slices[fsdp].astype(f32)
        for away in range(1, groups):
            slice_copy(away).wait_recv()
            total = total + slices_in[away - 1].astype(f32)
        context_slice[...] = total.astype(bf16)
        context_copy().start()

    @pl.when(step == tiles + 4)
    def _():
        total = piece[fsdp].astype(f32)
        for away in range(1, groups):
            piece_copy(away).wait_recv()
            total = total + piece_in[away - 1].astype(f32)
        block_piece[...] = total.astype(bf16)
        block_copy().start()

    @pl.when(step == tiles + 7)
    def _():
        block_copy().wait_recv()
        grad_weight_ref[...] = block_piece[...].astype(f32) + block_in[...].astype(f32)

    @pl.when(step == 2 * tiles - 1)
    def _():
        rows = [jnp.sum(sums[kind].T, axis=0, keepdims=True) for kind in range(2)]
        rank_sums[...] = jnp.concatenate(rows + [jnp.zeros((6, depth), f32)], axis=0)
        for away in range(1, ranks):
            rank_copy(away).start()

    @pl.when(step == 2 * tiles)
    def _():
        for away in range(1, ranks):
            rank_copy(away).wait_recv()
        pairs = [rank_sums[...] + rank_in[1], rank_in[0] + rank_in[2]]
        group_sums[...] = pairs[0] + pairs[1]
        for away in range(1, everyone):
            group_copy(away).start()

    @pl.when(step == 2 * tiles + 1)
    def _():
        all_small_ref[fsdp] = small_sum[...]
        for away in range(1, groups):
            sum_copy(away).wait_recv()
            all_small_ref[lax.rem(fsdp + groups - away, groups)] = small_groups[away - 1]
            sum_copy(away).wait_send()
            slice_copy(away).wait_send()
        context_copy().wait()
        pieces_ref[context] = context_slice[...]
        pieces_ref[1 - context] = context_in[...]
        out_copy().wait()
        grad_out_sum_ref[...] = grad_out_ref[...].astype(f32) + out_in[...].astype(f32)
        up_copy().wait_send()
        down_copy().wait_send()
        for away in range(1, in_plane):
            small_copy(away).wait_send()
        for one in result_copies() + result_moves():
            one.wait()
        all_sums_ref[place] = group_sums[...]
        for away in range(1, everyone):
            group_copy(away).wait_recv()
            all_sums_ref[lax.rem(place + everyone - away, everyone)] = group_in[away - 1]
        for tile in range(tiles):
            part_copy(tile).wait_send()
            pair_copy(tile).wait_send()
        for tile in range(half):
            chip_copy(tile).wait_send()
        for away in range(1, groups):
            piece_copy(away).wait_send()
        block_copy().wait_send()
        for away in range(1, ranks):
            rank_copy(away).wait_send()
        for away in range(1, everyone):
            group_copy(away).wait_send()


def ordered_sum(own, others, place):
    count = len(others) + 1
    total = 0.0
    for source in range(count):
        away = lax.rem(place - source + count, count)
        term = own
        for k, other in enumerate(others):
            term = jnp.where(away == k + 1, other, term)
        total = total + term
    return total


def entry_back_call(
    grad_query,
    grad_key,
    grad_value,
    hat_t,
    scaling,
    gain,
    shift,
    weight,
    grad_middle,
    middle_in,
    small,
    up,
    down,
    grad_out,
    result,
    result_in,
    groups,
    tile,
):
    group, length = grad_query.shape
    depth = hat_t.shape[0]
    tiles = length // tile
    half = tiles // 2
    rows = depth // 4
    weight_rows = depth // groups

    def lanes(step):
        first = (1 - lax.axis_index("context")) * half
        return 0, lax.rem(first + lax.rem(jnp.minimum(step, 2 * tiles - 1), tiles), tiles)

    whole = lambda step: (0, 0)
    whole3 = lambda step: (0, 0, 0)
    whole4 = lambda step: (0, 0, 0, 0)
    dma = lambda *shape: [pltpu.SemaphoreType.DMA(shape)] * 2
    hbm = pl.BlockSpec(memory_space=pl.ANY)
    piece = up.shape[1:]
    return pl.pallas_call(
        partial(entry_back_kernel, tiles=tiles, groups=groups),
        grid=(2 * tiles + 2,),
        in_specs=[
            pl.BlockSpec((group, tile), lanes),
            pl.BlockSpec((group, tile), lanes),
            pl.BlockSpec((group, tile), lanes),
            pl.BlockSpec((depth, tile), lanes),
            pl.BlockSpec((1, tile), lanes),
            pl.BlockSpec((depth, 1), whole),
            pl.BlockSpec((depth, 1), whole),
            pl.BlockSpec((depth, 3 * group), whole),
            pl.BlockSpec((1, depth, tile), lambda step: (lax.axis_index("context"), 0, 0)),
            pl.BlockSpec((depth, tile), whole),
            pl.BlockSpec(small.shape, whole),
            hbm,
            hbm,
            pl.BlockSpec(grad_out.shape, whole),
            hbm,
            hbm,
        ],
        out_specs=[
            pl.BlockSpec((2, half, rows, tile), whole4),
            pl.BlockSpec((weight_rows, 3 * group), whole),
            pl.BlockSpec((2 * groups, 8, depth), whole3),
            pl.BlockSpec((groups, *small.shape), whole3),
            pl.BlockSpec((2, 2, *piece[1:]), whole4),
            pl.BlockSpec(grad_out.shape, whole),
            hbm,
        ],
        out_shape=[
            jax.ShapeDtypeStruct((2, half, rows, tile), bf16),
            jax.ShapeDtypeStruct((weight_rows, 3 * group), f32),
            jax.ShapeDtypeStruct((2 * groups, 8, depth), f32),
            jax.ShapeDtypeStruct((groups, *small.shape), f32),
            jax.ShapeDtypeStruct((2, 2, *piece[1:]), bf16),
            jax.ShapeDtypeStruct(grad_out.shape, f32),
            jax.ShapeDtypeStruct((2, 4 * result.shape[1], depth), bf16),
        ],
        scratch_shapes=[
            *[pltpu.VMEM(piece, bf16)] * 4,
            pltpu.VMEM((groups, 2, *piece[1:]), bf16),
            pltpu.VMEM((groups - 1, 2, *piece[1:]), bf16),
            pltpu.VMEM((2, *piece[1:]), bf16),
            pltpu.VMEM((2, *piece[1:]), bf16),
            pltpu.VMEM((7, *small.shape), f32),
            pltpu.VMEM(small.shape, f32),
            pltpu.VMEM((groups - 1, *small.shape), f32),
            pltpu.VMEM(grad_out.shape, bf16),
            pltpu.SemaphoreType.DMA((2,)),
            *[pltpu.SemaphoreType.DMA] * 4,
            *dma(groups - 1),
            *[pltpu.SemaphoreType.DMA] * 2,
            *dma(7),
            *dma(groups - 1),
            *[pltpu.SemaphoreType.DMA] * 2,
            *dma(4),
            pltpu.SemaphoreType.DMA((4,)),
            pltpu.VMEM((depth, 3 * group), f32),
            pltpu.VMEM((2, depth, WIDE), f32),
            pltpu.VMEM((tiles, 2, 2, rows, tile), bf16),
            pltpu.VMEM((tiles, 2, rows, tile), bf16),
            pltpu.VMEM((tiles, 2, rows, tile), bf16),
            pltpu.VMEM((tiles, rows, tile), bf16),
            pltpu.VMEM((half, rows, tile), bf16),
            pltpu.VMEM((half, rows, tile), bf16),
            pltpu.VMEM((groups, weight_rows, 3 * group), bf16),
            pltpu.VMEM((groups - 1, weight_rows, 3 * group), bf16),
            pltpu.VMEM((weight_rows, 3 * group), bf16),
            pltpu.VMEM((weight_rows, 3 * group), bf16),
            pltpu.VMEM((8, depth), f32),
            pltpu.VMEM((3, 8, depth), f32),
            pltpu.VMEM((8, depth), f32),
            pltpu.VMEM((2 * groups - 1, 8, depth), f32),
            *dma(tiles),
            *dma(tiles),
            *dma(half),
            *dma(groups - 1),
            *[pltpu.SemaphoreType.DMA] * 2,
            *dma(3),
            *dma(2 * groups - 1),
        ],
        compiler_params=pltpu.CompilerParams(
            vmem_limit_bytes=VMEM, collective_id=3, has_side_effects=True
        ),
        cost_estimate=cost(12 * length * depth * group, grad_query, hat_t, hat_t),
        name="entry_back",
    )(
        grad_query,
        grad_key,
        grad_value,
        hat_t,
        scaling,
        gain,
        shift,
        weight,
        grad_middle,
        middle_in,
        small,
        up,
        down,
        grad_out,
        result,
        result_in,
    )


def add(left_side, right_side):
    return (left_side.astype(f32) + right_side.astype(f32)).astype(bf16)


def by_sequence(
    tokens,
    cotangent,
    segments,
    steps,
    table,
    ada_w,
    ada_b,
    gain_one,
    w_qkv,
    w_out,
    gain_two,
    w_up,
    b_up,
    w_down,
    b_down,
):
    fsdp, tensor = lax.axis_size("fsdp"), lax.axis_size("tensor")
    context = lax.axis_size("context")
    tensor_rank = lax.axis_index("tensor")
    context_rank = lax.axis_index("context")
    fsdp_rank = lax.axis_index("fsdp")
    sequences, own_rows, depth = tokens.shape
    length = segments.shape[1]
    group = w_out.shape[0]
    part_width = w_up.shape[1]
    heads = group // HDIM
    quarter = own_rows // tensor

    mine = lax.dynamic_slice_in_dim(tokens, tensor_rank * quarter, quarter, axis=1)
    partner = [(k, (k + 1) % context) for k in range(context)]
    arrived = lax.ppermute(
        lax.dynamic_index_in_dim(mine, lax.rem(context_rank + 1, context), 0, keepdims=True),
        "context",
        partner,
    )
    other_rows = lax.all_gather(arrived, "tensor", axis=1, tiled=True)

    by_kind = w_qkv.reshape(-1, heads, 3, HDIM).transpose(0, 2, 1, 3).reshape(-1, 3 * group)
    qkv = lax.all_gather(by_kind, "fsdp", axis=0, tiled=True)
    both = ("tensor", "fsdp")
    up = lax.all_gather(w_up, both, axis=0, tiled=True).reshape(tensor, depth, part_width)
    down = lax.all_gather(w_down.T, both, axis=0, tiled=True).reshape(tensor, depth, part_width)
    out_weight = (
        lax.all_gather(w_out, both, axis=0, tiled=False)
        .reshape(tensor, fsdp, group, depth // fsdp)
        .transpose(0, 2, 1, 3)
        .reshape(depth, depth)
    )

    all_steps = lax.all_gather(steps, "fsdp", axis=0, tiled=True)
    ada_full = ada_w.astype(f32)
    choose = (all_steps[:, None] == jnp.arange(table.shape[0], dtype=jnp.int32)[None, :]).astype(f32)
    before = exact_product(choose, table.astype(f32))
    embedding, silu_back = jax.vjp(jax.nn.silu, before)
    modulation = exact_product(embedding, ada_full) + ada_b.astype(f32)
    local_mods = lax.dynamic_slice_in_dim(modulation, fsdp_rank * sequences, sequences, axis=0)
    local_mods = local_mods.reshape(sequences, 6, depth)
    gain_first, gain_second = gain_one.astype(f32), gain_two.astype(f32)
    own_mods = lax.dynamic_index_in_dim(local_mods, context_rank, 0, keepdims=False)
    gain_column = (gain_first * (1.0 + own_mods[1]))[:, None]
    shift_column = own_mods[0][:, None]
    mods = jnp.stack(
        [
            local_mods[:, 2],
            local_mods[:, 3],
            gain_second * (1.0 + local_mods[:, 4]),
            local_mods[:, 5],
        ]
        + [jnp.zeros((sequences, depth), f32)] * 4,
        axis=1,
    )

    segment = lax.dynamic_index_in_dim(segments, context_rank, 0, keepdims=False)
    same, starts, ends = document_bounds(segment)
    offsets = jnp.arange(length, dtype=jnp.int32) - jnp.sum(jnp.where(same, starts[:, None], 0), axis=0)
    angles = frequencies()[:, None] * offsets.astype(f32)[None, :]
    cosine, sine = jnp.cos(angles), jnp.sin(angles)
    tile = length // (context * tensor)
    block = tile
    first_key = jnp.sum(jnp.where(same, starts[:, None], 0), axis=0)[::tile]
    last_key = jnp.sum(jnp.where(same, ends[:, None], 0), axis=0)[tile - 1 :: tile]

    entry = partial(
        entry_call,
        gain=gain_column,
        shift=shift_column,
        weight=qkv.T,
        cosine=cosine,
        sine=sine,
        segment=segment[None, :],
        tile=tile,
    )
    per_block = own_rows // tile
    made = entry(context_rank * per_block, tokens, context_rank, earlier=None)
    other = lax.rem(context_rank + context - 1, context)
    made = entry(other * per_block, other_rows, jnp.zeros_like(other), earlier=made)
    queries, keys, keys_t, values, values_t, hat_t, scaling, norms = made
    largest = jnp.max(norms, axis=1)[: 2 * heads].reshape(heads, 2)
    safe = jnp.max(largest[:, 0] * largest[:, 1]) <= SAFE_EXPONENT**2
    ranges = jnp.stack(
        [
            first_key // block,
            (last_key + block - 1) // block,
            jnp.broadcast_to(safe.astype(jnp.int32), first_key.shape),
        ]
    ).astype(jnp.int32)
    mixture, told = attend_call(ranges, queries, keys, values_t, tile, block)

    own_segments = lax.dynamic_slice_in_dim(
        segments, context_rank * own_rows + tensor_rank * quarter, quarter, axis=1
    )
    own_cotangent = lax.dynamic_slice_in_dim(cotangent, tensor_rank * quarter, quarter, axis=1)
    (
        result,
        grad_mixture,
        grad_middle,
        grad_out,
        sums,
        bias_sums,
        up_keep,
        up_send,
        down_keep,
        down_send,
    ) = middle_call(
        mixture,
        mine.reshape(-1, depth),
        own_cotangent.reshape(-1, depth),
        (own_segments != 0).astype(f32).reshape(-1, 1),
        mods,
        b_up.astype(f32).reshape(tensor, 1, part_width),
        b_down.astype(f32)[None, :],
        out_weight,
        up,
        down,
        fsdp,
        tile=min(tile, 256),
    )
    result = result.reshape(sequences, quarter, depth)
    across = [(k, (k + 2) % tensor) for k in range(tensor)]
    result_in = lax.ppermute(result, "tensor", across)
    middle_in = lax.ppermute(
        lax.dynamic_index_in_dim(grad_middle, 1 - context_rank, 0, keepdims=False), "context", partner
    )
    small = jnp.concatenate(
        [
            sums[:, :5].reshape(-1, depth),
            bias_sums.reshape(-1, depth),
        ]
    )
    small_rows = small.shape[0]
    small = jnp.pad(small, ((0, -small_rows % 8), (0, 0)))

    up_sum = add(up_keep, lax.ppermute(up_send, "tensor", across))
    down_sum = add(down_keep, lax.ppermute(down_send, "context", partner))
    grad_out = (
        grad_out.astype(bf16)
        .reshape(tensor, group, fsdp, depth // fsdp)
        .transpose(0, 2, 1, 3)
        .reshape(tensor * fsdp, group * (depth // fsdp) // part_width, part_width)
    )
    grad_out = lax.psum_scatter(grad_out, both, scatter_dimension=0, tiled=True)[0]

    grad_query, grad_key, grad_value = attend_back_call(
        ranges, told, keys, keys_t, values, mixture, grad_mixture, cosine, sine, tile, block
    )
    (grad_query, up_sum, down_sum, result_in, middle_in, grad_out) = lax.optimization_barrier(
        (grad_query, up_sum, down_sum, result_in, middle_in, grad_out)
    )
    part, grad_qkv, entry_sums, small, pieces, grad_out, block_out = entry_back_call(
        grad_query,
        grad_key,
        grad_value,
        hat_t,
        scaling,
        gain_column,
        shift_column,
        qkv,
        grad_middle,
        middle_in,
        small,
        up_sum,
        down_sum,
        grad_out,
        result,
        result_in,
        groups=fsdp,
        tile=tile,
    )
    pieces = pieces.transpose(1, 0, 2, 3)
    pieces = pieces.reshape(2, depth // fsdp, part_width).astype(f32)
    grad_w_up = pieces[0]
    grad_w_down = pieces[1].T
    grad_w_out = grad_out.reshape(group, depth // fsdp)
    small_sums = small[:, :10].reshape(fsdp * sequences, 5, depth)
    grad_b_up = jnp.sum(small[:, 10:small_rows], axis=0).reshape(-1)
    grad_b_down = jnp.sum(small_sums[:, 4], axis=0)
    grad_gain_two = jnp.sum(small_sums[:, 2] * (1.0 + modulation[:, 4 * depth : 5 * depth]), axis=0)
    middle_mod = jnp.concatenate(
        [small_sums[:, 0], small_sums[:, 1], small_sums[:, 2] * gain_second, small_sums[:, 3]], axis=1
    )
    part = part.transpose(0, 1, 3, 2).reshape(sequences, own_rows, depth // tensor)
    grad_tokens = part.astype(f32)
    grad_w_qkv = (
        grad_qkv.reshape(-1, 3, heads, HDIM).transpose(0, 2, 1, 3).reshape(-1, 3 * group)
    )
    grad_mod = jnp.concatenate(
        [entry_sums[:, 0], entry_sums[:, 1] * gain_first, middle_mod], axis=1
    )
    grad_gain_one = jnp.sum(entry_sums[:, 1] * (1.0 + modulation[:, depth : 2 * depth]), axis=0)
    grad_ada_b = jnp.sum(grad_mod, axis=0)
    grad_ada_w = exact_transposed(embedding, grad_mod)
    grad_before = silu_back(exact_against(grad_mod, ada_full))[0]
    grad_table = exact_transposed(choose, grad_before)
    return (
        block_out,
        grad_tokens,
        grad_table,
        grad_ada_w,
        grad_ada_b,
        grad_gain_one,
        grad_w_qkv,
        grad_w_out,
        grad_gain_two,
        grad_w_up,
        grad_b_up,
        grad_w_down,
        grad_b_down,
    )


def normalize(operand):
    center = operand - jnp.mean(operand, axis=-1, keepdims=True)
    scaling = lax.rsqrt(jnp.mean(center * center, axis=-1, keepdims=True) + 1e-05)
    return (center * scaling, scaling)


def norm_back(grad_hat, hatted, scaling):
    return scaling * (
        grad_hat
        - jnp.mean(grad_hat, axis=-1, keepdims=True)
        - hatted * jnp.mean(grad_hat * hatted, axis=-1, keepdims=True)
    )


def angles_of(offsets, half_width):
    frequency = 10000.0 ** (-jnp.arange(half_width, dtype=jnp.float32) / half_width)
    angles = offsets.astype(jnp.float32)[:, None] * frequency[None, :]
    return (jnp.cos(angles)[:, None, :], jnp.sin(angles)[:, None, :])


def rotate(operand, cosine, sine_part, direction):
    half_width = operand.shape[-1] // 2
    front_half = operand[..., :half_width]
    second = operand[..., half_width:]
    return jnp.concatenate(
        [
            front_half * cosine - direction * second * sine_part,
            direction * front_half * sine_part + second * cosine,
        ],
        axis=-1,
    )


def scores_of(queries, key_rows, allowed):
    raw_scores = (
        jnp.einsum("qhd,khd->hqk", queries, key_rows, preferred_element_type=jnp.float32) * 0.125
    )
    return jnp.where(allowed[None], raw_scores, -1e30)


def attend(queries, key_rows, values, allowed):
    scores = scores_of(queries, key_rows, allowed)
    row_max = jnp.max(scores, axis=-1, keepdims=True)
    weights_raw = jnp.exp(scores - row_max)
    row_total = jnp.sum(weights_raw, axis=-1, keepdims=True)
    weights_low = (weights_raw / row_total).astype(jnp.bfloat16)
    mixture = jnp.einsum("hqk,khd->qhd", weights_low, values, preferred_element_type=jnp.float32)
    return (mixture, row_max + jnp.log(row_total))


def attend_back(queries, key_rows, values, grad_mixture, logsum, allowed, row_delta):
    scores = scores_of(queries, key_rows, allowed)
    chances = jnp.exp(scores - logsum)
    grad_chances = jnp.einsum(
        "qhd,khd->hqk", grad_mixture, values, preferred_element_type=jnp.float32
    )
    row_delta = jnp.sum(chances * grad_chances, axis=-1, keepdims=True)
    grad_scores = (chances * (grad_chances - row_delta)).astype(jnp.bfloat16)
    return (chances.astype(jnp.bfloat16), grad_scores, row_delta)


def by_block(
    tokens,
    cotangent,
    segments,
    steps,
    table,
    ada_w,
    ada_b,
    gain_one,
    w_qkv,
    w_out,
    gain_two,
    w_up,
    b_up,
    w_down,
    b_down,
):
    w_qkv, w_up, w_out, w_down = (
        lax.all_gather(w_qkv, "fsdp", axis=0, tiled=True),
        lax.all_gather(w_up, "fsdp", axis=0, tiled=True),
        lax.all_gather(w_out, "fsdp", axis=1, tiled=True),
        lax.all_gather(w_down, "fsdp", axis=1, tiled=True),
    )
    tensor_rank = lax.axis_index("tensor")
    context_rank = lax.axis_index("context")
    sequences, own_rows, model_width = tokens.shape
    length = segments.shape[1]
    local_heads = w_out.shape[0] // HDIM
    hidden_width = w_up.shape[1]
    up_bias = lax.dynamic_slice_in_dim(b_up, tensor_rank * hidden_width, hidden_width).astype(
        jnp.float32
    )
    down_bias = b_down.astype(jnp.float32)
    gain_first = gain_one.astype(jnp.float32)
    gain_second = gain_two.astype(jnp.float32)
    leader = (tensor_rank == 0).astype(jnp.float32)
    ada_full = ada_w.astype(jnp.float32)
    choose = (steps[:, None] == jnp.arange(table.shape[0], dtype=jnp.int32)[None, :]).astype(
        jnp.float32
    )
    before = exact_product(choose, table.astype(jnp.float32))
    embedding, silu_back = jax.vjp(jax.nn.silu, before)
    modulation = exact_product(embedding, ada_full) + ada_b.astype(jnp.float32)
    grad_qkv = jnp.zeros(w_qkv.shape, jnp.float32)
    grad_out_w = jnp.zeros(w_out.shape, jnp.float32)
    grad_up = jnp.zeros(w_up.shape, jnp.float32)
    grad_down = jnp.zeros(w_down.shape, jnp.float32)
    grad_bias_up = jnp.zeros((hidden_width,), jnp.float32)
    grad_bias_down = jnp.zeros((model_width,), jnp.float32)
    grad_gain_first = jnp.zeros((model_width,), jnp.float32)
    grad_gain_second = jnp.zeros((model_width,), jnp.float32)
    results = []
    partial_inputs = []
    carried = []
    grad_mods = []
    for number in range(sequences):
        shift_one, scale_one, gate_one, shift_two, scale_two, gate_two = jnp.split(
            modulation[number], 6
        )
        segment = segments[number]
        offsets = positions(segment)
        own_segment = lax.dynamic_slice_in_dim(segment, context_rank * own_rows, own_rows)
        own_offsets = lax.dynamic_slice_in_dim(offsets, context_rank * own_rows, own_rows)
        cosine, sine_part = angles_of(own_offsets, HDIM // 2)
        allowed = own_segment[:, None] == segment[None, :]
        inputs_row = tokens[number].astype(jnp.float32)
        hat_one, scaling_one = normalize(inputs_row)
        lifted_one = hat_one * gain_first
        entry_one = (lifted_one * (1.0 + scale_one) + shift_one).astype(jnp.bfloat16)
        projected = product(entry_one, w_qkv).reshape(own_rows, local_heads, 3, HDIM)
        queries = rotate(projected[:, :, 0], cosine, sine_part, 1.0).astype(jnp.bfloat16)
        key_rows = rotate(projected[:, :, 1], cosine, sine_part, 1.0).astype(jnp.bfloat16)
        values = projected[:, :, 2].astype(jnp.bfloat16)
        key_value = jnp.stack([key_rows, values], axis=1).reshape(own_rows, 2 * local_heads * HDIM)
        gathered = lax.all_gather(key_value, "context", axis=0, tiled=True).reshape(
            length, 2, local_heads, HDIM
        )
        all_keys = gathered[:, 0]
        all_values = gathered[:, 1]
        mixture, logsum = attend(queries, all_keys, all_values, allowed)
        mixture_low = mixture.reshape(own_rows, local_heads * HDIM).astype(jnp.bfloat16)
        attended = lax.psum(product(mixture_low, w_out).astype(jnp.bfloat16), "tensor").astype(
            jnp.float32
        )
        middle = inputs_row + gate_one * attended
        hat_two, scaling_two = normalize(middle)
        lifted_two = hat_two * gain_second
        entry_two = (lifted_two * (1.0 + scale_two) + shift_two).astype(jnp.bfloat16)
        hidden = product(entry_two, w_up) + up_bias
        activated, gelu_back = jax.vjp(partial(jax.nn.gelu, approximate=True), hidden)
        activated_low = activated.astype(jnp.bfloat16)
        output = (
            lax.psum(product(activated_low, w_down).astype(jnp.bfloat16), "tensor").astype(
                jnp.float32
            )
            + down_bias
        )
        results.append((middle + gate_two * output).astype(jnp.bfloat16))
        valid = (own_segment != 0).astype(jnp.float32)[:, None]
        grad_result = cotangent[number].astype(jnp.float32) * valid
        grad_output = (gate_two * grad_result).astype(jnp.bfloat16)
        grad_gate_two = jnp.sum(grad_result * output, axis=0)
        grad_bias_down = grad_bias_down + jnp.sum(grad_output.astype(jnp.float32), axis=0)
        grad_down = grad_down + transposed(activated_low, grad_output)
        grad_active = against(grad_output, w_down)
        grad_hidden = gelu_back(grad_active)[0].astype(jnp.bfloat16)
        grad_bias_up = grad_bias_up + jnp.sum(grad_hidden.astype(jnp.float32), axis=0)
        grad_up = grad_up + transposed(entry_two, grad_hidden)
        grad_entry_two = against(grad_hidden, w_up)
        grad_shift_two = jnp.sum(grad_entry_two, axis=0)
        grad_scale_two = jnp.sum(grad_entry_two * lifted_two, axis=0)
        grad_lifted_two = grad_entry_two * (1.0 + scale_two)
        grad_gain_second = grad_gain_second + jnp.sum(grad_lifted_two * hat_two, axis=0)
        part_two = norm_back(grad_lifted_two * gain_second, hat_two, scaling_two)
        grad_middle = grad_result + lax.psum(part_two.astype(jnp.bfloat16), "tensor").astype(
            jnp.float32
        )
        grad_attended = (gate_one * grad_middle).astype(jnp.bfloat16)
        grad_gate_one = jnp.sum(grad_middle * attended, axis=0)
        grad_out_w = grad_out_w + transposed(mixture_low, grad_attended)
        grad_mixture = (
            against(grad_attended, w_out).astype(jnp.bfloat16).reshape(own_rows, local_heads, HDIM)
        )
        chances_low, grad_scores, row_delta = attend_back(
            queries, all_keys, all_values, grad_mixture, logsum, allowed, None
        )
        grad_queries = (
            jnp.einsum("hqk,khd->qhd", grad_scores, all_keys, preferred_element_type=jnp.float32)
            * 0.125
        )
        grad_all_keys = (
            jnp.einsum("hqk,qhd->khd", grad_scores, queries, preferred_element_type=jnp.float32)
            * 0.125
        )
        grad_all_values = jnp.einsum(
            "hqk,qhd->khd", chances_low, grad_mixture, preferred_element_type=jnp.float32
        )
        both_grads = jnp.stack([grad_all_keys, grad_all_values], axis=1).reshape(
            length, 2 * local_heads * HDIM
        )
        own_grads = (
            lax.psum_scatter(
                both_grads.astype(jnp.bfloat16), "context", scatter_dimension=0, tiled=True
            )
            .astype(jnp.float32)
            .reshape(own_rows, 2, local_heads, HDIM)
        )
        grad_keys = own_grads[:, 0]
        grad_values = own_grads[:, 1]
        grad_queries = rotate(grad_queries, cosine, sine_part, -1.0)
        grad_keys = rotate(grad_keys, cosine, sine_part, -1.0)
        grad_projected = (
            jnp.stack([grad_queries, grad_keys, grad_values], axis=2)
            .reshape(own_rows, local_heads * 3 * HDIM)
            .astype(jnp.bfloat16)
        )
        grad_qkv = grad_qkv + transposed(entry_one, grad_projected)
        grad_entry_one = against(grad_projected, w_qkv)
        grad_shift_one = jnp.sum(grad_entry_one, axis=0)
        grad_scale_one = jnp.sum(grad_entry_one * lifted_one, axis=0)
        grad_lifted_one = grad_entry_one * (1.0 + scale_one)
        grad_gain_first = grad_gain_first + jnp.sum(grad_lifted_one * hat_one, axis=0)
        partial_inputs.append(norm_back(grad_lifted_one * gain_first, hat_one, scaling_one))
        carried.append(grad_middle)
        grad_mods.append(
            jnp.concatenate(
                [
                    grad_shift_one,
                    grad_scale_one,
                    grad_gate_one * leader,
                    grad_shift_two,
                    grad_scale_two,
                    grad_gate_two * leader,
                ]
            )
        )
    summed_inputs = lax.psum_scatter(
        jnp.stack(partial_inputs).astype(jnp.bfloat16), "tensor", scatter_dimension=2, tiled=True
    ).astype(jnp.float32)
    slice_width = model_width // lax.axis_size("tensor")
    own_middle = lax.dynamic_slice_in_dim(
        jnp.stack(carried), tensor_rank * slice_width, slice_width, axis=2
    )
    grad_tokens = summed_inputs + own_middle
    grad_mod = jnp.stack(grad_mods)
    bias_up_full = lax.dynamic_update_slice_in_dim(
        jnp.zeros((b_up.shape[0],), jnp.float32), grad_bias_up, tensor_rank * hidden_width, 0
    )
    grad_qkv, grad_up, grad_out_w, grad_down = (
        lax.psum_scatter(
            grad_qkv.astype(jnp.bfloat16), "fsdp", scatter_dimension=0, tiled=True
        ).astype(jnp.float32),
        lax.psum_scatter(
            grad_up.astype(jnp.bfloat16), "fsdp", scatter_dimension=0, tiled=True
        ).astype(jnp.float32),
        lax.psum_scatter(
            grad_out_w.astype(jnp.bfloat16), "fsdp", scatter_dimension=1, tiled=True
        ).astype(jnp.float32),
        lax.psum_scatter(
            grad_down.astype(jnp.bfloat16), "fsdp", scatter_dimension=1, tiled=True
        ).astype(jnp.float32),
    )
    grad_qkv, grad_up, grad_out_w, grad_down = (
        lax.psum(grad_qkv.astype(jnp.bfloat16), "context").astype(jnp.float32),
        lax.psum(grad_up.astype(jnp.bfloat16), "context").astype(jnp.float32),
        lax.psum(grad_out_w.astype(jnp.bfloat16), "context").astype(jnp.float32),
        lax.psum(grad_down.astype(jnp.bfloat16), "context").astype(jnp.float32),
    )
    grad_ada_b = jnp.sum(grad_mod, axis=0)
    grad_ada_w = exact_transposed(embedding, grad_mod)
    grad_embedding = exact_against(grad_mod, ada_full)
    grad_before = silu_back(grad_embedding)[0]
    grad_table = exact_transposed(choose, grad_before)
    (
        grad_table,
        grad_ada_w,
        grad_ada_b,
        grad_gain_first,
        grad_gain_second,
        bias_up_full,
        grad_bias_down,
    ) = lax.psum(
        (
            grad_table,
            grad_ada_w,
            grad_ada_b,
            grad_gain_first,
            grad_gain_second,
            bias_up_full,
            grad_bias_down * leader,
        ),
        ("fsdp", "context", "tensor"),
    )
    return (
        jnp.stack(results),
        grad_tokens,
        grad_table,
        grad_ada_w,
        grad_ada_b,
        grad_gain_first,
        grad_qkv,
        grad_out_w,
        grad_gain_second,
        grad_up,
        bias_up_full,
        grad_down,
        grad_bias_down,
    )


def solution(mesh):
    axes = dict(zip(mesh.axis_names, mesh.devices.shape))

    def whole(tokens, *others):
        sequences = tokens.shape[0] // axes["fsdp"]
        local = by_sequence if sequences == axes["context"] == 2 and axes["tensor"] == 4 else by_block
        return mapped(local, mesh)(tokens, *others)

    return whole


def mapped(local, mesh):
    return jax.shard_map(
        local,
        mesh=mesh,
        in_specs=(
            P("fsdp", "context", None),
            P("fsdp", "context", None),
            P("fsdp", None),
            P("fsdp"),
            P(),
            P(),
            P(),
            P(),
            P("fsdp", "tensor"),
            P("tensor", "fsdp"),
            P(),
            P("fsdp", "tensor"),
            P(),
            P("tensor", "fsdp"),
            P(),
        ),
        out_specs=(
            P("fsdp", "context", None),
            P("fsdp", "context", "tensor"),
            P(),
            P(),
            P(),
            P(),
            P("fsdp", "tensor"),
            P("tensor", "fsdp"),
            P(),
            P("fsdp", "tensor"),
            P(),
            P("tensor", "fsdp"),
            P(),
        ),
        check_vma=False,
    )
```

```python
import math
from functools import partial

import jax
import jax.numpy as jnp
from jax import lax
from jax.experimental import pallas as pl
from jax.experimental.pallas import tpu as pltpu
from jax.sharding import PartitionSpec as P

HDIM = 64
HALF = HDIM // 2
SEGMENTS = 5
WIDE = 128
MASKED = 2.0**100
LOG2E = math.log2(math.e)
SAFE_EXPONENT = 60.0
EPSILON = 1e-05
VMEM = 56 * 2**20
VMEM_MOST = 60 * 2**20


def cost(flops, *arrays):
    size = sum(math.prod(one.shape) * one.dtype.itemsize for one in arrays)
    return pl.CostEstimate(flops=int(flops), bytes_accessed=int(size), transcendentals=0)


precise = lax.Precision.HIGHEST
f32 = jnp.float32
bf16 = jnp.bfloat16


def product(left_side, right_side):
    return jnp.dot(left_side, right_side, preferred_element_type=jnp.float32)


def transposed(left_side, right_side):
    return lax.dot_general(
        left_side, right_side, (((0,), (0,)), ((), ())), preferred_element_type=jnp.float32
    )


def against(left_side, right_side):
    return lax.dot_general(
        left_side, right_side, (((1,), (1,)), ((), ())), preferred_element_type=jnp.float32
    )


def exact_product(left_side, right_side):
    return jnp.dot(left_side, right_side, precision=precise, preferred_element_type=jnp.float32)


def exact_transposed(left_side, right_side):
    return lax.dot_general(
        left_side,
        right_side,
        (((0,), (0,)), ((), ())),
        precision=precise,
        preferred_element_type=jnp.float32,
    )


def exact_against(left_side, right_side):
    return lax.dot_general(
        left_side,
        right_side,
        (((1,), (1,)), ((), ())),
        precision=precise,
        preferred_element_type=jnp.float32,
    )


def document_bounds(segment):
    indices = jnp.arange(segment.shape[-1], dtype=jnp.int32)
    same = segment[..., None, :] == jnp.arange(SEGMENTS, dtype=jnp.int32)[:, None]
    starts = jnp.min(jnp.where(same, indices, segment.shape[-1]), axis=-1)
    ends = jnp.max(jnp.where(same, indices + 1, 0), axis=-1)
    return same, starts, ends


def positions(segment):
    same, starts, _ = document_bounds(segment)
    first = jnp.sum(jnp.where(same, starts[..., :, None], 0), axis=-2)
    return jnp.arange(segment.shape[-1], dtype=jnp.int32) - first


def frequencies():
    return 10000.0 ** (-jnp.arange(HALF, dtype=jnp.float32) / HALF)


def copy_to(source, target, sent, arrived, **device):
    return pltpu.make_async_remote_copy(
        src_ref=source,
        dst_ref=target,
        send_sem=sent,
        recv_sem=arrived,
        device_id=device,
        device_id_type=pl.DeviceIdType.MESH,
    )


def greet(devices):
    barrier = pltpu.get_barrier_semaphore()
    for device in devices:
        pl.semaphore_signal(barrier, inc=1, device_id=device, device_id_type=pl.DeviceIdType.MESH)
    pl.semaphore_wait(barrier, len(devices))


def quarter_at(number, tensor):
    core = lax.rem(tensor, 2)
    chip = jnp.where(number < 2, tensor // 2, 1 - tensor // 2)
    return chip * 2 + jnp.where(lax.rem(number, 2) == 0, core, 1 - core)


def entry_kernel(
    tokens_ref,
    rows_ref,
    shard_ref,
    own_forward_ref,
    gain_ref,
    shift_ref,
    cosine_ref,
    sine_ref,
    segment_ref,
    query_ref,
    key_ref,
    key_t_ref,
    value_ref,
    value_t_ref,
    hat_ref,
    scale_ref,
    norm_ref,
    weight_ref,
    forward_ref,
    shards,
    weight_t,
    rows,
    arrived,
    sent_shard,
    got_shard,
    own_shard,
    sent_block,
    got_block,
    sent_across,
    got_across,
    sent_sibling,
    got_sibling,
    sent_on,
    got_on,
    sent_forward,
    got_forward,
    own_forward,
    *,
    heads,
    groups,
):
    step = pl.program_id(0)
    fsdp, context, tensor = (lax.axis_index(name) for name in ("fsdp", "context", "tensor"))
    ranks = 4
    core = lax.rem(tensor, 2)
    sibling = tensor + 1 - 2 * core
    across = lax.rem(tensor + 2, ranks)
    quarter = rows.shape[0]
    chunks = sent_block.shape[0]
    height = quarter // chunks

    def shard_copy(away):
        return copy_to(
            shard_ref,
            shards.at[fsdp],
            sent_shard.at[away - 1],
            got_shard.at[away - 1],
            fsdp=lax.rem(fsdp + away, groups),
        )

    def shard_own():
        return pltpu.make_async_copy(shard_ref, shards.at[fsdp], own_shard)

    def chunk(rank, number):
        return arrived.at[rank, pl.ds(number * height, height), :]

    def block_copy(number):
        at = pl.multiple_of(tensor * quarter, quarter) + number * height
        return copy_to(
            tokens_ref.at[1 - context, pl.ds(at, height), :],
            chunk(tensor, number),
            sent_block.at[number],
            got_block.at[number],
            context=1 - context,
        )

    def across_copy(number):
        return copy_to(
            chunk(tensor, number),
            chunk(tensor, number),
            sent_across.at[number],
            got_across.at[number],
            tensor=across,
        )

    def sibling_copy(number):
        return copy_to(
            chunk(tensor, number),
            chunk(tensor, number),
            sent_sibling.at[number],
            got_sibling.at[number],
            tensor=sibling,
        )

    def on_copy(number):
        return copy_to(
            chunk(across, number),
            chunk(across, number),
            sent_on.at[number],
            got_on.at[number],
            tensor=sibling,
        )

    forward_rows = own_forward_ref.shape[0]

    def forward_place(rank):
        return forward_ref.at[pl.ds(pl.multiple_of(rank * forward_rows, forward_rows), forward_rows), :]

    def relay_copy(origin, upward):
        place = forward_place(origin)
        side = 0 if upward else 1
        return copy_to(
            place,
            place,
            sent_forward.at[side, origin],
            got_forward.at[origin],
            fsdp=fsdp + 1 if upward else fsdp - 1,
        )

    def forward_own():
        return pltpu.make_async_copy(own_forward_ref, forward_place(fsdp), own_forward)

    def relay(origin, upward):
        @pl.when(fsdp < groups - 1 if upward else fsdp > 0)
        def _():
            relay_copy(origin, upward).start()

    def from_below(distance, act):
        @pl.when(fsdp >= distance)
        def _():
            act(fsdp - distance, True)

    def from_above(distance, act):
        @pl.when(fsdp + distance < groups)
        def _():
            act(fsdp + distance, False)

    def hand_over(distance):
        def act(origin, upward):
            relay_copy(origin, upward).wait_recv()
            relay(origin, upward)

        from_below(distance, act)
        from_above(distance, act)

    def finish_forward():
        def sent(origin, upward):
            @pl.when(fsdp < groups - 1 if upward else fsdp > 0)
            def _():
                relay_copy(origin, upward).wait_send()

        sent(fsdp, True)
        sent(fsdp, False)
        for distance in range(1, groups):
            from_below(distance, sent)
            from_above(distance, sent)

    def take(numbers):
        for number in numbers:
            block_copy(number).wait_recv()
            across_copy(number).start()
            sibling_copy(number).start()

    def pass_on(numbers):
        for number in numbers:
            across_copy(number).wait_recv()
            on_copy(number).start()

    @pl.when(step == 0)
    def _():
        shard_own().start()
        greet(
            [{"fsdp": lax.rem(fsdp + away, groups)} for away in range(1, groups)]
            + [{"context": 1 - context}, {"tensor": sibling}, {"tensor": across}]
        )
        for away in range(1, groups):
            shard_copy(away).start()
        for number in range(chunks):
            block_copy(number).start()
        forward_own().start()
        take(range(chunks - 1))
        shard_own().wait()
        for away in range(1, groups):
            shard_copy(away).wait_recv()
        for number in range(groups):
            weight_ref[number * shards.shape[1] : (number + 1) * shards.shape[1], :] = shards[number]
        forward_own().wait()
        relay(fsdp, True)
        relay(fsdp, False)
        weight_t[...] = weight_ref[...].T

    @pl.when(step == 1)
    def _():
        take([chunks - 1])
        pass_on(range(chunks // 2))

    @pl.when(step == 2)
    def _():
        pass_on(range(chunks // 2, chunks))

    half = 4

    for distance in range(1, groups):

        @pl.when(step == 1 + 2 * distance)
        def _():
            hand_over(distance)

    @pl.when(step < half)
    def _():
        rows[...] = rows_ref[0]

    @pl.when(step == half + 1)
    def _():
        for number in range(chunks):
            sibling_copy(number).wait_recv()

    @pl.when(step == half + 3)
    def _():
        for number in range(chunks):
            on_copy(number).wait_recv()

    @pl.when(step >= half)
    def _():
        rows[...] = arrived[quarter_at(step - half, tensor)]

    inputs = rows[...].astype(f32).T
    center = inputs - jnp.mean(inputs, axis=0, keepdims=True)
    scaling = lax.rsqrt(jnp.mean(center * center, axis=0, keepdims=True) + EPSILON)
    hat = center * scaling
    hat_ref[...] = hat.astype(bf16)
    scale_ref[...] = scaling
    entry = (hat * gain_ref[...] + shift_ref[...]).astype(bf16)
    projected = product(weight_t[...], entry)
    cosine = cosine_ref[...]
    sine = sine_ref[...]
    tokens = cosine.shape[1]
    group = heads * HDIM
    segment = segment_ref[...]
    number = lax.broadcasted_iota(jnp.int32, (WIDE - HDIM, tokens), 0)
    same = (number == segment).astype(f32)
    extra_query = same
    extra_key = jnp.where(
        number < SEGMENTS, (same - 1.0) * MASKED, jnp.where(number < SEGMENTS + 3, 1.0, 0.0)
    )
    extra_value = jnp.where(number < 3, 1.0, 0.0)
    norms = []
    for head in range(heads):

        def turned(kind, factor):
            at = kind * group + head * HDIM
            front = projected[at : at + HALF]
            back = projected[at + HALF : at + HDIM]
            return jnp.concatenate(
                [(front * cosine - back * sine) * factor, (front * sine + back * cosine) * factor],
                axis=0,
            )

        queries = turned(0, 0.125 * LOG2E)
        keys = turned(1, 1.0)
        values = projected[2 * group + head * HDIM : 2 * group + (head + 1) * HDIM]
        norms.append(jnp.sum(queries * queries, axis=0, keepdims=True))
        norms.append(jnp.sum(keys * keys, axis=0, keepdims=True))
        query_ref[head] = jnp.concatenate([queries, extra_query], axis=0).astype(bf16)
        key_ref[head] = jnp.concatenate([keys, extra_key], axis=0).T.astype(bf16)
        key_t_ref[head] = keys.astype(bf16)
        wide_values = jnp.concatenate([values, extra_value], axis=0)
        value_ref[head] = wide_values.T.astype(bf16)
        value_t_ref[head] = wide_values[: value_t_ref.shape[1]].astype(bf16)
    norms += [jnp.zeros_like(norms[0])] * (norm_ref.shape[0] - len(norms))
    norm_ref[...] = jnp.concatenate(norms, axis=0)

    @pl.when(step == pl.num_programs(0) - 1)
    def _():
        for away in range(1, groups):
            shard_copy(away).wait_send()
        for number in range(chunks):
            block_copy(number).wait_send()
            across_copy(number).wait_send()
            sibling_copy(number).wait_send()
            on_copy(number).wait_send()
        finish_forward()


def entry_call(tokens, shard, forward_shard, gain, shift, cosine, sine, segment, groups, tile):
    length = cosine.shape[1]
    shard_rows, width = shard.shape
    depth = shard_rows * groups
    heads = width // (3 * HDIM)
    half = tokens.shape[1] // tile
    chunks = 4

    def place(i):
        context = lax.axis_index("context")
        other = (1 - context) * half + quarter_at(jnp.maximum(i - half, 0), lax.axis_index("tensor"))
        return jnp.where(i < half, context * half + i, other)

    lanes = lambda i: (0, place(i))
    heads_lanes = lambda i: (0, 0, place(i))
    heads_rows = lambda i: (0, place(i), 0)
    whole = lambda i: (0, 0)
    shapes = [
        jax.ShapeDtypeStruct((heads, WIDE, length), bf16),
        jax.ShapeDtypeStruct((heads, length, WIDE), bf16),
        jax.ShapeDtypeStruct((heads, HDIM, length), bf16),
        jax.ShapeDtypeStruct((heads, length, WIDE), bf16),
        jax.ShapeDtypeStruct((heads, HDIM + 16, length), bf16),
        jax.ShapeDtypeStruct((depth, length), bf16),
        jax.ShapeDtypeStruct((1, length), f32),
        jax.ShapeDtypeStruct((8, length), f32),
        jax.ShapeDtypeStruct((depth, width), bf16),
        jax.ShapeDtypeStruct((depth, forward_shard.shape[1]), bf16),
    ]
    dma = lambda *shape: [pltpu.SemaphoreType.DMA(shape)] * 2
    return pl.pallas_call(
        partial(entry_kernel, heads=heads, groups=groups),
        grid=(2 * half,),
        in_specs=[
            pl.BlockSpec(memory_space=pl.ANY),
            pl.BlockSpec(
                (1, tile, depth),
                lambda i: (lax.axis_index("context"), jnp.minimum(i, half - 1), 0),
            ),
            pl.BlockSpec(memory_space=pl.ANY),
            pl.BlockSpec(forward_shard.shape, whole),
            pl.BlockSpec((depth, 1), whole),
            pl.BlockSpec((depth, 1), whole),
            pl.BlockSpec((HALF, tile), lanes),
            pl.BlockSpec((HALF, tile), lanes),
            pl.BlockSpec((1, tile), lanes),
        ],
        out_specs=[
            pl.BlockSpec((heads, WIDE, tile), heads_lanes),
            pl.BlockSpec((heads, tile, WIDE), heads_rows),
            pl.BlockSpec((heads, HDIM, tile), heads_lanes),
            pl.BlockSpec((heads, tile, WIDE), heads_rows),
            pl.BlockSpec((heads, HDIM + 16, tile), heads_lanes),
            pl.BlockSpec((depth, tile), lanes),
            pl.BlockSpec((1, tile), lanes),
            pl.BlockSpec((8, tile), lanes),
            pl.BlockSpec((depth, width), whole),
            pl.BlockSpec(memory_space=pl.ANY),
        ],
        out_shape=shapes,
        scratch_shapes=[
            pltpu.VMEM((groups, shard_rows, width), bf16),
            pltpu.VMEM((width, depth), bf16),
            pltpu.VMEM((tile, depth), bf16),
            pltpu.VMEM((4, tile, depth), bf16),
            *dma(groups - 1),
            pltpu.SemaphoreType.DMA,
            *dma(chunks),
            *dma(chunks),
            *dma(chunks),
            *dma(chunks),
            pltpu.SemaphoreType.DMA((2, groups)),
            pltpu.SemaphoreType.DMA((groups,)),
            pltpu.SemaphoreType.DMA,
        ],
        compiler_params=pltpu.CompilerParams(
            vmem_limit_bytes=VMEM, collective_id=1, has_side_effects=True
        ),
        cost_estimate=cost(4 * tokens.shape[1] * depth * width, tokens, *shapes),
        name="entry",
    )(tokens, tokens, shard, forward_shard, gain, shift, cosine, sine, segment)


def attend_kernel(range_ref, query_ref, key_ref, value_ref, out_ref, told_ref, total_ref, top_ref, *, block):
    step = pl.program_id(0)
    first, last = range_ref[0, step], range_ref[1, step]
    heads = query_ref.shape[0]
    total_ref[...] = jnp.zeros_like(total_ref)

    def scores(head, at):
        return product(key_ref[head, pl.ds(at, block), :], query_ref[head])

    def mix(head, at, weights):
        return product(value_ref[head, :, pl.ds(at, block)], weights)

    @pl.when(range_ref[2, 0] == 1)
    def _():
        top_ref[...] = jnp.zeros_like(top_ref)

        def body(number, carry):
            at = pl.multiple_of(number * block, block)
            raw = [scores(head, at) for head in range(heads)]
            weights = [jnp.exp2(one).astype(bf16) for one in raw]
            for head in range(heads):
                total_ref[head] += mix(head, at, weights[head])
            return carry

        lax.fori_loop(first, last, body, 0)

    @pl.when(range_ref[2, 0] != 1)
    def _():
        top_ref[...] = jnp.full_like(top_ref, -3e38)

        def body(number, carry):
            at = pl.multiple_of(number * block, block)
            for head in range(heads):
                raw = scores(head, at)
                before = top_ref[head]
                top = jnp.maximum(before, jnp.max(raw, axis=0, keepdims=True))
                weights = jnp.exp2(raw - top).astype(bf16)
                total_ref[head] = total_ref[head] * jnp.exp2(before - top) + mix(head, at, weights)
                top_ref[head] = top
            return carry

        lax.fori_loop(first, last, body, 0)

    tile = query_ref.shape[2]
    number = lax.broadcasted_iota(jnp.int32, (16, tile), 0)
    for head in range(heads):
        total = total_ref[head]
        mass = total[HDIM : HDIM + 1]
        out_ref[0, pl.ds(head * HDIM, HDIM), :] = (total[:HDIM] * (1.0 / mass)).astype(bf16)
        rows = split_rows(-(top_ref[head] + jnp.log2(mass)), number, SEGMENTS)
        told_ref[head, :HDIM, :] = query_ref[head, :HDIM, :]
        told_ref[head, HDIM : HDIM + 16, :] = jnp.where(
            number < SEGMENTS, query_ref[head, HDIM : HDIM + 16, :].astype(f32), rows
        ).astype(bf16)
        told_ref[head, HDIM + 16 :, :] = query_ref[head, HDIM + 16 :, :]


def split_rows(values, number, first):
    high = values.astype(bf16).astype(f32)
    rest = values - high
    middle = rest.astype(bf16).astype(f32)
    low = rest - middle
    return jnp.where(
        number == first,
        high,
        jnp.where(number == first + 1, middle, jnp.where(number == first + 2, low, 0.0)),
    )


def attend_call(ranges, queries, keys, values_t, tile, block):
    heads, _, length = queries.shape
    rows = values_t.shape[1]
    return pl.pallas_call(
        partial(attend_kernel, block=block),
        grid_spec=pltpu.PrefetchScalarGridSpec(
            num_scalar_prefetch=1,
            grid=(length // tile,),
            in_specs=[
                pl.BlockSpec((heads, WIDE, tile), lambda i, r: (0, 0, i)),
                pl.BlockSpec((heads, length, WIDE), lambda i, r: (0, 0, 0)),
                pl.BlockSpec((heads, rows, length), lambda i, r: (0, 0, 0)),
            ],
            out_specs=[
                pl.BlockSpec((1, heads * HDIM, tile), lambda i, r: (i, 0, 0)),
                pl.BlockSpec((heads, WIDE, tile), lambda i, r: (0, 0, i)),
            ],
            scratch_shapes=[
                pltpu.VMEM((heads, rows, tile), f32),
                pltpu.VMEM((heads, 1, tile), f32),
            ],
        ),
        out_shape=[
            jax.ShapeDtypeStruct((length // tile, heads * HDIM, tile), bf16),
            jax.ShapeDtypeStruct((heads, WIDE, length), bf16),
        ],
        compiler_params=pltpu.CompilerParams(vmem_limit_bytes=VMEM),
        cost_estimate=cost(4 * heads * length * length * WIDE, queries, keys, values_t),
        name="attend",
    )(ranges, queries, keys, values_t)


def attend_back_kernel(
    range_ref,
    query_ref,
    key_ref,
    key_t_ref,
    value_ref,
    mixture_ref,
    grad_ref,
    cosine_ref,
    sine_ref,
    grad_query_ref,
    grad_key_ref,
    grad_value_ref,
    wide_ref,
    query_total,
    key_total,
    value_total,
    *,
    block,
):
    step = pl.program_id(0)
    first, last = range_ref[0, step], range_ref[1, step]
    heads, _, tile = query_ref.shape

    @pl.when(step == 0)
    def _():
        wide_ref[...] = jnp.zeros_like(wide_ref)
        key_total[...] = jnp.zeros_like(key_total)
        value_total[...] = jnp.zeros_like(value_total)

    number = lax.broadcasted_iota(jnp.int32, (16, tile), 0)
    query_total[...] = jnp.zeros_like(query_total)
    for head in range(heads):
        at = pl.ds(head * HDIM, HDIM)
        grad = grad_ref[0, at, :]
        delta = jnp.sum(grad.astype(f32) * mixture_ref[0, at, :].astype(f32), axis=0, keepdims=True)
        wide_ref[head, :HDIM, :] = grad
        wide_ref[head, HDIM : HDIM + 16, :] = split_rows(-delta, number, 0).astype(bf16)

    def body(number, carry):
        at = pl.multiple_of(number * block, block)
        rows = pl.ds(at, block)
        raw = [product(key_ref[head, rows, :], query_ref[head]) for head in range(heads)]
        slope = [product(value_ref[head, rows, :], wide_ref[head]) for head in range(heads)]
        for head in range(heads):
            weights = jnp.exp2(raw[head])
            grad_scores = (weights * slope[head]).astype(bf16)
            query_total[head] += product(key_t_ref[head, :, rows], grad_scores)
            key_total[head, :, rows] += against(query_ref[head, :HDIM, :], grad_scores)
            value_total[head, :, rows] += against(wide_ref[head, :HDIM, :], weights.astype(bf16))
        return carry

    lax.fori_loop(first, last, body, 0)

    def turned_back(grads, cosine, sine):
        front, back = grads[:HALF], grads[HALF:]
        return jnp.concatenate([front * cosine + back * sine, back * cosine - front * sine], axis=0)

    own = pl.ds(pl.multiple_of(step * tile, tile), tile)
    for head in range(heads):
        at = pl.ds(head * HDIM, HDIM)
        grad_query_ref[at, :] = turned_back(
            query_total[head] * 0.125, cosine_ref[:, own], sine_ref[:, own]
        ).astype(bf16)

    @pl.when(step == pl.num_programs(0) - 1)
    def _():
        for head in range(heads):
            at = pl.ds(head * HDIM, HDIM)
            grad_key_ref[at, :] = turned_back(
                key_total[head] * (1.0 / LOG2E), cosine_ref[...], sine_ref[...]
            ).astype(bf16)
            grad_value_ref[at, :] = value_total[head].astype(bf16)


def attend_back_call(
    ranges, queries, keys, keys_t, values, mixture, grad_mixture, cosine, sine, tile, block
):
    heads, _, length = queries.shape
    group = heads * HDIM
    whole2 = lambda i, r: (0, 0)
    whole3 = lambda i, r: (0, 0, 0)
    return pl.pallas_call(
        partial(attend_back_kernel, block=block),
        grid_spec=pltpu.PrefetchScalarGridSpec(
            num_scalar_prefetch=1,
            grid=(length // tile,),
            in_specs=[
                pl.BlockSpec((heads, WIDE, tile), lambda i, r: (0, 0, i)),
                pl.BlockSpec((heads, length, WIDE), whole3),
                pl.BlockSpec((heads, HDIM, length), whole3),
                pl.BlockSpec((heads, length, WIDE), whole3),
                pl.BlockSpec((1, group, tile), lambda i, r: (i, 0, 0)),
                pl.BlockSpec((1, group, tile), lambda i, r: (i, 0, 0)),
                pl.BlockSpec((HALF, length), whole2),
                pl.BlockSpec((HALF, length), whole2),
            ],
            out_specs=[
                pl.BlockSpec((group, tile), lambda i, r: (0, i)),
                pl.BlockSpec((group, length), whole2),
                pl.BlockSpec((group, length), whole2),
            ],
            scratch_shapes=[
                pltpu.VMEM((heads, WIDE, tile), bf16),
                pltpu.VMEM((heads, HDIM, tile), f32),
                pltpu.VMEM((heads, HDIM, length), f32),
                pltpu.VMEM((heads, HDIM, length), f32),
            ],
        ),
        out_shape=[jax.ShapeDtypeStruct((group, length), bf16)] * 3,
        compiler_params=pltpu.CompilerParams(vmem_limit_bytes=VMEM),
        cost_estimate=cost(10 * heads * length * length * WIDE, queries, keys, values),
        name="attend_back",
    )(ranges, queries, keys, keys_t, values, mixture, grad_mixture, cosine, sine)


def middle_kernel(
    mixture_ref,
    rows_ref,
    cotangent_ref,
    valid_ref,
    mod_ref,
    up_bias_ref,
    down_bias_ref,
    out_weight_ref,
    own_ref,
    other_ref,
    across_ref,
    result_ref,
    grad_mixture_ref,
    grad_middle_ref,
    grad_out_ref,
    sums_ref,
    bias_sums_ref,
    up_keep_ref,
    up_send_ref,
    down_keep_ref,
    down_send_ref,
    own_mixture,
    entry_rows,
    entry_columns,
    grad_output_rows,
    grad_output_columns,
    attended_rows,
    output_rows,
    grad_entry_rows,
    active,
    grad_hidden,
    grad_staged,
    forward_ref,
    landed,
    home_grads,
    to_sibling,
    from_sibling,
    staged_up,
    staged_down,
    sent_mixture,
    got_mixture,
    own_copied,
    sent_grad,
    got_grad,
    grad_copied,
    sent_part,
    got_part,
    kept,
    sent_next,
    got_next,
    loaded,
    sent_other,
    got_other,
    sent_last,
    got_last,
    *,
    tile,
    tiles,
    parts,
    groups,
):
    step = pl.program_id(0)
    context, tensor = lax.axis_index("context"), lax.axis_index("tensor")
    ranks = 4
    everyone = 2 * ranks
    place = context * ranks + tensor
    core = lax.rem(tensor, 2)
    sibling = tensor + 1 - 2 * core
    depth = rows_ref.shape[1]
    group = depth // ranks
    per_sequence = tiles // 2
    per_part = tiles + 1
    back_from = tiles + parts * per_part - 1
    last_step = back_from + tiles
    root = math.sqrt(2.0 / math.pi)

    def member(away):
        other = lax.rem(place + away, everyone)
        return other, {"context": other // ranks, "tensor": lax.rem(other, ranks)}

    def mixture_copy(away):
        other, device = member(away)
        return copy_to(
            mixture_ref.at[other],
            own_mixture.at[place],
            sent_mixture.at[away - 1],
            got_mixture.at[lax.rem(place + everyone, everyone)],
            **device,
        )

    def mixture_arrival(source):
        return pltpu.make_async_remote_copy(
            src_ref=mixture_ref.at[source],
            dst_ref=own_mixture.at[source],
            send_sem=sent_mixture.at[0],
            recv_sem=got_mixture.at[source],
            device_id={"tensor": sibling},
            device_id_type=pl.DeviceIdType.MESH,
        )

    def own_copy():
        return pltpu.make_async_copy(mixture_ref.at[place], own_mixture.at[place], own_copied)

    def part_copy(slot):
        return copy_to(
            to_sibling, from_sibling.at[slot], sent_part.at[slot], got_part.at[slot], tensor=sibling
        )

    across = lax.rem(tensor + 2, ranks)
    height = depth // groups

    def rows_of(number):
        return pl.ds(number * height, height)

    def next_copy(kind):
        return copy_to(
            forward_ref.at[kind],
            landed.at[0, kind],
            sent_next.at[kind],
            got_next.at[kind],
            tensor=sibling,
        )

    def weight_loads():
        return [
            pltpu.make_async_copy(own_ref, forward_ref.at[context], loaded.at[0]),
            pltpu.make_async_copy(other_ref, forward_ref.at[1 - context], loaded.at[1]),
            pltpu.make_async_copy(across_ref, landed.at[1, context], loaded.at[2]),
        ]

    def other_copy(kind, number):
        place = landed.at[1, kind, rows_of(number), :]
        return copy_to(place, place, sent_other.at[number], got_other.at[number], context=1 - context)

    def last_copy(kind, number):
        return copy_to(
            landed.at[1, kind, rows_of(number), :],
            landed.at[2, kind, rows_of(number), :],
            sent_last.at[kind, number],
            got_last.at[kind, number],
            tensor=sibling,
        )

    def take_other(numbers):
        for number in numbers:
            other_copy(1 - context, number).wait_recv()
            last_copy(1 - context, number).start()

    def gradient_lanes(at):
        return pl.ds(pl.multiple_of(lax.rem(at, per_sequence) * tile, tile), tile)

    def sequence_of(at):
        return lax.rem(at // per_sequence + context, 2)

    def gradient_copy(at, rank):
        return copy_to(
            grad_staged.at[at, rank],
            grad_mixture_ref.at[place, :, gradient_lanes(at)],
            sent_grad.at[at, rank],
            got_grad.at[place, lax.rem(at, per_sequence)],
            context=sequence_of(at),
            tensor=rank,
        )

    def gradient_own(at):
        return pltpu.make_async_copy(
            grad_staged.at[at, tensor],
            grad_mixture_ref.at[place, :, gradient_lanes(at)],
            grad_copied.at[lax.rem(at, per_sequence)],
        )

    def gradient_arrival(source, number):
        return pltpu.make_async_remote_copy(
            src_ref=grad_staged.at[0, 0],
            dst_ref=grad_mixture_ref.at[source, :, pl.ds(number * tile, tile)],
            send_sem=sent_grad.at[0, 0],
            recv_sem=got_grad.at[source, number],
            device_id={"tensor": sibling},
            device_id_type=pl.DeviceIdType.MESH,
        )

    def kept_copies(slot):
        if slot == 1:
            return [
                pltpu.make_async_copy(staged_up, up_send_ref, kept.at[0]),
                pltpu.make_async_copy(staged_down.at[0], down_keep_ref.at[0], kept.at[1]),
                pltpu.make_async_copy(staged_down.at[1], down_send_ref.at[0], kept.at[2]),
            ]
        return [
            pltpu.make_async_copy(staged_up, up_keep_ref, kept.at[3]),
            pltpu.make_async_copy(staged_down.at[0], down_keep_ref.at[1], kept.at[4]),
            pltpu.make_async_copy(staged_down.at[1], down_send_ref.at[1], kept.at[5]),
        ]

    def tile_of(at):
        sequence = sequence_of(at)
        rows = pl.ds(pl.multiple_of(at * tile, tile), tile)
        mods = mod_ref[sequence]
        lanes = gradient_lanes(at)
        mixture_t = jnp.concatenate(
            [own_mixture[sequence * ranks + rank, :, lanes] for rank in range(ranks)], axis=0
        )
        return rows, mixture_t, tuple(mods[k : k + 1] for k in range(4))

    def normal(attended, gate_one):
        middle = rows_ref[...].astype(f32) + gate_one * attended
        center = middle - jnp.mean(middle, axis=-1, keepdims=True)
        scaling = lax.rsqrt(jnp.mean(center * center, axis=-1, keepdims=True) + EPSILON)
        return middle, center * scaling, scaling

    @pl.when(step == 0)
    def _():
        own_copy().start()
        for one in weight_loads():
            one.start()
        greet([member(away)[1] for away in range(1, everyone)])
        for near in (True, False):
            for away in range(1, everyone):

                @pl.when((member(away)[0] // ranks == context) == near)
                def _():
                    mixture_copy(away).start()

        sums_ref[...] = jnp.zeros_like(sums_ref)
        bias_sums_ref[...] = jnp.zeros_like(bias_sums_ref)
        grad_out_ref[...] = jnp.zeros_like(grad_out_ref)

    for sequence in range(2):

        @pl.when(step == lax.rem(sequence + context, 2) * per_sequence)
        def _():
            for rank in range(ranks):
                source = sequence * ranks + rank

                @pl.when(place == source)
                def _():
                    own_copy().wait()

                @pl.when(place != source)
                def _():
                    mixture_arrival(source).wait_recv()

    @pl.when(step == per_sequence)
    def _():
        for one in weight_loads():
            one.wait()
        for kind in range(2):
            next_copy(kind).start()
        for number in range(groups):
            other_copy(context, number).start()
            last_copy(context, number).start()

    @pl.when(step == tiles + per_part)
    def _():
        for kind in range(2):
            next_copy(kind).wait_recv()

    @pl.when(step == tiles + 2 * per_part - 2)
    def _():
        take_other(range(groups // 2))

    @pl.when(step == tiles + 2 * per_part - 1)
    def _():
        take_other(range(groups // 2, groups))

    @pl.when(step == tiles + 2 * per_part)
    def _():
        for kind in range(2):
            for number in range(groups):
                last_copy(kind, number).wait_recv()

    @pl.when(step < tiles)
    def _():
        rows, mixture_t, (gate_one, shift_two, gain_two, gate_two) = tile_of(step)
        attended = product(mixture_t.T, out_weight_ref[...])
        attended_rows[rows, :] = attended
        _, hat, _ = normal(attended, gate_one)
        entry = (hat * gain_two + shift_two).astype(bf16)
        grad_output = (gate_two * (cotangent_ref[...].astype(f32) * valid_ref[...])).astype(bf16)
        entry_rows[rows, :] = entry
        entry_columns[:, rows] = entry.T
        grad_output_rows[rows, :] = grad_output
        grad_output_columns[:, rows] = grad_output.T
        output_rows[rows, :] = jnp.broadcast_to(down_bias_ref[...], (tile, depth))
        grad_entry_rows[rows, :] = jnp.zeros((tile, depth), f32)

    inner = lax.rem(step - tiles, per_part)
    position = (step - tiles) // per_part
    in_parts = (step >= tiles) & (step < back_from)

    def part_tile(up, down):
        rows = pl.ds(pl.multiple_of(inner * tile, tile), tile)
        number = part_at(position, tensor)
        hidden = product(entry_rows[rows, :], up[...]) + up_bias_ref[0]
        square = hidden * hidden
        bent = jnp.tanh(root * hidden * (1.0 + 0.044715 * square))
        half = 0.5 * (1.0 + bent)
        activated = (hidden * half).astype(bf16)
        slope = half + (0.5 * root) * hidden * (1.0 - bent * bent) * (1.0 + 0.134145 * square)
        grads = (product(grad_output_rows[rows, :], down[...]) * slope).astype(bf16)
        output_rows[rows, :] += against(activated, down[...])
        grad_entry_rows[rows, :] += against(grads, up[...])
        active[rows, :] = activated
        grad_hidden[rows, :] = grads
        bias_sums_ref[number] += jnp.sum(grads.astype(f32), axis=0, keepdims=True)

    @pl.when(in_parts & (inner < tiles) & (position == 0))
    def _():
        part_tile(forward_ref.at[0], forward_ref.at[1])

    @pl.when(in_parts & (inner < tiles) & (position > 0))
    def _():
        place = lax.rem((position - 1) * 2, 3)
        part_tile(landed.at[place, 0], landed.at[place, 1])

    def products(other):
        at = rows_of(other)
        return [
            product(entry_columns[at, :], grad_hidden[...]),
            product(grad_output_columns[at, :], active[...]),
        ]

    def gather_home(slot, own):
        part_copy(slot).wait_recv()
        if slot:
            for one in kept_copies(0):
                one.wait()
        for other in range(groups):
            for kind, (staged, term) in enumerate(zip((staged_up, staged_down), own(other))):
                total = (term + from_sibling[slot, kind, rows_of(other), :].astype(f32)).astype(bf16)
                staged[context, other] = total[: height // 2]
                staged[1 - context, other] = total[height // 2 :]
        for one in kept_copies(slot):
            one.start()

    for turn in range(parts):

        @pl.when(step == (tiles + turn * per_part + tiles if turn < parts - 1 else last_step))
        def _():
            if turn == 2:
                gather_home(0, lambda other: [home_grads[kind, rows_of(other), :].astype(f32) for kind in range(2)])
                part_copy(0).wait_send()
            if turn == 3:
                gather_home(1, products)
                return
            target = home_grads if turn == 0 else to_sibling
            for other in range(groups):
                for kind, term in enumerate(products(other)):
                    target[kind, rows_of(other), :] = term.astype(bf16)
            if turn:
                part_copy(turn - 1).start()

    @pl.when((step >= back_from) & (step < last_step))
    def _():
        at = lax.rem(step - back_from + per_sequence, tiles)
        sequence = sequence_of(at)
        rows, mixture_t, (gate_one, _, gain_two, gate_two) = tile_of(at)
        attended = attended_rows[rows, :]
        middle, hat, scaling = normal(attended, gate_one)
        output = output_rows[rows, :]
        grad_entry = grad_entry_rows[rows, :]
        grad_result = cotangent_ref[...].astype(f32) * valid_ref[...]
        result_ref[...] = (middle + gate_two * output).astype(bf16)
        grad_lifted = grad_entry * gain_two
        grad_middle = grad_result + scaling * (
            grad_lifted
            - jnp.mean(grad_lifted, axis=-1, keepdims=True)
            - hat * jnp.mean(grad_lifted * hat, axis=-1, keepdims=True)
        )
        grad_attended = (gate_one * grad_middle).astype(bf16)
        grad_mixture = against(out_weight_ref[...], grad_attended).astype(bf16)
        for rank in range(ranks):
            grad_staged[at, rank] = grad_mixture[rank * group : (rank + 1) * group]
        for rank in range(ranks):
            own = (sequence == context) & (tensor == rank)

            @pl.when(own)
            def _():
                gradient_own(at).start()

            @pl.when(jnp.logical_not(own))
            def _():
                gradient_copy(at, rank).start()

        grad_middle_ref[0] = grad_middle.T.astype(bf16)
        grad_out_ref[...] += product(mixture_t, grad_attended)
        lines = [
            jnp.sum(grad_middle * attended, axis=0, keepdims=True),
            jnp.sum(grad_entry, axis=0, keepdims=True),
            jnp.sum(grad_entry * hat, axis=0, keepdims=True),
            jnp.sum(grad_result * output, axis=0, keepdims=True),
            jnp.sum(grad_output_rows[rows, :].astype(f32), axis=0, keepdims=True),
        ]
        lines += [jnp.zeros_like(lines[0])] * (sums_ref.shape[1] - len(lines))
        sums_ref[sequence] += jnp.concatenate(lines, axis=0)

    @pl.when(step == last_step)
    def _():
        for source in range(everyone):
            for number in range(per_sequence):

                @pl.when(place != source)
                def _():
                    gradient_arrival(source, number).wait_recv()

        for at in range(tiles):
            for rank in range(ranks):
                own = (sequence_of(at) == context) & (tensor == rank)

                @pl.when(own)
                def _():
                    gradient_own(at).wait()

                @pl.when(jnp.logical_not(own))
                def _():
                    gradient_copy(at, rank).wait_send()

        for away in range(1, everyone):
            mixture_copy(away).wait_send()
        for kind in range(2):
            next_copy(kind).wait_send()
        for number in range(groups):
            other_copy(context, number).wait_send()
            for kind in range(2):
                last_copy(kind, number).wait_send()
        part_copy(1).wait_send()
        for one in kept_copies(1):
            one.wait()


def part_at(position, tensor):
    return quarter_at(jnp.where(position < 2, position, 5 - position), tensor)


def middle_call(
    mixture, rows, cotangent, valid, mods, up_bias, down_bias, out_weight, own_weight, other_weight, across, groups, tile
):
    pieces, group, own = mixture.shape
    tokens, depth = rows.shape
    parts, _, part_width = up_bias.shape
    tiles = tokens // tile
    per_sequence = tiles // 2
    per_part = tiles + 1
    back_from = tiles + parts * per_part - 1
    half = depth // groups // 2

    def in_order(at):
        sequence = lax.rem(at // per_sequence + lax.axis_index("context"), 2)
        return sequence, lax.rem(at, per_sequence)

    def back_number(i):
        return lax.rem(jnp.clip(i - back_from, 0, tiles - 1) + per_sequence, tiles)

    def token_tile(i):
        at = jnp.where(i < tiles, i, back_number(i))
        sequence, number = in_order(at)
        return sequence * per_sequence + number, 0

    def part_block(i):
        position = jnp.clip((i - tiles) // per_part, 0, parts - 1)
        return part_at(position, lax.axis_index("tensor")), 0, 0

    def back_tile(i):
        return in_order(back_number(i))

    whole2 = lambda i: (0, 0)
    whole3 = lambda i: (0, 0, 0)
    once = pl.Buffered(1)
    hbm = pl.BlockSpec(memory_space=pl.ANY)
    kept = jax.ShapeDtypeStruct((2, groups, half, part_width), bf16)
    wide = (tokens, depth)
    return pl.pallas_call(
        partial(middle_kernel, tile=tile, tiles=tiles, parts=parts, groups=groups),
        grid=(back_from + tiles + 1,),
        in_specs=[
            hbm,
            pl.BlockSpec((tile, depth), token_tile),
            pl.BlockSpec((tile, depth), token_tile),
            pl.BlockSpec((tile, 1), token_tile),
            pl.BlockSpec(mods.shape, whole3, pipeline_mode=once),
            pl.BlockSpec((1, 1, part_width), part_block),
            pl.BlockSpec((1, depth), whole2, pipeline_mode=once),
            pl.BlockSpec((depth, depth), whole2, pipeline_mode=once),
            hbm,
            hbm,
            hbm,
        ],
        out_specs=[
            pl.BlockSpec(
                (tile, depth), lambda i: (back_tile(i)[0] * per_sequence + back_tile(i)[1], 0)
            ),
            hbm,
            pl.BlockSpec(
                (1, depth, tile),
                lambda i: (back_tile(i)[0], 0, back_tile(i)[1]),
            ),
            pl.BlockSpec((depth, depth), whole2),
            pl.BlockSpec((2, 8, depth), whole3),
            pl.BlockSpec((parts, 1, part_width), whole3),
            hbm,
            hbm,
            hbm,
            hbm,
        ],
        out_shape=[
            jax.ShapeDtypeStruct((tokens, depth), bf16),
            jax.ShapeDtypeStruct(mixture.shape, bf16),
            jax.ShapeDtypeStruct((2, depth, own), bf16),
            jax.ShapeDtypeStruct((depth, depth), f32),
            jax.ShapeDtypeStruct((2, 8, depth), f32),
            jax.ShapeDtypeStruct((parts, 1, part_width), f32),
            kept,
            kept,
            kept,
            kept,
        ],
        scratch_shapes=[
            pltpu.VMEM(mixture.shape, bf16),
            pltpu.VMEM(wide, bf16),
            pltpu.VMEM((depth, tokens), bf16),
            pltpu.VMEM(wide, bf16),
            pltpu.VMEM((depth, tokens), bf16),
            pltpu.VMEM(wide, f32),
            pltpu.VMEM(wide, f32),
            pltpu.VMEM(wide, f32),
            pltpu.VMEM((tokens, part_width), bf16),
            pltpu.VMEM((tokens, part_width), bf16),
            pltpu.VMEM((tiles, 4, group, tile), bf16),
            pltpu.VMEM((2, depth, part_width), bf16),
            pltpu.VMEM((3, 2, depth, part_width), bf16),
            pltpu.VMEM((2, depth, part_width), bf16),
            pltpu.VMEM((2, depth, part_width), bf16),
            pltpu.VMEM((2, 2, depth, part_width), bf16),
            pltpu.VMEM((2, groups, half, part_width), bf16),
            pltpu.VMEM((2, groups, half, part_width), bf16),
            pltpu.SemaphoreType.DMA((pieces - 1,)),
            pltpu.SemaphoreType.DMA((pieces,)),
            pltpu.SemaphoreType.DMA,
            pltpu.SemaphoreType.DMA((tiles, 4)),
            pltpu.SemaphoreType.DMA((pieces, per_sequence)),
            pltpu.SemaphoreType.DMA((per_sequence,)),
            pltpu.SemaphoreType.DMA((2,)),
            pltpu.SemaphoreType.DMA((2,)),
            pltpu.SemaphoreType.DMA((6,)),
            *[pltpu.SemaphoreType.DMA((2,))] * 2,
            pltpu.SemaphoreType.DMA((3,)),
            *[pltpu.SemaphoreType.DMA((groups,))] * 2,
            *[pltpu.SemaphoreType.DMA((2, groups))] * 2,
        ],
        compiler_params=pltpu.CompilerParams(
            vmem_limit_bytes=VMEM_MOST, collective_id=2, has_side_effects=True
        ),
        cost_estimate=cost(6 * tokens * depth * (depth + 3 * parts * part_width), rows, rows, rows),
        name="middle",
    )(mixture, rows, cotangent, valid, mods, up_bias, down_bias, out_weight, own_weight, other_weight, across)


def entry_back_kernel(
    grad_query_ref,
    grad_key_ref,
    grad_value_ref,
    hat_ref,
    scale_ref,
    gain_ref,
    shift_ref,
    weight_ref,
    middle_ref,
    middle_in_ref,
    small_ref,
    up_ref,
    down_ref,
    grad_out_ref,
    result_ref,
    result_in_ref,
    out_ref,
    grad_weight_ref,
    all_sums_ref,
    all_small_ref,
    pieces_ref,
    grad_out_sum_ref,
    block_ref,
    up_own,
    up_in,
    down_own,
    down_in,
    slices,
    slices_in,
    context_slice,
    context_in,
    small_in,
    small_sum,
    small_groups,
    out_in,
    loaded,
    sent_up,
    got_up,
    sent_down,
    got_down,
    sent_slice,
    got_slice,
    sent_context,
    got_context,
    sent_small,
    got_small,
    sent_sum,
    got_sum,
    sent_out,
    got_out,
    sent_result,
    got_result,
    moved,
    taken,
    held,
    weight_total,
    sums,
    part,
    part_in,
    pair,
    pair_in,
    chip,
    chip_in,
    piece,
    piece_in,
    block_piece,
    block_in,
    rank_sums,
    rank_in,
    group_sums,
    group_in,
    sent_part,
    got_part,
    sent_pair,
    got_pair,
    sent_chip,
    got_chip,
    sent_piece,
    got_piece,
    sent_block,
    got_block,
    sent_rank,
    got_rank,
    sent_group,
    got_group,
    *,
    tiles,
    groups,
):
    step = pl.program_id(0)
    fsdp, context, tensor = (lax.axis_index(name) for name in ("fsdp", "context", "tensor"))
    ranks = 4
    half = tiles // 2
    core = lax.rem(tensor, 2)
    chip_x = tensor // 2
    sibling = tensor + 1 - 2 * core
    across = lax.rem(tensor + 2, ranks)
    place = fsdp * 2 + context
    depth = hat_ref.shape[0]
    slice_rows = depth // ranks
    weight_rows = depth // groups
    everyone = groups * 2

    def group_member(away):
        other = lax.rem(place + away, everyone)
        return {"fsdp": other // 2, "context": lax.rem(other, 2)}

    def group_away(number):
        return {"fsdp": lax.rem(fsdp + number // 2, groups), "context": number % 2}

    plane = context * ranks + tensor
    in_plane = 2 * ranks

    def plane_member(away):
        other = lax.rem(plane + away, in_plane)
        return {"context": other // ranks, "tensor": lax.rem(other, ranks)}

    def up_copy(other):
        return copy_to(
            up_ref.at[1, other], up_in.at[other], sent_up.at[other], got_up.at[other], context=1 - context
        )

    def down_copy(other):
        return copy_to(
            down_ref.at[0, other], down_in.at[other], sent_down.at[other], got_down.at[other], tensor=across
        )

    def loads():
        return [
            pltpu.make_async_copy(up_ref.at[0], up_own, loaded.at[0]),
            pltpu.make_async_copy(down_ref.at[1], down_own, loaded.at[1]),
        ]

    def slice_copy(away):
        other = lax.rem(fsdp + away, groups)
        return copy_to(
            slices.at[other],
            slices_in.at[away - 1],
            sent_slice.at[away - 1],
            got_slice.at[away - 1],
            fsdp=other,
        )

    def context_copy():
        return copy_to(context_slice, context_in, sent_context, got_context, context=1 - context)

    def small_copy(away):
        return copy_to(
            small_ref,
            small_in.at[away - 1],
            sent_small.at[away - 1],
            got_small.at[away - 1],
            **plane_member(away),
        )

    def sum_copy(away):
        return copy_to(
            small_sum,
            small_groups.at[away - 1],
            sent_sum.at[away - 1],
            got_sum.at[away - 1],
            fsdp=lax.rem(fsdp + away, groups),
        )

    def out_copy():
        return copy_to(grad_out_ref, out_in, sent_out, got_out, context=1 - context)

    quarter = result_ref.shape[1]

    def result_places():
        for number, (source, rank) in enumerate([(result_ref, tensor), (result_in_ref, across)]):
            rows = pl.ds(pl.multiple_of(rank * quarter, quarter), quarter)
            for sequence in range(2):
                yield number * 2 + sequence, source.at[sequence], block_ref.at[sequence, rows, :]

    def result_copies():
        return [
            copy_to(held.at[k], target, sent_result.at[k], got_result.at[k], tensor=sibling)
            for k, source, target in result_places()
        ]

    def result_loads():
        return [
            pltpu.make_async_copy(source, held.at[k], taken.at[k])
            for k, source, target in result_places()
        ]

    def result_moves():
        return [
            pltpu.make_async_copy(held.at[k], target, moved.at[k]) for k, source, target in result_places()
        ]

    def part_copy(tile):
        return copy_to(
            part.at[tile, 1 - core], part_in.at[tile], sent_part.at[tile], got_part.at[tile], tensor=sibling
        )

    def pair_copy(tile):
        return copy_to(
            pair.at[tile, 1 - chip_x], pair_in.at[tile], sent_pair.at[tile], got_pair.at[tile], tensor=across
        )

    def chip_copy(tile):
        return copy_to(
            chip.at[tile], chip_in.at[tile], sent_chip.at[tile], got_chip.at[tile], context=1 - context
        )

    def piece_copy(away):
        other = lax.rem(fsdp + away, groups)
        return copy_to(
            piece.at[other],
            piece_in.at[away - 1],
            sent_piece.at[away - 1],
            got_piece.at[away - 1],
            fsdp=other,
        )

    def block_copy():
        return copy_to(block_piece, block_in, sent_block, got_block, context=1 - context)

    def rank_copy(away):
        return copy_to(
            rank_sums,
            rank_in.at[away - 1],
            sent_rank.at[away - 1],
            got_rank.at[away - 1],
            tensor=lax.rem(tensor + away, ranks),
        )

    def group_copy(away):
        return copy_to(
            group_sums,
            group_in.at[away - 1],
            sent_group.at[away - 1],
            got_group.at[away - 1],
            **group_member(away),
        )

    @pl.when(step == 0)
    def _():
        greet(
            [plane_member(away) for away in range(1, in_plane)]
            + [group_away(away) for away in range(2, everyone)]
        )
        for away in range(1, groups + 1):
            other = lax.rem(fsdp + away, groups)
            up_copy(other).start()
            down_copy(other).start()
        out_copy().start()
        for away in range(1, in_plane):
            small_copy(away).start()
        for one in result_loads() + loads():
            one.start()
        weight_total[...] = jnp.zeros_like(weight_total)
        sums[...] = jnp.zeros_like(sums)

    @pl.when(step == 2)
    def _():
        for one in result_loads():
            one.wait()
        for one in result_copies() + result_moves():
            one.start()

    def grads():
        return jnp.concatenate([grad_query_ref[...], grad_key_ref[...], grad_value_ref[...]], axis=0)

    @pl.when(step < tiles)
    def _():
        tile = step
        columns = grads()
        grad_entry = product(weight_ref[...], columns)
        hat = hat_ref[...].astype(f32)
        lifted = hat * gain_ref[...]
        weight_total[...] += against((lifted + shift_ref[...]).astype(bf16), columns)
        grad_lifted = grad_entry * gain_ref[...]
        term = scale_ref[...] * (
            grad_lifted
            - jnp.mean(grad_lifted, axis=0, keepdims=True)
            - hat * jnp.mean(grad_lifted * hat, axis=0, keepdims=True)
        )
        extra = jnp.where(tile < half, middle_in_ref[...], middle_ref[0]).astype(f32)
        term = (term + jnp.where(lax.rem(tile, half) == tensor, extra, 0.0)).astype(bf16)
        for rank in range(ranks):
            part[tile, rank % 2, rank // 2] = term[rank * slice_rows : (rank + 1) * slice_rows]
        part_copy(tile).start()
        weighted = grad_entry * hat
        for lane in range(0, grad_entry.shape[1], WIDE):
            sums[0] += grad_entry[:, lane : lane + WIDE]
            sums[1] += weighted[:, lane : lane + WIDE]

    @pl.when(step == tiles - 1)
    def _():
        for other in range(groups):
            piece[other] = weight_total[other * weight_rows : (other + 1) * weight_rows].astype(bf16)
        for away in range(1, groups):
            piece_copy(away).start()

    @pl.when((step >= 1) & (step < tiles + 1))
    def _():
        tile = step - 1
        part_copy(tile).wait_recv()
        pair[tile] = (part[tile, core].astype(f32) + part_in[tile].astype(f32)).astype(bf16)
        pair_copy(tile).start()

    @pl.when((step >= 3) & (step < tiles + 3))
    def _():
        tile = step - 3
        pair_copy(tile).wait_recv()
        total = (pair[tile, chip_x].astype(f32) + pair_in[tile].astype(f32)).astype(bf16)

        @pl.when(tile < half)
        def _():
            chip[tile] = total
            chip_copy(tile).start()

        @pl.when(tile >= half)
        def _():
            out_ref[context, tile - half] = total

    @pl.when((step >= tiles - 1) & (step < tiles - 1 + half))
    def _():
        tile = step - tiles + 1
        chip_copy(tile).wait_recv()
        out_ref[1 - context, tile] = chip_in[tile]

    @pl.when(step == 4)
    def _():
        for away in range(1, in_plane):
            small_copy(away).wait_recv()
        small_sum[...] = ordered_sum(small_ref[...], [small_in[k] for k in range(in_plane - 1)], plane)
        for away in range(1, groups):
            sum_copy(away).start()

    for away in range(1, groups + 1):

        @pl.when(step == 1 + away)
        def _():
            if away == 1:
                for one in loads():
                    one.wait()
            other = lax.rem(fsdp + away, groups)
            up_copy(other).wait_recv()
            down_copy(other).wait_recv()
            slices[other, 0] = (up_own[other].astype(f32) + up_in[other].astype(f32)).astype(bf16)
            slices[other, 1] = (down_own[other].astype(f32) + down_in[other].astype(f32)).astype(bf16)
            if away < groups:
                slice_copy(away).start()

    @pl.when(step == tiles)
    def _():
        total = slices[fsdp].astype(f32)
        for away in range(1, groups):
            slice_copy(away).wait_recv()
            total = total + slices_in[away - 1].astype(f32)
        context_slice[...] = total.astype(bf16)
        context_copy().start()

    @pl.when(step == tiles + 2)
    def _():
        total = piece[fsdp].astype(f32)
        for away in range(1, groups):
            piece_copy(away).wait_recv()
            total = total + piece_in[away - 1].astype(f32)
        block_piece[...] = total.astype(bf16)
        block_copy().start()

    @pl.when(step == tiles + 2)
    def _():
        block_copy().wait_recv()
        grad_weight_ref[...] = block_piece[...].astype(f32) + block_in[...].astype(f32)

    @pl.when(step == tiles - 1)
    def _():
        rows = [jnp.sum(sums[kind].T, axis=0, keepdims=True) for kind in range(2)]
        rank_sums[...] = jnp.concatenate(rows + [jnp.zeros((6, depth), f32)], axis=0)
        for away in range(1, ranks):
            rank_copy(away).start()

    @pl.when(step == tiles)
    def _():
        for away in range(1, ranks):
            rank_copy(away).wait_recv()
        pairs = [rank_sums[...] + rank_in[1], rank_in[0] + rank_in[2]]
        group_sums[...] = pairs[0] + pairs[1]
        for away in range(1, everyone):
            group_copy(away).start()

    @pl.when(step == tiles + 2)
    def _():
        all_small_ref[fsdp] = small_sum[...]
        for away in range(1, groups):
            sum_copy(away).wait_recv()
            all_small_ref[lax.rem(fsdp + groups - away, groups)] = small_groups[away - 1]
            sum_copy(away).wait_send()
            slice_copy(away).wait_send()
        context_copy().wait()
        pieces_ref[context] = context_slice[...]
        pieces_ref[1 - context] = context_in[...]
        out_copy().wait()
        grad_out_sum_ref[...] = grad_out_ref[...].astype(f32) + out_in[...].astype(f32)
        for other in range(groups):
            up_copy(other).wait_send()
            down_copy(other).wait_send()
        for away in range(1, in_plane):
            small_copy(away).wait_send()
        for one in result_copies() + result_moves():
            one.wait()
        all_sums_ref[place] = group_sums[...]
        for away in range(1, everyone):
            group_copy(away).wait_recv()
            all_sums_ref[lax.rem(place + everyone - away, everyone)] = group_in[away - 1]
        for tile in range(tiles):
            part_copy(tile).wait_send()
            pair_copy(tile).wait_send()
        for tile in range(half):
            chip_copy(tile).wait_send()
        for away in range(1, groups):
            piece_copy(away).wait_send()
        block_copy().wait_send()
        for away in range(1, ranks):
            rank_copy(away).wait_send()
        for away in range(1, everyone):
            group_copy(away).wait_send()


def ordered_sum(own, others, place):
    count = len(others) + 1
    total = 0.0
    for source in range(count):
        away = lax.rem(place - source + count, count)
        term = own
        for k, other in enumerate(others):
            term = jnp.where(away == k + 1, other, term)
        total = total + term
    return total


def entry_back_call(
    grad_query,
    grad_key,
    grad_value,
    hat_t,
    scaling,
    gain,
    shift,
    weight,
    grad_middle,
    middle_in,
    small,
    up,
    down,
    grad_out,
    result,
    result_in,
    groups,
    tile,
):
    group, length = grad_query.shape
    depth = hat_t.shape[0]
    tiles = length // tile
    half = tiles // 2
    rows = depth // 4
    weight_rows = depth // groups

    def lanes(step):
        first = (1 - lax.axis_index("context")) * half
        return 0, lax.rem(first + jnp.minimum(step, tiles - 1), tiles)

    whole = lambda step: (0, 0)
    whole3 = lambda step: (0, 0, 0)
    whole4 = lambda step: (0, 0, 0, 0)
    dma = lambda *shape: [pltpu.SemaphoreType.DMA(shape)] * 2
    hbm = pl.BlockSpec(memory_space=pl.ANY)
    piece = up.shape[1:]
    return pl.pallas_call(
        partial(entry_back_kernel, tiles=tiles, groups=groups),
        grid=(tiles + 3,),
        in_specs=[
            pl.BlockSpec((group, tile), lanes),
            pl.BlockSpec((group, tile), lanes),
            pl.BlockSpec((group, tile), lanes),
            pl.BlockSpec((depth, tile), lanes),
            pl.BlockSpec((1, tile), lanes),
            pl.BlockSpec((depth, 1), whole),
            pl.BlockSpec((depth, 1), whole),
            pl.BlockSpec((depth, 3 * group), whole),
            pl.BlockSpec((1, depth, tile), lambda step: (lax.axis_index("context"), 0, 0)),
            pl.BlockSpec((depth, tile), whole),
            pl.BlockSpec(small.shape, whole),
            hbm,
            hbm,
            pl.BlockSpec(grad_out.shape, whole),
            hbm,
            hbm,
        ],
        out_specs=[
            pl.BlockSpec((2, half, rows, tile), whole4),
            pl.BlockSpec((weight_rows, 3 * group), whole),
            pl.BlockSpec((2 * groups, 8, depth), whole3),
            pl.BlockSpec((groups, *small.shape), whole3),
            pl.BlockSpec((2, 2, *piece[1:]), whole4),
            pl.BlockSpec(grad_out.shape, whole),
            hbm,
        ],
        out_shape=[
            jax.ShapeDtypeStruct((2, half, rows, tile), bf16),
            jax.ShapeDtypeStruct((weight_rows, 3 * group), f32),
            jax.ShapeDtypeStruct((2 * groups, 8, depth), f32),
            jax.ShapeDtypeStruct((groups, *small.shape), f32),
            jax.ShapeDtypeStruct((2, 2, *piece[1:]), bf16),
            jax.ShapeDtypeStruct(grad_out.shape, f32),
            jax.ShapeDtypeStruct((2, 4 * result.shape[1], depth), bf16),
        ],
        scratch_shapes=[
            *[pltpu.VMEM(piece, bf16)] * 4,
            pltpu.VMEM((groups, 2, *piece[1:]), bf16),
            pltpu.VMEM((groups - 1, 2, *piece[1:]), bf16),
            pltpu.VMEM((2, *piece[1:]), bf16),
            pltpu.VMEM((2, *piece[1:]), bf16),
            pltpu.VMEM((7, *small.shape), f32),
            pltpu.VMEM(small.shape, f32),
            pltpu.VMEM((groups - 1, *small.shape), f32),
            pltpu.VMEM(grad_out.shape, bf16),
            pltpu.SemaphoreType.DMA((2,)),
            *dma(groups),
            *dma(groups),
            *dma(groups - 1),
            *[pltpu.SemaphoreType.DMA] * 2,
            *dma(7),
            *dma(groups - 1),
            *[pltpu.SemaphoreType.DMA] * 2,
            *dma(4),
            pltpu.SemaphoreType.DMA((4,)),
            pltpu.SemaphoreType.DMA((4,)),
            pltpu.VMEM((4, *result.shape[1:]), bf16),
            pltpu.VMEM((depth, 3 * group), f32),
            pltpu.VMEM((2, depth, WIDE), f32),
            pltpu.VMEM((tiles, 2, 2, rows, tile), bf16),
            pltpu.VMEM((tiles, 2, rows, tile), bf16),
            pltpu.VMEM((tiles, 2, rows, tile), bf16),
            pltpu.VMEM((tiles, rows, tile), bf16),
            pltpu.VMEM((half, rows, tile), bf16),
            pltpu.VMEM((half, rows, tile), bf16),
            pltpu.VMEM((groups, weight_rows, 3 * group), bf16),
            pltpu.VMEM((groups - 1, weight_rows, 3 * group), bf16),
            pltpu.VMEM((weight_rows, 3 * group), bf16),
            pltpu.VMEM((weight_rows, 3 * group), bf16),
            pltpu.VMEM((8, depth), f32),
            pltpu.VMEM((3, 8, depth), f32),
            pltpu.VMEM((8, depth), f32),
            pltpu.VMEM((2 * groups - 1, 8, depth), f32),
            *dma(tiles),
            *dma(tiles),
            *dma(half),
            *dma(groups - 1),
            *[pltpu.SemaphoreType.DMA] * 2,
            *dma(3),
            *dma(2 * groups - 1),
        ],
        compiler_params=pltpu.CompilerParams(
            vmem_limit_bytes=VMEM, collective_id=3, has_side_effects=True
        ),
        cost_estimate=cost(12 * length * depth * group, grad_query, hat_t, hat_t),
        name="entry_back",
    )(
        grad_query,
        grad_key,
        grad_value,
        hat_t,
        scaling,
        gain,
        shift,
        weight,
        grad_middle,
        middle_in,
        small,
        up,
        down,
        grad_out,
        result,
        result_in,
    )


def add(left_side, right_side):
    return (left_side.astype(f32) + right_side.astype(f32)).astype(bf16)


def by_sequence(
    tokens,
    cotangent,
    segments,
    steps,
    table,
    ada_w,
    ada_b,
    gain_one,
    w_qkv,
    w_out,
    gain_two,
    w_up,
    b_up,
    w_down,
    b_down,
):
    fsdp, tensor = lax.axis_size("fsdp"), lax.axis_size("tensor")
    context = lax.axis_size("context")
    tensor_rank = lax.axis_index("tensor")
    context_rank = lax.axis_index("context")
    fsdp_rank = lax.axis_index("fsdp")
    sequences, own_rows, depth = tokens.shape
    length = segments.shape[1]
    group = w_out.shape[0]
    part_width = w_up.shape[1]
    heads = group // HDIM
    quarter = own_rows // tensor

    mine = lax.dynamic_slice_in_dim(tokens, tensor_rank * quarter, quarter, axis=1)
    partner = [(k, (k + 1) % context) for k in range(context)]

    by_kind = w_qkv.reshape(-1, heads, 3, HDIM).transpose(0, 2, 1, 3).reshape(-1, 3 * group)
    both = ("tensor", "fsdp")
    out_weight = (
        lax.all_gather(w_out, both, axis=0, tiled=False)
        .reshape(tensor, fsdp, group, depth // fsdp)
        .transpose(0, 2, 1, 3)
        .reshape(depth, depth)
    )

    numbers = jnp.arange(table.shape[0], dtype=jnp.int32)
    ada_full = ada_w.astype(f32)
    raw = exact_product((steps[:, None] == numbers[None, :]).astype(f32), table.astype(f32))
    local_mods = exact_product(jax.nn.silu(raw), ada_full) + ada_b.astype(f32)
    local_mods = local_mods.reshape(sequences, 6, depth)
    gain_first, gain_second = gain_one.astype(f32), gain_two.astype(f32)
    own_mods = lax.dynamic_index_in_dim(local_mods, context_rank, 0, keepdims=False)
    gain_column = (gain_first * (1.0 + own_mods[1]))[:, None]
    shift_column = own_mods[0][:, None]
    mods = jnp.stack(
        [
            local_mods[:, 2],
            local_mods[:, 3],
            gain_second * (1.0 + local_mods[:, 4]),
            local_mods[:, 5],
        ]
        + [jnp.zeros((sequences, depth), f32)] * 4,
        axis=1,
    )

    segment = lax.dynamic_index_in_dim(segments, context_rank, 0, keepdims=False)
    same, starts, ends = document_bounds(segment)
    offsets = jnp.arange(length, dtype=jnp.int32) - jnp.sum(jnp.where(same, starts[:, None], 0), axis=0)
    angles = frequencies()[:, None] * offsets.astype(f32)[None, :]
    cosine, sine = jnp.cos(angles), jnp.sin(angles)
    tile = length // (context * tensor)
    block = tile
    first_key = jnp.sum(jnp.where(same, starts[:, None], 0), axis=0)[::tile]
    last_key = jnp.sum(jnp.where(same, ends[:, None], 0), axis=0)[tile - 1 :: tile]

    queries, keys, keys_t, values, values_t, hat_t, scaling, norms, qkv, forward = entry_call(
        tokens,
        by_kind,
        jnp.where(context_rank == 0, w_up, w_down.T),
        gain_column,
        shift_column,
        cosine,
        sine,
        segment[None, :],
        groups=fsdp,
        tile=tile,
    )
    across = [(k, (k + 2) % tensor) for k in range(tensor)]
    across_weight = lax.ppermute(forward, "tensor", across)
    other_weight = lax.ppermute(forward, "context", partner)
    largest = jnp.max(norms, axis=1)[: 2 * heads].reshape(heads, 2)
    safe = jnp.max(largest[:, 0] * largest[:, 1]) <= SAFE_EXPONENT**2
    ranges = jnp.stack(
        [
            first_key // block,
            (last_key + block - 1) // block,
            jnp.broadcast_to(safe.astype(jnp.int32), first_key.shape),
        ]
    ).astype(jnp.int32)
    mixture, told = attend_call(ranges, queries, keys, values_t, tile, block)

    own_segments = lax.dynamic_slice_in_dim(
        segments, context_rank * own_rows + tensor_rank * quarter, quarter, axis=1
    )
    own_cotangent = lax.dynamic_slice_in_dim(cotangent, tensor_rank * quarter, quarter, axis=1)
    (
        result,
        grad_mixture,
        grad_middle,
        grad_out,
        sums,
        bias_sums,
        up_keep,
        up_send,
        down_keep,
        down_send,
    ) = middle_call(
        mixture,
        mine.reshape(-1, depth),
        own_cotangent.reshape(-1, depth),
        (own_segments != 0).astype(f32).reshape(-1, 1),
        mods,
        b_up.astype(f32).reshape(tensor, 1, part_width),
        b_down.astype(f32)[None, :],
        out_weight,
        forward,
        other_weight,
        across_weight,
        fsdp,
        tile=min(tile, 256),
    )
    result = result.reshape(sequences, quarter, depth)
    result_in = lax.ppermute(result, "tensor", across)
    middle_in = lax.ppermute(
        lax.dynamic_index_in_dim(grad_middle, 1 - context_rank, 0, keepdims=False), "context", partner
    )
    small = jnp.concatenate(
        [
            sums[:, :5].reshape(-1, depth),
            bias_sums.reshape(-1, depth),
        ]
    )
    small_rows = small.shape[0]
    cond = raw.shape[1]
    leads = (context_rank == 0) & (tensor_rank == 0)
    embedded = jnp.concatenate([raw, steps.astype(f32)[:, None]], axis=1)
    embedded = jnp.pad(jnp.where(leads, embedded, 0.0), ((0, 0), (0, depth - cond - 1)))
    small = jnp.concatenate([small, embedded])
    small = jnp.pad(small, ((0, -small.shape[0] % 8), (0, 0)))

    up_sum = add(up_keep, lax.ppermute(up_send, "tensor", across))
    down_sum = add(down_keep, lax.ppermute(down_send, "context", partner))
    grad_out = (
        grad_out.astype(bf16)
        .reshape(tensor, group, fsdp, depth // fsdp)
        .transpose(0, 2, 1, 3)
        .reshape(tensor * fsdp, group * (depth // fsdp) // part_width, part_width)
    )
    grad_out = lax.psum_scatter(grad_out, both, scatter_dimension=0, tiled=True)[0]

    grad_query, grad_key, grad_value = attend_back_call(
        ranges, told, keys, keys_t, values, mixture, grad_mixture, cosine, sine, tile, block
    )
    (grad_query, up_sum, down_sum, result_in, middle_in, grad_out) = lax.optimization_barrier(
        (grad_query, up_sum, down_sum, result_in, middle_in, grad_out)
    )
    part, grad_qkv, entry_sums, small, pieces, grad_out, block_out = entry_back_call(
        grad_query,
        grad_key,
        grad_value,
        hat_t,
        scaling,
        gain_column,
        shift_column,
        qkv,
        grad_middle,
        middle_in,
        small,
        up_sum,
        down_sum,
        grad_out,
        result,
        result_in,
        groups=fsdp,
        tile=tile,
    )
    pieces = pieces.transpose(1, 0, 2, 3)
    pieces = pieces.reshape(2, depth // fsdp, part_width).astype(f32)
    grad_w_up = pieces[0]
    grad_w_down = pieces[1].T
    grad_w_out = grad_out.reshape(group, depth // fsdp)
    small_sums = small[:, : 5 * sequences].reshape(fsdp * sequences, 5, depth)
    embedded = small[:, small_rows : small_rows + sequences].reshape(fsdp * sequences, depth)
    choose = (embedded[:, cond].astype(jnp.int32)[:, None] == numbers[None, :]).astype(f32)
    embedding, silu_back = jax.vjp(jax.nn.silu, embedded[:, :cond])
    modulation = exact_product(embedding, ada_full) + ada_b.astype(f32)
    grad_b_up = jnp.sum(small[:, 5 * sequences : small_rows], axis=0).reshape(-1)
    grad_b_down = jnp.sum(small_sums[:, 4], axis=0)
    grad_gain_two = jnp.sum(small_sums[:, 2] * (1.0 + modulation[:, 4 * depth : 5 * depth]), axis=0)
    middle_mod = jnp.concatenate(
        [small_sums[:, 0], small_sums[:, 1], small_sums[:, 2] * gain_second, small_sums[:, 3]], axis=1
    )
    part = part.transpose(0, 1, 3, 2).reshape(sequences, own_rows, depth // tensor)
    grad_tokens = part.astype(f32)
    grad_w_qkv = (
        grad_qkv.reshape(-1, 3, heads, HDIM).transpose(0, 2, 1, 3).reshape(-1, 3 * group)
    )
    grad_mod = jnp.concatenate(
        [entry_sums[:, 0], entry_sums[:, 1] * gain_first, middle_mod], axis=1
    )
    grad_gain_one = jnp.sum(entry_sums[:, 1] * (1.0 + modulation[:, depth : 2 * depth]), axis=0)
    grad_ada_b = jnp.sum(grad_mod, axis=0)
    grad_ada_w = exact_transposed(embedding, grad_mod)
    grad_before = silu_back(exact_against(grad_mod, ada_full))[0]
    grad_table = exact_transposed(choose, grad_before)
    return (
        block_out,
        grad_tokens,
        grad_table,
        grad_ada_w,
        grad_ada_b,
        grad_gain_one,
        grad_w_qkv,
        grad_w_out,
        grad_gain_two,
        grad_w_up,
        grad_b_up,
        grad_w_down,
        grad_b_down,
    )


def normalize(operand):
    center = operand - jnp.mean(operand, axis=-1, keepdims=True)
    scaling = lax.rsqrt(jnp.mean(center * center, axis=-1, keepdims=True) + 1e-05)
    return (center * scaling, scaling)


def norm_back(grad_hat, hatted, scaling):
    return scaling * (
        grad_hat
        - jnp.mean(grad_hat, axis=-1, keepdims=True)
        - hatted * jnp.mean(grad_hat * hatted, axis=-1, keepdims=True)
    )


def angles_of(offsets, half_width):
    frequency = 10000.0 ** (-jnp.arange(half_width, dtype=jnp.float32) / half_width)
    angles = offsets.astype(jnp.float32)[:, None] * frequency[None, :]
    return (jnp.cos(angles)[:, None, :], jnp.sin(angles)[:, None, :])


def rotate(operand, cosine, sine_part, direction):
    half_width = operand.shape[-1] // 2
    front_half = operand[..., :half_width]
    second = operand[..., half_width:]
    return jnp.concatenate(
        [
            front_half * cosine - direction * second * sine_part,
            direction * front_half * sine_part + second * cosine,
        ],
        axis=-1,
    )


def scores_of(queries, key_rows, allowed):
    raw_scores = (
        jnp.einsum("qhd,khd->hqk", queries, key_rows, preferred_element_type=jnp.float32) * 0.125
    )
    return jnp.where(allowed[None], raw_scores, -1e30)


def attend(queries, key_rows, values, allowed):
    scores = scores_of(queries, key_rows, allowed)
    row_max = jnp.max(scores, axis=-1, keepdims=True)
    weights_raw = jnp.exp(scores - row_max)
    row_total = jnp.sum(weights_raw, axis=-1, keepdims=True)
    weights_low = (weights_raw / row_total).astype(jnp.bfloat16)
    mixture = jnp.einsum("hqk,khd->qhd", weights_low, values, preferred_element_type=jnp.float32)
    return (mixture, row_max + jnp.log(row_total))


def attend_back(queries, key_rows, values, grad_mixture, logsum, allowed, row_delta):
    scores = scores_of(queries, key_rows, allowed)
    chances = jnp.exp(scores - logsum)
    grad_chances = jnp.einsum(
        "qhd,khd->hqk", grad_mixture, values, preferred_element_type=jnp.float32
    )
    row_delta = jnp.sum(chances * grad_chances, axis=-1, keepdims=True)
    grad_scores = (chances * (grad_chances - row_delta)).astype(jnp.bfloat16)
    return (chances.astype(jnp.bfloat16), grad_scores, row_delta)


def by_block(
    tokens,
    cotangent,
    segments,
    steps,
    table,
    ada_w,
    ada_b,
    gain_one,
    w_qkv,
    w_out,
    gain_two,
    w_up,
    b_up,
    w_down,
    b_down,
):
    w_qkv, w_up, w_out, w_down = (
        lax.all_gather(w_qkv, "fsdp", axis=0, tiled=True),
        lax.all_gather(w_up, "fsdp", axis=0, tiled=True),
        lax.all_gather(w_out, "fsdp", axis=1, tiled=True),
        lax.all_gather(w_down, "fsdp", axis=1, tiled=True),
    )
    tensor_rank = lax.axis_index("tensor")
    context_rank = lax.axis_index("context")
    sequences, own_rows, model_width = tokens.shape
    length = segments.shape[1]
    local_heads = w_out.shape[0] // HDIM
    hidden_width = w_up.shape[1]
    up_bias = lax.dynamic_slice_in_dim(b_up, tensor_rank * hidden_width, hidden_width).astype(
        jnp.float32
    )
    down_bias = b_down.astype(jnp.float32)
    gain_first = gain_one.astype(jnp.float32)
    gain_second = gain_two.astype(jnp.float32)
    leader = (tensor_rank == 0).astype(jnp.float32)
    ada_full = ada_w.astype(jnp.float32)
    choose = (steps[:, None] == jnp.arange(table.shape[0], dtype=jnp.int32)[None, :]).astype(
        jnp.float32
    )
    before = exact_product(choose, table.astype(jnp.float32))
    embedding, silu_back = jax.vjp(jax.nn.silu, before)
    modulation = exact_product(embedding, ada_full) + ada_b.astype(jnp.float32)
    grad_qkv = jnp.zeros(w_qkv.shape, jnp.float32)
    grad_out_w = jnp.zeros(w_out.shape, jnp.float32)
    grad_up = jnp.zeros(w_up.shape, jnp.float32)
    grad_down = jnp.zeros(w_down.shape, jnp.float32)
    grad_bias_up = jnp.zeros((hidden_width,), jnp.float32)
    grad_bias_down = jnp.zeros((model_width,), jnp.float32)
    grad_gain_first = jnp.zeros((model_width,), jnp.float32)
    grad_gain_second = jnp.zeros((model_width,), jnp.float32)
    results = []
    partial_inputs = []
    carried = []
    grad_mods = []
    for number in range(sequences):
        shift_one, scale_one, gate_one, shift_two, scale_two, gate_two = jnp.split(
            modulation[number], 6
        )
        segment = segments[number]
        offsets = positions(segment)
        own_segment = lax.dynamic_slice_in_dim(segment, context_rank * own_rows, own_rows)
        own_offsets = lax.dynamic_slice_in_dim(offsets, context_rank * own_rows, own_rows)
        cosine, sine_part = angles_of(own_offsets, HDIM // 2)
        allowed = own_segment[:, None] == segment[None, :]
        inputs_row = tokens[number].astype(jnp.float32)
        hat_one, scaling_one = normalize(inputs_row)
        lifted_one = hat_one * gain_first
        entry_one = (lifted_one * (1.0 + scale_one) + shift_one).astype(jnp.bfloat16)
        projected = product(entry_one, w_qkv).reshape(own_rows, local_heads, 3, HDIM)
        queries = rotate(projected[:, :, 0], cosine, sine_part, 1.0).astype(jnp.bfloat16)
        key_rows = rotate(projected[:, :, 1], cosine, sine_part, 1.0).astype(jnp.bfloat16)
        values = projected[:, :, 2].astype(jnp.bfloat16)
        key_value = jnp.stack([key_rows, values], axis=1).reshape(own_rows, 2 * local_heads * HDIM)
        gathered = lax.all_gather(key_value, "context", axis=0, tiled=True).reshape(
            length, 2, local_heads, HDIM
        )
        all_keys = gathered[:, 0]
        all_values = gathered[:, 1]
        mixture, logsum = attend(queries, all_keys, all_values, allowed)
        mixture_low = mixture.reshape(own_rows, local_heads * HDIM).astype(jnp.bfloat16)
        attended = lax.psum(product(mixture_low, w_out).astype(jnp.bfloat16), "tensor").astype(
            jnp.float32
        )
        middle = inputs_row + gate_one * attended
        hat_two, scaling_two = normalize(middle)
        lifted_two = hat_two * gain_second
        entry_two = (lifted_two * (1.0 + scale_two) + shift_two).astype(jnp.bfloat16)
        hidden = product(entry_two, w_up) + up_bias
        activated, gelu_back = jax.vjp(partial(jax.nn.gelu, approximate=True), hidden)
        activated_low = activated.astype(jnp.bfloat16)
        output = (
            lax.psum(product(activated_low, w_down).astype(jnp.bfloat16), "tensor").astype(
                jnp.float32
            )
            + down_bias
        )
        results.append((middle + gate_two * output).astype(jnp.bfloat16))
        valid = (own_segment != 0).astype(jnp.float32)[:, None]
        grad_result = cotangent[number].astype(jnp.float32) * valid
        grad_output = (gate_two * grad_result).astype(jnp.bfloat16)
        grad_gate_two = jnp.sum(grad_result * output, axis=0)
        grad_bias_down = grad_bias_down + jnp.sum(grad_output.astype(jnp.float32), axis=0)
        grad_down = grad_down + transposed(activated_low, grad_output)
        grad_active = against(grad_output, w_down)
        grad_hidden = gelu_back(grad_active)[0].astype(jnp.bfloat16)
        grad_bias_up = grad_bias_up + jnp.sum(grad_hidden.astype(jnp.float32), axis=0)
        grad_up = grad_up + transposed(entry_two, grad_hidden)
        grad_entry_two = against(grad_hidden, w_up)
        grad_shift_two = jnp.sum(grad_entry_two, axis=0)
        grad_scale_two = jnp.sum(grad_entry_two * lifted_two, axis=0)
        grad_lifted_two = grad_entry_two * (1.0 + scale_two)
        grad_gain_second = grad_gain_second + jnp.sum(grad_lifted_two * hat_two, axis=0)
        part_two = norm_back(grad_lifted_two * gain_second, hat_two, scaling_two)
        grad_middle = grad_result + lax.psum(part_two.astype(jnp.bfloat16), "tensor").astype(
            jnp.float32
        )
        grad_attended = (gate_one * grad_middle).astype(jnp.bfloat16)
        grad_gate_one = jnp.sum(grad_middle * attended, axis=0)
        grad_out_w = grad_out_w + transposed(mixture_low, grad_attended)
        grad_mixture = (
            against(grad_attended, w_out).astype(jnp.bfloat16).reshape(own_rows, local_heads, HDIM)
        )
        chances_low, grad_scores, row_delta = attend_back(
            queries, all_keys, all_values, grad_mixture, logsum, allowed, None
        )
        grad_queries = (
            jnp.einsum("hqk,khd->qhd", grad_scores, all_keys, preferred_element_type=jnp.float32)
            * 0.125
        )
        grad_all_keys = (
            jnp.einsum("hqk,qhd->khd", grad_scores, queries, preferred_element_type=jnp.float32)
            * 0.125
        )
        grad_all_values = jnp.einsum(
            "hqk,qhd->khd", chances_low, grad_mixture, preferred_element_type=jnp.float32
        )
        both_grads = jnp.stack([grad_all_keys, grad_all_values], axis=1).reshape(
            length, 2 * local_heads * HDIM
        )
        own_grads = (
            lax.psum_scatter(
                both_grads.astype(jnp.bfloat16), "context", scatter_dimension=0, tiled=True
            )
            .astype(jnp.float32)
            .reshape(own_rows, 2, local_heads, HDIM)
        )
        grad_keys = own_grads[:, 0]
        grad_values = own_grads[:, 1]
        grad_queries = rotate(grad_queries, cosine, sine_part, -1.0)
        grad_keys = rotate(grad_keys, cosine, sine_part, -1.0)
        grad_projected = (
            jnp.stack([grad_queries, grad_keys, grad_values], axis=2)
            .reshape(own_rows, local_heads * 3 * HDIM)
            .astype(jnp.bfloat16)
        )
        grad_qkv = grad_qkv + transposed(entry_one, grad_projected)
        grad_entry_one = against(grad_projected, w_qkv)
        grad_shift_one = jnp.sum(grad_entry_one, axis=0)
        grad_scale_one = jnp.sum(grad_entry_one * lifted_one, axis=0)
        grad_lifted_one = grad_entry_one * (1.0 + scale_one)
        grad_gain_first = grad_gain_first + jnp.sum(grad_lifted_one * hat_one, axis=0)
        partial_inputs.append(norm_back(grad_lifted_one * gain_first, hat_one, scaling_one))
        carried.append(grad_middle)
        grad_mods.append(
            jnp.concatenate(
                [
                    grad_shift_one,
                    grad_scale_one,
                    grad_gate_one * leader,
                    grad_shift_two,
                    grad_scale_two,
                    grad_gate_two * leader,
                ]
            )
        )
    summed_inputs = lax.psum_scatter(
        jnp.stack(partial_inputs).astype(jnp.bfloat16), "tensor", scatter_dimension=2, tiled=True
    ).astype(jnp.float32)
    slice_width = model_width // lax.axis_size("tensor")
    own_middle = lax.dynamic_slice_in_dim(
        jnp.stack(carried), tensor_rank * slice_width, slice_width, axis=2
    )
    grad_tokens = summed_inputs + own_middle
    grad_mod = jnp.stack(grad_mods)
    bias_up_full = lax.dynamic_update_slice_in_dim(
        jnp.zeros((b_up.shape[0],), jnp.float32), grad_bias_up, tensor_rank * hidden_width, 0
    )
    grad_qkv, grad_up, grad_out_w, grad_down = (
        lax.psum_scatter(
            grad_qkv.astype(jnp.bfloat16), "fsdp", scatter_dimension=0, tiled=True
        ).astype(jnp.float32),
        lax.psum_scatter(
            grad_up.astype(jnp.bfloat16), "fsdp", scatter_dimension=0, tiled=True
        ).astype(jnp.float32),
        lax.psum_scatter(
            grad_out_w.astype(jnp.bfloat16), "fsdp", scatter_dimension=1, tiled=True
        ).astype(jnp.float32),
        lax.psum_scatter(
            grad_down.astype(jnp.bfloat16), "fsdp", scatter_dimension=1, tiled=True
        ).astype(jnp.float32),
    )
    grad_qkv, grad_up, grad_out_w, grad_down = (
        lax.psum(grad_qkv.astype(jnp.bfloat16), "context").astype(jnp.float32),
        lax.psum(grad_up.astype(jnp.bfloat16), "context").astype(jnp.float32),
        lax.psum(grad_out_w.astype(jnp.bfloat16), "context").astype(jnp.float32),
        lax.psum(grad_down.astype(jnp.bfloat16), "context").astype(jnp.float32),
    )
    grad_ada_b = jnp.sum(grad_mod, axis=0)
    grad_ada_w = exact_transposed(embedding, grad_mod)
    grad_embedding = exact_against(grad_mod, ada_full)
    grad_before = silu_back(grad_embedding)[0]
    grad_table = exact_transposed(choose, grad_before)
    (
        grad_table,
        grad_ada_w,
        grad_ada_b,
        grad_gain_first,
        grad_gain_second,
        bias_up_full,
        grad_bias_down,
    ) = lax.psum(
        (
            grad_table,
            grad_ada_w,
            grad_ada_b,
            grad_gain_first,
            grad_gain_second,
            bias_up_full,
            grad_bias_down * leader,
        ),
        ("fsdp", "context", "tensor"),
    )
    return (
        jnp.stack(results),
        grad_tokens,
        grad_table,
        grad_ada_w,
        grad_ada_b,
        grad_gain_first,
        grad_qkv,
        grad_out_w,
        grad_gain_second,
        grad_up,
        bias_up_full,
        grad_down,
        grad_bias_down,
    )


def solution(mesh):
    axes = dict(zip(mesh.axis_names, mesh.devices.shape))

    def whole(tokens, *others):
        sequences = tokens.shape[0] // axes["fsdp"]
        local = by_sequence if sequences == axes["context"] == 2 and axes["tensor"] == 4 else by_block
        return mapped(local, mesh)(tokens, *others)

    return whole


def mapped(local, mesh):
    return jax.shard_map(
        local,
        mesh=mesh,
        in_specs=(
            P("fsdp", "context", None),
            P("fsdp", "context", None),
            P("fsdp", None),
            P("fsdp"),
            P(),
            P(),
            P(),
            P(),
            P("fsdp", "tensor"),
            P("tensor", "fsdp"),
            P(),
            P("fsdp", "tensor"),
            P(),
            P("tensor", "fsdp"),
            P(),
        ),
        out_specs=(
            P("fsdp", "context", None),
            P("fsdp", "context", "tensor"),
            P(),
            P(),
            P(),
            P(),
            P("fsdp", "tensor"),
            P("tensor", "fsdp"),
            P(),
            P("fsdp", "tensor"),
            P(),
            P("tensor", "fsdp"),
            P(),
        ),
        check_vma=False,
    )
```

```python
import math
from functools import partial

import jax
import jax.numpy as jnp
from jax import lax
from jax.experimental import pallas as pl
from jax.experimental.pallas import tpu as pltpu
from jax.sharding import PartitionSpec as P

HDIM = 64
HALF = HDIM // 2
SEGMENTS = 5
WIDE = 128
MASKED = 2.0**100
LOG2E = math.log2(math.e)
SAFE_EXPONENT = 60.0
EPSILON = 1e-05
VMEM = 56 * 2**20
VMEM_MOST = 60 * 2**20


def cost(flops, *arrays):
    size = sum(math.prod(one.shape) * one.dtype.itemsize for one in arrays)
    return pl.CostEstimate(flops=int(flops), bytes_accessed=int(size), transcendentals=0)


precise = lax.Precision.HIGHEST
f32 = jnp.float32
bf16 = jnp.bfloat16


def product(left_side, right_side):
    return jnp.dot(left_side, right_side, preferred_element_type=jnp.float32)


def transposed(left_side, right_side):
    return lax.dot_general(
        left_side, right_side, (((0,), (0,)), ((), ())), preferred_element_type=jnp.float32
    )


def against(left_side, right_side):
    return lax.dot_general(
        left_side, right_side, (((1,), (1,)), ((), ())), preferred_element_type=jnp.float32
    )


def exact_product(left_side, right_side):
    return jnp.dot(left_side, right_side, precision=precise, preferred_element_type=jnp.float32)


def exact_transposed(left_side, right_side):
    return lax.dot_general(
        left_side,
        right_side,
        (((0,), (0,)), ((), ())),
        precision=precise,
        preferred_element_type=jnp.float32,
    )


def exact_against(left_side, right_side):
    return lax.dot_general(
        left_side,
        right_side,
        (((1,), (1,)), ((), ())),
        precision=precise,
        preferred_element_type=jnp.float32,
    )


def document_bounds(segment):
    indices = jnp.arange(segment.shape[-1], dtype=jnp.int32)
    same = segment[..., None, :] == jnp.arange(SEGMENTS, dtype=jnp.int32)[:, None]
    starts = jnp.min(jnp.where(same, indices, segment.shape[-1]), axis=-1)
    ends = jnp.max(jnp.where(same, indices + 1, 0), axis=-1)
    return same, starts, ends


def positions(segment):
    same, starts, _ = document_bounds(segment)
    first = jnp.sum(jnp.where(same, starts[..., :, None], 0), axis=-2)
    return jnp.arange(segment.shape[-1], dtype=jnp.int32) - first


def frequencies():
    return 10000.0 ** (-jnp.arange(HALF, dtype=jnp.float32) / HALF)


def copy_to(source, target, sent, arrived, **device):
    return pltpu.make_async_remote_copy(
        src_ref=source,
        dst_ref=target,
        send_sem=sent,
        recv_sem=arrived,
        device_id=device,
        device_id_type=pl.DeviceIdType.MESH,
    )


def greet(devices):
    barrier = pltpu.get_barrier_semaphore()
    for device in devices:
        pl.semaphore_signal(barrier, inc=1, device_id=device, device_id_type=pl.DeviceIdType.MESH)
    pl.semaphore_wait(barrier, len(devices))


def quarter_at(number, tensor):
    core = lax.rem(tensor, 2)
    chip = jnp.where(number < 2, tensor // 2, 1 - tensor // 2)
    return chip * 2 + jnp.where(lax.rem(number, 2) == 0, core, 1 - core)


def entry_kernel(
    tokens_ref,
    rows_ref,
    shard_ref,
    own_forward_ref,
    gain_ref,
    shift_ref,
    cosine_ref,
    sine_ref,
    segment_ref,
    query_ref,
    key_ref,
    key_t_ref,
    value_t_ref,
    hat_ref,
    scale_ref,
    norm_ref,
    weight_ref,
    forward_ref,
    shards,
    weight_t,
    rows,
    arrived,
    sent_shard,
    got_shard,
    own_shard,
    sent_block,
    got_block,
    sent_across,
    got_across,
    sent_sibling,
    got_sibling,
    sent_on,
    got_on,
    sent_forward,
    got_forward,
    own_forward,
    *,
    heads,
    groups,
):
    step = pl.program_id(0)
    fsdp, context, tensor = (lax.axis_index(name) for name in ("fsdp", "context", "tensor"))
    ranks = 4
    core = lax.rem(tensor, 2)
    sibling = tensor + 1 - 2 * core
    across = lax.rem(tensor + 2, ranks)
    quarter = rows.shape[0]
    chunks = sent_block.shape[0]
    height = quarter // chunks

    def shard_copy(away):
        return copy_to(
            shard_ref,
            shards.at[fsdp],
            sent_shard.at[away - 1],
            got_shard.at[away - 1],
            fsdp=lax.rem(fsdp + away, groups),
        )

    def shard_own():
        return pltpu.make_async_copy(shard_ref, shards.at[fsdp], own_shard)

    def chunk(rank, number):
        return arrived.at[rank, pl.ds(number * height, height), :]

    def block_copy(number):
        at = pl.multiple_of(tensor * quarter, quarter) + number * height
        return copy_to(
            tokens_ref.at[1 - context, pl.ds(at, height), :],
            chunk(tensor, number),
            sent_block.at[number],
            got_block.at[number],
            context=1 - context,
        )

    def across_copy(number):
        return copy_to(
            chunk(tensor, number),
            chunk(tensor, number),
            sent_across.at[number],
            got_across.at[number],
            tensor=across,
        )

    def sibling_copy(number):
        return copy_to(
            chunk(tensor, number),
            chunk(tensor, number),
            sent_sibling.at[number],
            got_sibling.at[number],
            tensor=sibling,
        )

    def on_copy(number):
        return copy_to(
            chunk(across, number),
            chunk(across, number),
            sent_on.at[number],
            got_on.at[number],
            tensor=sibling,
        )

    forward_rows = own_forward_ref.shape[0]

    def forward_place(rank):
        return forward_ref.at[pl.ds(pl.multiple_of(rank * forward_rows, forward_rows), forward_rows), :]

    def relay_copy(origin, upward):
        place = forward_place(origin)
        side = 0 if upward else 1
        return copy_to(
            place,
            place,
            sent_forward.at[side, origin],
            got_forward.at[origin],
            fsdp=fsdp + 1 if upward else fsdp - 1,
        )

    def forward_own():
        return pltpu.make_async_copy(own_forward_ref, forward_place(fsdp), own_forward)

    def relay(origin, upward):
        @pl.when(fsdp < groups - 1 if upward else fsdp > 0)
        def _():
            relay_copy(origin, upward).start()

    def from_below(distance, act):
        @pl.when(fsdp >= distance)
        def _():
            act(fsdp - distance, True)

    def from_above(distance, act):
        @pl.when(fsdp + distance < groups)
        def _():
            act(fsdp + distance, False)

    def hand_over(distance):
        def act(origin, upward):
            relay_copy(origin, upward).wait_recv()
            relay(origin, upward)

        from_below(distance, act)
        from_above(distance, act)

    def finish_forward():
        def sent(origin, upward):
            @pl.when(fsdp < groups - 1 if upward else fsdp > 0)
            def _():
                relay_copy(origin, upward).wait_send()

        sent(fsdp, True)
        sent(fsdp, False)
        for distance in range(1, groups):
            from_below(distance, sent)
            from_above(distance, sent)

    def take(numbers):
        for number in numbers:
            block_copy(number).wait_recv()
            across_copy(number).start()
            sibling_copy(number).start()

    def pass_on(numbers):
        for number in numbers:
            across_copy(number).wait_recv()
            on_copy(number).start()

    @pl.when(step == 0)
    def _():
        shard_own().start()
        greet(
            [{"fsdp": lax.rem(fsdp + away, groups)} for away in range(1, groups)]
            + [{"context": 1 - context}, {"tensor": sibling}, {"tensor": across}]
        )
        for away in range(1, groups):
            shard_copy(away).start()
        for number in range(chunks):
            block_copy(number).start()
        forward_own().start()
        take(range(chunks - 1))
        shard_own().wait()
        for away in range(1, groups):
            shard_copy(away).wait_recv()
        for number in range(groups):
            weight_ref[number * shards.shape[1] : (number + 1) * shards.shape[1], :] = shards[number]
        forward_own().wait()
        relay(fsdp, True)
        relay(fsdp, False)
        weight_t[...] = weight_ref[...].T

    @pl.when(step == 1)
    def _():
        take([chunks - 1])
        pass_on(range(chunks // 2))

    @pl.when(step == 2)
    def _():
        pass_on(range(chunks // 2, chunks))

    half = 4

    for distance in range(1, groups):

        @pl.when(step == 1 + 2 * distance)
        def _():
            hand_over(distance)

    @pl.when(step < half)
    def _():
        rows[...] = rows_ref[0]

    @pl.when(step == half + 1)
    def _():
        for number in range(chunks):
            sibling_copy(number).wait_recv()

    @pl.when(step == half + 3)
    def _():
        for number in range(chunks):
            on_copy(number).wait_recv()

    @pl.when(step >= half)
    def _():
        rows[...] = arrived[quarter_at(step - half, tensor)]

    inputs = rows[...].astype(f32).T
    center = inputs - jnp.mean(inputs, axis=0, keepdims=True)
    scaling = lax.rsqrt(jnp.mean(center * center, axis=0, keepdims=True) + EPSILON)
    hat = center * scaling
    hat_ref[...] = hat.astype(bf16)
    scale_ref[...] = scaling
    entry = (hat * gain_ref[...] + shift_ref[...]).astype(bf16)
    projected = product(weight_t[...], entry)
    cosine = cosine_ref[...]
    sine = sine_ref[...]
    tokens = cosine.shape[1]
    group = heads * HDIM
    segment = segment_ref[...]
    number = lax.broadcasted_iota(jnp.int32, (WIDE - HDIM, tokens), 0)
    same = (number == segment).astype(f32)
    extra_query = same
    extra_key = jnp.where(
        number < SEGMENTS, (same - 1.0) * MASKED, jnp.where(number < SEGMENTS + 3, 1.0, 0.0)
    )
    extra_value = jnp.where(number < 3, 1.0, 0.0)
    norms = []
    for head in range(heads):

        def turned(kind, factor):
            at = kind * group + head * HDIM
            front = projected[at : at + HALF]
            back = projected[at + HALF : at + HDIM]
            return jnp.concatenate(
                [(front * cosine - back * sine) * factor, (front * sine + back * cosine) * factor],
                axis=0,
            )

        queries = turned(0, 0.125 * LOG2E)
        keys = turned(1, 1.0)
        values = projected[2 * group + head * HDIM : 2 * group + (head + 1) * HDIM]
        norms.append(jnp.sum(queries * queries, axis=0, keepdims=True))
        norms.append(jnp.sum(keys * keys, axis=0, keepdims=True))
        query_ref[head] = jnp.concatenate([queries, extra_query], axis=0).astype(bf16)
        wide_keys = jnp.concatenate([keys, extra_key], axis=0)
        key_ref[head] = wide_keys.T.astype(bf16)
        key_t_ref[head] = wide_keys.astype(bf16)
        value_t_ref[head] = jnp.concatenate([values, extra_value], axis=0).astype(bf16)
    norms += [jnp.zeros_like(norms[0])] * (norm_ref.shape[0] - len(norms))
    norm_ref[...] = jnp.concatenate(norms, axis=0)

    @pl.when(step == pl.num_programs(0) - 1)
    def _():
        for away in range(1, groups):
            shard_copy(away).wait_send()
        for number in range(chunks):
            block_copy(number).wait_send()
            across_copy(number).wait_send()
            sibling_copy(number).wait_send()
            on_copy(number).wait_send()
        finish_forward()


def entry_call(tokens, shard, forward_shard, gain, shift, cosine, sine, segment, groups, tile):
    length = cosine.shape[1]
    shard_rows, width = shard.shape
    depth = shard_rows * groups
    heads = width // (3 * HDIM)
    half = tokens.shape[1] // tile
    chunks = 4

    def place(i):
        context = lax.axis_index("context")
        other = (1 - context) * half + quarter_at(jnp.maximum(i - half, 0), lax.axis_index("tensor"))
        return jnp.where(i < half, context * half + i, other)

    lanes = lambda i: (0, place(i))
    heads_lanes = lambda i: (0, 0, place(i))
    heads_rows = lambda i: (0, place(i), 0)
    whole = lambda i: (0, 0)
    shapes = [
        jax.ShapeDtypeStruct((heads, WIDE, length), bf16),
        jax.ShapeDtypeStruct((heads, length, WIDE), bf16),
        jax.ShapeDtypeStruct((heads, WIDE, length), bf16),
        jax.ShapeDtypeStruct((heads, WIDE, length), bf16),
        jax.ShapeDtypeStruct((depth, length), bf16),
        jax.ShapeDtypeStruct((1, length), f32),
        jax.ShapeDtypeStruct((8, length), f32),
        jax.ShapeDtypeStruct((depth, width), bf16),
        jax.ShapeDtypeStruct((depth, forward_shard.shape[1]), bf16),
    ]
    dma = lambda *shape: [pltpu.SemaphoreType.DMA(shape)] * 2
    return pl.pallas_call(
        partial(entry_kernel, heads=heads, groups=groups),
        grid=(2 * half,),
        in_specs=[
            pl.BlockSpec(memory_space=pl.ANY),
            pl.BlockSpec(
                (1, tile, depth),
                lambda i: (lax.axis_index("context"), jnp.minimum(i, half - 1), 0),
            ),
            pl.BlockSpec(memory_space=pl.ANY),
            pl.BlockSpec(forward_shard.shape, whole),
            pl.BlockSpec((depth, 1), whole),
            pl.BlockSpec((depth, 1), whole),
            pl.BlockSpec((HALF, tile), lanes),
            pl.BlockSpec((HALF, tile), lanes),
            pl.BlockSpec((1, tile), lanes),
        ],
        out_specs=[
            pl.BlockSpec((heads, WIDE, tile), heads_lanes),
            pl.BlockSpec((heads, tile, WIDE), heads_rows),
            pl.BlockSpec((heads, WIDE, tile), heads_lanes),
            pl.BlockSpec((heads, WIDE, tile), heads_lanes),
            pl.BlockSpec((depth, tile), lanes),
            pl.BlockSpec((1, tile), lanes),
            pl.BlockSpec((8, tile), lanes),
            pl.BlockSpec((depth, width), whole),
            pl.BlockSpec(memory_space=pl.ANY),
        ],
        out_shape=shapes,
        scratch_shapes=[
            pltpu.VMEM((groups, shard_rows, width), bf16),
            pltpu.VMEM((width, depth), bf16),
            pltpu.VMEM((tile, depth), bf16),
            pltpu.VMEM((4, tile, depth), bf16),
            *dma(groups - 1),
            pltpu.SemaphoreType.DMA,
            *dma(chunks),
            *dma(chunks),
            *dma(chunks),
            *dma(chunks),
            pltpu.SemaphoreType.DMA((2, groups)),
            pltpu.SemaphoreType.DMA((groups,)),
            pltpu.SemaphoreType.DMA,
        ],
        compiler_params=pltpu.CompilerParams(
            vmem_limit_bytes=VMEM, collective_id=1, has_side_effects=True
        ),
        cost_estimate=cost(4 * tokens.shape[1] * depth * width, tokens, *shapes),
        name="entry",
    )(tokens, tokens, shard, forward_shard, gain, shift, cosine, sine, segment)


def attend_kernel(
    range_ref, query_ref, key_ref, value_ref, norm_ref, out_ref, told_ref, total_ref, top_ref, safe_ref, *, block
):
    step = pl.program_id(0)
    first, count = range_ref[0, step], range_ref[1, step]
    heads = query_ref.shape[0]
    total_ref[...] = jnp.zeros_like(total_ref)

    @pl.when(step == 0)
    def _():
        largest = 0.0
        for head in range(heads):
            queries, keys = norm_ref[2 * head : 2 * head + 1], norm_ref[2 * head + 1 : 2 * head + 2]
            largest = jnp.maximum(largest, jnp.max(queries) * jnp.max(keys))
        safe_ref[0] = (largest <= SAFE_EXPONENT**2).astype(jnp.int32)

    def scores(head, at):
        return product(key_ref[head, pl.ds(at, block), :], query_ref[head])

    def mix(head, at, weights):
        return product(value_ref[head, :, pl.ds(at, block)], weights)

    @pl.when(safe_ref[0] == 1)
    def _():
        top_ref[...] = jnp.zeros_like(top_ref)

        def body(number, carry):
            at = pl.multiple_of(first + number * block, WIDE)
            raw = [scores(head, at) for head in range(heads)]
            weights = [jnp.exp2(one).astype(bf16) for one in raw]
            for head in range(heads):
                total_ref[head] += mix(head, at, weights[head])
            return carry

        lax.fori_loop(0, count, body, 0)

    @pl.when(safe_ref[0] != 1)
    def _():
        top_ref[...] = jnp.full_like(top_ref, -3e38)

        def body(number, carry):
            at = pl.multiple_of(first + number * block, WIDE)
            for head in range(heads):
                raw = scores(head, at)
                before = top_ref[head]
                top = jnp.maximum(before, jnp.max(raw, axis=0, keepdims=True))
                weights = jnp.exp2(raw - top).astype(bf16)
                total_ref[head] = total_ref[head] * jnp.exp2(before - top) + mix(head, at, weights)
                top_ref[head] = top
            return carry

        lax.fori_loop(0, count, body, 0)

    tile = query_ref.shape[2]
    number = lax.broadcasted_iota(jnp.int32, (16, tile), 0)
    for head in range(heads):
        total = total_ref[head]
        mass = total[HDIM : HDIM + 1]
        out_ref[0, pl.ds(head * HDIM, HDIM), :] = (total[:HDIM] * (1.0 / mass)).astype(bf16)
        rows = split_rows(-(top_ref[head] + jnp.log2(mass)), number, SEGMENTS)
        told_ref[head, :HDIM, :] = query_ref[head, :HDIM, :]
        told_ref[head, HDIM : HDIM + 16, :] = jnp.where(
            number < SEGMENTS, query_ref[head, HDIM : HDIM + 16, :].astype(f32), rows
        ).astype(bf16)
        told_ref[head, HDIM + 16 :, :] = query_ref[head, HDIM + 16 :, :]


def split_rows(values, number, first):
    high = values.astype(bf16).astype(f32)
    rest = values - high
    middle = rest.astype(bf16).astype(f32)
    low = rest - middle
    return jnp.where(
        number == first,
        high,
        jnp.where(number == first + 1, middle, jnp.where(number == first + 2, low, 0.0)),
    )


def attend_call(ranges, queries, keys, values_t, norms, tile, block):
    heads, _, length = queries.shape
    rows = HDIM + 16
    return pl.pallas_call(
        partial(attend_kernel, block=block),
        grid_spec=pltpu.PrefetchScalarGridSpec(
            num_scalar_prefetch=1,
            grid=(length // tile,),
            in_specs=[
                pl.BlockSpec((heads, WIDE, tile), lambda i, r: (0, 0, i)),
                pl.BlockSpec((heads, length, WIDE), lambda i, r: (0, 0, 0)),
                pl.BlockSpec((heads, rows, length), lambda i, r: (0, 0, 0)),
                pl.BlockSpec(norms.shape, lambda i, r: (0, 0)),
            ],
            out_specs=[
                pl.BlockSpec((1, heads * HDIM, tile), lambda i, r: (i, 0, 0)),
                pl.BlockSpec((heads, WIDE, tile), lambda i, r: (0, 0, i)),
            ],
            scratch_shapes=[
                pltpu.VMEM((heads, rows, tile), f32),
                pltpu.VMEM((heads, 1, tile), f32),
                pltpu.SMEM((1,), jnp.int32),
            ],
        ),
        out_shape=[
            jax.ShapeDtypeStruct((length // tile, heads * HDIM, tile), bf16),
            jax.ShapeDtypeStruct((heads, WIDE, length), bf16),
        ],
        compiler_params=pltpu.CompilerParams(vmem_limit_bytes=VMEM),
        cost_estimate=cost(4 * heads * length * length * WIDE, queries, keys, values_t),
        name="attend",
    )(ranges, queries, keys, values_t, norms)


def attend_back_kernel(
    range_ref,
    query_ref,
    key_ref,
    value_ref,
    mixture_ref,
    grad_ref,
    cosine_ref,
    sine_ref,
    grad_query_ref,
    grad_key_ref,
    grad_value_ref,
    wide_ref,
    query_rows,
    grad_rows,
    query_total,
    key_total,
    value_total,
    *,
    block,
):
    step = pl.program_id(0)
    first, count = range_ref[0, step], range_ref[1, step]
    heads, _, tile = query_ref.shape

    @pl.when(step == 0)
    def _():
        wide_ref[...] = jnp.zeros_like(wide_ref)
        key_total[...] = jnp.zeros_like(key_total)
        value_total[...] = jnp.zeros_like(value_total)

    number = lax.broadcasted_iota(jnp.int32, (16, tile), 0)
    query_total[...] = jnp.zeros_like(query_total)
    for head in range(heads):
        at = pl.ds(head * HDIM, HDIM)
        grad = grad_ref[0, at, :]
        delta = jnp.sum(grad.astype(f32) * mixture_ref[0, at, :].astype(f32), axis=0, keepdims=True)
        wide_ref[head, :HDIM, :] = grad
        wide_ref[head, HDIM : HDIM + 16, :] = split_rows(-delta, number, 0).astype(bf16)
        query_rows[head] = query_ref[head].T
        grad_rows[head] = wide_ref[head].T

    def body(number, carry):
        at = pl.ds(pl.multiple_of(first + number * block, WIDE), block)
        raw = [product(query_rows[head], key_ref[head, :, at]) for head in range(heads)]
        slope = [product(grad_rows[head], value_ref[head, :, at]) for head in range(heads)]
        for head in range(heads):
            weights = jnp.exp2(raw[head])
            grad_scores = (weights * slope[head]).astype(bf16)
            value_total[head, :, at] += product(wide_ref[head, :HDIM, :], weights.astype(bf16))
            key_total[head, :, at] += product(query_ref[head, :HDIM, :], grad_scores)
            query_total[head] += against(key_ref[head, :HDIM, at], grad_scores)
        return carry

    lax.fori_loop(0, count, body, 0)

    def turned_back(grads, cosine, sine):
        front, back = grads[:HALF], grads[HALF:]
        return jnp.concatenate([front * cosine + back * sine, back * cosine - front * sine], axis=0)

    own = pl.ds(pl.multiple_of(step * tile, tile), tile)
    for head in range(heads):
        at = pl.ds(head * HDIM, HDIM)
        grad_query_ref[at, :] = turned_back(
            query_total[head] * 0.125, cosine_ref[:, own], sine_ref[:, own]
        ).astype(bf16)

    @pl.when(step == pl.num_programs(0) - 1)
    def _():
        for head in range(heads):
            at = pl.ds(head * HDIM, HDIM)
            grad_key_ref[at, :] = turned_back(
                key_total[head] * (1.0 / LOG2E), cosine_ref[...], sine_ref[...]
            ).astype(bf16)
            grad_value_ref[at, :] = value_total[head].astype(bf16)


def attend_back_call(
    ranges, queries, keys_t, values_t, mixture, grad_mixture, cosine, sine, tile, block
):
    heads, _, length = queries.shape
    group = heads * HDIM
    whole2 = lambda i, r: (0, 0)
    whole3 = lambda i, r: (0, 0, 0)
    return pl.pallas_call(
        partial(attend_back_kernel, block=block),
        grid_spec=pltpu.PrefetchScalarGridSpec(
            num_scalar_prefetch=1,
            grid=(length // tile,),
            in_specs=[
                pl.BlockSpec((heads, WIDE, tile), lambda i, r: (0, 0, i)),
                pl.BlockSpec((heads, WIDE, length), whole3),
                pl.BlockSpec((heads, WIDE, length), whole3),
                pl.BlockSpec((1, group, tile), lambda i, r: (i, 0, 0)),
                pl.BlockSpec((1, group, tile), lambda i, r: (i, 0, 0)),
                pl.BlockSpec((HALF, length), whole2),
                pl.BlockSpec((HALF, length), whole2),
            ],
            out_specs=[
                pl.BlockSpec((group, tile), lambda i, r: (0, i)),
                pl.BlockSpec((group, length), whole2),
                pl.BlockSpec((group, length), whole2),
            ],
            scratch_shapes=[
                pltpu.VMEM((heads, WIDE, tile), bf16),
                pltpu.VMEM((heads, tile, WIDE), bf16),
                pltpu.VMEM((heads, tile, WIDE), bf16),
                pltpu.VMEM((heads, HDIM, tile), f32),
                pltpu.VMEM((heads, HDIM, length), f32),
                pltpu.VMEM((heads, HDIM, length), f32),
            ],
        ),
        out_shape=[jax.ShapeDtypeStruct((group, length), bf16)] * 3,
        compiler_params=pltpu.CompilerParams(vmem_limit_bytes=VMEM),
        cost_estimate=cost(10 * heads * length * length * WIDE, queries, keys_t, values_t),
        name="attend_back",
    )(ranges, queries, keys_t, values_t, mixture, grad_mixture, cosine, sine)


def middle_kernel(
    mixture_ref,
    rows_ref,
    cotangent_ref,
    valid_ref,
    mod_ref,
    up_bias_ref,
    down_bias_ref,
    out_blocks_ref,
    own_ref,
    other_ref,
    across_ref,
    result_ref,
    grad_mixture_ref,
    grad_middle_ref,
    grad_out_blocks_ref,
    sums_ref,
    bias_sums_ref,
    up_keep_ref,
    up_send_ref,
    down_keep_ref,
    down_send_ref,
    own_mixture,
    out_weight_ref,
    grad_out_ref,
    entry_rows,
    entry_columns,
    grad_output_rows,
    grad_output_columns,
    attended_rows,
    output_rows,
    grad_entry_rows,
    active,
    grad_hidden,
    grad_staged,
    forward_ref,
    landed,
    home_grads,
    to_sibling,
    from_sibling,
    staged_up,
    staged_down,
    sent_mixture,
    got_mixture,
    own_copied,
    sent_grad,
    got_grad,
    grad_copied,
    sent_part,
    got_part,
    kept,
    sent_next,
    got_next,
    loaded,
    sent_other,
    got_other,
    sent_last,
    got_last,
    *,
    tile,
    tiles,
    parts,
    groups,
):
    step = pl.program_id(0)
    context, tensor = lax.axis_index("context"), lax.axis_index("tensor")
    ranks = 4
    everyone = 2 * ranks
    place = context * ranks + tensor
    core = lax.rem(tensor, 2)
    sibling = tensor + 1 - 2 * core
    depth = rows_ref.shape[2]
    group = depth // ranks
    per_sequence = tiles // 2
    per_part = tiles + 1
    back_from = tiles + parts * per_part - 1
    last_step = back_from + tiles
    root = math.sqrt(2.0 / math.pi)

    def member(away):
        other = lax.rem(place + away, everyone)
        return other, {"context": other // ranks, "tensor": lax.rem(other, ranks)}

    def mixture_copy(away):
        other, device = member(away)
        return copy_to(
            mixture_ref.at[other],
            own_mixture.at[place],
            sent_mixture.at[away - 1],
            got_mixture.at[lax.rem(place + everyone, everyone)],
            **device,
        )

    def mixture_arrival(source):
        return pltpu.make_async_remote_copy(
            src_ref=mixture_ref.at[source],
            dst_ref=own_mixture.at[source],
            send_sem=sent_mixture.at[0],
            recv_sem=got_mixture.at[source],
            device_id={"tensor": sibling},
            device_id_type=pl.DeviceIdType.MESH,
        )

    def own_copy():
        return pltpu.make_async_copy(mixture_ref.at[place], own_mixture.at[place], own_copied)

    def part_copy(slot):
        return copy_to(
            to_sibling, from_sibling.at[slot], sent_part.at[slot], got_part.at[slot], tensor=sibling
        )

    across = lax.rem(tensor + 2, ranks)
    height = depth // groups

    def rows_of(number):
        return pl.ds(number * height, height)

    def next_copy(kind):
        return copy_to(
            forward_ref.at[kind],
            landed.at[0, kind],
            sent_next.at[kind],
            got_next.at[kind],
            tensor=sibling,
        )

    def out_blocks():
        for rank in range(ranks):
            for number in range(groups):
                rows = slice(rank * group, (rank + 1) * group)
                yield rank * groups + number, (rows, slice(number * height, (number + 1) * height))

    def weight_loads():
        return [
            pltpu.make_async_copy(own_ref, forward_ref.at[context], loaded.at[0]),
            pltpu.make_async_copy(other_ref, forward_ref.at[1 - context], loaded.at[1]),
            pltpu.make_async_copy(across_ref, landed.at[1, context], loaded.at[2]),
        ]

    def other_copy(kind, number):
        place = landed.at[1, kind, rows_of(number), :]
        return copy_to(place, place, sent_other.at[number], got_other.at[number], context=1 - context)

    def last_copy(kind, number):
        return copy_to(
            landed.at[1, kind, rows_of(number), :],
            landed.at[2, kind, rows_of(number), :],
            sent_last.at[kind, number],
            got_last.at[kind, number],
            tensor=sibling,
        )

    def take_other(numbers):
        for number in numbers:
            other_copy(1 - context, number).wait_recv()
            last_copy(1 - context, number).start()

    def gradient_lanes(at):
        return pl.ds(pl.multiple_of(lax.rem(at, per_sequence) * tile, tile), tile)

    def sequence_of(at):
        return lax.rem(at // per_sequence + context, 2)

    def gradient_copy(at, rank):
        return copy_to(
            grad_staged.at[at, rank],
            grad_mixture_ref.at[place, :, gradient_lanes(at)],
            sent_grad.at[at, rank],
            got_grad.at[place, lax.rem(at, per_sequence)],
            context=sequence_of(at),
            tensor=rank,
        )

    def gradient_own(at):
        return pltpu.make_async_copy(
            grad_staged.at[at, tensor],
            grad_mixture_ref.at[place, :, gradient_lanes(at)],
            grad_copied.at[lax.rem(at, per_sequence)],
        )

    def gradient_arrival(source, number):
        return pltpu.make_async_remote_copy(
            src_ref=grad_staged.at[0, 0],
            dst_ref=grad_mixture_ref.at[source, :, pl.ds(number * tile, tile)],
            send_sem=sent_grad.at[0, 0],
            recv_sem=got_grad.at[source, number],
            device_id={"tensor": sibling},
            device_id_type=pl.DeviceIdType.MESH,
        )

    def kept_copies(slot):
        if slot == 1:
            return [
                pltpu.make_async_copy(staged_up, up_send_ref, kept.at[0]),
                pltpu.make_async_copy(staged_down.at[0], down_keep_ref.at[0], kept.at[1]),
                pltpu.make_async_copy(staged_down.at[1], down_send_ref.at[0], kept.at[2]),
            ]
        return [
            pltpu.make_async_copy(staged_up, up_keep_ref, kept.at[3]),
            pltpu.make_async_copy(staged_down.at[0], down_keep_ref.at[1], kept.at[4]),
            pltpu.make_async_copy(staged_down.at[1], down_send_ref.at[1], kept.at[5]),
        ]

    def tile_of(at):
        sequence = sequence_of(at)
        rows = pl.ds(pl.multiple_of(at * tile, tile), tile)
        mods = mod_ref[sequence]
        lanes = gradient_lanes(at)
        mixture_t = jnp.concatenate(
            [own_mixture[sequence * ranks + rank, :, lanes] for rank in range(ranks)], axis=0
        )
        return rows, mixture_t, tuple(mods[k : k + 1] for k in range(4))

    def normal(attended, gate_one):
        middle = rows_ref[0].astype(f32) + gate_one * attended
        center = middle - jnp.mean(middle, axis=-1, keepdims=True)
        scaling = lax.rsqrt(jnp.mean(center * center, axis=-1, keepdims=True) + EPSILON)
        return middle, center * scaling, scaling

    @pl.when(step == 0)
    def _():
        own_copy().start()
        for one in weight_loads():
            one.start()
        greet([member(away)[1] for away in range(1, everyone)])
        for near in (True, False):
            for away in range(1, everyone):

                @pl.when((member(away)[0] // ranks == context) == near)
                def _():
                    mixture_copy(away).start()

        for block, at in out_blocks():
            out_weight_ref[at] = out_blocks_ref[block]
        sums_ref[...] = jnp.zeros_like(sums_ref)
        bias_sums_ref[...] = jnp.zeros_like(bias_sums_ref)
        grad_out_ref[...] = jnp.zeros_like(grad_out_ref)

    for sequence in range(2):

        @pl.when(step == lax.rem(sequence + context, 2) * per_sequence)
        def _():
            for rank in range(ranks):
                source = sequence * ranks + rank

                @pl.when(place == source)
                def _():
                    own_copy().wait()

                @pl.when(place != source)
                def _():
                    mixture_arrival(source).wait_recv()

    @pl.when(step == per_sequence)
    def _():
        for one in weight_loads():
            one.wait()
        for kind in range(2):
            next_copy(kind).start()
        for number in range(groups):
            other_copy(context, number).start()
            last_copy(context, number).start()

    @pl.when(step == tiles + per_part)
    def _():
        for kind in range(2):
            next_copy(kind).wait_recv()

    @pl.when(step == tiles + 2 * per_part - 2)
    def _():
        take_other(range(groups // 2))

    @pl.when(step == tiles + 2 * per_part - 1)
    def _():
        take_other(range(groups // 2, groups))

    @pl.when(step == tiles + 2 * per_part)
    def _():
        for kind in range(2):
            for number in range(groups):
                last_copy(kind, number).wait_recv()

    @pl.when(step < tiles)
    def _():
        rows, mixture_t, (gate_one, shift_two, gain_two, gate_two) = tile_of(step)
        attended = product(mixture_t.T, out_weight_ref[...])
        attended_rows[rows, :] = attended
        _, hat, _ = normal(attended, gate_one)
        entry = (hat * gain_two + shift_two).astype(bf16)
        grad_output = (gate_two * (cotangent_ref[0].astype(f32) * valid_ref[...])).astype(bf16)
        entry_rows[rows, :] = entry
        entry_columns[:, rows] = entry.T
        grad_output_rows[rows, :] = grad_output
        grad_output_columns[:, rows] = grad_output.T
        output_rows[rows, :] = jnp.broadcast_to(down_bias_ref[...], (tile, depth))
        grad_entry_rows[rows, :] = jnp.zeros((tile, depth), f32)

    inner = lax.rem(step - tiles, per_part)
    position = (step - tiles) // per_part
    in_parts = (step >= tiles) & (step < back_from)

    def part_tile(up, down):
        rows = pl.ds(pl.multiple_of(inner * tile, tile), tile)
        number = part_at(position, tensor)
        hidden = product(entry_rows[rows, :], up[...]) + up_bias_ref[0]
        square = hidden * hidden
        bent = jnp.tanh(root * hidden * (1.0 + 0.044715 * square))
        half = 0.5 * (1.0 + bent)
        activated = (hidden * half).astype(bf16)
        slope = half + (0.5 * root) * hidden * (1.0 - bent * bent) * (1.0 + 0.134145 * square)
        grads = (product(grad_output_rows[rows, :], down[...]) * slope).astype(bf16)
        output_rows[rows, :] += against(activated, down[...])
        grad_entry_rows[rows, :] += against(grads, up[...])
        active[rows, :] = activated
        grad_hidden[rows, :] = grads
        bias_sums_ref[number] += jnp.sum(grads.astype(f32), axis=0, keepdims=True)

    @pl.when(in_parts & (inner < tiles) & (position == 0))
    def _():
        part_tile(forward_ref.at[0], forward_ref.at[1])

    @pl.when(in_parts & (inner < tiles) & (position > 0))
    def _():
        place = lax.rem((position - 1) * 2, 3)
        part_tile(landed.at[place, 0], landed.at[place, 1])

    def products(other):
        at = rows_of(other)
        return [
            product(entry_columns[at, :], grad_hidden[...]),
            product(grad_output_columns[at, :], active[...]),
        ]

    def gather_home(slot, own):
        part_copy(slot).wait_recv()
        if slot:
            for one in kept_copies(0):
                one.wait()
        for other in range(groups):
            for kind, (staged, term) in enumerate(zip((staged_up, staged_down), own(other))):
                total = (term + from_sibling[slot, kind, rows_of(other), :].astype(f32)).astype(bf16)
                staged[context, other] = total[: height // 2]
                staged[1 - context, other] = total[height // 2 :]
        for one in kept_copies(slot):
            one.start()

    for turn in range(parts):

        @pl.when(step == (tiles + turn * per_part + tiles if turn < parts - 1 else last_step))
        def _():
            if turn == 2:
                gather_home(0, lambda other: [home_grads[kind, rows_of(other), :].astype(f32) for kind in range(2)])
                part_copy(0).wait_send()
            if turn == 3:
                gather_home(1, products)
                return
            target = home_grads if turn == 0 else to_sibling
            for other in range(groups):
                for kind, term in enumerate(products(other)):
                    target[kind, rows_of(other), :] = term.astype(bf16)
            if turn:
                part_copy(turn - 1).start()

    @pl.when((step >= back_from) & (step < last_step))
    def _():
        at = lax.rem(step - back_from + per_sequence, tiles)
        sequence = sequence_of(at)
        rows, mixture_t, (gate_one, _, gain_two, gate_two) = tile_of(at)
        attended = attended_rows[rows, :]
        middle, hat, scaling = normal(attended, gate_one)
        output = output_rows[rows, :]
        grad_entry = grad_entry_rows[rows, :]
        grad_result = cotangent_ref[0].astype(f32) * valid_ref[...]
        result_ref[...] = (middle + gate_two * output).astype(bf16)
        grad_lifted = grad_entry * gain_two
        grad_middle = grad_result + scaling * (
            grad_lifted
            - jnp.mean(grad_lifted, axis=-1, keepdims=True)
            - hat * jnp.mean(grad_lifted * hat, axis=-1, keepdims=True)
        )
        grad_attended = (gate_one * grad_middle).astype(bf16)
        grad_mixture = against(out_weight_ref[...], grad_attended).astype(bf16)
        for rank in range(ranks):
            grad_staged[at, rank] = grad_mixture[rank * group : (rank + 1) * group]
        for rank in range(ranks):
            own = (sequence == context) & (tensor == rank)

            @pl.when(own)
            def _():
                gradient_own(at).start()

            @pl.when(jnp.logical_not(own))
            def _():
                gradient_copy(at, rank).start()

        grad_middle_ref[0] = grad_middle.T.astype(bf16)
        grad_out_ref[...] += product(mixture_t, grad_attended)
        lines = [
            jnp.sum(grad_middle * attended, axis=0, keepdims=True),
            jnp.sum(grad_entry, axis=0, keepdims=True),
            jnp.sum(grad_entry * hat, axis=0, keepdims=True),
            jnp.sum(grad_result * output, axis=0, keepdims=True),
            jnp.sum(grad_output_rows[rows, :].astype(f32), axis=0, keepdims=True),
        ]
        lines += [jnp.zeros_like(lines[0])] * (sums_ref.shape[1] - len(lines))
        sums_ref[sequence] += jnp.concatenate(lines, axis=0)

    @pl.when(step == last_step)
    def _():
        for block, at in out_blocks():
            grad_out_blocks_ref[block] = grad_out_ref[at].astype(bf16)
        for source in range(everyone):
            for number in range(per_sequence):

                @pl.when(place != source)
                def _():
                    gradient_arrival(source, number).wait_recv()

        for at in range(tiles):
            for rank in range(ranks):
                own = (sequence_of(at) == context) & (tensor == rank)

                @pl.when(own)
                def _():
                    gradient_own(at).wait()

                @pl.when(jnp.logical_not(own))
                def _():
                    gradient_copy(at, rank).wait_send()

        for away in range(1, everyone):
            mixture_copy(away).wait_send()
        for kind in range(2):
            next_copy(kind).wait_send()
        for number in range(groups):
            other_copy(context, number).wait_send()
            for kind in range(2):
                last_copy(kind, number).wait_send()
        part_copy(1).wait_send()
        for one in kept_copies(1):
            one.wait()


def part_at(position, tensor):
    return quarter_at(jnp.where(position < 2, position, 5 - position), tensor)


def middle_call(
    mixture, rows, cotangent, valid, mods, up_bias, down_bias, out_blocks, own_weight, other_weight, across, groups, tile
):
    pieces, group, own = mixture.shape
    depth = rows.shape[2]
    tokens = rows.shape[0] * own
    parts, _, part_width = up_bias.shape
    tiles = tokens // tile
    per_sequence = tiles // 2
    per_part = tiles + 1
    back_from = tiles + parts * per_part - 1
    half = depth // groups // 2

    def in_order(at):
        sequence = lax.rem(at // per_sequence + lax.axis_index("context"), 2)
        return sequence, lax.rem(at, per_sequence)

    def back_number(i):
        return lax.rem(jnp.clip(i - back_from, 0, tiles - 1) + per_sequence, tiles)

    def token_place(i):
        return in_order(jnp.where(i < tiles, i, back_number(i)))

    def token_tile(i):
        sequence, number = token_place(i)
        return sequence, lax.axis_index("tensor") * per_sequence + number, 0

    def valid_tile(i):
        sequence, number = token_place(i)
        return sequence * per_sequence + number, 0

    def part_block(i):
        position = jnp.clip((i - tiles) // per_part, 0, parts - 1)
        return part_at(position, lax.axis_index("tensor")), 0, 0

    def back_tile(i):
        return in_order(back_number(i))

    whole2 = lambda i: (0, 0)
    whole3 = lambda i: (0, 0, 0)
    once = pl.Buffered(1)
    hbm = pl.BlockSpec(memory_space=pl.ANY)
    kept = jax.ShapeDtypeStruct((2, groups, half, part_width), bf16)
    wide = (tokens, depth)
    return pl.pallas_call(
        partial(middle_kernel, tile=tile, tiles=tiles, parts=parts, groups=groups),
        grid=(back_from + tiles + 1,),
        in_specs=[
            hbm,
            pl.BlockSpec((1, tile, depth), token_tile),
            pl.BlockSpec((1, tile, depth), token_tile),
            pl.BlockSpec((tile, 1), valid_tile),
            pl.BlockSpec(mods.shape, whole3, pipeline_mode=once),
            pl.BlockSpec((1, 1, part_width), part_block),
            pl.BlockSpec((1, depth), whole2, pipeline_mode=once),
            pl.BlockSpec(out_blocks.shape, whole3, pipeline_mode=once),
            hbm,
            hbm,
            hbm,
        ],
        out_specs=[
            pl.BlockSpec(
                (tile, depth), lambda i: (back_tile(i)[0] * per_sequence + back_tile(i)[1], 0)
            ),
            hbm,
            pl.BlockSpec(
                (1, depth, tile),
                lambda i: (back_tile(i)[0], 0, back_tile(i)[1]),
            ),
            pl.BlockSpec(out_blocks.shape, whole3),
            pl.BlockSpec((2, 8, depth), whole3),
            pl.BlockSpec((parts, 1, part_width), whole3),
            hbm,
            hbm,
            hbm,
            hbm,
        ],
        out_shape=[
            jax.ShapeDtypeStruct((tokens, depth), bf16),
            jax.ShapeDtypeStruct(mixture.shape, bf16),
            jax.ShapeDtypeStruct((2, depth, own), bf16),
            jax.ShapeDtypeStruct(out_blocks.shape, bf16),
            jax.ShapeDtypeStruct((2, 8, depth), f32),
            jax.ShapeDtypeStruct((parts, 1, part_width), f32),
            kept,
            kept,
            kept,
            kept,
        ],
        scratch_shapes=[
            pltpu.VMEM(mixture.shape, bf16),
            pltpu.VMEM((depth, depth), bf16),
            pltpu.VMEM((depth, depth), f32),
            pltpu.VMEM(wide, bf16),
            pltpu.VMEM((depth, tokens), bf16),
            pltpu.VMEM(wide, bf16),
            pltpu.VMEM((depth, tokens), bf16),
            pltpu.VMEM(wide, f32),
            pltpu.VMEM(wide, f32),
            pltpu.VMEM(wide, f32),
            pltpu.VMEM((tokens, part_width), bf16),
            pltpu.VMEM((tokens, part_width), bf16),
            pltpu.VMEM((tiles, 4, group, tile), bf16),
            pltpu.VMEM((2, depth, part_width), bf16),
            pltpu.VMEM((3, 2, depth, part_width), bf16),
            pltpu.VMEM((2, depth, part_width), bf16),
            pltpu.VMEM((2, depth, part_width), bf16),
            pltpu.VMEM((2, 2, depth, part_width), bf16),
            pltpu.VMEM((2, groups, half, part_width), bf16),
            pltpu.VMEM((2, groups, half, part_width), bf16),
            pltpu.SemaphoreType.DMA((pieces - 1,)),
            pltpu.SemaphoreType.DMA((pieces,)),
            pltpu.SemaphoreType.DMA,
            pltpu.SemaphoreType.DMA((tiles, 4)),
            pltpu.SemaphoreType.DMA((pieces, per_sequence)),
            pltpu.SemaphoreType.DMA((per_sequence,)),
            pltpu.SemaphoreType.DMA((2,)),
            pltpu.SemaphoreType.DMA((2,)),
            pltpu.SemaphoreType.DMA((6,)),
            *[pltpu.SemaphoreType.DMA((2,))] * 2,
            pltpu.SemaphoreType.DMA((3,)),
            *[pltpu.SemaphoreType.DMA((groups,))] * 2,
            *[pltpu.SemaphoreType.DMA((2, groups))] * 2,
        ],
        compiler_params=pltpu.CompilerParams(
            vmem_limit_bytes=VMEM_MOST, collective_id=2, has_side_effects=True
        ),
        cost_estimate=cost(6 * tokens * depth * (depth + 3 * parts * part_width), rows, rows, rows),
        name="middle",
    )(mixture, rows, cotangent, valid, mods, up_bias, down_bias, out_blocks, own_weight, other_weight, across)


def entry_back_kernel(
    grad_query_ref,
    grad_key_ref,
    grad_value_ref,
    hat_ref,
    scale_ref,
    gain_ref,
    shift_ref,
    weight_ref,
    middle_ref,
    middle_in_ref,
    small_ref,
    up_ref,
    down_ref,
    grad_out_ref,
    result_ref,
    result_in_ref,
    out_ref,
    grad_weight_ref,
    all_sums_ref,
    all_small_ref,
    pieces_ref,
    grad_out_sum_ref,
    block_ref,
    up_own,
    up_in,
    down_own,
    down_in,
    slices,
    slices_in,
    context_slice,
    context_in,
    small_in,
    small_sum,
    small_groups,
    out_in,
    loaded,
    sent_up,
    got_up,
    sent_down,
    got_down,
    sent_slice,
    got_slice,
    sent_context,
    got_context,
    sent_small,
    got_small,
    sent_sum,
    got_sum,
    sent_out,
    got_out,
    sent_result,
    got_result,
    moved,
    taken,
    held,
    weight_total,
    sums,
    part,
    part_in,
    pair,
    pair_in,
    chip,
    chip_in,
    piece,
    piece_in,
    block_piece,
    block_in,
    rank_sums,
    rank_in,
    group_sums,
    group_in,
    sent_part,
    got_part,
    sent_pair,
    got_pair,
    sent_chip,
    got_chip,
    sent_piece,
    got_piece,
    sent_block,
    got_block,
    sent_rank,
    got_rank,
    sent_group,
    got_group,
    *,
    tiles,
    groups,
):
    step = pl.program_id(0)
    fsdp, context, tensor = (lax.axis_index(name) for name in ("fsdp", "context", "tensor"))
    ranks = 4
    half = tiles // 2
    core = lax.rem(tensor, 2)
    chip_x = tensor // 2
    sibling = tensor + 1 - 2 * core
    across = lax.rem(tensor + 2, ranks)
    place = fsdp * 2 + context
    depth = hat_ref.shape[0]
    slice_rows = depth // ranks
    weight_rows = depth // groups
    everyone = groups * 2

    def group_member(away):
        other = lax.rem(place + away, everyone)
        return {"fsdp": other // 2, "context": lax.rem(other, 2)}

    def group_away(number):
        return {"fsdp": lax.rem(fsdp + number // 2, groups), "context": number % 2}

    plane = context * ranks + tensor
    in_plane = 2 * ranks

    def plane_member(away):
        other = lax.rem(plane + away, in_plane)
        return {"context": other // ranks, "tensor": lax.rem(other, ranks)}

    def up_copy(other):
        return copy_to(
            up_ref.at[1, other], up_in.at[other], sent_up.at[other], got_up.at[other], context=1 - context
        )

    def down_copy(other):
        return copy_to(
            down_ref.at[0, other], down_in.at[other], sent_down.at[other], got_down.at[other], tensor=across
        )

    def loads():
        return [
            pltpu.make_async_copy(up_ref.at[0], up_own, loaded.at[0]),
            pltpu.make_async_copy(down_ref.at[1], down_own, loaded.at[1]),
        ]

    def slice_copy(away):
        other = lax.rem(fsdp + away, groups)
        return copy_to(
            slices.at[other],
            slices_in.at[away - 1],
            sent_slice.at[away - 1],
            got_slice.at[away - 1],
            fsdp=other,
        )

    def context_copy():
        return copy_to(context_slice, context_in, sent_context, got_context, context=1 - context)

    def small_copy(away):
        return copy_to(
            small_ref,
            small_in.at[away - 1],
            sent_small.at[away - 1],
            got_small.at[away - 1],
            **plane_member(away),
        )

    def sum_copy(away):
        return copy_to(
            small_sum,
            small_groups.at[away - 1],
            sent_sum.at[away - 1],
            got_sum.at[away - 1],
            fsdp=lax.rem(fsdp + away, groups),
        )

    def out_copy():
        return copy_to(grad_out_ref, out_in, sent_out, got_out, context=1 - context)

    quarter = result_ref.shape[1]

    def result_places():
        for number, (source, rank) in enumerate([(result_ref, tensor), (result_in_ref, across)]):
            rows = pl.ds(pl.multiple_of(rank * quarter, quarter), quarter)
            for sequence in range(2):
                yield number * 2 + sequence, source.at[sequence], block_ref.at[sequence, rows, :]

    def result_copies():
        return [
            copy_to(held.at[k], target, sent_result.at[k], got_result.at[k], tensor=sibling)
            for k, source, target in result_places()
        ]

    def result_loads():
        return [
            pltpu.make_async_copy(source, held.at[k], taken.at[k])
            for k, source, target in result_places()
        ]

    def result_moves():
        return [
            pltpu.make_async_copy(held.at[k], target, moved.at[k]) for k, source, target in result_places()
        ]

    def part_copy(tile):
        return copy_to(
            part.at[tile, 1 - core], part_in.at[tile], sent_part.at[tile], got_part.at[tile], tensor=sibling
        )

    def pair_copy(tile):
        return copy_to(
            pair.at[tile, 1 - chip_x], pair_in.at[tile], sent_pair.at[tile], got_pair.at[tile], tensor=across
        )

    def chip_copy(tile):
        return copy_to(
            chip.at[tile], chip_in.at[tile], sent_chip.at[tile], got_chip.at[tile], context=1 - context
        )

    def piece_copy(away):
        other = lax.rem(fsdp + away, groups)
        return copy_to(
            piece.at[other],
            piece_in.at[away - 1],
            sent_piece.at[away - 1],
            got_piece.at[away - 1],
            fsdp=other,
        )

    def block_copy():
        return copy_to(block_piece, block_in, sent_block, got_block, context=1 - context)

    def rank_copy(away):
        return copy_to(
            rank_sums,
            rank_in.at[away - 1],
            sent_rank.at[away - 1],
            got_rank.at[away - 1],
            tensor=lax.rem(tensor + away, ranks),
        )

    def group_copy(away):
        return copy_to(
            group_sums,
            group_in.at[away - 1],
            sent_group.at[away - 1],
            got_group.at[away - 1],
            **group_member(away),
        )

    @pl.when(step == 0)
    def _():
        greet(
            [plane_member(away) for away in range(1, in_plane)]
            + [group_away(away) for away in range(2, everyone)]
        )
        for away in range(1, groups + 1):
            other = lax.rem(fsdp + away, groups)
            up_copy(other).start()
            down_copy(other).start()
        out_copy().start()
        for away in range(1, in_plane):
            small_copy(away).start()
        for one in result_loads() + loads():
            one.start()
        weight_total[...] = jnp.zeros_like(weight_total)
        sums[...] = jnp.zeros_like(sums)

    @pl.when(step == 2)
    def _():
        for one in result_loads():
            one.wait()
        for one in result_copies() + result_moves():
            one.start()

    def grads():
        return jnp.concatenate([grad_query_ref[...], grad_key_ref[...], grad_value_ref[...]], axis=0)

    @pl.when(step < tiles)
    def _():
        tile = step
        columns = grads()
        grad_entry = product(weight_ref[...], columns)
        hat = hat_ref[...].astype(f32)
        lifted = hat * gain_ref[...]
        weight_total[...] += against((lifted + shift_ref[...]).astype(bf16), columns)
        grad_lifted = grad_entry * gain_ref[...]
        term = scale_ref[...] * (
            grad_lifted
            - jnp.mean(grad_lifted, axis=0, keepdims=True)
            - hat * jnp.mean(grad_lifted * hat, axis=0, keepdims=True)
        )
        extra = jnp.where(tile < half, middle_in_ref[...], middle_ref[0]).astype(f32)
        term = (term + jnp.where(lax.rem(tile, half) == tensor, extra, 0.0)).astype(bf16)
        for rank in range(ranks):
            part[tile, rank % 2, rank // 2] = term[rank * slice_rows : (rank + 1) * slice_rows]
        part_copy(tile).start()
        weighted = grad_entry * hat
        for lane in range(0, grad_entry.shape[1], WIDE):
            sums[0] += grad_entry[:, lane : lane + WIDE]
            sums[1] += weighted[:, lane : lane + WIDE]

    @pl.when(step == tiles - 1)
    def _():
        for other in range(groups):
            piece[other] = weight_total[other * weight_rows : (other + 1) * weight_rows].astype(bf16)
        for away in range(1, groups):
            piece_copy(away).start()

    @pl.when((step >= 1) & (step < tiles + 1))
    def _():
        tile = step - 1
        part_copy(tile).wait_recv()
        pair[tile] = (part[tile, core].astype(f32) + part_in[tile].astype(f32)).astype(bf16)
        pair_copy(tile).start()

    @pl.when((step >= 3) & (step < tiles + 3))
    def _():
        tile = step - 3
        pair_copy(tile).wait_recv()
        total = (pair[tile, chip_x].astype(f32) + pair_in[tile].astype(f32)).astype(bf16)

        @pl.when(tile < half)
        def _():
            chip[tile] = total
            chip_copy(tile).start()

        @pl.when(tile >= half)
        def _():
            out_ref[context, tile - half] = total

    @pl.when((step >= tiles - 1) & (step < tiles - 1 + half))
    def _():
        tile = step - tiles + 1
        chip_copy(tile).wait_recv()
        out_ref[1 - context, tile] = chip_in[tile]

    @pl.when(step == 4)
    def _():
        for away in range(1, in_plane):
            small_copy(away).wait_recv()
        small_sum[...] = ordered_sum(small_ref[...], [small_in[k] for k in range(in_plane - 1)], plane)
        for away in range(1, groups):
            sum_copy(away).start()

    for away in range(1, groups + 1):

        @pl.when(step == 1 + away)
        def _():
            if away == 1:
                for one in loads():
                    one.wait()
            other = lax.rem(fsdp + away, groups)
            up_copy(other).wait_recv()
            down_copy(other).wait_recv()
            slices[other, 0] = (up_own[other].astype(f32) + up_in[other].astype(f32)).astype(bf16)
            slices[other, 1] = (down_own[other].astype(f32) + down_in[other].astype(f32)).astype(bf16)
            if away < groups:
                slice_copy(away).start()

    @pl.when(step == tiles)
    def _():
        total = slices[fsdp].astype(f32)
        for away in range(1, groups):
            slice_copy(away).wait_recv()
            total = total + slices_in[away - 1].astype(f32)
        context_slice[...] = total.astype(bf16)
        context_copy().start()

    @pl.when(step == tiles + 2)
    def _():
        total = piece[fsdp].astype(f32)
        for away in range(1, groups):
            piece_copy(away).wait_recv()
            total = total + piece_in[away - 1].astype(f32)
        block_piece[...] = total.astype(bf16)
        block_copy().start()

    @pl.when(step == tiles + 2)
    def _():
        block_copy().wait_recv()
        grad_weight_ref[...] = block_piece[...].astype(f32) + block_in[...].astype(f32)

    @pl.when(step == tiles - 1)
    def _():
        rows = [jnp.sum(sums[kind].T, axis=0, keepdims=True) for kind in range(2)]
        rank_sums[...] = jnp.concatenate(rows + [jnp.zeros((6, depth), f32)], axis=0)
        for away in range(1, ranks):
            rank_copy(away).start()

    @pl.when(step == tiles)
    def _():
        for away in range(1, ranks):
            rank_copy(away).wait_recv()
        pairs = [rank_sums[...] + rank_in[1], rank_in[0] + rank_in[2]]
        group_sums[...] = pairs[0] + pairs[1]
        for away in range(1, everyone):
            group_copy(away).start()

    @pl.when(step == tiles + 2)
    def _():
        all_small_ref[fsdp] = small_sum[...]
        for away in range(1, groups):
            sum_copy(away).wait_recv()
            all_small_ref[lax.rem(fsdp + groups - away, groups)] = small_groups[away - 1]
            sum_copy(away).wait_send()
            slice_copy(away).wait_send()
        context_copy().wait()
        pieces_ref[context] = context_slice[...]
        pieces_ref[1 - context] = context_in[...]
        out_copy().wait()
        grad_out_sum_ref[...] = grad_out_ref[...].astype(f32) + out_in[...].astype(f32)
        for other in range(groups):
            up_copy(other).wait_send()
            down_copy(other).wait_send()
        for away in range(1, in_plane):
            small_copy(away).wait_send()
        for one in result_copies() + result_moves():
            one.wait()
        all_sums_ref[place] = group_sums[...]
        for away in range(1, everyone):
            group_copy(away).wait_recv()
            all_sums_ref[lax.rem(place + everyone - away, everyone)] = group_in[away - 1]
        for tile in range(tiles):
            part_copy(tile).wait_send()
            pair_copy(tile).wait_send()
        for tile in range(half):
            chip_copy(tile).wait_send()
        for away in range(1, groups):
            piece_copy(away).wait_send()
        block_copy().wait_send()
        for away in range(1, ranks):
            rank_copy(away).wait_send()
        for away in range(1, everyone):
            group_copy(away).wait_send()


def ordered_sum(own, others, place):
    count = len(others) + 1
    total = 0.0
    for source in range(count):
        away = lax.rem(place - source + count, count)
        term = own
        for k, other in enumerate(others):
            term = jnp.where(away == k + 1, other, term)
        total = total + term
    return total


def entry_back_call(
    grad_query,
    grad_key,
    grad_value,
    hat_t,
    scaling,
    gain,
    shift,
    weight,
    grad_middle,
    middle_in,
    small,
    up,
    down,
    grad_out,
    result,
    result_in,
    groups,
    tile,
):
    group, length = grad_query.shape
    depth = hat_t.shape[0]
    tiles = length // tile
    half = tiles // 2
    rows = depth // 4
    weight_rows = depth // groups

    def lanes(step):
        first = (1 - lax.axis_index("context")) * half
        return 0, lax.rem(first + jnp.minimum(step, tiles - 1), tiles)

    whole = lambda step: (0, 0)
    whole3 = lambda step: (0, 0, 0)
    whole4 = lambda step: (0, 0, 0, 0)
    dma = lambda *shape: [pltpu.SemaphoreType.DMA(shape)] * 2
    hbm = pl.BlockSpec(memory_space=pl.ANY)
    piece = up.shape[1:]
    return pl.pallas_call(
        partial(entry_back_kernel, tiles=tiles, groups=groups),
        grid=(tiles + 3,),
        in_specs=[
            pl.BlockSpec((group, tile), lanes),
            pl.BlockSpec((group, tile), lanes),
            pl.BlockSpec((group, tile), lanes),
            pl.BlockSpec((depth, tile), lanes),
            pl.BlockSpec((1, tile), lanes),
            pl.BlockSpec((depth, 1), whole),
            pl.BlockSpec((depth, 1), whole),
            pl.BlockSpec((depth, 3 * group), whole),
            pl.BlockSpec((1, depth, tile), lambda step: (lax.axis_index("context"), 0, 0)),
            pl.BlockSpec((depth, tile), whole),
            pl.BlockSpec(small.shape, whole),
            hbm,
            hbm,
            pl.BlockSpec(grad_out.shape, whole),
            hbm,
            hbm,
        ],
        out_specs=[
            pl.BlockSpec((2, half, rows, tile), whole4),
            pl.BlockSpec((weight_rows, 3 * group), whole),
            pl.BlockSpec((2 * groups, 8, depth), whole3),
            pl.BlockSpec((groups, *small.shape), whole3),
            pl.BlockSpec((2, 2, *piece[1:]), whole4),
            pl.BlockSpec(grad_out.shape, whole),
            hbm,
        ],
        out_shape=[
            jax.ShapeDtypeStruct((2, half, rows, tile), bf16),
            jax.ShapeDtypeStruct((weight_rows, 3 * group), f32),
            jax.ShapeDtypeStruct((2 * groups, 8, depth), f32),
            jax.ShapeDtypeStruct((groups, *small.shape), f32),
            jax.ShapeDtypeStruct((2, 2, *piece[1:]), bf16),
            jax.ShapeDtypeStruct(grad_out.shape, f32),
            jax.ShapeDtypeStruct((2, 4 * result.shape[1], depth), bf16),
        ],
        scratch_shapes=[
            *[pltpu.VMEM(piece, bf16)] * 4,
            pltpu.VMEM((groups, 2, *piece[1:]), bf16),
            pltpu.VMEM((groups - 1, 2, *piece[1:]), bf16),
            pltpu.VMEM((2, *piece[1:]), bf16),
            pltpu.VMEM((2, *piece[1:]), bf16),
            pltpu.VMEM((7, *small.shape), f32),
            pltpu.VMEM(small.shape, f32),
            pltpu.VMEM((groups - 1, *small.shape), f32),
            pltpu.VMEM(grad_out.shape, bf16),
            pltpu.SemaphoreType.DMA((2,)),
            *dma(groups),
            *dma(groups),
            *dma(groups - 1),
            *[pltpu.SemaphoreType.DMA] * 2,
            *dma(7),
            *dma(groups - 1),
            *[pltpu.SemaphoreType.DMA] * 2,
            *dma(4),
            pltpu.SemaphoreType.DMA((4,)),
            pltpu.SemaphoreType.DMA((4,)),
            pltpu.VMEM((4, *result.shape[1:]), bf16),
            pltpu.VMEM((depth, 3 * group), f32),
            pltpu.VMEM((2, depth, WIDE), f32),
            pltpu.VMEM((tiles, 2, 2, rows, tile), bf16),
            pltpu.VMEM((tiles, 2, rows, tile), bf16),
            pltpu.VMEM((tiles, 2, rows, tile), bf16),
            pltpu.VMEM((tiles, rows, tile), bf16),
            pltpu.VMEM((half, rows, tile), bf16),
            pltpu.VMEM((half, rows, tile), bf16),
            pltpu.VMEM((groups, weight_rows, 3 * group), bf16),
            pltpu.VMEM((groups - 1, weight_rows, 3 * group), bf16),
            pltpu.VMEM((weight_rows, 3 * group), bf16),
            pltpu.VMEM((weight_rows, 3 * group), bf16),
            pltpu.VMEM((8, depth), f32),
            pltpu.VMEM((3, 8, depth), f32),
            pltpu.VMEM((8, depth), f32),
            pltpu.VMEM((2 * groups - 1, 8, depth), f32),
            *dma(tiles),
            *dma(tiles),
            *dma(half),
            *dma(groups - 1),
            *[pltpu.SemaphoreType.DMA] * 2,
            *dma(3),
            *dma(2 * groups - 1),
        ],
        compiler_params=pltpu.CompilerParams(
            vmem_limit_bytes=VMEM, collective_id=3, has_side_effects=True
        ),
        cost_estimate=cost(12 * length * depth * group, grad_query, hat_t, hat_t),
        name="entry_back",
    )(
        grad_query,
        grad_key,
        grad_value,
        hat_t,
        scaling,
        gain,
        shift,
        weight,
        grad_middle,
        middle_in,
        small,
        up,
        down,
        grad_out,
        result,
        result_in,
    )


def add(left_side, right_side):
    return (left_side.astype(f32) + right_side.astype(f32)).astype(bf16)


def by_sequence(
    tokens,
    cotangent,
    segments,
    steps,
    table,
    ada_w,
    ada_b,
    gain_one,
    w_qkv,
    w_out,
    gain_two,
    w_up,
    b_up,
    w_down,
    b_down,
):
    fsdp, tensor = lax.axis_size("fsdp"), lax.axis_size("tensor")
    context = lax.axis_size("context")
    tensor_rank = lax.axis_index("tensor")
    context_rank = lax.axis_index("context")
    fsdp_rank = lax.axis_index("fsdp")
    sequences, own_rows, depth = tokens.shape
    length = segments.shape[1]
    group = w_out.shape[0]
    part_width = w_up.shape[1]
    heads = group // HDIM
    quarter = own_rows // tensor

    partner = [(k, (k + 1) % context) for k in range(context)]

    by_kind = w_qkv.reshape(-1, heads, 3, HDIM).transpose(0, 2, 1, 3).reshape(-1, 3 * group)
    both = ("tensor", "fsdp")
    out_blocks = lax.all_gather(w_out, both, axis=0, tiled=False)

    numbers = jnp.arange(table.shape[0], dtype=jnp.int32)
    ada_full = ada_w.astype(f32)
    raw = exact_product((steps[:, None] == numbers[None, :]).astype(f32), table.astype(f32))
    local_mods = exact_product(jax.nn.silu(raw), ada_full) + ada_b.astype(f32)
    local_mods = local_mods.reshape(sequences, 6, depth)
    gain_first, gain_second = gain_one.astype(f32), gain_two.astype(f32)
    own_mods = lax.dynamic_index_in_dim(local_mods, context_rank, 0, keepdims=False)
    gain_column = (gain_first * (1.0 + own_mods[1]))[:, None]
    shift_column = own_mods[0][:, None]
    mods = jnp.stack(
        [
            local_mods[:, 2],
            local_mods[:, 3],
            gain_second * (1.0 + local_mods[:, 4]),
            local_mods[:, 5],
        ]
        + [jnp.zeros((sequences, depth), f32)] * 4,
        axis=1,
    )

    segment = lax.dynamic_index_in_dim(segments, context_rank, 0, keepdims=False)
    same, starts, ends = document_bounds(segment)
    offsets = jnp.arange(length, dtype=jnp.int32) - jnp.sum(jnp.where(same, starts[:, None], 0), axis=0)
    angles = frequencies()[:, None] * offsets.astype(f32)[None, :]
    cosine, sine = jnp.cos(angles), jnp.sin(angles)
    tile = length // (context * tensor)
    block = tile
    first_key = jnp.sum(jnp.where(same, starts[:, None], 0), axis=0)[::tile]
    last_key = jnp.sum(jnp.where(same, ends[:, None], 0), axis=0)[tile - 1 :: tile]

    low_key = first_key // WIDE * WIDE
    high_key = (last_key + WIDE - 1) // WIDE * WIDE

    def ranges_of(size):
        count = (high_key - low_key + size - 1) // size
        return jnp.stack([jnp.maximum(high_key - count * size, 0), count]).astype(jnp.int32)

    back_block = block // 2
    ranges, back_ranges = ranges_of(block), ranges_of(back_block)

    queries, keys, keys_t, values_t, hat_t, scaling, norms, qkv, forward = entry_call(
        tokens,
        by_kind,
        jnp.where(context_rank == 0, w_up, w_down.T),
        gain_column,
        shift_column,
        cosine,
        sine,
        segment[None, :],
        groups=fsdp,
        tile=tile,
    )
    across = [(k, (k + 2) % tensor) for k in range(tensor)]
    across_weight = lax.ppermute(forward, "tensor", across)
    other_weight = lax.ppermute(forward, "context", partner)
    mixture, told = attend_call(ranges, queries, keys, values_t, norms, tile, block)

    own_segments = lax.dynamic_slice_in_dim(
        segments, context_rank * own_rows + tensor_rank * quarter, quarter, axis=1
    )
    (
        result,
        grad_mixture,
        grad_middle,
        grad_out,
        sums,
        bias_sums,
        up_keep,
        up_send,
        down_keep,
        down_send,
    ) = middle_call(
        mixture,
        tokens,
        cotangent,
        (own_segments != 0).astype(f32).reshape(-1, 1),
        mods,
        b_up.astype(f32).reshape(tensor, 1, part_width),
        b_down.astype(f32)[None, :],
        out_blocks,
        forward,
        other_weight,
        across_weight,
        fsdp,
        tile=min(tile, 256),
    )
    result = result.reshape(sequences, quarter, depth)
    result_in = lax.ppermute(result, "tensor", across)
    middle_in = lax.ppermute(
        lax.dynamic_index_in_dim(grad_middle, 1 - context_rank, 0, keepdims=False), "context", partner
    )
    small = jnp.concatenate(
        [
            sums[:, :5].reshape(-1, depth),
            bias_sums.reshape(-1, depth),
        ]
    )
    small_rows = small.shape[0]
    cond = raw.shape[1]
    leads = (context_rank == 0) & (tensor_rank == 0)
    embedded = jnp.concatenate([raw, steps.astype(f32)[:, None]], axis=1)
    embedded = jnp.pad(jnp.where(leads, embedded, 0.0), ((0, 0), (0, depth - cond - 1)))
    small = jnp.concatenate([small, embedded])
    small = jnp.pad(small, ((0, -small.shape[0] % 8), (0, 0)))

    up_sum = add(up_keep, lax.ppermute(up_send, "tensor", across))
    down_sum = add(down_keep, lax.ppermute(down_send, "context", partner))
    grad_out = lax.psum_scatter(grad_out, both, scatter_dimension=0, tiled=True)[0]

    grad_query, grad_key, grad_value = attend_back_call(
        back_ranges, told, keys_t, values_t, mixture, grad_mixture, cosine, sine, tile, back_block
    )
    (grad_query, up_sum, down_sum, result_in, middle_in, grad_out) = lax.optimization_barrier(
        (grad_query, up_sum, down_sum, result_in, middle_in, grad_out)
    )
    part, grad_qkv, entry_sums, small, pieces, grad_out, block_out = entry_back_call(
        grad_query,
        grad_key,
        grad_value,
        hat_t,
        scaling,
        gain_column,
        shift_column,
        qkv,
        grad_middle,
        middle_in,
        small,
        up_sum,
        down_sum,
        grad_out,
        result,
        result_in,
        groups=fsdp,
        tile=tile,
    )
    pieces = pieces.transpose(1, 0, 2, 3)
    pieces = pieces.reshape(2, depth // fsdp, part_width).astype(f32)
    grad_w_up = pieces[0]
    grad_w_down = pieces[1].T
    grad_w_out = grad_out
    small_sums = small[:, : 5 * sequences].reshape(fsdp * sequences, 5, depth)
    embedded = small[:, small_rows : small_rows + sequences].reshape(fsdp * sequences, depth)
    choose = (embedded[:, cond].astype(jnp.int32)[:, None] == numbers[None, :]).astype(f32)
    embedding, silu_back = jax.vjp(jax.nn.silu, embedded[:, :cond])
    modulation = exact_product(embedding, ada_full) + ada_b.astype(f32)
    grad_b_up = jnp.sum(small[:, 5 * sequences : small_rows], axis=0).reshape(-1)
    grad_b_down = jnp.sum(small_sums[:, 4], axis=0)
    grad_gain_two = jnp.sum(small_sums[:, 2] * (1.0 + modulation[:, 4 * depth : 5 * depth]), axis=0)
    middle_mod = jnp.concatenate(
        [small_sums[:, 0], small_sums[:, 1], small_sums[:, 2] * gain_second, small_sums[:, 3]], axis=1
    )
    part = part.transpose(0, 1, 3, 2).reshape(sequences, own_rows, depth // tensor)
    grad_tokens = part.astype(f32)
    grad_w_qkv = (
        grad_qkv.reshape(-1, 3, heads, HDIM).transpose(0, 2, 1, 3).reshape(-1, 3 * group)
    )
    grad_mod = jnp.concatenate(
        [entry_sums[:, 0], entry_sums[:, 1] * gain_first, middle_mod], axis=1
    )
    grad_gain_one = jnp.sum(entry_sums[:, 1] * (1.0 + modulation[:, depth : 2 * depth]), axis=0)
    grad_ada_b = jnp.sum(grad_mod, axis=0)
    grad_ada_w = exact_transposed(embedding, grad_mod)
    grad_before = silu_back(exact_against(grad_mod, ada_full))[0]
    grad_table = exact_transposed(choose, grad_before)
    return (
        block_out,
        grad_tokens,
        grad_table,
        grad_ada_w,
        grad_ada_b,
        grad_gain_one,
        grad_w_qkv,
        grad_w_out,
        grad_gain_two,
        grad_w_up,
        grad_b_up,
        grad_w_down,
        grad_b_down,
    )


def normalize(operand):
    center = operand - jnp.mean(operand, axis=-1, keepdims=True)
    scaling = lax.rsqrt(jnp.mean(center * center, axis=-1, keepdims=True) + 1e-05)
    return (center * scaling, scaling)


def norm_back(grad_hat, hatted, scaling):
    return scaling * (
        grad_hat
        - jnp.mean(grad_hat, axis=-1, keepdims=True)
        - hatted * jnp.mean(grad_hat * hatted, axis=-1, keepdims=True)
    )


def angles_of(offsets, half_width):
    frequency = 10000.0 ** (-jnp.arange(half_width, dtype=jnp.float32) / half_width)
    angles = offsets.astype(jnp.float32)[:, None] * frequency[None, :]
    return (jnp.cos(angles)[:, None, :], jnp.sin(angles)[:, None, :])


def rotate(operand, cosine, sine_part, direction):
    half_width = operand.shape[-1] // 2
    front_half = operand[..., :half_width]
    second = operand[..., half_width:]
    return jnp.concatenate(
        [
            front_half * cosine - direction * second * sine_part,
            direction * front_half * sine_part + second * cosine,
        ],
        axis=-1,
    )


def scores_of(queries, key_rows, allowed):
    raw_scores = (
        jnp.einsum("qhd,khd->hqk", queries, key_rows, preferred_element_type=jnp.float32) * 0.125
    )
    return jnp.where(allowed[None], raw_scores, -1e30)


def attend(queries, key_rows, values, allowed):
    scores = scores_of(queries, key_rows, allowed)
    row_max = jnp.max(scores, axis=-1, keepdims=True)
    weights_raw = jnp.exp(scores - row_max)
    row_total = jnp.sum(weights_raw, axis=-1, keepdims=True)
    weights_low = (weights_raw / row_total).astype(jnp.bfloat16)
    mixture = jnp.einsum("hqk,khd->qhd", weights_low, values, preferred_element_type=jnp.float32)
    return (mixture, row_max + jnp.log(row_total))


def attend_back(queries, key_rows, values, grad_mixture, logsum, allowed, row_delta):
    scores = scores_of(queries, key_rows, allowed)
    chances = jnp.exp(scores - logsum)
    grad_chances = jnp.einsum(
        "qhd,khd->hqk", grad_mixture, values, preferred_element_type=jnp.float32
    )
    row_delta = jnp.sum(chances * grad_chances, axis=-1, keepdims=True)
    grad_scores = (chances * (grad_chances - row_delta)).astype(jnp.bfloat16)
    return (chances.astype(jnp.bfloat16), grad_scores, row_delta)


def by_block(
    tokens,
    cotangent,
    segments,
    steps,
    table,
    ada_w,
    ada_b,
    gain_one,
    w_qkv,
    w_out,
    gain_two,
    w_up,
    b_up,
    w_down,
    b_down,
):
    w_qkv, w_up, w_out, w_down = (
        lax.all_gather(w_qkv, "fsdp", axis=0, tiled=True),
        lax.all_gather(w_up, "fsdp", axis=0, tiled=True),
        lax.all_gather(w_out, "fsdp", axis=1, tiled=True),
        lax.all_gather(w_down, "fsdp", axis=1, tiled=True),
    )
    tensor_rank = lax.axis_index("tensor")
    context_rank = lax.axis_index("context")
    sequences, own_rows, model_width = tokens.shape
    length = segments.shape[1]
    local_heads = w_out.shape[0] // HDIM
    hidden_width = w_up.shape[1]
    up_bias = lax.dynamic_slice_in_dim(b_up, tensor_rank * hidden_width, hidden_width).astype(
        jnp.float32
    )
    down_bias = b_down.astype(jnp.float32)
    gain_first = gain_one.astype(jnp.float32)
    gain_second = gain_two.astype(jnp.float32)
    leader = (tensor_rank == 0).astype(jnp.float32)
    ada_full = ada_w.astype(jnp.float32)
    choose = (steps[:, None] == jnp.arange(table.shape[0], dtype=jnp.int32)[None, :]).astype(
        jnp.float32
    )
    before = exact_product(choose, table.astype(jnp.float32))
    embedding, silu_back = jax.vjp(jax.nn.silu, before)
    modulation = exact_product(embedding, ada_full) + ada_b.astype(jnp.float32)
    grad_qkv = jnp.zeros(w_qkv.shape, jnp.float32)
    grad_out_w = jnp.zeros(w_out.shape, jnp.float32)
    grad_up = jnp.zeros(w_up.shape, jnp.float32)
    grad_down = jnp.zeros(w_down.shape, jnp.float32)
    grad_bias_up = jnp.zeros((hidden_width,), jnp.float32)
    grad_bias_down = jnp.zeros((model_width,), jnp.float32)
    grad_gain_first = jnp.zeros((model_width,), jnp.float32)
    grad_gain_second = jnp.zeros((model_width,), jnp.float32)
    results = []
    partial_inputs = []
    carried = []
    grad_mods = []
    for number in range(sequences):
        shift_one, scale_one, gate_one, shift_two, scale_two, gate_two = jnp.split(
            modulation[number], 6
        )
        segment = segments[number]
        offsets = positions(segment)
        own_segment = lax.dynamic_slice_in_dim(segment, context_rank * own_rows, own_rows)
        own_offsets = lax.dynamic_slice_in_dim(offsets, context_rank * own_rows, own_rows)
        cosine, sine_part = angles_of(own_offsets, HDIM // 2)
        allowed = own_segment[:, None] == segment[None, :]
        inputs_row = tokens[number].astype(jnp.float32)
        hat_one, scaling_one = normalize(inputs_row)
        lifted_one = hat_one * gain_first
        entry_one = (lifted_one * (1.0 + scale_one) + shift_one).astype(jnp.bfloat16)
        projected = product(entry_one, w_qkv).reshape(own_rows, local_heads, 3, HDIM)
        queries = rotate(projected[:, :, 0], cosine, sine_part, 1.0).astype(jnp.bfloat16)
        key_rows = rotate(projected[:, :, 1], cosine, sine_part, 1.0).astype(jnp.bfloat16)
        values = projected[:, :, 2].astype(jnp.bfloat16)
        key_value = jnp.stack([key_rows, values], axis=1).reshape(own_rows, 2 * local_heads * HDIM)
        gathered = lax.all_gather(key_value, "context", axis=0, tiled=True).reshape(
            length, 2, local_heads, HDIM
        )
        all_keys = gathered[:, 0]
        all_values = gathered[:, 1]
        mixture, logsum = attend(queries, all_keys, all_values, allowed)
        mixture_low = mixture.reshape(own_rows, local_heads * HDIM).astype(jnp.bfloat16)
        attended = lax.psum(product(mixture_low, w_out).astype(jnp.bfloat16), "tensor").astype(
            jnp.float32
        )
        middle = inputs_row + gate_one * attended
        hat_two, scaling_two = normalize(middle)
        lifted_two = hat_two * gain_second
        entry_two = (lifted_two * (1.0 + scale_two) + shift_two).astype(jnp.bfloat16)
        hidden = product(entry_two, w_up) + up_bias
        activated, gelu_back = jax.vjp(partial(jax.nn.gelu, approximate=True), hidden)
        activated_low = activated.astype(jnp.bfloat16)
        output = (
            lax.psum(product(activated_low, w_down).astype(jnp.bfloat16), "tensor").astype(
                jnp.float32
            )
            + down_bias
        )
        results.append((middle + gate_two * output).astype(jnp.bfloat16))
        valid = (own_segment != 0).astype(jnp.float32)[:, None]
        grad_result = cotangent[number].astype(jnp.float32) * valid
        grad_output = (gate_two * grad_result).astype(jnp.bfloat16)
        grad_gate_two = jnp.sum(grad_result * output, axis=0)
        grad_bias_down = grad_bias_down + jnp.sum(grad_output.astype(jnp.float32), axis=0)
        grad_down = grad_down + transposed(activated_low, grad_output)
        grad_active = against(grad_output, w_down)
        grad_hidden = gelu_back(grad_active)[0].astype(jnp.bfloat16)
        grad_bias_up = grad_bias_up + jnp.sum(grad_hidden.astype(jnp.float32), axis=0)
        grad_up = grad_up + transposed(entry_two, grad_hidden)
        grad_entry_two = against(grad_hidden, w_up)
        grad_shift_two = jnp.sum(grad_entry_two, axis=0)
        grad_scale_two = jnp.sum(grad_entry_two * lifted_two, axis=0)
        grad_lifted_two = grad_entry_two * (1.0 + scale_two)
        grad_gain_second = grad_gain_second + jnp.sum(grad_lifted_two * hat_two, axis=0)
        part_two = norm_back(grad_lifted_two * gain_second, hat_two, scaling_two)
        grad_middle = grad_result + lax.psum(part_two.astype(jnp.bfloat16), "tensor").astype(
            jnp.float32
        )
        grad_attended = (gate_one * grad_middle).astype(jnp.bfloat16)
        grad_gate_one = jnp.sum(grad_middle * attended, axis=0)
        grad_out_w = grad_out_w + transposed(mixture_low, grad_attended)
        grad_mixture = (
            against(grad_attended, w_out).astype(jnp.bfloat16).reshape(own_rows, local_heads, HDIM)
        )
        chances_low, grad_scores, row_delta = attend_back(
            queries, all_keys, all_values, grad_mixture, logsum, allowed, None
        )
        grad_queries = (
            jnp.einsum("hqk,khd->qhd", grad_scores, all_keys, preferred_element_type=jnp.float32)
            * 0.125
        )
        grad_all_keys = (
            jnp.einsum("hqk,qhd->khd", grad_scores, queries, preferred_element_type=jnp.float32)
            * 0.125
        )
        grad_all_values = jnp.einsum(
            "hqk,qhd->khd", chances_low, grad_mixture, preferred_element_type=jnp.float32
        )
        both_grads = jnp.stack([grad_all_keys, grad_all_values], axis=1).reshape(
            length, 2 * local_heads * HDIM
        )
        own_grads = (
            lax.psum_scatter(
                both_grads.astype(jnp.bfloat16), "context", scatter_dimension=0, tiled=True
            )
            .astype(jnp.float32)
            .reshape(own_rows, 2, local_heads, HDIM)
        )
        grad_keys = own_grads[:, 0]
        grad_values = own_grads[:, 1]
        grad_queries = rotate(grad_queries, cosine, sine_part, -1.0)
        grad_keys = rotate(grad_keys, cosine, sine_part, -1.0)
        grad_projected = (
            jnp.stack([grad_queries, grad_keys, grad_values], axis=2)
            .reshape(own_rows, local_heads * 3 * HDIM)
            .astype(jnp.bfloat16)
        )
        grad_qkv = grad_qkv + transposed(entry_one, grad_projected)
        grad_entry_one = against(grad_projected, w_qkv)
        grad_shift_one = jnp.sum(grad_entry_one, axis=0)
        grad_scale_one = jnp.sum(grad_entry_one * lifted_one, axis=0)
        grad_lifted_one = grad_entry_one * (1.0 + scale_one)
        grad_gain_first = grad_gain_first + jnp.sum(grad_lifted_one * hat_one, axis=0)
        partial_inputs.append(norm_back(grad_lifted_one * gain_first, hat_one, scaling_one))
        carried.append(grad_middle)
        grad_mods.append(
            jnp.concatenate(
                [
                    grad_shift_one,
                    grad_scale_one,
                    grad_gate_one * leader,
                    grad_shift_two,
                    grad_scale_two,
                    grad_gate_two * leader,
                ]
            )
        )
    summed_inputs = lax.psum_scatter(
        jnp.stack(partial_inputs).astype(jnp.bfloat16), "tensor", scatter_dimension=2, tiled=True
    ).astype(jnp.float32)
    slice_width = model_width // lax.axis_size("tensor")
    own_middle = lax.dynamic_slice_in_dim(
        jnp.stack(carried), tensor_rank * slice_width, slice_width, axis=2
    )
    grad_tokens = summed_inputs + own_middle
    grad_mod = jnp.stack(grad_mods)
    bias_up_full = lax.dynamic_update_slice_in_dim(
        jnp.zeros((b_up.shape[0],), jnp.float32), grad_bias_up, tensor_rank * hidden_width, 0
    )
    grad_qkv, grad_up, grad_out_w, grad_down = (
        lax.psum_scatter(
            grad_qkv.astype(jnp.bfloat16), "fsdp", scatter_dimension=0, tiled=True
        ).astype(jnp.float32),
        lax.psum_scatter(
            grad_up.astype(jnp.bfloat16), "fsdp", scatter_dimension=0, tiled=True
        ).astype(jnp.float32),
        lax.psum_scatter(
            grad_out_w.astype(jnp.bfloat16), "fsdp", scatter_dimension=1, tiled=True
        ).astype(jnp.float32),
        lax.psum_scatter(
            grad_down.astype(jnp.bfloat16), "fsdp", scatter_dimension=1, tiled=True
        ).astype(jnp.float32),
    )
    grad_qkv, grad_up, grad_out_w, grad_down = (
        lax.psum(grad_qkv.astype(jnp.bfloat16), "context").astype(jnp.float32),
        lax.psum(grad_up.astype(jnp.bfloat16), "context").astype(jnp.float32),
        lax.psum(grad_out_w.astype(jnp.bfloat16), "context").astype(jnp.float32),
        lax.psum(grad_down.astype(jnp.bfloat16), "context").astype(jnp.float32),
    )
    grad_ada_b = jnp.sum(grad_mod, axis=0)
    grad_ada_w = exact_transposed(embedding, grad_mod)
    grad_embedding = exact_against(grad_mod, ada_full)
    grad_before = silu_back(grad_embedding)[0]
    grad_table = exact_transposed(choose, grad_before)
    (
        grad_table,
        grad_ada_w,
        grad_ada_b,
        grad_gain_first,
        grad_gain_second,
        bias_up_full,
        grad_bias_down,
    ) = lax.psum(
        (
            grad_table,
            grad_ada_w,
            grad_ada_b,
            grad_gain_first,
            grad_gain_second,
            bias_up_full,
            grad_bias_down * leader,
        ),
        ("fsdp", "context", "tensor"),
    )
    return (
        jnp.stack(results),
        grad_tokens,
        grad_table,
        grad_ada_w,
        grad_ada_b,
        grad_gain_first,
        grad_qkv,
        grad_out_w,
        grad_gain_second,
        grad_up,
        bias_up_full,
        grad_down,
        grad_bias_down,
    )


def solution(mesh):
    axes = dict(zip(mesh.axis_names, mesh.devices.shape))

    def whole(tokens, *others):
        sequences = tokens.shape[0] // axes["fsdp"]
        local = by_sequence if sequences == axes["context"] == 2 and axes["tensor"] == 4 else by_block
        return mapped(local, mesh)(tokens, *others)

    return whole


def mapped(local, mesh):
    return jax.shard_map(
        local,
        mesh=mesh,
        in_specs=(
            P("fsdp", "context", None),
            P("fsdp", "context", None),
            P("fsdp", None),
            P("fsdp"),
            P(),
            P(),
            P(),
            P(),
            P("fsdp", "tensor"),
            P("tensor", "fsdp"),
            P(),
            P("fsdp", "tensor"),
            P(),
            P("tensor", "fsdp"),
            P(),
        ),
        out_specs=(
            P("fsdp", "context", None),
            P("fsdp", "context", "tensor"),
            P(),
            P(),
            P(),
            P(),
            P("fsdp", "tensor"),
            P("tensor", "fsdp"),
            P(),
            P("fsdp", "tensor"),
            P(),
            P("tensor", "fsdp"),
            P(),
        ),
        check_vma=False,
    )
```

```python
import math
from functools import partial

import jax
import jax.numpy as jnp
from jax import lax
from jax.experimental import pallas as pl
from jax.experimental.pallas import tpu as pltpu
from jax.sharding import PartitionSpec as P

HDIM = 64
HALF = HDIM // 2
SEGMENTS = 5
WIDE = 128
MASKED = 2.0**100
LOG2E = math.log2(math.e)
SAFE_EXPONENT = 60.0
EPSILON = 1e-05
VMEM = 56 * 2**20
PART_TILES = 2
PART_CUTS = 1
VMEM_MOST = 60 * 2**20


def cost(flops, *arrays):
    size = sum(math.prod(one.shape) * one.dtype.itemsize for one in arrays)
    return pl.CostEstimate(flops=int(flops), bytes_accessed=int(size), transcendentals=0)


precise = lax.Precision.HIGHEST
f32 = jnp.float32
bf16 = jnp.bfloat16


def product(left_side, right_side):
    return jnp.dot(left_side, right_side, preferred_element_type=jnp.float32)


def transposed(left_side, right_side):
    return lax.dot_general(
        left_side, right_side, (((0,), (0,)), ((), ())), preferred_element_type=jnp.float32
    )


def against(left_side, right_side):
    return lax.dot_general(
        left_side, right_side, (((1,), (1,)), ((), ())), preferred_element_type=jnp.float32
    )


def exact_product(left_side, right_side):
    return jnp.dot(left_side, right_side, precision=precise, preferred_element_type=jnp.float32)


def exact_transposed(left_side, right_side):
    return lax.dot_general(
        left_side,
        right_side,
        (((0,), (0,)), ((), ())),
        precision=precise,
        preferred_element_type=jnp.float32,
    )


def exact_against(left_side, right_side):
    return lax.dot_general(
        left_side,
        right_side,
        (((1,), (1,)), ((), ())),
        precision=precise,
        preferred_element_type=jnp.float32,
    )


def document_bounds(segment):
    indices = jnp.arange(segment.shape[-1], dtype=jnp.int32)
    same = segment[..., None, :] == jnp.arange(SEGMENTS, dtype=jnp.int32)[:, None]
    starts = jnp.min(jnp.where(same, indices, segment.shape[-1]), axis=-1)
    ends = jnp.max(jnp.where(same, indices + 1, 0), axis=-1)
    return same, starts, ends


def positions(segment):
    same, starts, _ = document_bounds(segment)
    first = jnp.sum(jnp.where(same, starts[..., :, None], 0), axis=-2)
    return jnp.arange(segment.shape[-1], dtype=jnp.int32) - first


def frequencies():
    return 10000.0 ** (-jnp.arange(HALF, dtype=jnp.float32) / HALF)


def copy_to(source, target, sent, arrived, **device):
    return pltpu.make_async_remote_copy(
        src_ref=source,
        dst_ref=target,
        send_sem=sent,
        recv_sem=arrived,
        device_id=device,
        device_id_type=pl.DeviceIdType.MESH,
    )


def greet(devices):
    barrier = pltpu.get_barrier_semaphore()
    for device in devices:
        pl.semaphore_signal(barrier, inc=1, device_id=device, device_id_type=pl.DeviceIdType.MESH)
    pl.semaphore_wait(barrier, len(devices))


def quarter_at(number, tensor):
    core = lax.rem(tensor, 2)
    chip = jnp.where(number < 2, tensor // 2, 1 - tensor // 2)
    return chip * 2 + jnp.where(lax.rem(number, 2) == 0, core, 1 - core)


def entry_kernel(
    tokens_ref,
    rows_ref,
    shard_ref,
    own_forward_ref,
    gain_ref,
    shift_ref,
    cosine_ref,
    sine_ref,
    segment_ref,
    query_ref,
    key_ref,
    key_t_ref,
    value_t_ref,
    hat_ref,
    scale_ref,
    norm_ref,
    weight_ref,
    forward_ref,
    shards,
    weight_t,
    rows,
    arrived,
    sent_shard,
    got_shard,
    own_shard,
    sent_block,
    got_block,
    sent_across,
    got_across,
    sent_sibling,
    got_sibling,
    sent_on,
    got_on,
    sent_forward,
    got_forward,
    own_forward,
    *,
    heads,
    groups,
):
    step = pl.program_id(0)
    fsdp, context, tensor = (lax.axis_index(name) for name in ("fsdp", "context", "tensor"))
    ranks = 4
    core = lax.rem(tensor, 2)
    sibling = tensor + 1 - 2 * core
    across = lax.rem(tensor + 2, ranks)
    quarter = rows.shape[0]
    chunks = sent_block.shape[0]
    height = quarter // chunks

    def shard_copy(away):
        return copy_to(
            shard_ref,
            shards.at[fsdp],
            sent_shard.at[away - 1],
            got_shard.at[away - 1],
            fsdp=lax.rem(fsdp + away, groups),
        )

    def shard_own():
        return pltpu.make_async_copy(shard_ref, shards.at[fsdp], own_shard)

    def chunk(rank, number):
        return arrived.at[rank, pl.ds(number * height, height), :]

    def block_copy(number):
        at = pl.multiple_of(tensor * quarter, quarter) + number * height
        return copy_to(
            tokens_ref.at[1 - context, pl.ds(at, height), :],
            chunk(tensor, number),
            sent_block.at[number],
            got_block.at[number],
            context=1 - context,
        )

    def across_copy(number):
        return copy_to(
            chunk(tensor, number),
            chunk(tensor, number),
            sent_across.at[number],
            got_across.at[number],
            tensor=across,
        )

    def sibling_copy(number):
        return copy_to(
            chunk(tensor, number),
            chunk(tensor, number),
            sent_sibling.at[number],
            got_sibling.at[number],
            tensor=sibling,
        )

    def on_copy(number):
        return copy_to(
            chunk(across, number),
            chunk(across, number),
            sent_on.at[number],
            got_on.at[number],
            tensor=sibling,
        )

    forward_rows = own_forward_ref.shape[0]

    def forward_place(rank):
        return forward_ref.at[pl.ds(pl.multiple_of(rank * forward_rows, forward_rows), forward_rows), :]

    def relay_copy(origin, upward):
        place = forward_place(origin)
        side = 0 if upward else 1
        return copy_to(
            place,
            place,
            sent_forward.at[side, origin],
            got_forward.at[origin],
            fsdp=fsdp + 1 if upward else fsdp - 1,
        )

    def forward_own():
        return pltpu.make_async_copy(own_forward_ref, forward_place(fsdp), own_forward)

    def relay(origin, upward):
        @pl.when(fsdp < groups - 1 if upward else fsdp > 0)
        def _():
            relay_copy(origin, upward).start()

    def from_below(distance, act):
        @pl.when(fsdp >= distance)
        def _():
            act(fsdp - distance, True)

    def from_above(distance, act):
        @pl.when(fsdp + distance < groups)
        def _():
            act(fsdp + distance, False)

    def hand_over(distance):
        def act(origin, upward):
            relay_copy(origin, upward).wait_recv()
            relay(origin, upward)

        from_below(distance, act)
        from_above(distance, act)

    def finish_forward():
        def sent(origin, upward):
            @pl.when(fsdp < groups - 1 if upward else fsdp > 0)
            def _():
                relay_copy(origin, upward).wait_send()

        sent(fsdp, True)
        sent(fsdp, False)
        for distance in range(1, groups):
            from_below(distance, sent)
            from_above(distance, sent)

    def take(numbers):
        for number in numbers:
            block_copy(number).wait_recv()
            across_copy(number).start()
            sibling_copy(number).start()

    def pass_on(numbers):
        for number in numbers:
            across_copy(number).wait_recv()
            on_copy(number).start()

    @pl.when(step == 0)
    def _():
        shard_own().start()
        greet(
            [{"fsdp": lax.rem(fsdp + away, groups)} for away in range(1, groups)]
            + [{"context": 1 - context}, {"tensor": sibling}, {"tensor": across}]
        )
        for away in range(1, groups):
            shard_copy(away).start()
        for number in range(chunks):
            block_copy(number).start()
        forward_own().start()
        take(range(chunks - 1))
        shard_own().wait()
        for away in range(1, groups):
            shard_copy(away).wait_recv()
        for number in range(groups):
            weight_ref[number * shards.shape[1] : (number + 1) * shards.shape[1], :] = shards[number]
        forward_own().wait()
        relay(fsdp, True)
        relay(fsdp, False)
        weight_t[...] = weight_ref[...].T

    @pl.when(step == 1)
    def _():
        take([chunks - 1])
        pass_on(range(chunks // 2))

    @pl.when(step == 2)
    def _():
        pass_on(range(chunks // 2, chunks))

    half = 4

    for distance in range(1, groups):

        @pl.when(step == 1 + 2 * distance)
        def _():
            hand_over(distance)

    @pl.when(step < half)
    def _():
        rows[...] = rows_ref[0]

    @pl.when(step == half + 1)
    def _():
        for number in range(chunks):
            sibling_copy(number).wait_recv()

    @pl.when(step == half + 3)
    def _():
        for number in range(chunks):
            on_copy(number).wait_recv()

    @pl.when(step >= half)
    def _():
        rows[...] = arrived[quarter_at(step - half, tensor)]

    inputs = rows[...].astype(f32).T
    center = inputs - jnp.mean(inputs, axis=0, keepdims=True)
    scaling = lax.rsqrt(jnp.mean(center * center, axis=0, keepdims=True) + EPSILON)
    hat = center * scaling
    hat_ref[...] = hat.astype(bf16)
    scale_ref[...] = scaling
    entry = (hat * gain_ref[...] + shift_ref[...]).astype(bf16)
    projected = product(weight_t[...], entry)
    cosine = cosine_ref[...]
    sine = sine_ref[...]
    tokens = cosine.shape[1]
    group = heads * HDIM
    segment = segment_ref[...]
    number = lax.broadcasted_iota(jnp.int32, (WIDE - HDIM, tokens), 0)
    same = (number == segment).astype(f32)
    extra_query = same
    extra_key = jnp.where(
        number < SEGMENTS, (same - 1.0) * MASKED, jnp.where(number < SEGMENTS + 3, 1.0, 0.0)
    )
    extra_value = jnp.where(number < 3, 1.0, 0.0)
    norms = []
    for head in range(heads):

        def turned(kind, factor):
            at = kind * group + head * HDIM
            front = projected[at : at + HALF]
            back = projected[at + HALF : at + HDIM]
            return jnp.concatenate(
                [(front * cosine - back * sine) * factor, (front * sine + back * cosine) * factor],
                axis=0,
            )

        queries = turned(0, 0.125 * LOG2E)
        keys = turned(1, 1.0)
        values = projected[2 * group + head * HDIM : 2 * group + (head + 1) * HDIM]
        norms.append(jnp.sum(queries * queries, axis=0, keepdims=True))
        norms.append(jnp.sum(keys * keys, axis=0, keepdims=True))
        query_ref[head] = jnp.concatenate([queries, extra_query], axis=0).astype(bf16)
        wide_keys = jnp.concatenate([keys, extra_key], axis=0)
        key_ref[head] = wide_keys.T.astype(bf16)
        key_t_ref[head] = wide_keys.astype(bf16)
        value_t_ref[head] = jnp.concatenate([values, extra_value], axis=0).astype(bf16)
    norms += [jnp.zeros_like(norms[0])] * (norm_ref.shape[0] - len(norms))
    norm_ref[...] = jnp.concatenate(norms, axis=0)

    @pl.when(step == pl.num_programs(0) - 1)
    def _():
        for away in range(1, groups):
            shard_copy(away).wait_send()
        for number in range(chunks):
            block_copy(number).wait_send()
            across_copy(number).wait_send()
            sibling_copy(number).wait_send()
            on_copy(number).wait_send()
        finish_forward()


def entry_call(tokens, shard, forward_shard, gain, shift, cosine, sine, segment, groups, tile):
    length = cosine.shape[1]
    shard_rows, width = shard.shape
    depth = shard_rows * groups
    heads = width // (3 * HDIM)
    half = tokens.shape[1] // tile
    chunks = 4

    def place(i):
        context = lax.axis_index("context")
        other = (1 - context) * half + quarter_at(jnp.maximum(i - half, 0), lax.axis_index("tensor"))
        return jnp.where(i < half, context * half + i, other)

    lanes = lambda i: (0, place(i))
    heads_lanes = lambda i: (0, 0, place(i))
    heads_rows = lambda i: (0, place(i), 0)
    whole = lambda i: (0, 0)
    shapes = [
        jax.ShapeDtypeStruct((heads, WIDE, length), bf16),
        jax.ShapeDtypeStruct((heads, length, WIDE), bf16),
        jax.ShapeDtypeStruct((heads, WIDE, length), bf16),
        jax.ShapeDtypeStruct((heads, WIDE, length), bf16),
        jax.ShapeDtypeStruct((depth, length), bf16),
        jax.ShapeDtypeStruct((1, length), f32),
        jax.ShapeDtypeStruct((8, length), f32),
        jax.ShapeDtypeStruct((depth, width), bf16),
        jax.ShapeDtypeStruct((depth, forward_shard.shape[1]), bf16),
    ]
    dma = lambda *shape: [pltpu.SemaphoreType.DMA(shape)] * 2
    return pl.pallas_call(
        partial(entry_kernel, heads=heads, groups=groups),
        grid=(2 * half,),
        in_specs=[
            pl.BlockSpec(memory_space=pl.ANY),
            pl.BlockSpec(
                (1, tile, depth),
                lambda i: (lax.axis_index("context"), jnp.minimum(i, half - 1), 0),
            ),
            pl.BlockSpec(memory_space=pl.ANY),
            pl.BlockSpec(forward_shard.shape, whole),
            pl.BlockSpec((depth, 1), whole),
            pl.BlockSpec((depth, 1), whole),
            pl.BlockSpec((HALF, tile), lanes),
            pl.BlockSpec((HALF, tile), lanes),
            pl.BlockSpec((1, tile), lanes),
        ],
        out_specs=[
            pl.BlockSpec((heads, WIDE, tile), heads_lanes),
            pl.BlockSpec((heads, tile, WIDE), heads_rows),
            pl.BlockSpec((heads, WIDE, tile), heads_lanes),
            pl.BlockSpec((heads, WIDE, tile), heads_lanes),
            pl.BlockSpec((depth, tile), lanes),
            pl.BlockSpec((1, tile), lanes),
            pl.BlockSpec((8, tile), lanes),
            pl.BlockSpec((depth, width), whole),
            pl.BlockSpec(memory_space=pl.ANY),
        ],
        out_shape=shapes,
        scratch_shapes=[
            pltpu.VMEM((groups, shard_rows, width), bf16),
            pltpu.VMEM((width, depth), bf16),
            pltpu.VMEM((tile, depth), bf16),
            pltpu.VMEM((4, tile, depth), bf16),
            *dma(groups - 1),
            pltpu.SemaphoreType.DMA,
            *dma(chunks),
            *dma(chunks),
            *dma(chunks),
            *dma(chunks),
            pltpu.SemaphoreType.DMA((2, groups)),
            pltpu.SemaphoreType.DMA((groups,)),
            pltpu.SemaphoreType.DMA,
        ],
        compiler_params=pltpu.CompilerParams(
            vmem_limit_bytes=VMEM, collective_id=1, has_side_effects=True
        ),
        cost_estimate=cost(4 * tokens.shape[1] * depth * width, tokens, *shapes),
        name="entry",
    )(tokens, tokens, shard, forward_shard, gain, shift, cosine, sine, segment)


def attend_kernel(
    range_ref, query_ref, key_ref, value_ref, norm_ref, out_ref, told_ref, total_ref, top_ref, safe_ref, *, block
):
    step = pl.program_id(0)
    first, count = range_ref[0, step], range_ref[1, step]
    heads = query_ref.shape[0]
    total_ref[...] = jnp.zeros_like(total_ref)

    @pl.when(step == 0)
    def _():
        largest = 0.0
        for head in range(heads):
            queries, keys = norm_ref[2 * head : 2 * head + 1], norm_ref[2 * head + 1 : 2 * head + 2]
            largest = jnp.maximum(largest, jnp.max(queries) * jnp.max(keys))
        safe_ref[0] = (largest <= SAFE_EXPONENT**2).astype(jnp.int32)

    def scores(head, at):
        return product(key_ref[head, pl.ds(at, block), :], query_ref[head])

    def mix(head, at, weights):
        return product(value_ref[head, :, pl.ds(at, block)], weights)

    @pl.when(safe_ref[0] == 1)
    def _():
        top_ref[...] = jnp.zeros_like(top_ref)

        def body(number, carry):
            at = pl.multiple_of(first + number * block, WIDE)
            raw = [scores(head, at) for head in range(heads)]
            weights = [jnp.exp2(one).astype(bf16) for one in raw]
            for head in range(heads):
                total_ref[head] += mix(head, at, weights[head])
            return carry

        lax.fori_loop(0, count, body, 0)

    @pl.when(safe_ref[0] != 1)
    def _():
        top_ref[...] = jnp.full_like(top_ref, -3e38)

        def body(number, carry):
            at = pl.multiple_of(first + number * block, WIDE)
            for head in range(heads):
                raw = scores(head, at)
                before = top_ref[head]
                top = jnp.maximum(before, jnp.max(raw, axis=0, keepdims=True))
                weights = jnp.exp2(raw - top).astype(bf16)
                total_ref[head] = total_ref[head] * jnp.exp2(before - top) + mix(head, at, weights)
                top_ref[head] = top
            return carry

        lax.fori_loop(0, count, body, 0)

    tile = query_ref.shape[2]
    number = lax.broadcasted_iota(jnp.int32, (16, tile), 0)
    for head in range(heads):
        total = total_ref[head]
        mass = total[HDIM : HDIM + 1]
        out_ref[0, pl.ds(head * HDIM, HDIM), :] = (total[:HDIM] * (1.0 / mass)).astype(bf16)
        rows = split_rows(-(top_ref[head] + jnp.log2(mass)), number, SEGMENTS)
        told_ref[head, :HDIM, :] = query_ref[head, :HDIM, :]
        told_ref[head, HDIM : HDIM + 16, :] = jnp.where(
            number < SEGMENTS, query_ref[head, HDIM : HDIM + 16, :].astype(f32), rows
        ).astype(bf16)
        told_ref[head, HDIM + 16 :, :] = query_ref[head, HDIM + 16 :, :]


def split_rows(values, number, first):
    high = values.astype(bf16).astype(f32)
    rest = values - high
    middle = rest.astype(bf16).astype(f32)
    low = rest - middle
    return jnp.where(
        number == first,
        high,
        jnp.where(number == first + 1, middle, jnp.where(number == first + 2, low, 0.0)),
    )


def attend_call(ranges, queries, keys, values_t, norms, tile, block):
    heads, _, length = queries.shape
    rows = HDIM + 16
    return pl.pallas_call(
        partial(attend_kernel, block=block),
        grid_spec=pltpu.PrefetchScalarGridSpec(
            num_scalar_prefetch=1,
            grid=(length // tile,),
            in_specs=[
                pl.BlockSpec((heads, WIDE, tile), lambda i, r: (0, 0, i)),
                pl.BlockSpec((heads, length, WIDE), lambda i, r: (0, 0, 0)),
                pl.BlockSpec((heads, rows, length), lambda i, r: (0, 0, 0)),
                pl.BlockSpec(norms.shape, lambda i, r: (0, 0)),
            ],
            out_specs=[
                pl.BlockSpec((1, heads * HDIM, tile), lambda i, r: (i, 0, 0)),
                pl.BlockSpec((heads, WIDE, tile), lambda i, r: (0, 0, i)),
            ],
            scratch_shapes=[
                pltpu.VMEM((heads, rows, tile), f32),
                pltpu.VMEM((heads, 1, tile), f32),
                pltpu.SMEM((1,), jnp.int32),
            ],
        ),
        out_shape=[
            jax.ShapeDtypeStruct((length // tile, heads * HDIM, tile), bf16),
            jax.ShapeDtypeStruct((heads, WIDE, length), bf16),
        ],
        compiler_params=pltpu.CompilerParams(vmem_limit_bytes=VMEM),
        cost_estimate=cost(4 * heads * length * length * WIDE, queries, keys, values_t),
        name="attend",
    )(ranges, queries, keys, values_t, norms)


def attend_back_kernel(
    range_ref,
    query_ref,
    key_ref,
    value_ref,
    mixture_ref,
    grad_ref,
    cosine_ref,
    sine_ref,
    grad_query_ref,
    grad_key_ref,
    grad_value_ref,
    wide_ref,
    query_rows,
    grad_rows,
    query_total,
    key_total,
    value_total,
    *,
    block,
):
    step = pl.program_id(0)
    first, count = range_ref[0, step], range_ref[1, step]
    heads, _, tile = query_ref.shape

    @pl.when(step == 0)
    def _():
        wide_ref[...] = jnp.zeros_like(wide_ref)
        key_total[...] = jnp.zeros_like(key_total)
        value_total[...] = jnp.zeros_like(value_total)

    number = lax.broadcasted_iota(jnp.int32, (16, tile), 0)
    query_total[...] = jnp.zeros_like(query_total)
    for head in range(heads):
        at = pl.ds(head * HDIM, HDIM)
        grad = grad_ref[0, at, :]
        delta = jnp.sum(grad.astype(f32) * mixture_ref[0, at, :].astype(f32), axis=0, keepdims=True)
        wide_ref[head, :HDIM, :] = grad
        wide_ref[head, HDIM : HDIM + 16, :] = split_rows(-delta, number, 0).astype(bf16)
        query_rows[head] = query_ref[head].T
        grad_rows[head] = wide_ref[head].T

    def body(number, carry):
        at = pl.ds(pl.multiple_of(first + number * block, WIDE), block)
        raw = [product(query_rows[head], key_ref[head, :, at]) for head in range(heads)]
        slope = [product(grad_rows[head], value_ref[head, :, at]) for head in range(heads)]
        for head in range(heads):
            weights = jnp.exp2(raw[head])
            grad_scores = (weights * slope[head]).astype(bf16)
            value_total[head, :, at] += product(wide_ref[head, :HDIM, :], weights.astype(bf16))
            key_total[head, :, at] += product(query_ref[head, :HDIM, :], grad_scores)
            query_total[head] += against(key_ref[head, :HDIM, at], grad_scores)
        return carry

    lax.fori_loop(0, count, body, 0)

    def turned_back(grads, cosine, sine):
        front, back = grads[:HALF], grads[HALF:]
        return jnp.concatenate([front * cosine + back * sine, back * cosine - front * sine], axis=0)

    own = pl.ds(pl.multiple_of(step * tile, tile), tile)
    for head in range(heads):
        at = pl.ds(head * HDIM, HDIM)
        grad_query_ref[at, :] = turned_back(
            query_total[head] * 0.125, cosine_ref[:, own], sine_ref[:, own]
        ).astype(bf16)

    @pl.when(step == pl.num_programs(0) - 1)
    def _():
        for head in range(heads):
            at = pl.ds(head * HDIM, HDIM)
            grad_key_ref[at, :] = turned_back(
                key_total[head] * (1.0 / LOG2E), cosine_ref[...], sine_ref[...]
            ).astype(bf16)
            grad_value_ref[at, :] = value_total[head].astype(bf16)


def attend_back_call(
    ranges, queries, keys_t, values_t, mixture, grad_mixture, cosine, sine, tile, block
):
    heads, _, length = queries.shape
    group = heads * HDIM
    whole2 = lambda i, r: (0, 0)
    whole3 = lambda i, r: (0, 0, 0)
    return pl.pallas_call(
        partial(attend_back_kernel, block=block),
        grid_spec=pltpu.PrefetchScalarGridSpec(
            num_scalar_prefetch=1,
            grid=(length // tile,),
            in_specs=[
                pl.BlockSpec((heads, WIDE, tile), lambda i, r: (0, 0, i)),
                pl.BlockSpec((heads, WIDE, length), whole3),
                pl.BlockSpec((heads, WIDE, length), whole3),
                pl.BlockSpec((1, group, tile), lambda i, r: (i, 0, 0)),
                pl.BlockSpec((1, group, tile), lambda i, r: (i, 0, 0)),
                pl.BlockSpec((HALF, length), whole2),
                pl.BlockSpec((HALF, length), whole2),
            ],
            out_specs=[
                pl.BlockSpec((group, tile), lambda i, r: (0, i)),
                pl.BlockSpec((group, length), whole2),
                pl.BlockSpec((group, length), whole2),
            ],
            scratch_shapes=[
                pltpu.VMEM((heads, WIDE, tile), bf16),
                pltpu.VMEM((heads, tile, WIDE), bf16),
                pltpu.VMEM((heads, tile, WIDE), bf16),
                pltpu.VMEM((heads, HDIM, tile), f32),
                pltpu.VMEM((heads, HDIM, length), f32),
                pltpu.VMEM((heads, HDIM, length), f32),
            ],
        ),
        out_shape=[jax.ShapeDtypeStruct((group, length), bf16)] * 3,
        compiler_params=pltpu.CompilerParams(vmem_limit_bytes=VMEM),
        cost_estimate=cost(10 * heads * length * length * WIDE, queries, keys_t, values_t),
        name="attend_back",
    )(ranges, queries, keys_t, values_t, mixture, grad_mixture, cosine, sine)


def middle_kernel(
    mixture_ref,
    rows_ref,
    cotangent_ref,
    valid_ref,
    mod_ref,
    up_bias_ref,
    down_bias_ref,
    out_blocks_ref,
    own_ref,
    other_ref,
    across_ref,
    result_ref,
    grad_mixture_ref,
    grad_middle_ref,
    grad_out_blocks_ref,
    sums_ref,
    bias_sums_ref,
    up_keep_ref,
    up_send_ref,
    down_keep_ref,
    down_send_ref,
    own_mixture,
    out_weight_ref,
    grad_out_ref,
    entry_rows,
    entry_columns,
    grad_output_rows,
    grad_output_columns,
    attended_rows,
    output_rows,
    grad_entry_rows,
    active,
    grad_hidden,
    grad_staged,
    forward_ref,
    landed,
    home_grads,
    to_sibling,
    from_sibling,
    staged_up,
    staged_down,
    sent_mixture,
    got_mixture,
    own_copied,
    sent_grad,
    got_grad,
    grad_copied,
    sent_part,
    got_part,
    kept,
    sent_next,
    got_next,
    loaded,
    sent_other,
    got_other,
    sent_last,
    got_last,
    *,
    tile,
    tiles,
    parts,
    groups,
):
    step = pl.program_id(0)
    context, tensor = lax.axis_index("context"), lax.axis_index("tensor")
    ranks = 4
    everyone = 2 * ranks
    place = context * ranks + tensor
    core = lax.rem(tensor, 2)
    sibling = tensor + 1 - 2 * core
    depth = rows_ref.shape[2]
    group = depth // ranks
    per_sequence = tiles // 2
    part_tiles = tiles // PART_TILES
    per_part = part_tiles + 1
    back_from = tiles + parts * per_part - 1
    last_step = back_from + tiles
    root = math.sqrt(2.0 / math.pi)

    def member(away):
        other = lax.rem(place + away, everyone)
        return other, {"context": other // ranks, "tensor": lax.rem(other, ranks)}

    def mixture_copy(away):
        other, device = member(away)
        return copy_to(
            mixture_ref.at[other],
            own_mixture.at[place],
            sent_mixture.at[away - 1],
            got_mixture.at[lax.rem(place + everyone, everyone)],
            **device,
        )

    def mixture_arrival(source):
        return pltpu.make_async_remote_copy(
            src_ref=mixture_ref.at[source],
            dst_ref=own_mixture.at[source],
            send_sem=sent_mixture.at[0],
            recv_sem=got_mixture.at[source],
            device_id={"tensor": sibling},
            device_id_type=pl.DeviceIdType.MESH,
        )

    def own_copy():
        return pltpu.make_async_copy(mixture_ref.at[place], own_mixture.at[place], own_copied)

    def part_copy(slot):
        return copy_to(
            to_sibling, from_sibling.at[slot], sent_part.at[slot], got_part.at[slot], tensor=sibling
        )

    across = lax.rem(tensor + 2, ranks)
    height = depth // groups

    def rows_of(number):
        return pl.ds(number * height, height)

    def next_copy(kind):
        return copy_to(
            forward_ref.at[kind],
            landed.at[0, kind],
            sent_next.at[kind],
            got_next.at[kind],
            tensor=sibling,
        )

    def out_blocks():
        for rank in range(ranks):
            for number in range(groups):
                rows = slice(rank * group, (rank + 1) * group)
                yield rank * groups + number, (rows, slice(number * height, (number + 1) * height))

    def weight_loads():
        return [
            pltpu.make_async_copy(own_ref, forward_ref.at[context], loaded.at[0]),
            pltpu.make_async_copy(other_ref, forward_ref.at[1 - context], loaded.at[1]),
            pltpu.make_async_copy(across_ref, landed.at[1, context], loaded.at[2]),
        ]

    def other_copy(kind, number):
        place = landed.at[1, kind, rows_of(number), :]
        return copy_to(place, place, sent_other.at[number], got_other.at[number], context=1 - context)

    def last_copy(kind, number):
        return copy_to(
            landed.at[1, kind, rows_of(number), :],
            landed.at[2, kind, rows_of(number), :],
            sent_last.at[kind, number],
            got_last.at[kind, number],
            tensor=sibling,
        )

    def take_other(numbers):
        for number in numbers:
            other_copy(1 - context, number).wait_recv()
            last_copy(1 - context, number).start()

    def gradient_lanes(at):
        return pl.ds(pl.multiple_of(lax.rem(at, per_sequence) * tile, tile), tile)

    def sequence_of(at):
        return lax.rem(at // per_sequence + context, 2)

    def gradient_copy(at, rank):
        return copy_to(
            grad_staged.at[at, rank],
            grad_mixture_ref.at[place, :, gradient_lanes(at)],
            sent_grad.at[at, rank],
            got_grad.at[place, lax.rem(at, per_sequence)],
            context=sequence_of(at),
            tensor=rank,
        )

    def gradient_own(at):
        return pltpu.make_async_copy(
            grad_staged.at[at, tensor],
            grad_mixture_ref.at[place, :, gradient_lanes(at)],
            grad_copied.at[lax.rem(at, per_sequence)],
        )

    def gradient_arrival(source, number):
        return pltpu.make_async_remote_copy(
            src_ref=grad_staged.at[0, 0],
            dst_ref=grad_mixture_ref.at[source, :, pl.ds(number * tile, tile)],
            send_sem=sent_grad.at[0, 0],
            recv_sem=got_grad.at[source, number],
            device_id={"tensor": sibling},
            device_id_type=pl.DeviceIdType.MESH,
        )

    def kept_copies(slot):
        if slot == 1:
            return [
                pltpu.make_async_copy(staged_up, up_send_ref, kept.at[0]),
                pltpu.make_async_copy(staged_down.at[0], down_keep_ref.at[0], kept.at[1]),
                pltpu.make_async_copy(staged_down.at[1], down_send_ref.at[0], kept.at[2]),
            ]
        return [
            pltpu.make_async_copy(staged_up, up_keep_ref, kept.at[3]),
            pltpu.make_async_copy(staged_down.at[0], down_keep_ref.at[1], kept.at[4]),
            pltpu.make_async_copy(staged_down.at[1], down_send_ref.at[1], kept.at[5]),
        ]

    def tile_of(at):
        sequence = sequence_of(at)
        rows = pl.ds(pl.multiple_of(at * tile, tile), tile)
        mods = mod_ref[sequence]
        lanes = gradient_lanes(at)
        mixture_t = jnp.concatenate(
            [own_mixture[sequence * ranks + rank, :, lanes] for rank in range(ranks)], axis=0
        )
        return rows, mixture_t, tuple(mods[k : k + 1] for k in range(4))

    def normal(attended, gate_one):
        middle = rows_ref[0].astype(f32) + gate_one * attended
        center = middle - jnp.mean(middle, axis=-1, keepdims=True)
        scaling = lax.rsqrt(jnp.mean(center * center, axis=-1, keepdims=True) + EPSILON)
        return middle, center * scaling, scaling

    @pl.when(step == 0)
    def _():
        own_copy().start()
        for one in weight_loads():
            one.start()
        greet([member(away)[1] for away in range(1, everyone)])
        for near in (True, False):
            for away in range(1, everyone):

                @pl.when((member(away)[0] // ranks == context) == near)
                def _():
                    mixture_copy(away).start()

        for block, at in out_blocks():
            out_weight_ref[at] = out_blocks_ref[block]
        sums_ref[...] = jnp.zeros_like(sums_ref)
        bias_sums_ref[...] = jnp.zeros_like(bias_sums_ref)
        grad_out_ref[...] = jnp.zeros_like(grad_out_ref)

    for sequence in range(2):

        @pl.when(step == lax.rem(sequence + context, 2) * per_sequence)
        def _():
            for rank in range(ranks):
                source = sequence * ranks + rank

                @pl.when(place == source)
                def _():
                    own_copy().wait()

                @pl.when(place != source)
                def _():
                    mixture_arrival(source).wait_recv()

    @pl.when(step == per_sequence)
    def _():
        for one in weight_loads():
            one.wait()
        for kind in range(2):
            next_copy(kind).start()
        for number in range(groups):
            other_copy(context, number).start()
            last_copy(context, number).start()

    @pl.when(step == tiles + per_part)
    def _():
        for kind in range(2):
            next_copy(kind).wait_recv()

    @pl.when(step == tiles + 2 * per_part - 1)
    def _():
        take_other(range(groups // 2))

    @pl.when(step == tiles + 2 * per_part)
    def _():
        take_other(range(groups // 2, groups))

    @pl.when(step == tiles + 2 * per_part)
    def _():
        for kind in range(2):
            for number in range(groups):
                last_copy(kind, number).wait_recv()

    @pl.when(step < tiles)
    def _():
        rows, mixture_t, (gate_one, shift_two, gain_two, gate_two) = tile_of(step)
        attended = product(mixture_t.T, out_weight_ref[...])
        attended_rows[rows, :] = attended
        _, hat, _ = normal(attended, gate_one)
        entry = (hat * gain_two + shift_two).astype(bf16)
        grad_output = (gate_two * (cotangent_ref[0].astype(f32) * valid_ref[...])).astype(bf16)
        entry_rows[rows, :] = entry
        entry_columns[:, rows] = entry.T
        grad_output_rows[rows, :] = grad_output
        grad_output_columns[:, rows] = grad_output.T
        output_rows[rows, :] = jnp.broadcast_to(down_bias_ref[...], (tile, depth))
        grad_entry_rows[rows, :] = jnp.zeros((tile, depth), f32)

    inner = lax.rem(step - tiles, per_part)
    position = (step - tiles) // per_part
    in_parts = (step >= tiles) & (step < back_from)

    def part_tile(up, down):
        number = part_at(position, tensor)
        size = tile * PART_TILES // PART_CUTS
        for sub in range(PART_CUTS):
            rows = pl.ds(pl.multiple_of((inner * PART_CUTS + sub) * size, size), size)
            hidden = product(entry_rows[rows, :], up[...]) + up_bias_ref[0]
            square = hidden * hidden
            bent = jnp.tanh(root * hidden * (1.0 + 0.044715 * square))
            half = 0.5 * (1.0 + bent)
            activated = (hidden * half).astype(bf16)
            slope = half + (0.5 * root) * hidden * (1.0 - bent * bent) * (1.0 + 0.134145 * square)
            grads = (product(grad_output_rows[rows, :], down[...]) * slope).astype(bf16)
            output_rows[rows, :] += against(activated, down[...])
            grad_entry_rows[rows, :] += against(grads, up[...])
            active[rows, :] = activated
            grad_hidden[rows, :] = grads
            bias_sums_ref[number] += jnp.sum(grads.astype(f32), axis=0, keepdims=True)

    @pl.when(in_parts & (inner < part_tiles) & (position == 0))
    def _():
        part_tile(forward_ref.at[0], forward_ref.at[1])

    @pl.when(in_parts & (inner < part_tiles) & (position > 0))
    def _():
        place = lax.rem((position - 1) * 2, 3)
        part_tile(landed.at[place, 0], landed.at[place, 1])

    def products():
        both = [product(entry_columns[...], grad_hidden[...]), product(grad_output_columns[...], active[...])]
        return lambda other: [one[other * height : (other + 1) * height] for one in both]

    def kept_terms():
        return lambda other: [home_grads[kind, rows_of(other), :].astype(f32) for kind in range(2)]

    def gather_home(slot, own):
        part_copy(slot).wait_recv()
        if slot:
            for one in kept_copies(0):
                one.wait()
        terms = own()
        for other in range(groups):
            for kind, (staged, term) in enumerate(zip((staged_up, staged_down), terms(other))):
                total = (term + from_sibling[slot, kind, rows_of(other), :].astype(f32)).astype(bf16)
                staged[context, other] = total[: height // 2]
                staged[1 - context, other] = total[height // 2 :]
        for one in kept_copies(slot):
            one.start()

    for turn in range(parts):

        @pl.when(step == (tiles + turn * per_part + part_tiles if turn < parts - 1 else last_step))
        def _():
            if turn == 2:
                gather_home(0, kept_terms)
                part_copy(0).wait_send()
            if turn == 3:
                gather_home(1, products)
                return
            target = home_grads if turn == 0 else to_sibling
            terms = products()
            for other in range(groups):
                for kind, term in enumerate(terms(other)):
                    target[kind, rows_of(other), :] = term.astype(bf16)
            if turn:
                part_copy(turn - 1).start()

    @pl.when((step >= back_from) & (step < last_step))
    def _():
        at = lax.rem(step - back_from + per_sequence, tiles)
        sequence = sequence_of(at)
        rows, mixture_t, (gate_one, _, gain_two, gate_two) = tile_of(at)
        attended = attended_rows[rows, :]
        middle, hat, scaling = normal(attended, gate_one)
        output = output_rows[rows, :]
        grad_entry = grad_entry_rows[rows, :]
        grad_result = cotangent_ref[0].astype(f32) * valid_ref[...]
        result_ref[...] = (middle + gate_two * output).astype(bf16)
        grad_lifted = grad_entry * gain_two
        grad_middle = grad_result + scaling * (
            grad_lifted
            - jnp.mean(grad_lifted, axis=-1, keepdims=True)
            - hat * jnp.mean(grad_lifted * hat, axis=-1, keepdims=True)
        )
        grad_attended = (gate_one * grad_middle).astype(bf16)
        grad_mixture = against(out_weight_ref[...], grad_attended).astype(bf16)
        for rank in range(ranks):
            grad_staged[at, rank] = grad_mixture[rank * group : (rank + 1) * group]
        for rank in range(ranks):
            own = (sequence == context) & (tensor == rank)

            @pl.when(own)
            def _():
                gradient_own(at).start()

            @pl.when(jnp.logical_not(own))
            def _():
                gradient_copy(at, rank).start()

        grad_middle_ref[0] = grad_middle.T.astype(bf16)
        grad_out_ref[...] += product(mixture_t, grad_attended)
        lines = [
            jnp.sum(grad_middle * attended, axis=0, keepdims=True),
            jnp.sum(grad_entry, axis=0, keepdims=True),
            jnp.sum(grad_entry * hat, axis=0, keepdims=True),
            jnp.sum(grad_result * output, axis=0, keepdims=True),
            jnp.sum(grad_output_rows[rows, :].astype(f32), axis=0, keepdims=True),
        ]
        lines += [jnp.zeros_like(lines[0])] * (sums_ref.shape[1] - len(lines))
        sums_ref[sequence] += jnp.concatenate(lines, axis=0)

    @pl.when(step == last_step)
    def _():
        for block, at in out_blocks():
            grad_out_blocks_ref[block] = grad_out_ref[at].astype(bf16)
        for source in range(everyone):
            for number in range(per_sequence):

                @pl.when(place != source)
                def _():
                    gradient_arrival(source, number).wait_recv()

        for at in range(tiles):
            for rank in range(ranks):
                own = (sequence_of(at) == context) & (tensor == rank)

                @pl.when(own)
                def _():
                    gradient_own(at).wait()

                @pl.when(jnp.logical_not(own))
                def _():
                    gradient_copy(at, rank).wait_send()

        for away in range(1, everyone):
            mixture_copy(away).wait_send()
        for kind in range(2):
            next_copy(kind).wait_send()
        for number in range(groups):
            other_copy(context, number).wait_send()
            for kind in range(2):
                last_copy(kind, number).wait_send()
        part_copy(1).wait_send()
        for one in kept_copies(1):
            one.wait()


def part_at(position, tensor):
    return quarter_at(jnp.where(position < 2, position, 5 - position), tensor)


def middle_call(
    mixture, rows, cotangent, valid, mods, up_bias, down_bias, out_blocks, own_weight, other_weight, across, groups, tile
):
    pieces, group, own = mixture.shape
    depth = rows.shape[2]
    tokens = rows.shape[0] * own
    parts, _, part_width = up_bias.shape
    tiles = tokens // tile
    per_sequence = tiles // 2
    per_part = tiles // PART_TILES + 1
    back_from = tiles + parts * per_part - 1
    half = depth // groups // 2

    def in_order(at):
        sequence = lax.rem(at // per_sequence + lax.axis_index("context"), 2)
        return sequence, lax.rem(at, per_sequence)

    def back_number(i):
        return lax.rem(jnp.clip(i - back_from, 0, tiles - 1) + per_sequence, tiles)

    def token_place(i):
        return in_order(jnp.where(i < tiles, i, back_number(i)))

    def token_tile(i):
        sequence, number = token_place(i)
        return sequence, lax.axis_index("tensor") * per_sequence + number, 0

    def valid_tile(i):
        sequence, number = token_place(i)
        return sequence * per_sequence + number, 0

    def part_block(i):
        position = jnp.clip((i - tiles) // per_part, 0, parts - 1)
        return part_at(position, lax.axis_index("tensor")), 0, 0

    def back_tile(i):
        return in_order(back_number(i))

    whole2 = lambda i: (0, 0)
    whole3 = lambda i: (0, 0, 0)
    once = pl.Buffered(1)
    hbm = pl.BlockSpec(memory_space=pl.ANY)
    kept = jax.ShapeDtypeStruct((2, groups, half, part_width), bf16)
    wide = (tokens, depth)
    return pl.pallas_call(
        partial(middle_kernel, tile=tile, tiles=tiles, parts=parts, groups=groups),
        grid=(back_from + tiles + 1,),
        in_specs=[
            hbm,
            pl.BlockSpec((1, tile, depth), token_tile),
            pl.BlockSpec((1, tile, depth), token_tile),
            pl.BlockSpec((tile, 1), valid_tile),
            pl.BlockSpec(mods.shape, whole3, pipeline_mode=once),
            pl.BlockSpec((1, 1, part_width), part_block),
            pl.BlockSpec((1, depth), whole2, pipeline_mode=once),
            pl.BlockSpec(out_blocks.shape, whole3, pipeline_mode=once),
            hbm,
            hbm,
            hbm,
        ],
        out_specs=[
            pl.BlockSpec(
                (tile, depth), lambda i: (back_tile(i)[0] * per_sequence + back_tile(i)[1], 0)
            ),
            hbm,
            pl.BlockSpec(
                (1, depth, tile),
                lambda i: (back_tile(i)[0], 0, back_tile(i)[1]),
            ),
            pl.BlockSpec(out_blocks.shape, whole3),
            pl.BlockSpec((2, 8, depth), whole3),
            pl.BlockSpec((parts, 1, part_width), whole3),
            hbm,
            hbm,
            hbm,
            hbm,
        ],
        out_shape=[
            jax.ShapeDtypeStruct((tokens, depth), bf16),
            jax.ShapeDtypeStruct(mixture.shape, bf16),
            jax.ShapeDtypeStruct((2, depth, own), bf16),
            jax.ShapeDtypeStruct(out_blocks.shape, bf16),
            jax.ShapeDtypeStruct((2, 8, depth), f32),
            jax.ShapeDtypeStruct((parts, 1, part_width), f32),
            kept,
            kept,
            kept,
            kept,
        ],
        scratch_shapes=[
            pltpu.VMEM(mixture.shape, bf16),
            pltpu.VMEM((depth, depth), bf16),
            pltpu.VMEM((depth, depth), f32),
            pltpu.VMEM(wide, bf16),
            pltpu.VMEM((depth, tokens), bf16),
            pltpu.VMEM(wide, bf16),
            pltpu.VMEM((depth, tokens), bf16),
            pltpu.VMEM(wide, f32),
            pltpu.VMEM(wide, f32),
            pltpu.VMEM(wide, f32),
            pltpu.VMEM((tokens, part_width), bf16),
            pltpu.VMEM((tokens, part_width), bf16),
            pltpu.VMEM((tiles, 4, group, tile), bf16),
            pltpu.VMEM((2, depth, part_width), bf16),
            pltpu.VMEM((3, 2, depth, part_width), bf16),
            pltpu.VMEM((2, depth, part_width), bf16),
            pltpu.VMEM((2, depth, part_width), bf16),
            pltpu.VMEM((2, 2, depth, part_width), bf16),
            pltpu.VMEM((2, groups, half, part_width), bf16),
            pltpu.VMEM((2, groups, half, part_width), bf16),
            pltpu.SemaphoreType.DMA((pieces - 1,)),
            pltpu.SemaphoreType.DMA((pieces,)),
            pltpu.SemaphoreType.DMA,
            pltpu.SemaphoreType.DMA((tiles, 4)),
            pltpu.SemaphoreType.DMA((pieces, per_sequence)),
            pltpu.SemaphoreType.DMA((per_sequence,)),
            pltpu.SemaphoreType.DMA((2,)),
            pltpu.SemaphoreType.DMA((2,)),
            pltpu.SemaphoreType.DMA((6,)),
            *[pltpu.SemaphoreType.DMA((2,))] * 2,
            pltpu.SemaphoreType.DMA((3,)),
            *[pltpu.SemaphoreType.DMA((groups,))] * 2,
            *[pltpu.SemaphoreType.DMA((2, groups))] * 2,
        ],
        compiler_params=pltpu.CompilerParams(
            vmem_limit_bytes=VMEM_MOST, collective_id=2, has_side_effects=True
        ),
        cost_estimate=cost(6 * tokens * depth * (depth + 3 * parts * part_width), rows, rows, rows),
        name="middle",
    )(mixture, rows, cotangent, valid, mods, up_bias, down_bias, out_blocks, own_weight, other_weight, across)


class Relay:
    def __init__(self, own, out, arrived, sent, got, fsdp, groups):
        self.own, self.out, self.arrived, self.sent, self.got = own, out, arrived, sent, got
        self.fsdp, self.groups = fsdp, groups

    def copy(self, side, target):
        return copy_to(
            self.out.at[side, target],
            self.arrived.at[side, target],
            self.sent.at[side, target],
            self.got.at[side, target],
            fsdp=self.fsdp - 1 if side else self.fsdp + 1,
        )

    def begin(self, target):
        for side, end in ((0, 0), (1, self.groups - 1)):
            if target != end:

                @pl.when(self.fsdp == end)
                def _():
                    self.out[side, target] = self.own[target]
                    self.copy(side, target).start()

    def turn(self, number):
        last = self.groups - 1
        for side in range(2):
            behind = last - self.fsdp if side else self.fsdp

            @pl.when((behind >= 1) & (behind <= number))
            def _():
                target = self.fsdp + (number - last if side else last - number)
                self.copy(side, target).wait_recv()
                if number < last:
                    total = self.own[target].astype(f32) + self.arrived[side, target].astype(f32)
                    self.out[side, target] = total.astype(bf16)
                    self.copy(side, target).start()

    def total(self, sum_ref):
        sum_ref[...] = self.own[self.fsdp].astype(f32)
        for side, end in ((0, 0), (1, self.groups - 1)):

            @pl.when(self.fsdp != end)
            def _():
                sum_ref[...] += self.arrived[side, self.fsdp].astype(f32)

    def finish(self):
        for target in range(self.groups):
            for side, sends in ((0, self.fsdp < target), (1, self.fsdp > target)):

                @pl.when(sends)
                def _():
                    self.copy(side, target).wait_send()


def entry_back_kernel(
    grad_query_ref,
    grad_key_ref,
    grad_value_ref,
    hat_ref,
    scale_ref,
    gain_ref,
    shift_ref,
    weight_ref,
    middle_ref,
    middle_in_ref,
    small_ref,
    up_ref,
    down_ref,
    grad_out_ref,
    result_ref,
    result_in_ref,
    out_ref,
    grad_weight_ref,
    lines_ref,
    vectors_ref,
    pieces_ref,
    grad_out_sum_ref,
    block_ref,
    up_own,
    up_in,
    down_own,
    down_in,
    slices,
    slices_out,
    slices_in,
    slice_sum,
    context_slice,
    context_in,
    all_sums_ref,
    all_small_ref,
    small_part,
    small_in,
    small_sum,
    small_groups,
    out_in,
    loaded,
    sent_up,
    got_up,
    sent_down,
    got_down,
    sent_slice,
    got_slice,
    sent_context,
    got_context,
    sent_small,
    got_small,
    sent_sum,
    got_sum,
    sent_out,
    got_out,
    sent_result,
    got_result,
    moved,
    taken,
    held,
    weight_total,
    sums,
    part,
    part_in,
    pair,
    pair_in,
    chip,
    chip_in,
    piece,
    piece_out,
    piece_in,
    piece_sum,
    block_piece,
    block_in,
    rank_sums,
    rank_in,
    group_sums,
    group_in,
    sent_part,
    got_part,
    sent_pair,
    got_pair,
    sent_chip,
    got_chip,
    sent_piece,
    got_piece,
    sent_block,
    got_block,
    sent_rank,
    got_rank,
    sent_group,
    got_group,
    *,
    tiles,
    groups,
):
    step = pl.program_id(0)
    fsdp, context, tensor = (lax.axis_index(name) for name in ("fsdp", "context", "tensor"))
    ranks = 4
    half = tiles // 2
    core = lax.rem(tensor, 2)
    chip_x = tensor // 2
    sibling = tensor + 1 - 2 * core
    across = lax.rem(tensor + 2, ranks)
    place = fsdp * 2 + context
    depth = hat_ref.shape[0]
    slice_rows = depth // ranks
    weight_rows = depth // groups
    def up_copy(other):
        return copy_to(
            up_ref.at[1, other], up_in.at[other], sent_up.at[other], got_up.at[other], context=1 - context
        )

    def down_copy(other):
        return copy_to(
            down_ref.at[0, other], down_in.at[other], sent_down.at[other], got_down.at[other], tensor=across
        )

    def loads():
        return [
            pltpu.make_async_copy(up_ref.at[0], up_own, loaded.at[0]),
            pltpu.make_async_copy(down_ref.at[1], down_own, loaded.at[1]),
        ]

    far_first = [groups - 1, 0] + list(range(groups - 2, 0, -1))
    slice_relay = Relay(slices, slices_out, slices_in, sent_slice, got_slice, fsdp, groups)
    piece_relay = Relay(piece, piece_out, piece_in, sent_piece, got_piece, fsdp, groups)

    def context_copy():
        return copy_to(context_slice, context_in, sent_context, got_context, context=1 - context)

    rounds = [{"tensor": sibling}, {"tensor": across}, {"context": 1 - context}]

    def small_copy(number):
        return copy_to(
            small_part.at[number], small_in.at[number], sent_small.at[number], got_small.at[number], **rounds[number]
        )

    def sum_copy(away):
        return copy_to(
            small_sum,
            small_groups.at[away - 1],
            sent_sum.at[away - 1],
            got_sum.at[away - 1],
            fsdp=lax.rem(fsdp + away, groups),
        )

    def out_copy():
        return copy_to(grad_out_ref, out_in, sent_out, got_out, context=1 - context)

    quarter = result_ref.shape[1]

    def result_places():
        for number, (source, rank) in enumerate([(result_ref, tensor), (result_in_ref, across)]):
            rows = pl.ds(pl.multiple_of(rank * quarter, quarter), quarter)
            for sequence in range(2):
                yield number * 2 + sequence, source.at[sequence], block_ref.at[sequence, rows, :]

    def result_copies():
        return [
            copy_to(held.at[k], target, sent_result.at[k], got_result.at[k], tensor=sibling)
            for k, source, target in result_places()
        ]

    def result_loads():
        return [
            pltpu.make_async_copy(source, held.at[k], taken.at[k])
            for k, source, target in result_places()
        ]

    def result_moves():
        return [
            pltpu.make_async_copy(held.at[k], target, moved.at[k]) for k, source, target in result_places()
        ]

    def part_copy(tile):
        return copy_to(
            part.at[tile, 1 - core], part_in.at[tile], sent_part.at[tile], got_part.at[tile], tensor=sibling
        )

    def pair_copy(tile):
        return copy_to(
            pair.at[tile, 1 - chip_x], pair_in.at[tile], sent_pair.at[tile], got_pair.at[tile], tensor=across
        )

    def chip_copy(tile):
        return copy_to(
            chip.at[tile], chip_in.at[tile], sent_chip.at[tile], got_chip.at[tile], context=1 - context
        )

    def block_copy():
        return copy_to(block_piece, block_in, sent_block, got_block, context=1 - context)

    def rank_copy(number):
        return copy_to(
            rank_sums.at[number], rank_in.at[number], sent_rank.at[number], got_rank.at[number], **rounds[number]
        )

    def group_copy(away):
        return copy_to(
            group_sums,
            group_in.at[away - 1],
            sent_group.at[away - 1],
            got_group.at[away - 1],
            fsdp=lax.rem(fsdp + away, groups),
        )

    @pl.when(step == 0)
    def _():
        greet(
            rounds + [{"fsdp": lax.rem(fsdp + away, groups)} for away in range(1, groups)]
        )
        for other in far_first:
            up_copy(other).start()
            down_copy(other).start()
        out_copy().start()
        small_part[0] = small_ref[...]
        small_copy(0).start()
        for one in result_loads() + loads():
            one.start()
        weight_total[...] = jnp.zeros_like(weight_total)
        sums[...] = jnp.zeros_like(sums)

    @pl.when(step == 2)
    def _():
        for one in result_loads():
            one.wait()
        for one in result_copies() + result_moves():
            one.start()

    def grads():
        return jnp.concatenate([grad_query_ref[...], grad_key_ref[...], grad_value_ref[...]], axis=0)

    @pl.when(step < tiles)
    def _():
        tile = step
        columns = grads()
        grad_entry = product(weight_ref[...], columns)
        hat = hat_ref[...].astype(f32)
        lifted = hat * gain_ref[...]
        weight_total[...] += against((lifted + shift_ref[...]).astype(bf16), columns)
        grad_lifted = grad_entry * gain_ref[...]
        term = scale_ref[...] * (
            grad_lifted
            - jnp.mean(grad_lifted, axis=0, keepdims=True)
            - hat * jnp.mean(grad_lifted * hat, axis=0, keepdims=True)
        )
        extra = jnp.where(tile < half, middle_in_ref[...], middle_ref[0]).astype(f32)
        term = (term + jnp.where(lax.rem(tile, half) == tensor, extra, 0.0)).astype(bf16)
        for rank in range(ranks):
            part[tile, rank % 2, rank // 2] = term[rank * slice_rows : (rank + 1) * slice_rows]
        part_copy(tile).start()
        weighted = grad_entry * hat
        for lane in range(0, grad_entry.shape[1], WIDE):
            sums[0] += grad_entry[:, lane : lane + WIDE]
            sums[1] += weighted[:, lane : lane + WIDE]

    @pl.when(step == tiles - 1)
    def _():
        for other in range(groups):
            piece[other] = weight_total[other * weight_rows : (other + 1) * weight_rows].astype(bf16)
        for target in far_first:
            piece_relay.begin(target)

    @pl.when((step >= 1) & (step < tiles + 1))
    def _():
        tile = step - 1
        part_copy(tile).wait_recv()
        pair[tile] = (part[tile, core].astype(f32) + part_in[tile].astype(f32)).astype(bf16)
        pair_copy(tile).start()

    @pl.when((step >= 5) & (step < tiles + 5))
    def _():
        tile = step - 5
        pair_copy(tile).wait_recv()
        total = (pair[tile, chip_x].astype(f32) + pair_in[tile].astype(f32)).astype(bf16)

        @pl.when(tile < half)
        def _():
            chip[tile] = total
            chip_copy(tile).start()

        @pl.when(tile >= half)
        def _():
            out_ref[context, tile - half] = total

    @pl.when((step >= tiles + 1) & (step < tiles + 1 + half))
    def _():
        tile = step - tiles - 1
        chip_copy(tile).wait_recv()
        out_ref[1 - context, tile] = chip_in[tile]

    for number in range(3):

        @pl.when(step == (2, 5, 7)[number])
        def _():
            small_copy(number).wait_recv()
            total = small_part[number] + small_in[number]
            if number < 2:
                small_part[number + 1] = total
                small_copy(number + 1).start()
            else:
                small_sum[...] = total
                for away in range(1, groups):
                    sum_copy(away).start()

    for number, other in enumerate(far_first):

        @pl.when(step == 1 + number)
        def _():
            if number == 0:
                for one in loads():
                    one.wait()
            up_copy(other).wait_recv()
            down_copy(other).wait_recv()
            slices[other, 0] = (up_own[other].astype(f32) + up_in[other].astype(f32)).astype(bf16)
            slices[other, 1] = (down_own[other].astype(f32) + down_in[other].astype(f32)).astype(bf16)
            slice_relay.begin(other)

    for number in range(1, groups):

        @pl.when(step == tiles - 2 * (groups - 1 - number))
        def _():
            slice_relay.turn(number)

    @pl.when(step == tiles)
    def _():
        slice_relay.total(slice_sum)
        context_slice[...] = slice_sum[...].astype(bf16)
        context_copy().start()

    for number in range(1, groups):

        @pl.when(step == tiles + number - 1)
        def _():
            piece_relay.turn(number)

    @pl.when(step == tiles + 2)
    def _():
        piece_relay.total(piece_sum)
        block_piece[...] = piece_sum[...].astype(bf16)
        block_copy().start()

    @pl.when(step == tiles + 4)
    def _():
        block_copy().wait_recv()
        grad_weight_ref[...] = block_piece[...].astype(f32) + block_in[...].astype(f32)

    @pl.when(step == tiles - 1)
    def _():
        rows = [jnp.sum(sums[kind].T, axis=0, keepdims=True) for kind in range(2)]
        rank_sums[0] = jnp.concatenate(rows + [jnp.zeros((6, depth), f32)], axis=0)
        rank_copy(0).start()

    @pl.when(step == tiles)
    def _():
        rank_copy(0).wait_recv()
        rank_sums[1] = rank_sums[0] + rank_in[0]
        rank_copy(1).start()

    @pl.when(step == tiles + 3)
    def _():
        rank_copy(1).wait_recv()
        rank_sums[2] = rank_sums[1] + rank_in[1]
        rank_copy(2).start()

    @pl.when(step == tiles + 4)
    def _():
        rank_copy(2).wait_recv()
        group_sums[context] = rank_sums[2]
        group_sums[1 - context] = rank_in[2]
        for away in range(1, groups):
            group_copy(away).start()

    @pl.when(step == tiles + 4)
    def _():
        all_small_ref[fsdp] = small_sum[...]
        for away in range(1, groups):
            sum_copy(away).wait_recv()
            all_small_ref[lax.rem(fsdp + groups - away, groups)] = small_groups[away - 1]
            sum_copy(away).wait_send()
        context_copy().wait()
        pieces_ref[context] = context_slice[...]
        pieces_ref[1 - context] = context_in[...]
        out_copy().wait()
        grad_out_sum_ref[...] = grad_out_ref[...].astype(f32) + out_in[...].astype(f32)
        for other in range(groups):
            up_copy(other).wait_send()
            down_copy(other).wait_send()
        for number in range(3):
            small_copy(number).wait_send()
            rank_copy(number).wait_send()
        for one in result_copies() + result_moves():
            one.wait()
        for number in range(2):
            all_sums_ref[2 * fsdp + number] = group_sums[number]
        for away in range(1, groups):
            group_copy(away).wait_recv()
            for number in range(2):
                source = lax.rem(fsdp + groups - away, groups)
                all_sums_ref[2 * source + number] = group_in[away - 1, number]
            group_copy(away).wait_send()
        for source in range(2 * groups):
            line = slice(source, source + 1)
            for kind in range(2):
                lines_ref[kind, line] = all_sums_ref[source, kind : kind + 1]
            first = source % 2 * 5
            for kind in range(4):
                lines_ref[2 + kind, line] = all_small_ref[source // 2, first + kind : first + kind + 1]
            last = 10 + ranks + source % 2
            lines_ref[6, line] = all_small_ref[source // 2, last : last + 1]
        vectors_ref[...] = jnp.zeros_like(vectors_ref)
        for source in range(groups):
            vectors_ref[0:ranks] += all_small_ref[source, 10 : 10 + ranks]
            vectors_ref[ranks : ranks + 1] += all_small_ref[source, 4:5] + all_small_ref[source, 9:10]
        for tile in range(tiles):
            part_copy(tile).wait_send()
            pair_copy(tile).wait_send()
        for tile in range(half):
            chip_copy(tile).wait_send()
        slice_relay.finish()
        piece_relay.finish()
        block_copy().wait_send()


def entry_back_call(
    grad_query,
    grad_key,
    grad_value,
    hat_t,
    scaling,
    gain,
    shift,
    weight,
    grad_middle,
    middle_in,
    small,
    up,
    down,
    grad_out,
    result,
    result_in,
    groups,
    tile,
):
    group, length = grad_query.shape
    depth = hat_t.shape[0]
    tiles = length // tile
    half = tiles // 2
    rows = depth // 4
    weight_rows = depth // groups

    def lanes(step):
        first = (1 - lax.axis_index("context")) * half
        return 0, lax.rem(first + jnp.minimum(step, tiles - 1), tiles)

    whole = lambda step: (0, 0)
    whole3 = lambda step: (0, 0, 0)
    whole4 = lambda step: (0, 0, 0, 0)
    dma = lambda *shape: [pltpu.SemaphoreType.DMA(shape)] * 2
    hbm = pl.BlockSpec(memory_space=pl.ANY)
    piece = up.shape[1:]
    return pl.pallas_call(
        partial(entry_back_kernel, tiles=tiles, groups=groups),
        grid=(tiles + 5,),
        in_specs=[
            pl.BlockSpec((group, tile), lanes),
            pl.BlockSpec((group, tile), lanes),
            pl.BlockSpec((group, tile), lanes),
            pl.BlockSpec((depth, tile), lanes),
            pl.BlockSpec((1, tile), lanes),
            pl.BlockSpec((depth, 1), whole),
            pl.BlockSpec((depth, 1), whole),
            pl.BlockSpec((depth, 3 * group), whole),
            pl.BlockSpec((1, depth, tile), lambda step: (lax.axis_index("context"), 0, 0)),
            pl.BlockSpec((depth, tile), whole),
            pl.BlockSpec(small.shape, whole),
            hbm,
            hbm,
            pl.BlockSpec(grad_out.shape, whole),
            hbm,
            hbm,
        ],
        out_specs=[
            pl.BlockSpec((2, half, rows, tile), whole4),
            pl.BlockSpec((weight_rows, 3 * group), whole),
            pl.BlockSpec((7, 2 * groups, depth), whole3),
            pl.BlockSpec((8, depth), whole),
            pl.BlockSpec((2, 2, *piece[1:]), whole4),
            pl.BlockSpec(grad_out.shape, whole),
            hbm,
        ],
        out_shape=[
            jax.ShapeDtypeStruct((2, half, rows, tile), bf16),
            jax.ShapeDtypeStruct((weight_rows, 3 * group), f32),
            jax.ShapeDtypeStruct((7, 2 * groups, depth), f32),
            jax.ShapeDtypeStruct((8, depth), f32),
            jax.ShapeDtypeStruct((2, 2, *piece[1:]), bf16),
            jax.ShapeDtypeStruct(grad_out.shape, f32),
            jax.ShapeDtypeStruct((2, 4 * result.shape[1], depth), bf16),
        ],
        scratch_shapes=[
            *[pltpu.VMEM(piece, bf16)] * 4,
            pltpu.VMEM((groups, 2, *piece[1:]), bf16),
            *[pltpu.VMEM((2, groups, 2, *piece[1:]), bf16)] * 2,
            pltpu.VMEM((2, *piece[1:]), f32),
            pltpu.VMEM((2, *piece[1:]), bf16),
            pltpu.VMEM((2, *piece[1:]), bf16),
            pltpu.VMEM((2 * groups, 8, depth), f32),
            pltpu.VMEM((groups, *small.shape), f32),
            *[pltpu.VMEM((3, *small.shape), f32)] * 2,
            pltpu.VMEM(small.shape, f32),
            pltpu.VMEM((groups - 1, *small.shape), f32),
            pltpu.VMEM(grad_out.shape, bf16),
            pltpu.SemaphoreType.DMA((2,)),
            *dma(groups),
            *dma(groups),
            *dma(2, groups),
            *[pltpu.SemaphoreType.DMA] * 2,
            *dma(3),
            *dma(groups - 1),
            *[pltpu.SemaphoreType.DMA] * 2,
            *dma(4),
            pltpu.SemaphoreType.DMA((4,)),
            pltpu.SemaphoreType.DMA((4,)),
            pltpu.VMEM((4, *result.shape[1:]), bf16),
            pltpu.VMEM((depth, 3 * group), f32),
            pltpu.VMEM((2, depth, WIDE), f32),
            pltpu.VMEM((tiles, 2, 2, rows, tile), bf16),
            pltpu.VMEM((tiles, 2, rows, tile), bf16),
            pltpu.VMEM((tiles, 2, rows, tile), bf16),
            pltpu.VMEM((tiles, rows, tile), bf16),
            pltpu.VMEM((half, rows, tile), bf16),
            pltpu.VMEM((half, rows, tile), bf16),
            pltpu.VMEM((groups, weight_rows, 3 * group), bf16),
            *[pltpu.VMEM((2, groups, weight_rows, 3 * group), bf16)] * 2,
            pltpu.VMEM((weight_rows, 3 * group), f32),
            pltpu.VMEM((weight_rows, 3 * group), bf16),
            pltpu.VMEM((weight_rows, 3 * group), bf16),
            *[pltpu.VMEM((3, 8, depth), f32)] * 2,
            pltpu.VMEM((2, 8, depth), f32),
            pltpu.VMEM((groups - 1, 2, 8, depth), f32),
            *dma(tiles),
            *dma(tiles),
            *dma(half),
            *dma(2, groups),
            *[pltpu.SemaphoreType.DMA] * 2,
            *dma(3),
            *dma(groups - 1),
        ],
        compiler_params=pltpu.CompilerParams(
            vmem_limit_bytes=VMEM, collective_id=3, has_side_effects=True
        ),
        cost_estimate=cost(12 * length * depth * group, grad_query, hat_t, hat_t),
        name="entry_back",
    )(
        grad_query,
        grad_key,
        grad_value,
        hat_t,
        scaling,
        gain,
        shift,
        weight,
        grad_middle,
        middle_in,
        small,
        up,
        down,
        grad_out,
        result,
        result_in,
    )


def add(left_side, right_side):
    return (left_side.astype(f32) + right_side.astype(f32)).astype(bf16)


def by_sequence(
    tokens,
    cotangent,
    segments,
    steps,
    table,
    ada_w,
    ada_b,
    gain_one,
    w_qkv,
    w_out,
    gain_two,
    w_up,
    b_up,
    w_down,
    b_down,
):
    fsdp, tensor = lax.axis_size("fsdp"), lax.axis_size("tensor")
    context = lax.axis_size("context")
    tensor_rank = lax.axis_index("tensor")
    context_rank = lax.axis_index("context")
    fsdp_rank = lax.axis_index("fsdp")
    sequences, own_rows, depth = tokens.shape
    length = segments.shape[1]
    group = w_out.shape[0]
    part_width = w_up.shape[1]
    heads = group // HDIM
    quarter = own_rows // tensor

    partner = [(k, (k + 1) % context) for k in range(context)]

    by_kind = w_qkv.reshape(-1, heads, 3, HDIM).transpose(0, 2, 1, 3).reshape(-1, 3 * group)
    both = ("tensor", "fsdp")
    out_blocks = lax.all_gather(w_out, both, axis=0, tiled=False)

    numbers = jnp.arange(table.shape[0], dtype=jnp.int32)
    ada_full = ada_w.astype(f32)
    raw = exact_product((steps[:, None] == numbers[None, :]).astype(f32), table.astype(f32))
    local_mods = exact_product(jax.nn.silu(raw), ada_full) + ada_b.astype(f32)
    local_mods = local_mods.reshape(sequences, 6, depth)
    gain_first, gain_second = gain_one.astype(f32), gain_two.astype(f32)
    own_mods = lax.dynamic_index_in_dim(local_mods, context_rank, 0, keepdims=False)
    gain_column = (gain_first * (1.0 + own_mods[1]))[:, None]
    shift_column = own_mods[0][:, None]
    mods = jnp.stack(
        [
            local_mods[:, 2],
            local_mods[:, 3],
            gain_second * (1.0 + local_mods[:, 4]),
            local_mods[:, 5],
        ]
        + [jnp.zeros((sequences, depth), f32)] * 4,
        axis=1,
    )

    segment = lax.dynamic_index_in_dim(segments, context_rank, 0, keepdims=False)
    same, starts, ends = document_bounds(segment)
    offsets = jnp.arange(length, dtype=jnp.int32) - jnp.sum(jnp.where(same, starts[:, None], 0), axis=0)
    angles = frequencies()[:, None] * offsets.astype(f32)[None, :]
    cosine, sine = jnp.cos(angles), jnp.sin(angles)
    tile = length // (context * tensor)
    block = tile
    first_key = jnp.sum(jnp.where(same, starts[:, None], 0), axis=0)[::tile]
    last_key = jnp.sum(jnp.where(same, ends[:, None], 0), axis=0)[tile - 1 :: tile]

    low_key = first_key // WIDE * WIDE
    high_key = (last_key + WIDE - 1) // WIDE * WIDE

    def ranges_of(size):
        count = (high_key - low_key + size - 1) // size
        return jnp.stack([jnp.maximum(high_key - count * size, 0), count]).astype(jnp.int32)

    back_block = block // 2
    ranges, back_ranges = ranges_of(block), ranges_of(back_block)

    queries, keys, keys_t, values_t, hat_t, scaling, norms, qkv, forward = entry_call(
        tokens,
        by_kind,
        jnp.where(context_rank == 0, w_up, w_down.T),
        gain_column,
        shift_column,
        cosine,
        sine,
        segment[None, :],
        groups=fsdp,
        tile=tile,
    )
    across = [(k, (k + 2) % tensor) for k in range(tensor)]
    across_weight = lax.ppermute(forward, "tensor", across)
    other_weight = lax.ppermute(forward, "context", partner)
    mixture, told = attend_call(ranges, queries, keys, values_t, norms, tile, block)

    own_segments = lax.dynamic_slice_in_dim(
        segments, context_rank * own_rows + tensor_rank * quarter, quarter, axis=1
    )
    (
        result,
        grad_mixture,
        grad_middle,
        grad_out,
        sums,
        bias_sums,
        up_keep,
        up_send,
        down_keep,
        down_send,
    ) = middle_call(
        mixture,
        tokens,
        cotangent,
        (own_segments != 0).astype(f32).reshape(-1, 1),
        mods,
        b_up.astype(f32).reshape(tensor, 1, part_width),
        b_down.astype(f32)[None, :],
        out_blocks,
        forward,
        other_weight,
        across_weight,
        fsdp,
        tile=min(tile, 256),
    )
    result = result.reshape(sequences, quarter, depth)
    result_in = lax.ppermute(result, "tensor", across)
    middle_in = lax.ppermute(
        lax.dynamic_index_in_dim(grad_middle, 1 - context_rank, 0, keepdims=False), "context", partner
    )
    small = jnp.concatenate(
        [
            sums[:, :5].reshape(-1, depth),
            bias_sums.reshape(-1, depth),
        ]
    )
    small_rows = small.shape[0]
    cond = raw.shape[1]
    leads = (context_rank == 0) & (tensor_rank == 0)
    embedded = jnp.concatenate([raw, steps.astype(f32)[:, None]], axis=1)
    embedded = jnp.pad(jnp.where(leads, embedded, 0.0), ((0, 0), (0, depth - cond - 1)))
    small = jnp.concatenate([small, embedded])
    small = jnp.pad(small, ((0, -small.shape[0] % 8), (0, 0)))

    up_sum = add(up_keep, lax.ppermute(up_send, "tensor", across))
    down_sum = add(down_keep, lax.ppermute(down_send, "context", partner))
    grad_out = lax.psum_scatter(grad_out, both, scatter_dimension=0, tiled=True)[0]

    grad_query, grad_key, grad_value = attend_back_call(
        back_ranges, told, keys_t, values_t, mixture, grad_mixture, cosine, sine, tile, back_block
    )
    (grad_query, up_sum, down_sum, result_in, middle_in, grad_out) = lax.optimization_barrier(
        (grad_query, up_sum, down_sum, result_in, middle_in, grad_out)
    )
    part, grad_qkv, lines, vectors, pieces, grad_out, block_out = entry_back_call(
        grad_query,
        grad_key,
        grad_value,
        hat_t,
        scaling,
        gain_column,
        shift_column,
        qkv,
        grad_middle,
        middle_in,
        small,
        up_sum,
        down_sum,
        grad_out,
        result,
        result_in,
        groups=fsdp,
        tile=tile,
    )
    pieces = pieces.transpose(1, 0, 2, 3)
    pieces = pieces.reshape(2, depth // fsdp, part_width).astype(f32)
    grad_w_up = pieces[0]
    grad_w_down = pieces[1].T
    grad_w_out = grad_out
    embedded = lines[6]
    choose = (embedded[:, cond].astype(jnp.int32)[:, None] == numbers[None, :]).astype(f32)
    embedding, silu_back = jax.vjp(jax.nn.silu, embedded[:, :cond])
    scale_columns = [slice(k * depth, (k + 1) * depth) for k in (1, 4)]
    scales_one, scales_two = (
        exact_product(embedding, ada_full[:, columns]) + ada_b[columns].astype(f32)
        for columns in scale_columns
    )
    grad_b_up = vectors[:tensor].reshape(-1)
    grad_b_down = vectors[tensor]
    grad_gain_one = jnp.sum(lines[1] * (1.0 + scales_one), axis=0)
    grad_gain_two = jnp.sum(lines[4] * (1.0 + scales_two), axis=0)
    part = part.transpose(0, 1, 3, 2).reshape(sequences, own_rows, depth // tensor)
    grad_tokens = part.astype(f32)
    grad_w_qkv = (
        grad_qkv.reshape(-1, 3, heads, HDIM).transpose(0, 2, 1, 3).reshape(-1, 3 * group)
    )
    grad_mod = jnp.concatenate(
        [lines[0], lines[1] * gain_first, lines[2], lines[3], lines[4] * gain_second, lines[5]], axis=1
    )
    grad_ada_b = jnp.sum(grad_mod, axis=0)
    grad_ada_w = exact_transposed(embedding, grad_mod)
    grad_before = silu_back(exact_against(grad_mod, ada_full))[0]
    grad_table = exact_transposed(choose, grad_before)
    return (
        block_out,
        grad_tokens,
        grad_table,
        grad_ada_w,
        grad_ada_b,
        grad_gain_one,
        grad_w_qkv,
        grad_w_out,
        grad_gain_two,
        grad_w_up,
        grad_b_up,
        grad_w_down,
        grad_b_down,
    )


def normalize(operand):
    center = operand - jnp.mean(operand, axis=-1, keepdims=True)
    scaling = lax.rsqrt(jnp.mean(center * center, axis=-1, keepdims=True) + 1e-05)
    return (center * scaling, scaling)


def norm_back(grad_hat, hatted, scaling):
    return scaling * (
        grad_hat
        - jnp.mean(grad_hat, axis=-1, keepdims=True)
        - hatted * jnp.mean(grad_hat * hatted, axis=-1, keepdims=True)
    )


def angles_of(offsets, half_width):
    frequency = 10000.0 ** (-jnp.arange(half_width, dtype=jnp.float32) / half_width)
    angles = offsets.astype(jnp.float32)[:, None] * frequency[None, :]
    return (jnp.cos(angles)[:, None, :], jnp.sin(angles)[:, None, :])


def rotate(operand, cosine, sine_part, direction):
    half_width = operand.shape[-1] // 2
    front_half = operand[..., :half_width]
    second = operand[..., half_width:]
    return jnp.concatenate(
        [
            front_half * cosine - direction * second * sine_part,
            direction * front_half * sine_part + second * cosine,
        ],
        axis=-1,
    )


def scores_of(queries, key_rows, allowed):
    raw_scores = (
        jnp.einsum("qhd,khd->hqk", queries, key_rows, preferred_element_type=jnp.float32) * 0.125
    )
    return jnp.where(allowed[None], raw_scores, -1e30)


def attend(queries, key_rows, values, allowed):
    scores = scores_of(queries, key_rows, allowed)
    row_max = jnp.max(scores, axis=-1, keepdims=True)
    weights_raw = jnp.exp(scores - row_max)
    row_total = jnp.sum(weights_raw, axis=-1, keepdims=True)
    weights_low = (weights_raw / row_total).astype(jnp.bfloat16)
    mixture = jnp.einsum("hqk,khd->qhd", weights_low, values, preferred_element_type=jnp.float32)
    return (mixture, row_max + jnp.log(row_total))


def attend_back(queries, key_rows, values, grad_mixture, logsum, allowed, row_delta):
    scores = scores_of(queries, key_rows, allowed)
    chances = jnp.exp(scores - logsum)
    grad_chances = jnp.einsum(
        "qhd,khd->hqk", grad_mixture, values, preferred_element_type=jnp.float32
    )
    row_delta = jnp.sum(chances * grad_chances, axis=-1, keepdims=True)
    grad_scores = (chances * (grad_chances - row_delta)).astype(jnp.bfloat16)
    return (chances.astype(jnp.bfloat16), grad_scores, row_delta)


def by_block(
    tokens,
    cotangent,
    segments,
    steps,
    table,
    ada_w,
    ada_b,
    gain_one,
    w_qkv,
    w_out,
    gain_two,
    w_up,
    b_up,
    w_down,
    b_down,
):
    w_qkv, w_up, w_out, w_down = (
        lax.all_gather(w_qkv, "fsdp", axis=0, tiled=True),
        lax.all_gather(w_up, "fsdp", axis=0, tiled=True),
        lax.all_gather(w_out, "fsdp", axis=1, tiled=True),
        lax.all_gather(w_down, "fsdp", axis=1, tiled=True),
    )
    tensor_rank = lax.axis_index("tensor")
    context_rank = lax.axis_index("context")
    sequences, own_rows, model_width = tokens.shape
    length = segments.shape[1]
    local_heads = w_out.shape[0] // HDIM
    hidden_width = w_up.shape[1]
    up_bias = lax.dynamic_slice_in_dim(b_up, tensor_rank * hidden_width, hidden_width).astype(
        jnp.float32
    )
    down_bias = b_down.astype(jnp.float32)
    gain_first = gain_one.astype(jnp.float32)
    gain_second = gain_two.astype(jnp.float32)
    leader = (tensor_rank == 0).astype(jnp.float32)
    ada_full = ada_w.astype(jnp.float32)
    choose = (steps[:, None] == jnp.arange(table.shape[0], dtype=jnp.int32)[None, :]).astype(
        jnp.float32
    )
    before = exact_product(choose, table.astype(jnp.float32))
    embedding, silu_back = jax.vjp(jax.nn.silu, before)
    modulation = exact_product(embedding, ada_full) + ada_b.astype(jnp.float32)
    grad_qkv = jnp.zeros(w_qkv.shape, jnp.float32)
    grad_out_w = jnp.zeros(w_out.shape, jnp.float32)
    grad_up = jnp.zeros(w_up.shape, jnp.float32)
    grad_down = jnp.zeros(w_down.shape, jnp.float32)
    grad_bias_up = jnp.zeros((hidden_width,), jnp.float32)
    grad_bias_down = jnp.zeros((model_width,), jnp.float32)
    grad_gain_first = jnp.zeros((model_width,), jnp.float32)
    grad_gain_second = jnp.zeros((model_width,), jnp.float32)
    results = []
    partial_inputs = []
    carried = []
    grad_mods = []
    for number in range(sequences):
        shift_one, scale_one, gate_one, shift_two, scale_two, gate_two = jnp.split(
            modulation[number], 6
        )
        segment = segments[number]
        offsets = positions(segment)
        own_segment = lax.dynamic_slice_in_dim(segment, context_rank * own_rows, own_rows)
        own_offsets = lax.dynamic_slice_in_dim(offsets, context_rank * own_rows, own_rows)
        cosine, sine_part = angles_of(own_offsets, HDIM // 2)
        allowed = own_segment[:, None] == segment[None, :]
        inputs_row = tokens[number].astype(jnp.float32)
        hat_one, scaling_one = normalize(inputs_row)
        lifted_one = hat_one * gain_first
        entry_one = (lifted_one * (1.0 + scale_one) + shift_one).astype(jnp.bfloat16)
        projected = product(entry_one, w_qkv).reshape(own_rows, local_heads, 3, HDIM)
        queries = rotate(projected[:, :, 0], cosine, sine_part, 1.0).astype(jnp.bfloat16)
        key_rows = rotate(projected[:, :, 1], cosine, sine_part, 1.0).astype(jnp.bfloat16)
        values = projected[:, :, 2].astype(jnp.bfloat16)
        key_value = jnp.stack([key_rows, values], axis=1).reshape(own_rows, 2 * local_heads * HDIM)
        gathered = lax.all_gather(key_value, "context", axis=0, tiled=True).reshape(
            length, 2, local_heads, HDIM
        )
        all_keys = gathered[:, 0]
        all_values = gathered[:, 1]
        mixture, logsum = attend(queries, all_keys, all_values, allowed)
        mixture_low = mixture.reshape(own_rows, local_heads * HDIM).astype(jnp.bfloat16)
        attended = lax.psum(product(mixture_low, w_out).astype(jnp.bfloat16), "tensor").astype(
            jnp.float32
        )
        middle = inputs_row + gate_one * attended
        hat_two, scaling_two = normalize(middle)
        lifted_two = hat_two * gain_second
        entry_two = (lifted_two * (1.0 + scale_two) + shift_two).astype(jnp.bfloat16)
        hidden = product(entry_two, w_up) + up_bias
        activated, gelu_back = jax.vjp(partial(jax.nn.gelu, approximate=True), hidden)
        activated_low = activated.astype(jnp.bfloat16)
        output = (
            lax.psum(product(activated_low, w_down).astype(jnp.bfloat16), "tensor").astype(
                jnp.float32
            )
            + down_bias
        )
        results.append((middle + gate_two * output).astype(jnp.bfloat16))
        valid = (own_segment != 0).astype(jnp.float32)[:, None]
        grad_result = cotangent[number].astype(jnp.float32) * valid
        grad_output = (gate_two * grad_result).astype(jnp.bfloat16)
        grad_gate_two = jnp.sum(grad_result * output, axis=0)
        grad_bias_down = grad_bias_down + jnp.sum(grad_output.astype(jnp.float32), axis=0)
        grad_down = grad_down + transposed(activated_low, grad_output)
        grad_active = against(grad_output, w_down)
        grad_hidden = gelu_back(grad_active)[0].astype(jnp.bfloat16)
        grad_bias_up = grad_bias_up + jnp.sum(grad_hidden.astype(jnp.float32), axis=0)
        grad_up = grad_up + transposed(entry_two, grad_hidden)
        grad_entry_two = against(grad_hidden, w_up)
        grad_shift_two = jnp.sum(grad_entry_two, axis=0)
        grad_scale_two = jnp.sum(grad_entry_two * lifted_two, axis=0)
        grad_lifted_two = grad_entry_two * (1.0 + scale_two)
        grad_gain_second = grad_gain_second + jnp.sum(grad_lifted_two * hat_two, axis=0)
        part_two = norm_back(grad_lifted_two * gain_second, hat_two, scaling_two)
        grad_middle = grad_result + lax.psum(part_two.astype(jnp.bfloat16), "tensor").astype(
            jnp.float32
        )
        grad_attended = (gate_one * grad_middle).astype(jnp.bfloat16)
        grad_gate_one = jnp.sum(grad_middle * attended, axis=0)
        grad_out_w = grad_out_w + transposed(mixture_low, grad_attended)
        grad_mixture = (
            against(grad_attended, w_out).astype(jnp.bfloat16).reshape(own_rows, local_heads, HDIM)
        )
        chances_low, grad_scores, row_delta = attend_back(
            queries, all_keys, all_values, grad_mixture, logsum, allowed, None
        )
        grad_queries = (
            jnp.einsum("hqk,khd->qhd", grad_scores, all_keys, preferred_element_type=jnp.float32)
            * 0.125
        )
        grad_all_keys = (
            jnp.einsum("hqk,qhd->khd", grad_scores, queries, preferred_element_type=jnp.float32)
            * 0.125
        )
        grad_all_values = jnp.einsum(
            "hqk,qhd->khd", chances_low, grad_mixture, preferred_element_type=jnp.float32
        )
        both_grads = jnp.stack([grad_all_keys, grad_all_values], axis=1).reshape(
            length, 2 * local_heads * HDIM
        )
        own_grads = (
            lax.psum_scatter(
                both_grads.astype(jnp.bfloat16), "context", scatter_dimension=0, tiled=True
            )
            .astype(jnp.float32)
            .reshape(own_rows, 2, local_heads, HDIM)
        )
        grad_keys = own_grads[:, 0]
        grad_values = own_grads[:, 1]
        grad_queries = rotate(grad_queries, cosine, sine_part, -1.0)
        grad_keys = rotate(grad_keys, cosine, sine_part, -1.0)
        grad_projected = (
            jnp.stack([grad_queries, grad_keys, grad_values], axis=2)
            .reshape(own_rows, local_heads * 3 * HDIM)
            .astype(jnp.bfloat16)
        )
        grad_qkv = grad_qkv + transposed(entry_one, grad_projected)
        grad_entry_one = against(grad_projected, w_qkv)
        grad_shift_one = jnp.sum(grad_entry_one, axis=0)
        grad_scale_one = jnp.sum(grad_entry_one * lifted_one, axis=0)
        grad_lifted_one = grad_entry_one * (1.0 + scale_one)
        grad_gain_first = grad_gain_first + jnp.sum(grad_lifted_one * hat_one, axis=0)
        partial_inputs.append(norm_back(grad_lifted_one * gain_first, hat_one, scaling_one))
        carried.append(grad_middle)
        grad_mods.append(
            jnp.concatenate(
                [
                    grad_shift_one,
                    grad_scale_one,
                    grad_gate_one * leader,
                    grad_shift_two,
                    grad_scale_two,
                    grad_gate_two * leader,
                ]
            )
        )
    summed_inputs = lax.psum_scatter(
        jnp.stack(partial_inputs).astype(jnp.bfloat16), "tensor", scatter_dimension=2, tiled=True
    ).astype(jnp.float32)
    slice_width = model_width // lax.axis_size("tensor")
    own_middle = lax.dynamic_slice_in_dim(
        jnp.stack(carried), tensor_rank * slice_width, slice_width, axis=2
    )
    grad_tokens = summed_inputs + own_middle
    grad_mod = jnp.stack(grad_mods)
    bias_up_full = lax.dynamic_update_slice_in_dim(
        jnp.zeros((b_up.shape[0],), jnp.float32), grad_bias_up, tensor_rank * hidden_width, 0
    )
    grad_qkv, grad_up, grad_out_w, grad_down = (
        lax.psum_scatter(
            grad_qkv.astype(jnp.bfloat16), "fsdp", scatter_dimension=0, tiled=True
        ).astype(jnp.float32),
        lax.psum_scatter(
            grad_up.astype(jnp.bfloat16), "fsdp", scatter_dimension=0, tiled=True
        ).astype(jnp.float32),
        lax.psum_scatter(
            grad_out_w.astype(jnp.bfloat16), "fsdp", scatter_dimension=1, tiled=True
        ).astype(jnp.float32),
        lax.psum_scatter(
            grad_down.astype(jnp.bfloat16), "fsdp", scatter_dimension=1, tiled=True
        ).astype(jnp.float32),
    )
    grad_qkv, grad_up, grad_out_w, grad_down = (
        lax.psum(grad_qkv.astype(jnp.bfloat16), "context").astype(jnp.float32),
        lax.psum(grad_up.astype(jnp.bfloat16), "context").astype(jnp.float32),
        lax.psum(grad_out_w.astype(jnp.bfloat16), "context").astype(jnp.float32),
        lax.psum(grad_down.astype(jnp.bfloat16), "context").astype(jnp.float32),
    )
    grad_ada_b = jnp.sum(grad_mod, axis=0)
    grad_ada_w = exact_transposed(embedding, grad_mod)
    grad_embedding = exact_against(grad_mod, ada_full)
    grad_before = silu_back(grad_embedding)[0]
    grad_table = exact_transposed(choose, grad_before)
    (
        grad_table,
        grad_ada_w,
        grad_ada_b,
        grad_gain_first,
        grad_gain_second,
        bias_up_full,
        grad_bias_down,
    ) = lax.psum(
        (
            grad_table,
            grad_ada_w,
            grad_ada_b,
            grad_gain_first,
            grad_gain_second,
            bias_up_full,
            grad_bias_down * leader,
        ),
        ("fsdp", "context", "tensor"),
    )
    return (
        jnp.stack(results),
        grad_tokens,
        grad_table,
        grad_ada_w,
        grad_ada_b,
        grad_gain_first,
        grad_qkv,
        grad_out_w,
        grad_gain_second,
        grad_up,
        bias_up_full,
        grad_down,
        grad_bias_down,
    )


def solution(mesh):
    axes = dict(zip(mesh.axis_names, mesh.devices.shape))

    def whole(tokens, *others):
        sequences = tokens.shape[0] // axes["fsdp"]
        local = by_sequence if sequences == axes["context"] == 2 and axes["tensor"] == 4 else by_block
        return mapped(local, mesh)(tokens, *others)

    return whole


def mapped(local, mesh):
    return jax.shard_map(
        local,
        mesh=mesh,
        in_specs=(
            P("fsdp", "context", None),
            P("fsdp", "context", None),
            P("fsdp", None),
            P("fsdp"),
            P(),
            P(),
            P(),
            P(),
            P("fsdp", "tensor"),
            P("tensor", "fsdp"),
            P(),
            P("fsdp", "tensor"),
            P(),
            P("tensor", "fsdp"),
            P(),
        ),
        out_specs=(
            P("fsdp", "context", None),
            P("fsdp", "context", "tensor"),
            P(),
            P(),
            P(),
            P(),
            P("fsdp", "tensor"),
            P("tensor", "fsdp"),
            P(),
            P("fsdp", "tensor"),
            P(),
            P("tensor", "fsdp"),
            P(),
        ),
        check_vma=False,
    )
```

```python
import math
from functools import partial

import jax
import jax.numpy as jnp
from jax import lax
from jax.experimental import pallas as pl
from jax.experimental.pallas import tpu as pltpu
from jax.sharding import PartitionSpec as P

HDIM = 64
HALF = HDIM // 2
SEGMENTS = 5
WIDE = 128
MASKED = 2.0**100
LOG2E = math.log2(math.e)
SAFE_EXPONENT = 60.0
EPSILON = 1e-05
VMEM = 56 * 2**20
PART_TILES = 2
PART_CUTS = 1
VMEM_MOST = 60 * 2**20


def cost(flops, *arrays):
    size = sum(math.prod(one.shape) * one.dtype.itemsize for one in arrays)
    return pl.CostEstimate(flops=int(flops), bytes_accessed=int(size), transcendentals=0)


precise = lax.Precision.HIGHEST
f32 = jnp.float32
bf16 = jnp.bfloat16


def product(left_side, right_side):
    return jnp.dot(left_side, right_side, preferred_element_type=jnp.float32)


def transposed(left_side, right_side):
    return lax.dot_general(
        left_side, right_side, (((0,), (0,)), ((), ())), preferred_element_type=jnp.float32
    )


def against(left_side, right_side):
    return lax.dot_general(
        left_side, right_side, (((1,), (1,)), ((), ())), preferred_element_type=jnp.float32
    )


def exact_product(left_side, right_side):
    return jnp.dot(left_side, right_side, precision=precise, preferred_element_type=jnp.float32)


def exact_transposed(left_side, right_side):
    return lax.dot_general(
        left_side,
        right_side,
        (((0,), (0,)), ((), ())),
        precision=precise,
        preferred_element_type=jnp.float32,
    )


def exact_against(left_side, right_side):
    return lax.dot_general(
        left_side,
        right_side,
        (((1,), (1,)), ((), ())),
        precision=precise,
        preferred_element_type=jnp.float32,
    )


def document_bounds(segment):
    indices = jnp.arange(segment.shape[-1], dtype=jnp.int32)
    same = segment[..., None, :] == jnp.arange(SEGMENTS, dtype=jnp.int32)[:, None]
    starts = jnp.min(jnp.where(same, indices, segment.shape[-1]), axis=-1)
    ends = jnp.max(jnp.where(same, indices + 1, 0), axis=-1)
    return same, starts, ends


def positions(segment):
    same, starts, _ = document_bounds(segment)
    first = jnp.sum(jnp.where(same, starts[..., :, None], 0), axis=-2)
    return jnp.arange(segment.shape[-1], dtype=jnp.int32) - first


def frequencies():
    return 10000.0 ** (-jnp.arange(HALF, dtype=jnp.float32) / HALF)


def copy_to(source, target, sent, arrived, **device):
    return pltpu.make_async_remote_copy(
        src_ref=source,
        dst_ref=target,
        send_sem=sent,
        recv_sem=arrived,
        device_id=device,
        device_id_type=pl.DeviceIdType.MESH,
    )


def greet(devices):
    barrier = pltpu.get_barrier_semaphore()
    for device in devices:
        pl.semaphore_signal(barrier, inc=1, device_id=device, device_id_type=pl.DeviceIdType.MESH)
    pl.semaphore_wait(barrier, len(devices))


def quarter_at(number, tensor):
    core = lax.rem(tensor, 2)
    chip = jnp.where(number < 2, tensor // 2, 1 - tensor // 2)
    return chip * 2 + jnp.where(lax.rem(number, 2) == 0, core, 1 - core)


def entry_kernel(
    tokens_ref,
    rows_ref,
    shard_ref,
    own_forward_ref,
    gain_ref,
    shift_ref,
    cosine_ref,
    sine_ref,
    segment_ref,
    query_ref,
    key_ref,
    key_t_ref,
    value_t_ref,
    hat_ref,
    scale_ref,
    norm_ref,
    weight_ref,
    forward_ref,
    shards,
    weight_t,
    rows,
    arrived,
    sent_shard,
    got_shard,
    own_shard,
    sent_block,
    got_block,
    sent_across,
    got_across,
    sent_sibling,
    got_sibling,
    sent_on,
    got_on,
    sent_forward,
    got_forward,
    own_forward,
    *,
    heads,
    groups,
):
    step = pl.program_id(0)
    fsdp, context, tensor = (lax.axis_index(name) for name in ("fsdp", "context", "tensor"))
    ranks = 4
    core = lax.rem(tensor, 2)
    sibling = tensor + 1 - 2 * core
    across = lax.rem(tensor + 2, ranks)
    quarter = rows.shape[0]
    chunks = sent_block.shape[0]
    height = quarter // chunks

    def shard_copy(away):
        return copy_to(
            shard_ref,
            shards.at[fsdp],
            sent_shard.at[away - 1],
            got_shard.at[away - 1],
            fsdp=lax.rem(fsdp + away, groups),
        )

    def shard_own():
        return pltpu.make_async_copy(shard_ref, shards.at[fsdp], own_shard)

    def chunk(rank, number):
        return arrived.at[rank, pl.ds(number * height, height), :]

    def block_copy(number):
        at = pl.multiple_of(tensor * quarter, quarter) + number * height
        return copy_to(
            tokens_ref.at[1 - context, pl.ds(at, height), :],
            chunk(tensor, number),
            sent_block.at[number],
            got_block.at[number],
            context=1 - context,
        )

    def across_copy(number):
        return copy_to(
            chunk(tensor, number),
            chunk(tensor, number),
            sent_across.at[number],
            got_across.at[number],
            tensor=across,
        )

    def sibling_copy(number):
        return copy_to(
            chunk(tensor, number),
            chunk(tensor, number),
            sent_sibling.at[number],
            got_sibling.at[number],
            tensor=sibling,
        )

    def on_copy(number):
        return copy_to(
            chunk(across, number),
            chunk(across, number),
            sent_on.at[number],
            got_on.at[number],
            tensor=sibling,
        )

    forward_rows = own_forward_ref.shape[0]

    def forward_place(rank):
        return forward_ref.at[pl.ds(pl.multiple_of(rank * forward_rows, forward_rows), forward_rows), :]

    def relay_copy(origin, upward):
        place = forward_place(origin)
        side = 0 if upward else 1
        return copy_to(
            place,
            place,
            sent_forward.at[side, origin],
            got_forward.at[origin],
            fsdp=fsdp + 1 if upward else fsdp - 1,
        )

    def forward_own():
        return pltpu.make_async_copy(own_forward_ref, forward_place(fsdp), own_forward)

    def relay(origin, upward):
        @pl.when(fsdp < groups - 1 if upward else fsdp > 0)
        def _():
            relay_copy(origin, upward).start()

    def from_below(distance, act):
        @pl.when(fsdp >= distance)
        def _():
            act(fsdp - distance, True)

    def from_above(distance, act):
        @pl.when(fsdp + distance < groups)
        def _():
            act(fsdp + distance, False)

    def hand_over(distance):
        def act(origin, upward):
            relay_copy(origin, upward).wait_recv()
            relay(origin, upward)

        from_below(distance, act)
        from_above(distance, act)

    def finish_forward():
        def sent(origin, upward):
            @pl.when(fsdp < groups - 1 if upward else fsdp > 0)
            def _():
                relay_copy(origin, upward).wait_send()

        sent(fsdp, True)
        sent(fsdp, False)
        for distance in range(1, groups):
            from_below(distance, sent)
            from_above(distance, sent)

    def take(numbers):
        for number in numbers:
            block_copy(number).wait_recv()
            across_copy(number).start()
            sibling_copy(number).start()

    def pass_on(numbers):
        for number in numbers:
            across_copy(number).wait_recv()
            on_copy(number).start()

    @pl.when(step == 0)
    def _():
        shard_own().start()
        greet(
            [{"fsdp": lax.rem(fsdp + away, groups)} for away in range(1, groups)]
            + [{"context": 1 - context}, {"tensor": sibling}, {"tensor": across}]
        )
        for away in range(1, groups):
            shard_copy(away).start()
        for number in range(chunks):
            block_copy(number).start()
        forward_own().start()
        take(range(chunks - 1))
        shard_own().wait()
        for away in range(1, groups):
            shard_copy(away).wait_recv()
        for number in range(groups):
            weight_ref[number * shards.shape[1] : (number + 1) * shards.shape[1], :] = shards[number]
        forward_own().wait()
        relay(fsdp, True)
        relay(fsdp, False)
        weight_t[...] = weight_ref[...].T

    @pl.when(step == 1)
    def _():
        take([chunks - 1])
        pass_on(range(chunks // 2))

    @pl.when(step == 2)
    def _():
        pass_on(range(chunks // 2, chunks))

    half = 4

    for distance in range(1, groups):

        @pl.when(step == 1 + 2 * distance)
        def _():
            hand_over(distance)

    @pl.when(step < half)
    def _():
        rows[...] = rows_ref[0]

    @pl.when(step == half + 1)
    def _():
        for number in range(chunks):
            sibling_copy(number).wait_recv()

    @pl.when(step == half + 3)
    def _():
        for number in range(chunks):
            on_copy(number).wait_recv()

    @pl.when(step >= half)
    def _():
        rows[...] = arrived[quarter_at(step - half, tensor)]

    inputs = rows[...].astype(f32).T
    center = inputs - jnp.mean(inputs, axis=0, keepdims=True)
    scaling = lax.rsqrt(jnp.mean(center * center, axis=0, keepdims=True) + EPSILON)
    hat = center * scaling
    hat_ref[...] = hat.astype(bf16)
    scale_ref[...] = scaling
    entry = (hat * gain_ref[...] + shift_ref[...]).astype(bf16)
    projected = product(weight_t[...], entry)
    cosine = cosine_ref[...]
    sine = sine_ref[...]
    tokens = cosine.shape[1]
    group = heads * HDIM
    segment = segment_ref[...]
    number = lax.broadcasted_iota(jnp.int32, (WIDE - HDIM, tokens), 0)
    same = (number == segment).astype(f32)
    extra_query = same
    extra_key = jnp.where(
        number < SEGMENTS, (same - 1.0) * MASKED, jnp.where(number < SEGMENTS + 3, 1.0, 0.0)
    )
    extra_value = jnp.where(number < 3, 1.0, 0.0)
    norms = []
    for head in range(heads):

        def turned(kind, factor):
            at = kind * group + head * HDIM
            front = projected[at : at + HALF]
            back = projected[at + HALF : at + HDIM]
            return jnp.concatenate(
                [(front * cosine - back * sine) * factor, (front * sine + back * cosine) * factor],
                axis=0,
            )

        queries = turned(0, 0.125 * LOG2E)
        keys = turned(1, 1.0)
        values = projected[2 * group + head * HDIM : 2 * group + (head + 1) * HDIM]
        norms.append(jnp.sum(queries * queries, axis=0, keepdims=True))
        norms.append(jnp.sum(keys * keys, axis=0, keepdims=True))
        query_ref[head] = jnp.concatenate([queries, extra_query], axis=0).astype(bf16)
        wide_keys = jnp.concatenate([keys, extra_key], axis=0)
        key_ref[head] = wide_keys.T.astype(bf16)
        key_t_ref[head] = wide_keys.astype(bf16)
        value_t_ref[head] = jnp.concatenate([values, extra_value], axis=0).astype(bf16)
    norms += [jnp.zeros_like(norms[0])] * (norm_ref.shape[0] - len(norms))
    norm_ref[...] = jnp.concatenate(norms, axis=0)

    @pl.when(step == pl.num_programs(0) - 1)
    def _():
        for away in range(1, groups):
            shard_copy(away).wait_send()
        for number in range(chunks):
            block_copy(number).wait_send()
            across_copy(number).wait_send()
            sibling_copy(number).wait_send()
            on_copy(number).wait_send()
        finish_forward()


def entry_call(tokens, shard, forward_shard, gain, shift, cosine, sine, segment, groups, tile):
    length = cosine.shape[1]
    shard_rows, width = shard.shape
    depth = shard_rows * groups
    heads = width // (3 * HDIM)
    half = tokens.shape[1] // tile
    chunks = 4

    def place(i):
        context = lax.axis_index("context")
        other = (1 - context) * half + quarter_at(jnp.maximum(i - half, 0), lax.axis_index("tensor"))
        return jnp.where(i < half, context * half + i, other)

    lanes = lambda i: (0, place(i))
    heads_lanes = lambda i: (0, 0, place(i))
    heads_rows = lambda i: (0, place(i), 0)
    whole = lambda i: (0, 0)
    shapes = [
        jax.ShapeDtypeStruct((heads, WIDE, length), bf16),
        jax.ShapeDtypeStruct((heads, length, WIDE), bf16),
        jax.ShapeDtypeStruct((heads, WIDE, length), bf16),
        jax.ShapeDtypeStruct((heads, WIDE, length), bf16),
        jax.ShapeDtypeStruct((depth, length), bf16),
        jax.ShapeDtypeStruct((1, length), f32),
        jax.ShapeDtypeStruct((8, length), f32),
        jax.ShapeDtypeStruct((depth, width), bf16),
        jax.ShapeDtypeStruct((depth, forward_shard.shape[1]), bf16),
    ]
    dma = lambda *shape: [pltpu.SemaphoreType.DMA(shape)] * 2
    return pl.pallas_call(
        partial(entry_kernel, heads=heads, groups=groups),
        grid=(2 * half,),
        in_specs=[
            pl.BlockSpec(memory_space=pl.ANY),
            pl.BlockSpec(
                (1, tile, depth),
                lambda i: (lax.axis_index("context"), jnp.minimum(i, half - 1), 0),
            ),
            pl.BlockSpec(memory_space=pl.ANY),
            pl.BlockSpec(forward_shard.shape, whole),
            pl.BlockSpec((depth, 1), whole),
            pl.BlockSpec((depth, 1), whole),
            pl.BlockSpec((HALF, tile), lanes),
            pl.BlockSpec((HALF, tile), lanes),
            pl.BlockSpec((1, tile), lanes),
        ],
        out_specs=[
            pl.BlockSpec((heads, WIDE, tile), heads_lanes),
            pl.BlockSpec((heads, tile, WIDE), heads_rows),
            pl.BlockSpec((heads, WIDE, tile), heads_lanes),
            pl.BlockSpec((heads, WIDE, tile), heads_lanes),
            pl.BlockSpec((depth, tile), lanes),
            pl.BlockSpec((1, tile), lanes),
            pl.BlockSpec((8, tile), lanes),
            pl.BlockSpec((depth, width), whole),
            pl.BlockSpec(memory_space=pl.ANY),
        ],
        out_shape=shapes,
        scratch_shapes=[
            pltpu.VMEM((groups, shard_rows, width), bf16),
            pltpu.VMEM((width, depth), bf16),
            pltpu.VMEM((tile, depth), bf16),
            pltpu.VMEM((4, tile, depth), bf16),
            *dma(groups - 1),
            pltpu.SemaphoreType.DMA,
            *dma(chunks),
            *dma(chunks),
            *dma(chunks),
            *dma(chunks),
            pltpu.SemaphoreType.DMA((2, groups)),
            pltpu.SemaphoreType.DMA((groups,)),
            pltpu.SemaphoreType.DMA,
        ],
        compiler_params=pltpu.CompilerParams(
            vmem_limit_bytes=VMEM, collective_id=1, has_side_effects=True
        ),
        cost_estimate=cost(4 * tokens.shape[1] * depth * width, tokens, *shapes),
        name="entry",
    )(tokens, tokens, shard, forward_shard, gain, shift, cosine, sine, segment)


def attend_kernel(
    range_ref, query_ref, key_ref, value_ref, norm_ref, out_ref, told_ref, total_ref, top_ref, safe_ref, *, block
):
    step = pl.program_id(0)
    first, count = range_ref[0, step], range_ref[1, step]
    heads = query_ref.shape[0]
    total_ref[...] = jnp.zeros_like(total_ref)

    @pl.when(step == 0)
    def _():
        largest = 0.0
        for head in range(heads):
            queries, keys = norm_ref[2 * head : 2 * head + 1], norm_ref[2 * head + 1 : 2 * head + 2]
            largest = jnp.maximum(largest, jnp.max(queries) * jnp.max(keys))
        safe_ref[0] = (largest <= SAFE_EXPONENT**2).astype(jnp.int32)

    def scores(head, at):
        return product(key_ref[head, pl.ds(at, block), :], query_ref[head])

    def mix(head, at, weights):
        return product(value_ref[head, :, pl.ds(at, block)], weights)

    @pl.when(safe_ref[0] == 1)
    def _():
        top_ref[...] = jnp.zeros_like(top_ref)

        def body(number, carry):
            at = pl.multiple_of(first + number * block, WIDE)
            raw = [scores(head, at) for head in range(heads)]
            weights = [jnp.exp2(one).astype(bf16) for one in raw]
            for head in range(heads):
                total_ref[head] += mix(head, at, weights[head])
            return carry

        lax.fori_loop(0, count, body, 0)

    @pl.when(safe_ref[0] != 1)
    def _():
        top_ref[...] = jnp.full_like(top_ref, -3e38)

        def body(number, carry):
            at = pl.multiple_of(first + number * block, WIDE)
            for head in range(heads):
                raw = scores(head, at)
                before = top_ref[head]
                top = jnp.maximum(before, jnp.max(raw, axis=0, keepdims=True))
                weights = jnp.exp2(raw - top).astype(bf16)
                total_ref[head] = total_ref[head] * jnp.exp2(before - top) + mix(head, at, weights)
                top_ref[head] = top
            return carry

        lax.fori_loop(0, count, body, 0)

    tile = query_ref.shape[2]
    number = lax.broadcasted_iota(jnp.int32, (16, tile), 0)
    for head in range(heads):
        total = total_ref[head]
        mass = total[HDIM : HDIM + 1]
        out_ref[0, pl.ds(head * HDIM, HDIM), :] = (total[:HDIM] * (1.0 / mass)).astype(bf16)
        rows = split_rows(-(top_ref[head] + jnp.log2(mass)), number, SEGMENTS)
        told_ref[head, :HDIM, :] = query_ref[head, :HDIM, :]
        told_ref[head, HDIM : HDIM + 16, :] = jnp.where(
            number < SEGMENTS, query_ref[head, HDIM : HDIM + 16, :].astype(f32), rows
        ).astype(bf16)
        told_ref[head, HDIM + 16 :, :] = query_ref[head, HDIM + 16 :, :]


def split_rows(values, number, first):
    high = values.astype(bf16).astype(f32)
    rest = values - high
    middle = rest.astype(bf16).astype(f32)
    low = rest - middle
    return jnp.where(
        number == first,
        high,
        jnp.where(number == first + 1, middle, jnp.where(number == first + 2, low, 0.0)),
    )


def attend_call(ranges, queries, keys, values_t, norms, tile, block):
    heads, _, length = queries.shape
    rows = HDIM + 16
    return pl.pallas_call(
        partial(attend_kernel, block=block),
        grid_spec=pltpu.PrefetchScalarGridSpec(
            num_scalar_prefetch=1,
            grid=(length // tile,),
            in_specs=[
                pl.BlockSpec((heads, WIDE, tile), lambda i, r: (0, 0, i)),
                pl.BlockSpec((heads, length, WIDE), lambda i, r: (0, 0, 0)),
                pl.BlockSpec((heads, rows, length), lambda i, r: (0, 0, 0)),
                pl.BlockSpec(norms.shape, lambda i, r: (0, 0)),
            ],
            out_specs=[
                pl.BlockSpec((1, heads * HDIM, tile), lambda i, r: (i, 0, 0)),
                pl.BlockSpec((heads, WIDE, tile), lambda i, r: (0, 0, i)),
            ],
            scratch_shapes=[
                pltpu.VMEM((heads, rows, tile), f32),
                pltpu.VMEM((heads, 1, tile), f32),
                pltpu.SMEM((1,), jnp.int32),
            ],
        ),
        out_shape=[
            jax.ShapeDtypeStruct((length // tile, heads * HDIM, tile), bf16),
            jax.ShapeDtypeStruct((heads, WIDE, length), bf16),
        ],
        compiler_params=pltpu.CompilerParams(vmem_limit_bytes=VMEM),
        cost_estimate=cost(4 * heads * length * length * WIDE, queries, keys, values_t),
        name="attend",
    )(ranges, queries, keys, values_t, norms)


def attend_back_kernel(
    range_ref,
    query_ref,
    key_ref,
    value_ref,
    mixture_ref,
    grad_ref,
    cosine_ref,
    sine_ref,
    grad_query_ref,
    grad_key_ref,
    grad_value_ref,
    wide_ref,
    query_rows,
    grad_rows,
    query_total,
    key_total,
    value_total,
    *,
    block,
):
    step = pl.program_id(0)
    first, count = range_ref[0, step], range_ref[1, step]
    heads, _, tile = query_ref.shape

    @pl.when(step == 0)
    def _():
        wide_ref[...] = jnp.zeros_like(wide_ref)
        key_total[...] = jnp.zeros_like(key_total)
        value_total[...] = jnp.zeros_like(value_total)

    number = lax.broadcasted_iota(jnp.int32, (16, tile), 0)
    query_total[...] = jnp.zeros_like(query_total)
    for head in range(heads):
        at = pl.ds(head * HDIM, HDIM)
        grad = grad_ref[0, at, :]
        delta = jnp.sum(grad.astype(f32) * mixture_ref[0, at, :].astype(f32), axis=0, keepdims=True)
        wide_ref[head, :HDIM, :] = grad
        wide_ref[head, HDIM : HDIM + 16, :] = split_rows(-delta, number, 0).astype(bf16)
        query_rows[head] = query_ref[head].T
        grad_rows[head] = wide_ref[head].T

    def body(number, carry):
        at = pl.ds(pl.multiple_of(first + number * block, WIDE), block)
        raw = [product(query_rows[head], key_ref[head, :, at]) for head in range(heads)]
        slope = [product(grad_rows[head], value_ref[head, :, at]) for head in range(heads)]
        for head in range(heads):
            weights = jnp.exp2(raw[head])
            grad_scores = (weights * slope[head]).astype(bf16)
            value_total[head, :, at] += product(wide_ref[head, :HDIM, :], weights.astype(bf16))
            key_total[head, :, at] += product(query_ref[head, :HDIM, :], grad_scores)
            query_total[head] += against(key_ref[head, :HDIM, at], grad_scores)
        return carry

    lax.fori_loop(0, count, body, 0)

    def turned_back(grads, cosine, sine):
        front, back = grads[:HALF], grads[HALF:]
        return jnp.concatenate([front * cosine + back * sine, back * cosine - front * sine], axis=0)

    own = pl.ds(pl.multiple_of(step * tile, tile), tile)
    for head in range(heads):
        at = pl.ds(head * HDIM, HDIM)
        grad_query_ref[at, :] = turned_back(
            query_total[head] * 0.125, cosine_ref[:, own], sine_ref[:, own]
        ).astype(bf16)

    @pl.when(step == pl.num_programs(0) - 1)
    def _():
        for head in range(heads):
            at = pl.ds(head * HDIM, HDIM)
            grad_key_ref[at, :] = turned_back(
                key_total[head] * (1.0 / LOG2E), cosine_ref[...], sine_ref[...]
            ).astype(bf16)
            grad_value_ref[at, :] = value_total[head].astype(bf16)


def attend_back_call(
    ranges, queries, keys_t, values_t, mixture, grad_mixture, cosine, sine, tile, block
):
    heads, _, length = queries.shape
    group = heads * HDIM
    whole2 = lambda i, r: (0, 0)
    whole3 = lambda i, r: (0, 0, 0)
    return pl.pallas_call(
        partial(attend_back_kernel, block=block),
        grid_spec=pltpu.PrefetchScalarGridSpec(
            num_scalar_prefetch=1,
            grid=(length // tile,),
            in_specs=[
                pl.BlockSpec((heads, WIDE, tile), lambda i, r: (0, 0, i)),
                pl.BlockSpec((heads, WIDE, length), whole3),
                pl.BlockSpec((heads, WIDE, length), whole3),
                pl.BlockSpec((1, group, tile), lambda i, r: (i, 0, 0)),
                pl.BlockSpec((1, group, tile), lambda i, r: (i, 0, 0)),
                pl.BlockSpec((HALF, length), whole2),
                pl.BlockSpec((HALF, length), whole2),
            ],
            out_specs=[
                pl.BlockSpec((group, tile), lambda i, r: (0, i)),
                pl.BlockSpec((group, length), whole2),
                pl.BlockSpec((group, length), whole2),
            ],
            scratch_shapes=[
                pltpu.VMEM((heads, WIDE, tile), bf16),
                pltpu.VMEM((heads, tile, WIDE), bf16),
                pltpu.VMEM((heads, tile, WIDE), bf16),
                pltpu.VMEM((heads, HDIM, tile), f32),
                pltpu.VMEM((heads, HDIM, length), f32),
                pltpu.VMEM((heads, HDIM, length), f32),
            ],
        ),
        out_shape=[jax.ShapeDtypeStruct((group, length), bf16)] * 3,
        compiler_params=pltpu.CompilerParams(vmem_limit_bytes=VMEM),
        cost_estimate=cost(10 * heads * length * length * WIDE, queries, keys_t, values_t),
        name="attend_back",
    )(ranges, queries, keys_t, values_t, mixture, grad_mixture, cosine, sine)


def middle_kernel(
    mixture_ref,
    rows_ref,
    cotangent_ref,
    valid_ref,
    mod_ref,
    up_bias_ref,
    down_bias_ref,
    out_blocks_ref,
    own_ref,
    other_ref,
    across_ref,
    result_ref,
    grad_mixture_ref,
    grad_middle_ref,
    grad_out_blocks_ref,
    sums_ref,
    bias_sums_ref,
    up_keep_ref,
    up_send_ref,
    down_keep_ref,
    down_send_ref,
    own_mixture,
    out_weight_ref,
    grad_out_ref,
    entry_rows,
    entry_columns,
    grad_output_rows,
    grad_output_columns,
    attended_rows,
    output_rows,
    grad_entry_rows,
    active,
    grad_hidden,
    grad_staged,
    forward_ref,
    landed,
    home_grads,
    to_sibling,
    from_sibling,
    staged_up,
    staged_down,
    sent_mixture,
    got_mixture,
    own_copied,
    sent_grad,
    got_grad,
    grad_copied,
    sent_part,
    got_part,
    kept,
    sent_next,
    got_next,
    loaded,
    sent_other,
    got_other,
    sent_last,
    got_last,
    *,
    tile,
    tiles,
    parts,
    groups,
):
    step = pl.program_id(0)
    context, tensor = lax.axis_index("context"), lax.axis_index("tensor")
    ranks = 4
    everyone = 2 * ranks
    place = context * ranks + tensor
    core = lax.rem(tensor, 2)
    sibling = tensor + 1 - 2 * core
    depth = rows_ref.shape[2]
    group = depth // ranks
    per_sequence = tiles // 2
    part_tiles = tiles // PART_TILES
    per_part = part_tiles + 1
    back_from = tiles + parts * per_part - 1
    last_step = back_from + tiles
    root = math.sqrt(2.0 / math.pi)

    def member(away):
        other = lax.rem(place + away, everyone)
        return other, {"context": other // ranks, "tensor": lax.rem(other, ranks)}

    def mixture_copy(away):
        other, device = member(away)
        return copy_to(
            mixture_ref.at[other],
            own_mixture.at[place],
            sent_mixture.at[away - 1],
            got_mixture.at[lax.rem(place + everyone, everyone)],
            **device,
        )

    def mixture_arrival(source):
        return pltpu.make_async_remote_copy(
            src_ref=mixture_ref.at[source],
            dst_ref=own_mixture.at[source],
            send_sem=sent_mixture.at[0],
            recv_sem=got_mixture.at[source],
            device_id={"tensor": sibling},
            device_id_type=pl.DeviceIdType.MESH,
        )

    def own_copy():
        return pltpu.make_async_copy(mixture_ref.at[place], own_mixture.at[place], own_copied)

    def part_copy(slot):
        return copy_to(
            to_sibling, from_sibling.at[slot], sent_part.at[slot], got_part.at[slot], tensor=sibling
        )

    across = lax.rem(tensor + 2, ranks)
    height = depth // groups

    def rows_of(number):
        return pl.ds(number * height, height)

    def next_copy(kind):
        return copy_to(
            forward_ref.at[kind],
            landed.at[0, kind],
            sent_next.at[kind],
            got_next.at[kind],
            tensor=sibling,
        )

    def out_blocks():
        for rank in range(ranks):
            for number in range(groups):
                rows = slice(rank * group, (rank + 1) * group)
                yield rank * groups + number, (rows, slice(number * height, (number + 1) * height))

    def weight_loads():
        return [
            pltpu.make_async_copy(own_ref, forward_ref.at[context], loaded.at[0]),
            pltpu.make_async_copy(other_ref, forward_ref.at[1 - context], loaded.at[1]),
            pltpu.make_async_copy(across_ref, landed.at[1, context], loaded.at[2]),
        ]

    def other_copy(kind, number):
        place = landed.at[1, kind, rows_of(number), :]
        return copy_to(place, place, sent_other.at[number], got_other.at[number], context=1 - context)

    def last_copy(kind, number):
        return copy_to(
            landed.at[1, kind, rows_of(number), :],
            landed.at[2, kind, rows_of(number), :],
            sent_last.at[kind, number],
            got_last.at[kind, number],
            tensor=sibling,
        )

    def take_other(numbers):
        for number in numbers:
            other_copy(1 - context, number).wait_recv()
            last_copy(1 - context, number).start()

    def gradient_lanes(at):
        return pl.ds(pl.multiple_of(lax.rem(at, per_sequence) * tile, tile), tile)

    def sequence_of(at):
        return lax.rem(at // per_sequence + context, 2)

    def gradient_copy(at, rank):
        return copy_to(
            grad_staged.at[at, rank],
            grad_mixture_ref.at[place, :, gradient_lanes(at)],
            sent_grad.at[at, rank],
            got_grad.at[place, lax.rem(at, per_sequence)],
            context=sequence_of(at),
            tensor=rank,
        )

    def gradient_own(at):
        return pltpu.make_async_copy(
            grad_staged.at[at, tensor],
            grad_mixture_ref.at[place, :, gradient_lanes(at)],
            grad_copied.at[lax.rem(at, per_sequence)],
        )

    def gradient_arrival(source, number):
        return pltpu.make_async_remote_copy(
            src_ref=grad_staged.at[0, 0],
            dst_ref=grad_mixture_ref.at[source, :, pl.ds(number * tile, tile)],
            send_sem=sent_grad.at[0, 0],
            recv_sem=got_grad.at[source, number],
            device_id={"tensor": sibling},
            device_id_type=pl.DeviceIdType.MESH,
        )

    def kept_copies(slot):
        if slot == 1:
            return [
                pltpu.make_async_copy(staged_up, up_send_ref, kept.at[0]),
                pltpu.make_async_copy(staged_down.at[0], down_keep_ref.at[0], kept.at[1]),
                pltpu.make_async_copy(staged_down.at[1], down_send_ref.at[0], kept.at[2]),
            ]
        return [
            pltpu.make_async_copy(staged_up, up_keep_ref, kept.at[3]),
            pltpu.make_async_copy(staged_down.at[0], down_keep_ref.at[1], kept.at[4]),
            pltpu.make_async_copy(staged_down.at[1], down_send_ref.at[1], kept.at[5]),
        ]

    def tile_of(at):
        sequence = sequence_of(at)
        rows = pl.ds(pl.multiple_of(at * tile, tile), tile)
        mods = mod_ref[sequence]
        lanes = gradient_lanes(at)
        mixture_t = jnp.concatenate(
            [own_mixture[sequence * ranks + rank, :, lanes] for rank in range(ranks)], axis=0
        )
        return rows, mixture_t, tuple(mods[k : k + 1] for k in range(4))

    def normal(attended, gate_one):
        middle = rows_ref[0].astype(f32) + gate_one * attended
        center = middle - jnp.mean(middle, axis=-1, keepdims=True)
        scaling = lax.rsqrt(jnp.mean(center * center, axis=-1, keepdims=True) + EPSILON)
        return middle, center * scaling, scaling

    @pl.when(step == 0)
    def _():
        own_copy().start()
        for one in weight_loads():
            one.start()
        greet([member(away)[1] for away in range(1, everyone)])
        for near in (True, False):
            for away in range(1, everyone):

                @pl.when((member(away)[0] // ranks == context) == near)
                def _():
                    mixture_copy(away).start()

        for block, at in out_blocks():
            out_weight_ref[at] = out_blocks_ref[block]
        sums_ref[...] = jnp.zeros_like(sums_ref)
        bias_sums_ref[...] = jnp.zeros_like(bias_sums_ref)
        grad_out_ref[...] = jnp.zeros_like(grad_out_ref)

    for sequence in range(2):

        @pl.when(step == lax.rem(sequence + context, 2) * per_sequence)
        def _():
            for rank in range(ranks):
                source = sequence * ranks + rank

                @pl.when(place == source)
                def _():
                    own_copy().wait()

                @pl.when(place != source)
                def _():
                    mixture_arrival(source).wait_recv()

    @pl.when(step == per_sequence)
    def _():
        for one in weight_loads():
            one.wait()
        for kind in range(2):
            next_copy(kind).start()
        for number in range(groups):
            other_copy(context, number).start()
            last_copy(context, number).start()

    @pl.when(step == tiles + per_part)
    def _():
        for kind in range(2):
            next_copy(kind).wait_recv()

    @pl.when(step == tiles + 2 * per_part - 1)
    def _():
        take_other(range(groups // 2))

    @pl.when(step == tiles + 2 * per_part)
    def _():
        take_other(range(groups // 2, groups))

    @pl.when(step == tiles + 2 * per_part)
    def _():
        for kind in range(2):
            for number in range(groups):
                last_copy(kind, number).wait_recv()

    @pl.when(step < tiles)
    def _():
        rows, mixture_t, (gate_one, shift_two, gain_two, gate_two) = tile_of(step)
        attended = product(mixture_t.T, out_weight_ref[...])
        attended_rows[rows, :] = attended
        _, hat, _ = normal(attended, gate_one)
        entry = (hat * gain_two + shift_two).astype(bf16)
        grad_output = (gate_two * (cotangent_ref[0].astype(f32) * valid_ref[...])).astype(bf16)
        entry_rows[rows, :] = entry
        entry_columns[:, rows] = entry.T
        grad_output_rows[rows, :] = grad_output
        grad_output_columns[:, rows] = grad_output.T
        output_rows[rows, :] = jnp.broadcast_to(down_bias_ref[...], (tile, depth))
        grad_entry_rows[rows, :] = jnp.zeros((tile, depth), f32)

    inner = lax.rem(step - tiles, per_part)
    position = (step - tiles) // per_part
    in_parts = (step >= tiles) & (step < back_from)

    def part_tile(up, down):
        number = part_at(position, tensor)
        size = tile * PART_TILES // PART_CUTS
        for sub in range(PART_CUTS):
            rows = pl.ds(pl.multiple_of((inner * PART_CUTS + sub) * size, size), size)
            hidden = product(entry_rows[rows, :], up[...]) + up_bias_ref[0]
            square = hidden * hidden
            bent = jnp.tanh(root * hidden * (1.0 + 0.044715 * square))
            half = 0.5 * (1.0 + bent)
            activated = (hidden * half).astype(bf16)
            slope = half + (0.5 * root) * hidden * (1.0 - bent * bent) * (1.0 + 0.134145 * square)
            grads = (product(grad_output_rows[rows, :], down[...]) * slope).astype(bf16)
            output_rows[rows, :] += against(activated, down[...])
            grad_entry_rows[rows, :] += against(grads, up[...])
            active[rows, :] = activated
            grad_hidden[rows, :] = grads
            bias_sums_ref[number] += jnp.sum(grads.astype(f32), axis=0, keepdims=True)

    @pl.when(in_parts & (inner < part_tiles) & (position == 0))
    def _():
        part_tile(forward_ref.at[0], forward_ref.at[1])

    @pl.when(in_parts & (inner < part_tiles) & (position > 0))
    def _():
        place = lax.rem((position - 1) * 2, 3)
        part_tile(landed.at[place, 0], landed.at[place, 1])

    def products():
        both = [product(entry_columns[...], grad_hidden[...]), product(grad_output_columns[...], active[...])]
        return lambda other: [one[other * height : (other + 1) * height] for one in both]

    def kept_terms():
        return lambda other: [home_grads[kind, rows_of(other), :].astype(f32) for kind in range(2)]

    def gather_home(slot, own):
        part_copy(slot).wait_recv()
        if slot:
            for one in kept_copies(0):
                one.wait()
        terms = own()
        for other in range(groups):
            for kind, (staged, term) in enumerate(zip((staged_up, staged_down), terms(other))):
                total = (term + from_sibling[slot, kind, rows_of(other), :].astype(f32)).astype(bf16)
                staged[context, other] = total[: height // 2]
                staged[1 - context, other] = total[height // 2 :]
        for one in kept_copies(slot):
            one.start()

    for turn in range(parts):

        @pl.when(step == (tiles + turn * per_part + part_tiles if turn < parts - 1 else last_step))
        def _():
            if turn == 2:
                gather_home(0, kept_terms)
                part_copy(0).wait_send()
            if turn == 3:
                gather_home(1, products)
                return
            target = home_grads if turn == 0 else to_sibling
            terms = products()
            for other in range(groups):
                for kind, term in enumerate(terms(other)):
                    target[kind, rows_of(other), :] = term.astype(bf16)
            if turn:
                part_copy(turn - 1).start()

    @pl.when((step >= back_from) & (step < last_step))
    def _():
        at = lax.rem(step - back_from + per_sequence, tiles)
        sequence = sequence_of(at)
        rows, mixture_t, (gate_one, _, gain_two, gate_two) = tile_of(at)
        attended = attended_rows[rows, :]
        middle, hat, scaling = normal(attended, gate_one)
        output = output_rows[rows, :]
        grad_entry = grad_entry_rows[rows, :]
        grad_result = cotangent_ref[0].astype(f32) * valid_ref[...]
        result_ref[...] = (middle + gate_two * output).astype(bf16)
        grad_lifted = grad_entry * gain_two
        grad_middle = grad_result + scaling * (
            grad_lifted
            - jnp.mean(grad_lifted, axis=-1, keepdims=True)
            - hat * jnp.mean(grad_lifted * hat, axis=-1, keepdims=True)
        )
        grad_attended = (gate_one * grad_middle).astype(bf16)
        grad_mixture = against(out_weight_ref[...], grad_attended).astype(bf16)
        for rank in range(ranks):
            grad_staged[at, rank] = grad_mixture[rank * group : (rank + 1) * group]
        for rank in range(ranks):
            own = (sequence == context) & (tensor == rank)

            @pl.when(own)
            def _():
                gradient_own(at).start()

            @pl.when(jnp.logical_not(own))
            def _():
                gradient_copy(at, rank).start()

        grad_middle_ref[0] = grad_middle.T.astype(bf16)
        grad_out_ref[...] += product(mixture_t, grad_attended)
        lines = [
            jnp.sum(grad_middle * attended, axis=0, keepdims=True),
            jnp.sum(grad_entry, axis=0, keepdims=True),
            jnp.sum(grad_entry * hat, axis=0, keepdims=True),
            jnp.sum(grad_result * output, axis=0, keepdims=True),
            jnp.sum(grad_output_rows[rows, :].astype(f32), axis=0, keepdims=True),
        ]
        lines += [jnp.zeros_like(lines[0])] * (sums_ref.shape[1] - len(lines))
        sums_ref[sequence] += jnp.concatenate(lines, axis=0)

    @pl.when(step == last_step)
    def _():
        for block, at in out_blocks():
            grad_out_blocks_ref[block] = grad_out_ref[at].astype(bf16)
        for source in range(everyone):
            for number in range(per_sequence):

                @pl.when(place != source)
                def _():
                    gradient_arrival(source, number).wait_recv()

        for at in range(tiles):
            for rank in range(ranks):
                own = (sequence_of(at) == context) & (tensor == rank)

                @pl.when(own)
                def _():
                    gradient_own(at).wait()

                @pl.when(jnp.logical_not(own))
                def _():
                    gradient_copy(at, rank).wait_send()

        for away in range(1, everyone):
            mixture_copy(away).wait_send()
        for kind in range(2):
            next_copy(kind).wait_send()
        for number in range(groups):
            other_copy(context, number).wait_send()
            for kind in range(2):
                last_copy(kind, number).wait_send()
        part_copy(1).wait_send()
        for one in kept_copies(1):
            one.wait()


def part_at(position, tensor):
    return quarter_at(jnp.where(position < 2, position, 5 - position), tensor)


def middle_call(
    mixture, rows, cotangent, valid, mods, up_bias, down_bias, out_blocks, own_weight, other_weight, across, groups, tile
):
    pieces, group, own = mixture.shape
    depth = rows.shape[2]
    tokens = rows.shape[0] * own
    parts, _, part_width = up_bias.shape
    tiles = tokens // tile
    per_sequence = tiles // 2
    per_part = tiles // PART_TILES + 1
    back_from = tiles + parts * per_part - 1
    half = depth // groups // 2

    def in_order(at):
        sequence = lax.rem(at // per_sequence + lax.axis_index("context"), 2)
        return sequence, lax.rem(at, per_sequence)

    def back_number(i):
        return lax.rem(jnp.clip(i - back_from, 0, tiles - 1) + per_sequence, tiles)

    def token_place(i):
        return in_order(jnp.where(i < tiles, i, back_number(i)))

    def token_tile(i):
        sequence, number = token_place(i)
        return sequence, lax.axis_index("tensor") * per_sequence + number, 0

    def valid_tile(i):
        sequence, number = token_place(i)
        return sequence * per_sequence + number, 0

    def part_block(i):
        position = jnp.clip((i - tiles) // per_part, 0, parts - 1)
        return part_at(position, lax.axis_index("tensor")), 0, 0

    def back_tile(i):
        return in_order(back_number(i))

    whole2 = lambda i: (0, 0)
    whole3 = lambda i: (0, 0, 0)
    once = pl.Buffered(1)
    hbm = pl.BlockSpec(memory_space=pl.ANY)
    kept = jax.ShapeDtypeStruct((2, groups, half, part_width), bf16)
    wide = (tokens, depth)
    return pl.pallas_call(
        partial(middle_kernel, tile=tile, tiles=tiles, parts=parts, groups=groups),
        grid=(back_from + tiles + 1,),
        in_specs=[
            hbm,
            pl.BlockSpec((1, tile, depth), token_tile),
            pl.BlockSpec((1, tile, depth), token_tile),
            pl.BlockSpec((tile, 1), valid_tile),
            pl.BlockSpec(mods.shape, whole3, pipeline_mode=once),
            pl.BlockSpec((1, 1, part_width), part_block),
            pl.BlockSpec((1, depth), whole2, pipeline_mode=once),
            pl.BlockSpec(out_blocks.shape, whole3, pipeline_mode=once),
            hbm,
            hbm,
            hbm,
        ],
        out_specs=[
            pl.BlockSpec(
                (tile, depth), lambda i: (back_tile(i)[0] * per_sequence + back_tile(i)[1], 0)
            ),
            hbm,
            pl.BlockSpec(
                (1, depth, tile),
                lambda i: (back_tile(i)[0], 0, back_tile(i)[1]),
            ),
            pl.BlockSpec(out_blocks.shape, whole3),
            pl.BlockSpec((2, 8, depth), whole3),
            pl.BlockSpec((parts, 1, part_width), whole3),
            hbm,
            hbm,
            hbm,
            hbm,
        ],
        out_shape=[
            jax.ShapeDtypeStruct((tokens, depth), bf16),
            jax.ShapeDtypeStruct(mixture.shape, bf16),
            jax.ShapeDtypeStruct((2, depth, own), bf16),
            jax.ShapeDtypeStruct(out_blocks.shape, bf16),
            jax.ShapeDtypeStruct((2, 8, depth), f32),
            jax.ShapeDtypeStruct((parts, 1, part_width), f32),
            kept,
            kept,
            kept,
            kept,
        ],
        scratch_shapes=[
            pltpu.VMEM(mixture.shape, bf16),
            pltpu.VMEM((depth, depth), bf16),
            pltpu.VMEM((depth, depth), f32),
            pltpu.VMEM(wide, bf16),
            pltpu.VMEM((depth, tokens), bf16),
            pltpu.VMEM(wide, bf16),
            pltpu.VMEM((depth, tokens), bf16),
            pltpu.VMEM(wide, f32),
            pltpu.VMEM(wide, f32),
            pltpu.VMEM(wide, f32),
            pltpu.VMEM((tokens, part_width), bf16),
            pltpu.VMEM((tokens, part_width), bf16),
            pltpu.VMEM((tiles, 4, group, tile), bf16),
            pltpu.VMEM((2, depth, part_width), bf16),
            pltpu.VMEM((3, 2, depth, part_width), bf16),
            pltpu.VMEM((2, depth, part_width), bf16),
            pltpu.VMEM((2, depth, part_width), bf16),
            pltpu.VMEM((2, 2, depth, part_width), bf16),
            pltpu.VMEM((2, groups, half, part_width), bf16),
            pltpu.VMEM((2, groups, half, part_width), bf16),
            pltpu.SemaphoreType.DMA((pieces - 1,)),
            pltpu.SemaphoreType.DMA((pieces,)),
            pltpu.SemaphoreType.DMA,
            pltpu.SemaphoreType.DMA((tiles, 4)),
            pltpu.SemaphoreType.DMA((pieces, per_sequence)),
            pltpu.SemaphoreType.DMA((per_sequence,)),
            pltpu.SemaphoreType.DMA((2,)),
            pltpu.SemaphoreType.DMA((2,)),
            pltpu.SemaphoreType.DMA((6,)),
            *[pltpu.SemaphoreType.DMA((2,))] * 2,
            pltpu.SemaphoreType.DMA((3,)),
            *[pltpu.SemaphoreType.DMA((groups,))] * 2,
            *[pltpu.SemaphoreType.DMA((2, groups))] * 2,
        ],
        compiler_params=pltpu.CompilerParams(
            vmem_limit_bytes=VMEM_MOST, collective_id=2, has_side_effects=True
        ),
        cost_estimate=cost(6 * tokens * depth * (depth + 3 * parts * part_width), rows, rows, rows),
        name="middle",
    )(mixture, rows, cotangent, valid, mods, up_bias, down_bias, out_blocks, own_weight, other_weight, across)


class Relay:
    def __init__(self, own, out, arrived, sent, got, fsdp, groups):
        self.own, self.out, self.arrived, self.sent, self.got = own, out, arrived, sent, got
        self.fsdp, self.groups = fsdp, groups

    def copy(self, side, target):
        return copy_to(
            self.out.at[side, target],
            self.arrived.at[side, target],
            self.sent.at[side, target],
            self.got.at[side, target],
            fsdp=self.fsdp - 1 if side else self.fsdp + 1,
        )

    def begin(self, target):
        for side, end in ((0, 0), (1, self.groups - 1)):
            if target != end:

                @pl.when(self.fsdp == end)
                def _():
                    self.out[side, target] = self.own[target]
                    self.copy(side, target).start()

    def turn(self, number):
        last = self.groups - 1
        for side in range(2):
            behind = last - self.fsdp if side else self.fsdp

            @pl.when((behind >= 1) & (behind <= number))
            def _():
                target = self.fsdp + (number - last if side else last - number)
                self.copy(side, target).wait_recv()
                if number < last:
                    total = self.own[target].astype(f32) + self.arrived[side, target].astype(f32)
                    self.out[side, target] = total.astype(bf16)
                    self.copy(side, target).start()

    def total(self, sum_ref):
        sum_ref[...] = self.own[self.fsdp].astype(f32)
        for side, end in ((0, 0), (1, self.groups - 1)):

            @pl.when(self.fsdp != end)
            def _():
                sum_ref[...] += self.arrived[side, self.fsdp].astype(f32)

    def finish(self):
        for target in range(self.groups):
            for side, sends in ((0, self.fsdp < target), (1, self.fsdp > target)):

                @pl.when(sends)
                def _():
                    self.copy(side, target).wait_send()


def entry_back_kernel(
    grad_query_ref,
    grad_key_ref,
    grad_value_ref,
    hat_ref,
    scale_ref,
    gain_ref,
    shift_ref,
    weight_ref,
    middle_ref,
    middle_in_ref,
    small_ref,
    up_ref,
    down_ref,
    grad_out_ref,
    result_ref,
    result_in_ref,
    out_ref,
    grad_weight_ref,
    lines_ref,
    embedded_ref,
    vectors_ref,
    pieces_ref,
    grad_out_sum_ref,
    block_ref,
    up_own,
    up_in,
    down_own,
    down_in,
    slices,
    slices_out,
    slices_in,
    slice_sum,
    context_slice,
    context_in,
    all_sums_ref,
    all_small_ref,
    small_part,
    small_in,
    small_sum,
    small_groups,
    out_in,
    loaded,
    sent_up,
    got_up,
    sent_down,
    got_down,
    sent_slice,
    got_slice,
    sent_context,
    got_context,
    sent_small,
    got_small,
    sent_sum,
    got_sum,
    sent_out,
    got_out,
    sent_result,
    got_result,
    moved,
    taken,
    held,
    weight_total,
    sums,
    part,
    part_in,
    pair,
    pair_in,
    chip,
    chip_in,
    piece,
    piece_out,
    piece_in,
    piece_sum,
    block_piece,
    block_in,
    rank_sums,
    rank_in,
    group_sums,
    group_in,
    sent_part,
    got_part,
    sent_pair,
    got_pair,
    sent_chip,
    got_chip,
    sent_piece,
    got_piece,
    sent_block,
    got_block,
    sent_rank,
    got_rank,
    sent_group,
    got_group,
    *,
    tiles,
    groups,
):
    step = pl.program_id(0)
    fsdp, context, tensor = (lax.axis_index(name) for name in ("fsdp", "context", "tensor"))
    ranks = 4
    half = tiles // 2
    core = lax.rem(tensor, 2)
    chip_x = tensor // 2
    sibling = tensor + 1 - 2 * core
    across = lax.rem(tensor + 2, ranks)
    place = fsdp * 2 + context
    depth = hat_ref.shape[0]
    slice_rows = depth // ranks
    weight_rows = depth // groups
    def up_copy(other):
        return copy_to(
            up_ref.at[1, other], up_in.at[other], sent_up.at[other], got_up.at[other], context=1 - context
        )

    def down_copy(other):
        return copy_to(
            down_ref.at[0, other], down_in.at[other], sent_down.at[other], got_down.at[other], tensor=across
        )

    def loads():
        return [
            pltpu.make_async_copy(up_ref.at[0], up_own, loaded.at[0]),
            pltpu.make_async_copy(down_ref.at[1], down_own, loaded.at[1]),
        ]

    far_first = [groups - 1, 0] + list(range(groups - 2, 0, -1))
    slice_relay = Relay(slices, slices_out, slices_in, sent_slice, got_slice, fsdp, groups)
    piece_relay = Relay(piece, piece_out, piece_in, sent_piece, got_piece, fsdp, groups)

    def context_copy():
        return copy_to(context_slice, context_in, sent_context, got_context, context=1 - context)

    rounds = [{"tensor": sibling}, {"tensor": across}, {"context": 1 - context}]

    def small_copy(number):
        return copy_to(
            small_part.at[number], small_in.at[number], sent_small.at[number], got_small.at[number], **rounds[number]
        )

    def sum_copy(away):
        return copy_to(
            small_sum,
            small_groups.at[away - 1],
            sent_sum.at[away - 1],
            got_sum.at[away - 1],
            fsdp=lax.rem(fsdp + away, groups),
        )

    def out_copy():
        return copy_to(grad_out_ref, out_in, sent_out, got_out, context=1 - context)

    quarter = result_ref.shape[1]

    def result_places():
        for number, (source, rank) in enumerate([(result_ref, tensor), (result_in_ref, across)]):
            rows = pl.ds(pl.multiple_of(rank * quarter, quarter), quarter)
            for sequence in range(2):
                yield number * 2 + sequence, source.at[sequence], block_ref.at[sequence, rows, :]

    def result_copies():
        return [
            copy_to(held.at[k], target, sent_result.at[k], got_result.at[k], tensor=sibling)
            for k, source, target in result_places()
        ]

    def result_loads():
        return [
            pltpu.make_async_copy(source, held.at[k], taken.at[k])
            for k, source, target in result_places()
        ]

    def result_moves():
        return [
            pltpu.make_async_copy(held.at[k], target, moved.at[k]) for k, source, target in result_places()
        ]

    def part_copy(tile):
        return copy_to(
            part.at[tile, 1 - core], part_in.at[tile], sent_part.at[tile], got_part.at[tile], tensor=sibling
        )

    def pair_copy(tile):
        return copy_to(
            pair.at[tile, 1 - chip_x], pair_in.at[tile], sent_pair.at[tile], got_pair.at[tile], tensor=across
        )

    def chip_copy(tile):
        return copy_to(
            chip.at[tile], chip_in.at[tile], sent_chip.at[tile], got_chip.at[tile], context=1 - context
        )

    def block_copy():
        return copy_to(block_piece, block_in, sent_block, got_block, context=1 - context)

    def rank_copy(number):
        return copy_to(
            rank_sums.at[number], rank_in.at[number], sent_rank.at[number], got_rank.at[number], **rounds[number]
        )

    def group_copy(away):
        return copy_to(
            group_sums,
            group_in.at[away - 1],
            sent_group.at[away - 1],
            got_group.at[away - 1],
            fsdp=lax.rem(fsdp + away, groups),
        )

    @pl.when(step == 0)
    def _():
        greet(
            rounds + [{"fsdp": lax.rem(fsdp + away, groups)} for away in range(1, groups)]
        )
        for other in far_first:
            up_copy(other).start()
            down_copy(other).start()
        out_copy().start()
        small_part[0] = small_ref[...]
        small_copy(0).start()
        for one in result_loads() + loads():
            one.start()
        weight_total[...] = jnp.zeros_like(weight_total)
        sums[...] = jnp.zeros_like(sums)

    @pl.when(step == 2)
    def _():
        for one in result_loads():
            one.wait()
        for one in result_copies() + result_moves():
            one.start()

    def grads():
        return jnp.concatenate([grad_query_ref[...], grad_key_ref[...], grad_value_ref[...]], axis=0)

    @pl.when(step < tiles)
    def _():
        tile = step
        columns = grads()
        grad_entry = product(weight_ref[...], columns)
        hat = hat_ref[...].astype(f32)
        lifted = hat * gain_ref[...]
        weight_total[...] += against((lifted + shift_ref[...]).astype(bf16), columns)
        grad_lifted = grad_entry * gain_ref[...]
        term = scale_ref[...] * (
            grad_lifted
            - jnp.mean(grad_lifted, axis=0, keepdims=True)
            - hat * jnp.mean(grad_lifted * hat, axis=0, keepdims=True)
        )
        extra = jnp.where(tile < half, middle_in_ref[...], middle_ref[0]).astype(f32)
        term = (term + jnp.where(lax.rem(tile, half) == tensor, extra, 0.0)).astype(bf16)
        for rank in range(ranks):
            part[tile, rank % 2, rank // 2] = term[rank * slice_rows : (rank + 1) * slice_rows]
        part_copy(tile).start()
        weighted = grad_entry * hat
        for lane in range(0, grad_entry.shape[1], WIDE):
            sums[0] += grad_entry[:, lane : lane + WIDE]
            sums[1] += weighted[:, lane : lane + WIDE]

    @pl.when(step == tiles - 1)
    def _():
        for other in range(groups):
            piece[other] = weight_total[other * weight_rows : (other + 1) * weight_rows].astype(bf16)
        for target in far_first:
            piece_relay.begin(target)

    @pl.when((step >= 1) & (step < tiles + 1))
    def _():
        tile = step - 1
        part_copy(tile).wait_recv()
        pair[tile] = (part[tile, core].astype(f32) + part_in[tile].astype(f32)).astype(bf16)
        pair_copy(tile).start()

    @pl.when((step >= 5) & (step < tiles + 5))
    def _():
        tile = step - 5
        pair_copy(tile).wait_recv()
        total = (pair[tile, chip_x].astype(f32) + pair_in[tile].astype(f32)).astype(bf16)

        @pl.when(tile < half)
        def _():
            chip[tile] = total
            chip_copy(tile).start()

        @pl.when(tile >= half)
        def _():
            out_ref[context, tile - half] = total

    @pl.when((step >= tiles + 1) & (step < tiles + 1 + half))
    def _():
        tile = step - tiles - 1
        chip_copy(tile).wait_recv()
        out_ref[1 - context, tile] = chip_in[tile]

    for number in range(3):

        @pl.when(step == (2, 5, 7)[number])
        def _():
            small_copy(number).wait_recv()
            total = small_part[number] + small_in[number]
            if number < 2:
                small_part[number + 1] = total
                small_copy(number + 1).start()
            else:
                small_sum[...] = total
                for away in range(1, groups):
                    sum_copy(away).start()

    for number, other in enumerate(far_first):

        @pl.when(step == 1 + number)
        def _():
            if number == 0:
                for one in loads():
                    one.wait()
            up_copy(other).wait_recv()
            down_copy(other).wait_recv()
            slices[other, 0] = (up_own[other].astype(f32) + up_in[other].astype(f32)).astype(bf16)
            slices[other, 1] = (down_own[other].astype(f32) + down_in[other].astype(f32)).astype(bf16)
            slice_relay.begin(other)

    for number in range(1, groups):

        @pl.when(step == tiles - 2 * (groups - 1 - number))
        def _():
            slice_relay.turn(number)

    @pl.when(step == tiles)
    def _():
        slice_relay.total(slice_sum)
        context_slice[...] = slice_sum[...].astype(bf16)
        context_copy().start()

    for number in range(1, groups):

        @pl.when(step == tiles + number - 1)
        def _():
            piece_relay.turn(number)

    @pl.when(step == tiles + 2)
    def _():
        piece_relay.total(piece_sum)
        block_piece[...] = piece_sum[...].astype(bf16)
        block_copy().start()

    @pl.when(step == tiles + 4)
    def _():
        block_copy().wait_recv()
        grad_weight_ref[...] = block_piece[...].astype(f32) + block_in[...].astype(f32)

    @pl.when(step == tiles - 1)
    def _():
        rows = [jnp.sum(sums[kind].T, axis=0, keepdims=True) for kind in range(2)]
        rank_sums[0] = jnp.concatenate(rows + [jnp.zeros((6, depth), f32)], axis=0)
        rank_copy(0).start()

    @pl.when(step == tiles)
    def _():
        rank_copy(0).wait_recv()
        rank_sums[1] = rank_sums[0] + rank_in[0]
        rank_copy(1).start()

    @pl.when(step == tiles + 3)
    def _():
        rank_copy(1).wait_recv()
        rank_sums[2] = rank_sums[1] + rank_in[1]
        rank_copy(2).start()

    @pl.when(step == tiles + 4)
    def _():
        rank_copy(2).wait_recv()
        group_sums[context] = rank_sums[2]
        group_sums[1 - context] = rank_in[2]
        for away in range(1, groups):
            group_copy(away).start()

    @pl.when(step == tiles + 4)
    def _():
        all_small_ref[fsdp] = small_sum[...]
        for away in range(1, groups):
            sum_copy(away).wait_recv()
            all_small_ref[lax.rem(fsdp + groups - away, groups)] = small_groups[away - 1]
            sum_copy(away).wait_send()
        context_copy().wait()
        pieces_ref[context] = context_slice[...]
        pieces_ref[1 - context] = context_in[...]
        out_copy().wait()
        grad_out_sum_ref[...] = grad_out_ref[...].astype(f32) + out_in[...].astype(f32)
        for other in range(groups):
            up_copy(other).wait_send()
            down_copy(other).wait_send()
        for number in range(3):
            small_copy(number).wait_send()
            rank_copy(number).wait_send()
        for one in result_copies() + result_moves():
            one.wait()
        for number in range(2):
            all_sums_ref[2 * fsdp + number] = group_sums[number]
        for away in range(1, groups):
            group_copy(away).wait_recv()
            for number in range(2):
                source = lax.rem(fsdp + groups - away, groups)
                all_sums_ref[2 * source + number] = group_in[away - 1, number]
            group_copy(away).wait_send()
        for source in range(2 * groups):
            line = slice(source, source + 1)
            first = source % 2 * 5
            terms = [all_sums_ref[source, kind : kind + 1] for kind in range(2)]
            terms += [all_small_ref[source // 2, first + kind : first + kind + 1] for kind in range(4)]
            for kind, term in enumerate(terms):
                lines_ref[line, kind * depth : (kind + 1) * depth] = term
            last = 10 + ranks + source % 2
            embedded_ref[line] = all_small_ref[source // 2, last : last + 1]
        vectors_ref[...] = jnp.zeros_like(vectors_ref)
        for source in range(groups):
            vectors_ref[0:ranks] += all_small_ref[source, 10 : 10 + ranks]
            vectors_ref[ranks : ranks + 1] += all_small_ref[source, 4:5] + all_small_ref[source, 9:10]
        for tile in range(tiles):
            part_copy(tile).wait_send()
            pair_copy(tile).wait_send()
        for tile in range(half):
            chip_copy(tile).wait_send()
        slice_relay.finish()
        piece_relay.finish()
        block_copy().wait_send()


def entry_back_call(
    grad_query,
    grad_key,
    grad_value,
    hat_t,
    scaling,
    gain,
    shift,
    weight,
    grad_middle,
    middle_in,
    small,
    up,
    down,
    grad_out,
    result,
    result_in,
    groups,
    tile,
):
    group, length = grad_query.shape
    depth = hat_t.shape[0]
    tiles = length // tile
    half = tiles // 2
    rows = depth // 4
    weight_rows = depth // groups

    def lanes(step):
        first = (1 - lax.axis_index("context")) * half
        return 0, lax.rem(first + jnp.minimum(step, tiles - 1), tiles)

    whole = lambda step: (0, 0)
    whole3 = lambda step: (0, 0, 0)
    whole4 = lambda step: (0, 0, 0, 0)
    dma = lambda *shape: [pltpu.SemaphoreType.DMA(shape)] * 2
    hbm = pl.BlockSpec(memory_space=pl.ANY)
    piece = up.shape[1:]
    return pl.pallas_call(
        partial(entry_back_kernel, tiles=tiles, groups=groups),
        grid=(tiles + 5,),
        in_specs=[
            pl.BlockSpec((group, tile), lanes),
            pl.BlockSpec((group, tile), lanes),
            pl.BlockSpec((group, tile), lanes),
            pl.BlockSpec((depth, tile), lanes),
            pl.BlockSpec((1, tile), lanes),
            pl.BlockSpec((depth, 1), whole),
            pl.BlockSpec((depth, 1), whole),
            pl.BlockSpec((depth, 3 * group), whole),
            pl.BlockSpec((1, depth, tile), lambda step: (lax.axis_index("context"), 0, 0)),
            pl.BlockSpec((depth, tile), whole),
            pl.BlockSpec(small.shape, whole),
            hbm,
            hbm,
            pl.BlockSpec(grad_out.shape, whole),
            hbm,
            hbm,
        ],
        out_specs=[
            pl.BlockSpec((2, half, rows, tile), whole4),
            pl.BlockSpec((weight_rows, 3 * group), whole),
            pl.BlockSpec((2 * groups, 6 * depth), whole),
            pl.BlockSpec((2 * groups, depth), whole),
            pl.BlockSpec((8, depth), whole),
            pl.BlockSpec((2, 2, *piece[1:]), whole4),
            pl.BlockSpec(grad_out.shape, whole),
            hbm,
        ],
        out_shape=[
            jax.ShapeDtypeStruct((2, half, rows, tile), bf16),
            jax.ShapeDtypeStruct((weight_rows, 3 * group), f32),
            jax.ShapeDtypeStruct((2 * groups, 6 * depth), f32),
            jax.ShapeDtypeStruct((2 * groups, depth), f32),
            jax.ShapeDtypeStruct((8, depth), f32),
            jax.ShapeDtypeStruct((2, 2, *piece[1:]), bf16),
            jax.ShapeDtypeStruct(grad_out.shape, f32),
            jax.ShapeDtypeStruct((2, 4 * result.shape[1], depth), bf16),
        ],
        scratch_shapes=[
            *[pltpu.VMEM(piece, bf16)] * 4,
            pltpu.VMEM((groups, 2, *piece[1:]), bf16),
            *[pltpu.VMEM((2, groups, 2, *piece[1:]), bf16)] * 2,
            pltpu.VMEM((2, *piece[1:]), f32),
            pltpu.VMEM((2, *piece[1:]), bf16),
            pltpu.VMEM((2, *piece[1:]), bf16),
            pltpu.VMEM((2 * groups, 8, depth), f32),
            pltpu.VMEM((groups, *small.shape), f32),
            *[pltpu.VMEM((3, *small.shape), f32)] * 2,
            pltpu.VMEM(small.shape, f32),
            pltpu.VMEM((groups - 1, *small.shape), f32),
            pltpu.VMEM(grad_out.shape, bf16),
            pltpu.SemaphoreType.DMA((2,)),
            *dma(groups),
            *dma(groups),
            *dma(2, groups),
            *[pltpu.SemaphoreType.DMA] * 2,
            *dma(3),
            *dma(groups - 1),
            *[pltpu.SemaphoreType.DMA] * 2,
            *dma(4),
            pltpu.SemaphoreType.DMA((4,)),
            pltpu.SemaphoreType.DMA((4,)),
            pltpu.VMEM((4, *result.shape[1:]), bf16),
            pltpu.VMEM((depth, 3 * group), f32),
            pltpu.VMEM((2, depth, WIDE), f32),
            pltpu.VMEM((tiles, 2, 2, rows, tile), bf16),
            pltpu.VMEM((tiles, 2, rows, tile), bf16),
            pltpu.VMEM((tiles, 2, rows, tile), bf16),
            pltpu.VMEM((tiles, rows, tile), bf16),
            pltpu.VMEM((half, rows, tile), bf16),
            pltpu.VMEM((half, rows, tile), bf16),
            pltpu.VMEM((groups, weight_rows, 3 * group), bf16),
            *[pltpu.VMEM((2, groups, weight_rows, 3 * group), bf16)] * 2,
            pltpu.VMEM((weight_rows, 3 * group), f32),
            pltpu.VMEM((weight_rows, 3 * group), bf16),
            pltpu.VMEM((weight_rows, 3 * group), bf16),
            *[pltpu.VMEM((3, 8, depth), f32)] * 2,
            pltpu.VMEM((2, 8, depth), f32),
            pltpu.VMEM((groups - 1, 2, 8, depth), f32),
            *dma(tiles),
            *dma(tiles),
            *dma(half),
            *dma(2, groups),
            *[pltpu.SemaphoreType.DMA] * 2,
            *dma(3),
            *dma(groups - 1),
        ],
        compiler_params=pltpu.CompilerParams(
            vmem_limit_bytes=VMEM, collective_id=3, has_side_effects=True
        ),
        cost_estimate=cost(12 * length * depth * group, grad_query, hat_t, hat_t),
        name="entry_back",
    )(
        grad_query,
        grad_key,
        grad_value,
        hat_t,
        scaling,
        gain,
        shift,
        weight,
        grad_middle,
        middle_in,
        small,
        up,
        down,
        grad_out,
        result,
        result_in,
    )


def add(left_side, right_side):
    return (left_side.astype(f32) + right_side.astype(f32)).astype(bf16)


def by_sequence(
    tokens,
    cotangent,
    segments,
    steps,
    table,
    ada_w,
    ada_b,
    gain_one,
    w_qkv,
    w_out,
    gain_two,
    w_up,
    b_up,
    w_down,
    b_down,
):
    fsdp, tensor = lax.axis_size("fsdp"), lax.axis_size("tensor")
    context = lax.axis_size("context")
    tensor_rank = lax.axis_index("tensor")
    context_rank = lax.axis_index("context")
    fsdp_rank = lax.axis_index("fsdp")
    sequences, own_rows, depth = tokens.shape
    length = segments.shape[1]
    group = w_out.shape[0]
    part_width = w_up.shape[1]
    heads = group // HDIM
    quarter = own_rows // tensor

    partner = [(k, (k + 1) % context) for k in range(context)]

    by_kind = w_qkv.reshape(-1, heads, 3, HDIM).transpose(0, 2, 1, 3).reshape(-1, 3 * group)
    both = ("tensor", "fsdp")
    out_blocks = lax.all_gather(w_out, both, axis=0, tiled=False)

    numbers = jnp.arange(table.shape[0], dtype=jnp.int32)
    ada_full = ada_w.astype(f32)
    raw = exact_product((steps[:, None] == numbers[None, :]).astype(f32), table.astype(f32))
    local_mods = exact_product(jax.nn.silu(raw), ada_full) + ada_b.astype(f32)
    local_mods = local_mods.reshape(sequences, 6, depth)
    gain_first, gain_second = gain_one.astype(f32), gain_two.astype(f32)
    own_mods = lax.dynamic_index_in_dim(local_mods, context_rank, 0, keepdims=False)
    gain_column = (gain_first * (1.0 + own_mods[1]))[:, None]
    shift_column = own_mods[0][:, None]
    mods = jnp.stack(
        [
            local_mods[:, 2],
            local_mods[:, 3],
            gain_second * (1.0 + local_mods[:, 4]),
            local_mods[:, 5],
        ]
        + [jnp.zeros((sequences, depth), f32)] * 4,
        axis=1,
    )

    segment = lax.dynamic_index_in_dim(segments, context_rank, 0, keepdims=False)
    same, starts, ends = document_bounds(segment)
    offsets = jnp.arange(length, dtype=jnp.int32) - jnp.sum(jnp.where(same, starts[:, None], 0), axis=0)
    angles = frequencies()[:, None] * offsets.astype(f32)[None, :]
    cosine, sine = jnp.cos(angles), jnp.sin(angles)
    tile = length // (context * tensor)
    block = tile
    first_key = jnp.sum(jnp.where(same, starts[:, None], 0), axis=0)[::tile]
    last_key = jnp.sum(jnp.where(same, ends[:, None], 0), axis=0)[tile - 1 :: tile]

    low_key = first_key // WIDE * WIDE
    high_key = (last_key + WIDE - 1) // WIDE * WIDE

    def ranges_of(size):
        count = (high_key - low_key + size - 1) // size
        return jnp.stack([jnp.maximum(high_key - count * size, 0), count]).astype(jnp.int32)

    back_block = block // 2
    ranges, back_ranges = ranges_of(block), ranges_of(back_block)

    queries, keys, keys_t, values_t, hat_t, scaling, norms, qkv, forward = entry_call(
        tokens,
        by_kind,
        jnp.where(context_rank == 0, w_up, w_down.T),
        gain_column,
        shift_column,
        cosine,
        sine,
        segment[None, :],
        groups=fsdp,
        tile=tile,
    )
    across = [(k, (k + 2) % tensor) for k in range(tensor)]
    across_weight = lax.ppermute(forward, "tensor", across)
    other_weight = lax.ppermute(forward, "context", partner)
    mixture, told = attend_call(ranges, queries, keys, values_t, norms, tile, block)

    own_segments = lax.dynamic_slice_in_dim(
        segments, context_rank * own_rows + tensor_rank * quarter, quarter, axis=1
    )
    (
        result,
        grad_mixture,
        grad_middle,
        grad_out,
        sums,
        bias_sums,
        up_keep,
        up_send,
        down_keep,
        down_send,
    ) = middle_call(
        mixture,
        tokens,
        cotangent,
        (own_segments != 0).astype(f32).reshape(-1, 1),
        mods,
        b_up.astype(f32).reshape(tensor, 1, part_width),
        b_down.astype(f32)[None, :],
        out_blocks,
        forward,
        other_weight,
        across_weight,
        fsdp,
        tile=min(tile, 256),
    )
    result = result.reshape(sequences, quarter, depth)
    result_in = lax.ppermute(result, "tensor", across)
    middle_in = lax.ppermute(
        lax.dynamic_index_in_dim(grad_middle, 1 - context_rank, 0, keepdims=False), "context", partner
    )
    small = jnp.concatenate(
        [
            sums[:, :5].reshape(-1, depth),
            bias_sums.reshape(-1, depth),
        ]
    )
    small_rows = small.shape[0]
    cond = raw.shape[1]
    leads = (context_rank == 0) & (tensor_rank == 0)
    embedded = jnp.concatenate([raw, steps.astype(f32)[:, None]], axis=1)
    embedded = jnp.pad(jnp.where(leads, embedded, 0.0), ((0, 0), (0, depth - cond - 1)))
    small = jnp.concatenate([small, embedded])
    small = jnp.pad(small, ((0, -small.shape[0] % 8), (0, 0)))

    up_sum = add(up_keep, lax.ppermute(up_send, "tensor", across))
    down_sum = add(down_keep, lax.ppermute(down_send, "context", partner))
    grad_out = lax.psum_scatter(grad_out, both, scatter_dimension=0, tiled=True)[0]

    grad_query, grad_key, grad_value = attend_back_call(
        back_ranges, told, keys_t, values_t, mixture, grad_mixture, cosine, sine, tile, back_block
    )
    (grad_query, up_sum, down_sum, result_in, middle_in, grad_out) = lax.optimization_barrier(
        (grad_query, up_sum, down_sum, result_in, middle_in, grad_out)
    )
    part, grad_qkv, lines, embedded, vectors, pieces, grad_out, block_out = entry_back_call(
        grad_query,
        grad_key,
        grad_value,
        hat_t,
        scaling,
        gain_column,
        shift_column,
        qkv,
        grad_middle,
        middle_in,
        small,
        up_sum,
        down_sum,
        grad_out,
        result,
        result_in,
        groups=fsdp,
        tile=tile,
    )
    pieces = pieces.transpose(1, 0, 2, 3)
    pieces = pieces.reshape(2, depth // fsdp, part_width).astype(f32)
    grad_w_up = pieces[0]
    grad_w_down = pieces[1].T
    grad_w_out = grad_out
    choose = (embedded[:, cond].astype(jnp.int32)[:, None] == numbers[None, :]).astype(f32)
    embedding, silu_back = jax.vjp(jax.nn.silu, embedded[:, :cond])
    scale_columns = [slice(k * depth, (k + 1) * depth) for k in (1, 4)]
    scales_one, scales_two = (
        exact_product(embedding, ada_full[:, columns]) + ada_b[columns].astype(f32)
        for columns in scale_columns
    )
    grad_b_up = vectors[:tensor].reshape(-1)
    grad_b_down = vectors[tensor]
    grad_gain_one = jnp.sum(lines[:, scale_columns[0]] * (1.0 + scales_one), axis=0)
    grad_gain_two = jnp.sum(lines[:, scale_columns[1]] * (1.0 + scales_two), axis=0)
    part = part.transpose(0, 1, 3, 2).reshape(sequences, own_rows, depth // tensor)
    grad_tokens = part.astype(f32)
    grad_w_qkv = (
        grad_qkv.reshape(-1, 3, heads, HDIM).transpose(0, 2, 1, 3).reshape(-1, 3 * group)
    )
    ones = jnp.ones((depth,), f32)
    grad_mod = lines * jnp.concatenate([ones, gain_first, ones, ones, gain_second, ones])[None, :]
    grad_ada_b = jnp.sum(grad_mod, axis=0)
    grad_ada_w = exact_transposed(embedding, grad_mod)
    grad_before = silu_back(exact_against(grad_mod, ada_full))[0]
    grad_table = exact_transposed(choose, grad_before)
    return (
        block_out,
        grad_tokens,
        grad_table,
        grad_ada_w,
        grad_ada_b,
        grad_gain_one,
        grad_w_qkv,
        grad_w_out,
        grad_gain_two,
        grad_w_up,
        grad_b_up,
        grad_w_down,
        grad_b_down,
    )


def normalize(operand):
    center = operand - jnp.mean(operand, axis=-1, keepdims=True)
    scaling = lax.rsqrt(jnp.mean(center * center, axis=-1, keepdims=True) + 1e-05)
    return (center * scaling, scaling)


def norm_back(grad_hat, hatted, scaling):
    return scaling * (
        grad_hat
        - jnp.mean(grad_hat, axis=-1, keepdims=True)
        - hatted * jnp.mean(grad_hat * hatted, axis=-1, keepdims=True)
    )


def angles_of(offsets, half_width):
    frequency = 10000.0 ** (-jnp.arange(half_width, dtype=jnp.float32) / half_width)
    angles = offsets.astype(jnp.float32)[:, None] * frequency[None, :]
    return (jnp.cos(angles)[:, None, :], jnp.sin(angles)[:, None, :])


def rotate(operand, cosine, sine_part, direction):
    half_width = operand.shape[-1] // 2
    front_half = operand[..., :half_width]
    second = operand[..., half_width:]
    return jnp.concatenate(
        [
            front_half * cosine - direction * second * sine_part,
            direction * front_half * sine_part + second * cosine,
        ],
        axis=-1,
    )


def scores_of(queries, key_rows, allowed):
    raw_scores = (
        jnp.einsum("qhd,khd->hqk", queries, key_rows, preferred_element_type=jnp.float32) * 0.125
    )
    return jnp.where(allowed[None], raw_scores, -1e30)


def attend(queries, key_rows, values, allowed):
    scores = scores_of(queries, key_rows, allowed)
    row_max = jnp.max(scores, axis=-1, keepdims=True)
    weights_raw = jnp.exp(scores - row_max)
    row_total = jnp.sum(weights_raw, axis=-1, keepdims=True)
    weights_low = (weights_raw / row_total).astype(jnp.bfloat16)
    mixture = jnp.einsum("hqk,khd->qhd", weights_low, values, preferred_element_type=jnp.float32)
    return (mixture, row_max + jnp.log(row_total))


def attend_back(queries, key_rows, values, grad_mixture, logsum, allowed, row_delta):
    scores = scores_of(queries, key_rows, allowed)
    chances = jnp.exp(scores - logsum)
    grad_chances = jnp.einsum(
        "qhd,khd->hqk", grad_mixture, values, preferred_element_type=jnp.float32
    )
    row_delta = jnp.sum(chances * grad_chances, axis=-1, keepdims=True)
    grad_scores = (chances * (grad_chances - row_delta)).astype(jnp.bfloat16)
    return (chances.astype(jnp.bfloat16), grad_scores, row_delta)


def by_block(
    tokens,
    cotangent,
    segments,
    steps,
    table,
    ada_w,
    ada_b,
    gain_one,
    w_qkv,
    w_out,
    gain_two,
    w_up,
    b_up,
    w_down,
    b_down,
):
    w_qkv, w_up, w_out, w_down = (
        lax.all_gather(w_qkv, "fsdp", axis=0, tiled=True),
        lax.all_gather(w_up, "fsdp", axis=0, tiled=True),
        lax.all_gather(w_out, "fsdp", axis=1, tiled=True),
        lax.all_gather(w_down, "fsdp", axis=1, tiled=True),
    )
    tensor_rank = lax.axis_index("tensor")
    context_rank = lax.axis_index("context")
    sequences, own_rows, model_width = tokens.shape
    length = segments.shape[1]
    local_heads = w_out.shape[0] // HDIM
    hidden_width = w_up.shape[1]
    up_bias = lax.dynamic_slice_in_dim(b_up, tensor_rank * hidden_width, hidden_width).astype(
        jnp.float32
    )
    down_bias = b_down.astype(jnp.float32)
    gain_first = gain_one.astype(jnp.float32)
    gain_second = gain_two.astype(jnp.float32)
    leader = (tensor_rank == 0).astype(jnp.float32)
    ada_full = ada_w.astype(jnp.float32)
    choose = (steps[:, None] == jnp.arange(table.shape[0], dtype=jnp.int32)[None, :]).astype(
        jnp.float32
    )
    before = exact_product(choose, table.astype(jnp.float32))
    embedding, silu_back = jax.vjp(jax.nn.silu, before)
    modulation = exact_product(embedding, ada_full) + ada_b.astype(jnp.float32)
    grad_qkv = jnp.zeros(w_qkv.shape, jnp.float32)
    grad_out_w = jnp.zeros(w_out.shape, jnp.float32)
    grad_up = jnp.zeros(w_up.shape, jnp.float32)
    grad_down = jnp.zeros(w_down.shape, jnp.float32)
    grad_bias_up = jnp.zeros((hidden_width,), jnp.float32)
    grad_bias_down = jnp.zeros((model_width,), jnp.float32)
    grad_gain_first = jnp.zeros((model_width,), jnp.float32)
    grad_gain_second = jnp.zeros((model_width,), jnp.float32)
    results = []
    partial_inputs = []
    carried = []
    grad_mods = []
    for number in range(sequences):
        shift_one, scale_one, gate_one, shift_two, scale_two, gate_two = jnp.split(
            modulation[number], 6
        )
        segment = segments[number]
        offsets = positions(segment)
        own_segment = lax.dynamic_slice_in_dim(segment, context_rank * own_rows, own_rows)
        own_offsets = lax.dynamic_slice_in_dim(offsets, context_rank * own_rows, own_rows)
        cosine, sine_part = angles_of(own_offsets, HDIM // 2)
        allowed = own_segment[:, None] == segment[None, :]
        inputs_row = tokens[number].astype(jnp.float32)
        hat_one, scaling_one = normalize(inputs_row)
        lifted_one = hat_one * gain_first
        entry_one = (lifted_one * (1.0 + scale_one) + shift_one).astype(jnp.bfloat16)
        projected = product(entry_one, w_qkv).reshape(own_rows, local_heads, 3, HDIM)
        queries = rotate(projected[:, :, 0], cosine, sine_part, 1.0).astype(jnp.bfloat16)
        key_rows = rotate(projected[:, :, 1], cosine, sine_part, 1.0).astype(jnp.bfloat16)
        values = projected[:, :, 2].astype(jnp.bfloat16)
        key_value = jnp.stack([key_rows, values], axis=1).reshape(own_rows, 2 * local_heads * HDIM)
        gathered = lax.all_gather(key_value, "context", axis=0, tiled=True).reshape(
            length, 2, local_heads, HDIM
        )
        all_keys = gathered[:, 0]
        all_values = gathered[:, 1]
        mixture, logsum = attend(queries, all_keys, all_values, allowed)
        mixture_low = mixture.reshape(own_rows, local_heads * HDIM).astype(jnp.bfloat16)
        attended = lax.psum(product(mixture_low, w_out).astype(jnp.bfloat16), "tensor").astype(
            jnp.float32
        )
        middle = inputs_row + gate_one * attended
        hat_two, scaling_two = normalize(middle)
        lifted_two = hat_two * gain_second
        entry_two = (lifted_two * (1.0 + scale_two) + shift_two).astype(jnp.bfloat16)
        hidden = product(entry_two, w_up) + up_bias
        activated, gelu_back = jax.vjp(partial(jax.nn.gelu, approximate=True), hidden)
        activated_low = activated.astype(jnp.bfloat16)
        output = (
            lax.psum(product(activated_low, w_down).astype(jnp.bfloat16), "tensor").astype(
                jnp.float32
            )
            + down_bias
        )
        results.append((middle + gate_two * output).astype(jnp.bfloat16))
        valid = (own_segment != 0).astype(jnp.float32)[:, None]
        grad_result = cotangent[number].astype(jnp.float32) * valid
        grad_output = (gate_two * grad_result).astype(jnp.bfloat16)
        grad_gate_two = jnp.sum(grad_result * output, axis=0)
        grad_bias_down = grad_bias_down + jnp.sum(grad_output.astype(jnp.float32), axis=0)
        grad_down = grad_down + transposed(activated_low, grad_output)
        grad_active = against(grad_output, w_down)
        grad_hidden = gelu_back(grad_active)[0].astype(jnp.bfloat16)
        grad_bias_up = grad_bias_up + jnp.sum(grad_hidden.astype(jnp.float32), axis=0)
        grad_up = grad_up + transposed(entry_two, grad_hidden)
        grad_entry_two = against(grad_hidden, w_up)
        grad_shift_two = jnp.sum(grad_entry_two, axis=0)
        grad_scale_two = jnp.sum(grad_entry_two * lifted_two, axis=0)
        grad_lifted_two = grad_entry_two * (1.0 + scale_two)
        grad_gain_second = grad_gain_second + jnp.sum(grad_lifted_two * hat_two, axis=0)
        part_two = norm_back(grad_lifted_two * gain_second, hat_two, scaling_two)
        grad_middle = grad_result + lax.psum(part_two.astype(jnp.bfloat16), "tensor").astype(
            jnp.float32
        )
        grad_attended = (gate_one * grad_middle).astype(jnp.bfloat16)
        grad_gate_one = jnp.sum(grad_middle * attended, axis=0)
        grad_out_w = grad_out_w + transposed(mixture_low, grad_attended)
        grad_mixture = (
            against(grad_attended, w_out).astype(jnp.bfloat16).reshape(own_rows, local_heads, HDIM)
        )
        chances_low, grad_scores, row_delta = attend_back(
            queries, all_keys, all_values, grad_mixture, logsum, allowed, None
        )
        grad_queries = (
            jnp.einsum("hqk,khd->qhd", grad_scores, all_keys, preferred_element_type=jnp.float32)
            * 0.125
        )
        grad_all_keys = (
            jnp.einsum("hqk,qhd->khd", grad_scores, queries, preferred_element_type=jnp.float32)
            * 0.125
        )
        grad_all_values = jnp.einsum(
            "hqk,qhd->khd", chances_low, grad_mixture, preferred_element_type=jnp.float32
        )
        both_grads = jnp.stack([grad_all_keys, grad_all_values], axis=1).reshape(
            length, 2 * local_heads * HDIM
        )
        own_grads = (
            lax.psum_scatter(
                both_grads.astype(jnp.bfloat16), "context", scatter_dimension=0, tiled=True
            )
            .astype(jnp.float32)
            .reshape(own_rows, 2, local_heads, HDIM)
        )
        grad_keys = own_grads[:, 0]
        grad_values = own_grads[:, 1]
        grad_queries = rotate(grad_queries, cosine, sine_part, -1.0)
        grad_keys = rotate(grad_keys, cosine, sine_part, -1.0)
        grad_projected = (
            jnp.stack([grad_queries, grad_keys, grad_values], axis=2)
            .reshape(own_rows, local_heads * 3 * HDIM)
            .astype(jnp.bfloat16)
        )
        grad_qkv = grad_qkv + transposed(entry_one, grad_projected)
        grad_entry_one = against(grad_projected, w_qkv)
        grad_shift_one = jnp.sum(grad_entry_one, axis=0)
        grad_scale_one = jnp.sum(grad_entry_one * lifted_one, axis=0)
        grad_lifted_one = grad_entry_one * (1.0 + scale_one)
        grad_gain_first = grad_gain_first + jnp.sum(grad_lifted_one * hat_one, axis=0)
        partial_inputs.append(norm_back(grad_lifted_one * gain_first, hat_one, scaling_one))
        carried.append(grad_middle)
        grad_mods.append(
            jnp.concatenate(
                [
                    grad_shift_one,
                    grad_scale_one,
                    grad_gate_one * leader,
                    grad_shift_two,
                    grad_scale_two,
                    grad_gate_two * leader,
                ]
            )
        )
    summed_inputs = lax.psum_scatter(
        jnp.stack(partial_inputs).astype(jnp.bfloat16), "tensor", scatter_dimension=2, tiled=True
    ).astype(jnp.float32)
    slice_width = model_width // lax.axis_size("tensor")
    own_middle = lax.dynamic_slice_in_dim(
        jnp.stack(carried), tensor_rank * slice_width, slice_width, axis=2
    )
    grad_tokens = summed_inputs + own_middle
    grad_mod = jnp.stack(grad_mods)
    bias_up_full = lax.dynamic_update_slice_in_dim(
        jnp.zeros((b_up.shape[0],), jnp.float32), grad_bias_up, tensor_rank * hidden_width, 0
    )
    grad_qkv, grad_up, grad_out_w, grad_down = (
        lax.psum_scatter(
            grad_qkv.astype(jnp.bfloat16), "fsdp", scatter_dimension=0, tiled=True
        ).astype(jnp.float32),
        lax.psum_scatter(
            grad_up.astype(jnp.bfloat16), "fsdp", scatter_dimension=0, tiled=True
        ).astype(jnp.float32),
        lax.psum_scatter(
            grad_out_w.astype(jnp.bfloat16), "fsdp", scatter_dimension=1, tiled=True
        ).astype(jnp.float32),
        lax.psum_scatter(
            grad_down.astype(jnp.bfloat16), "fsdp", scatter_dimension=1, tiled=True
        ).astype(jnp.float32),
    )
    grad_qkv, grad_up, grad_out_w, grad_down = (
        lax.psum(grad_qkv.astype(jnp.bfloat16), "context").astype(jnp.float32),
        lax.psum(grad_up.astype(jnp.bfloat16), "context").astype(jnp.float32),
        lax.psum(grad_out_w.astype(jnp.bfloat16), "context").astype(jnp.float32),
        lax.psum(grad_down.astype(jnp.bfloat16), "context").astype(jnp.float32),
    )
    grad_ada_b = jnp.sum(grad_mod, axis=0)
    grad_ada_w = exact_transposed(embedding, grad_mod)
    grad_embedding = exact_against(grad_mod, ada_full)
    grad_before = silu_back(grad_embedding)[0]
    grad_table = exact_transposed(choose, grad_before)
    (
        grad_table,
        grad_ada_w,
        grad_ada_b,
        grad_gain_first,
        grad_gain_second,
        bias_up_full,
        grad_bias_down,
    ) = lax.psum(
        (
            grad_table,
            grad_ada_w,
            grad_ada_b,
            grad_gain_first,
            grad_gain_second,
            bias_up_full,
            grad_bias_down * leader,
        ),
        ("fsdp", "context", "tensor"),
    )
    return (
        jnp.stack(results),
        grad_tokens,
        grad_table,
        grad_ada_w,
        grad_ada_b,
        grad_gain_first,
        grad_qkv,
        grad_out_w,
        grad_gain_second,
        grad_up,
        bias_up_full,
        grad_down,
        grad_bias_down,
    )


def solution(mesh):
    axes = dict(zip(mesh.axis_names, mesh.devices.shape))

    def whole(tokens, *others):
        sequences = tokens.shape[0] // axes["fsdp"]
        local = by_sequence if sequences == axes["context"] == 2 and axes["tensor"] == 4 else by_block
        return mapped(local, mesh)(tokens, *others)

    return whole


def mapped(local, mesh):
    return jax.shard_map(
        local,
        mesh=mesh,
        in_specs=(
            P("fsdp", "context", None),
            P("fsdp", "context", None),
            P("fsdp", None),
            P("fsdp"),
            P(),
            P(),
            P(),
            P(),
            P("fsdp", "tensor"),
            P("tensor", "fsdp"),
            P(),
            P("fsdp", "tensor"),
            P(),
            P("tensor", "fsdp"),
            P(),
        ),
        out_specs=(
            P("fsdp", "context", None),
            P("fsdp", "context", "tensor"),
            P(),
            P(),
            P(),
            P(),
            P("fsdp", "tensor"),
            P("tensor", "fsdp"),
            P(),
            P("fsdp", "tensor"),
            P(),
            P("tensor", "fsdp"),
            P(),
        ),
        check_vma=False,
    )
```

```python
import math
from functools import partial

import jax
import jax.numpy as jnp
from jax import lax
from jax.experimental import pallas as pl
from jax.experimental.pallas import tpu as pltpu
from jax.sharding import PartitionSpec as P

HDIM = 64
HALF = HDIM // 2
SEGMENTS = 5
WIDE = 128
MASKED = 2.0**100
LOG2E = math.log2(math.e)
SAFE_EXPONENT = 60.0
EPSILON = 1e-05
VMEM = 56 * 2**20
PART_TILES = 2
PART_CUTS = 1
VMEM_MOST = 60 * 2**20


def cost(flops, *arrays):
    size = sum(math.prod(one.shape) * one.dtype.itemsize for one in arrays)
    return pl.CostEstimate(flops=int(flops), bytes_accessed=int(size), transcendentals=0)


precise = lax.Precision.HIGHEST
f32 = jnp.float32
bf16 = jnp.bfloat16


def product(left_side, right_side):
    return jnp.dot(left_side, right_side, preferred_element_type=jnp.float32)


def transposed(left_side, right_side):
    return lax.dot_general(
        left_side, right_side, (((0,), (0,)), ((), ())), preferred_element_type=jnp.float32
    )


def against(left_side, right_side):
    return lax.dot_general(
        left_side, right_side, (((1,), (1,)), ((), ())), preferred_element_type=jnp.float32
    )


def exact_product(left_side, right_side):
    return jnp.dot(left_side, right_side, precision=precise, preferred_element_type=jnp.float32)


def exact_transposed(left_side, right_side):
    return lax.dot_general(
        left_side,
        right_side,
        (((0,), (0,)), ((), ())),
        precision=precise,
        preferred_element_type=jnp.float32,
    )


def exact_against(left_side, right_side):
    return lax.dot_general(
        left_side,
        right_side,
        (((1,), (1,)), ((), ())),
        precision=precise,
        preferred_element_type=jnp.float32,
    )


def document_bounds(segment):
    indices = jnp.arange(segment.shape[-1], dtype=jnp.int32)
    same = segment[..., None, :] == jnp.arange(SEGMENTS, dtype=jnp.int32)[:, None]
    starts = jnp.min(jnp.where(same, indices, segment.shape[-1]), axis=-1)
    ends = jnp.max(jnp.where(same, indices + 1, 0), axis=-1)
    return same, starts, ends


def positions(segment):
    same, starts, _ = document_bounds(segment)
    first = jnp.sum(jnp.where(same, starts[..., :, None], 0), axis=-2)
    return jnp.arange(segment.shape[-1], dtype=jnp.int32) - first


def frequencies():
    return 10000.0 ** (-jnp.arange(HALF, dtype=jnp.float32) / HALF)


def copy_to(source, target, sent, arrived, **device):
    return pltpu.make_async_remote_copy(
        src_ref=source,
        dst_ref=target,
        send_sem=sent,
        recv_sem=arrived,
        device_id=device,
        device_id_type=pl.DeviceIdType.MESH,
    )


def greet(devices):
    barrier = pltpu.get_barrier_semaphore()
    for device in devices:
        pl.semaphore_signal(barrier, inc=1, device_id=device, device_id_type=pl.DeviceIdType.MESH)
    pl.semaphore_wait(barrier, len(devices))


def quarter_at(number, tensor):
    core = lax.rem(tensor, 2)
    chip = jnp.where(number < 2, tensor // 2, 1 - tensor // 2)
    return chip * 2 + jnp.where(lax.rem(number, 2) == 0, core, 1 - core)


def entry_kernel(
    tokens_ref,
    rows_ref,
    shard_ref,
    own_forward_ref,
    gain_ref,
    shift_ref,
    cosine_ref,
    sine_ref,
    segment_ref,
    query_ref,
    key_ref,
    key_t_ref,
    value_t_ref,
    hat_ref,
    scale_ref,
    norm_ref,
    weight_ref,
    forward_ref,
    shards,
    weight_t,
    rows,
    arrived,
    sent_shard,
    got_shard,
    own_shard,
    sent_block,
    got_block,
    sent_across,
    got_across,
    sent_sibling,
    got_sibling,
    sent_on,
    got_on,
    sent_forward,
    got_forward,
    own_forward,
    *,
    heads,
    groups,
):
    step = pl.program_id(0)
    fsdp, context, tensor = (lax.axis_index(name) for name in ("fsdp", "context", "tensor"))
    ranks = 4
    core = lax.rem(tensor, 2)
    sibling = tensor + 1 - 2 * core
    across = lax.rem(tensor + 2, ranks)
    quarter = rows.shape[0]
    chunks = sent_block.shape[0]
    height = quarter // chunks

    def shard_copy(away):
        return copy_to(
            shard_ref,
            shards.at[fsdp],
            sent_shard.at[away - 1],
            got_shard.at[away - 1],
            fsdp=lax.rem(fsdp + away, groups),
        )

    def shard_own():
        return pltpu.make_async_copy(shard_ref, shards.at[fsdp], own_shard)

    def chunk(rank, number):
        return arrived.at[rank, pl.ds(number * height, height), :]

    def block_copy(number):
        at = pl.multiple_of(tensor * quarter, quarter) + number * height
        return copy_to(
            tokens_ref.at[1 - context, pl.ds(at, height), :],
            chunk(tensor, number),
            sent_block.at[number],
            got_block.at[number],
            context=1 - context,
        )

    def across_copy(number):
        return copy_to(
            chunk(tensor, number),
            chunk(tensor, number),
            sent_across.at[number],
            got_across.at[number],
            tensor=across,
        )

    def sibling_copy(number):
        return copy_to(
            chunk(tensor, number),
            chunk(tensor, number),
            sent_sibling.at[number],
            got_sibling.at[number],
            tensor=sibling,
        )

    def on_copy(number):
        return copy_to(
            chunk(across, number),
            chunk(across, number),
            sent_on.at[number],
            got_on.at[number],
            tensor=sibling,
        )

    forward_rows = own_forward_ref.shape[0]

    def forward_place(rank):
        return forward_ref.at[pl.ds(pl.multiple_of(rank * forward_rows, forward_rows), forward_rows), :]

    def relay_copy(origin, upward):
        place = forward_place(origin)
        side = 0 if upward else 1
        return copy_to(
            place,
            place,
            sent_forward.at[side, origin],
            got_forward.at[origin],
            fsdp=fsdp + 1 if upward else fsdp - 1,
        )

    def forward_own():
        return pltpu.make_async_copy(own_forward_ref, forward_place(fsdp), own_forward)

    def relay(origin, upward):
        @pl.when(fsdp < groups - 1 if upward else fsdp > 0)
        def _():
            relay_copy(origin, upward).start()

    def from_below(distance, act):
        @pl.when(fsdp >= distance)
        def _():
            act(fsdp - distance, True)

    def from_above(distance, act):
        @pl.when(fsdp + distance < groups)
        def _():
            act(fsdp + distance, False)

    def hand_over(distance):
        def act(origin, upward):
            relay_copy(origin, upward).wait_recv()
            relay(origin, upward)

        from_below(distance, act)
        from_above(distance, act)

    def finish_forward():
        def sent(origin, upward):
            @pl.when(fsdp < groups - 1 if upward else fsdp > 0)
            def _():
                relay_copy(origin, upward).wait_send()

        sent(fsdp, True)
        sent(fsdp, False)
        for distance in range(1, groups):
            from_below(distance, sent)
            from_above(distance, sent)

    def take(numbers):
        for number in numbers:
            block_copy(number).wait_recv()
            across_copy(number).start()
            sibling_copy(number).start()

    def pass_on(numbers):
        for number in numbers:
            across_copy(number).wait_recv()
            on_copy(number).start()

    @pl.when(step == 0)
    def _():
        shard_own().start()
        greet(
            [{"fsdp": lax.rem(fsdp + away, groups)} for away in range(1, groups)]
            + [{"context": 1 - context}, {"tensor": sibling}, {"tensor": across}]
        )
        for away in range(1, groups):
            shard_copy(away).start()
        for number in range(chunks):
            block_copy(number).start()
        forward_own().start()
        take(range(chunks - 1))
        shard_own().wait()
        for away in range(1, groups):
            shard_copy(away).wait_recv()
        for number in range(groups):
            weight_ref[number * shards.shape[1] : (number + 1) * shards.shape[1], :] = shards[number]
        forward_own().wait()
        relay(fsdp, True)
        relay(fsdp, False)
        weight_t[...] = weight_ref[...].T

    @pl.when(step == 1)
    def _():
        take([chunks - 1])
        pass_on(range(chunks // 2))

    @pl.when(step == 2)
    def _():
        pass_on(range(chunks // 2, chunks))

    half = 4

    for distance in range(1, groups - 1):

        @pl.when(step == 3 * distance - 1)
        def _():
            hand_over(distance)

    @pl.when(step < half)
    def _():
        rows[...] = rows_ref[0]

    @pl.when(step == half + 1)
    def _():
        for number in range(chunks):
            sibling_copy(number).wait_recv()

    @pl.when(step == half + 3)
    def _():
        for number in range(chunks):
            on_copy(number).wait_recv()

    @pl.when(step >= half)
    def _():
        rows[...] = arrived[quarter_at(step - half, tensor)]

    inputs = rows[...].astype(f32).T
    center = inputs - jnp.mean(inputs, axis=0, keepdims=True)
    scaling = lax.rsqrt(jnp.mean(center * center, axis=0, keepdims=True) + EPSILON)
    hat = center * scaling
    hat_ref[...] = hat.astype(bf16)
    scale_ref[...] = scaling
    entry = (hat * gain_ref[...] + shift_ref[...]).astype(bf16)
    projected = product(weight_t[...], entry)
    cosine = cosine_ref[...]
    sine = sine_ref[...]
    tokens = cosine.shape[1]
    group = heads * HDIM
    segment = segment_ref[...]
    number = lax.broadcasted_iota(jnp.int32, (WIDE - HDIM, tokens), 0)
    same = (number == segment).astype(f32)
    extra_query = same
    extra_key = jnp.where(
        number < SEGMENTS, (same - 1.0) * MASKED, jnp.where(number < SEGMENTS + 3, 1.0, 0.0)
    )
    extra_value = jnp.where(number < 3, 1.0, 0.0)
    norms = []
    for head in range(heads):

        def turned(kind, factor):
            at = kind * group + head * HDIM
            front = projected[at : at + HALF]
            back = projected[at + HALF : at + HDIM]
            return jnp.concatenate(
                [(front * cosine - back * sine) * factor, (front * sine + back * cosine) * factor],
                axis=0,
            )

        queries = turned(0, 0.125 * LOG2E)
        keys = turned(1, 1.0)
        values = projected[2 * group + head * HDIM : 2 * group + (head + 1) * HDIM]
        norms.append(jnp.sum(queries * queries, axis=0, keepdims=True))
        norms.append(jnp.sum(keys * keys, axis=0, keepdims=True))
        query_ref[head] = jnp.concatenate([queries, extra_query], axis=0).astype(bf16)
        wide_keys = jnp.concatenate([keys, extra_key], axis=0)
        key_ref[head] = wide_keys.T.astype(bf16)
        key_t_ref[head] = wide_keys.astype(bf16)
        value_t_ref[head] = jnp.concatenate([values, extra_value], axis=0).astype(bf16)
    norms += [jnp.zeros_like(norms[0])] * (norm_ref.shape[0] - len(norms))
    norm_ref[...] = jnp.concatenate(norms, axis=0)

    @pl.when(step == pl.num_programs(0) - 1)
    def _():
        for away in range(1, groups):
            shard_copy(away).wait_send()
        for number in range(chunks):
            block_copy(number).wait_send()
            across_copy(number).wait_send()
            sibling_copy(number).wait_send()
            on_copy(number).wait_send()
        hand_over(groups - 1)
        finish_forward()


def entry_call(tokens, shard, forward_shard, gain, shift, cosine, sine, segment, groups, tile):
    length = cosine.shape[1]
    shard_rows, width = shard.shape
    depth = shard_rows * groups
    heads = width // (3 * HDIM)
    half = tokens.shape[1] // tile
    chunks = 4

    def place(i):
        context = lax.axis_index("context")
        other = (1 - context) * half + quarter_at(jnp.maximum(i - half, 0), lax.axis_index("tensor"))
        return jnp.where(i < half, context * half + i, other)

    lanes = lambda i: (0, place(i))
    heads_lanes = lambda i: (0, 0, place(i))
    heads_rows = lambda i: (0, place(i), 0)
    whole = lambda i: (0, 0)
    shapes = [
        jax.ShapeDtypeStruct((heads, WIDE, length), bf16),
        jax.ShapeDtypeStruct((heads, length, WIDE), bf16),
        jax.ShapeDtypeStruct((heads, WIDE, length), bf16),
        jax.ShapeDtypeStruct((heads, WIDE, length), bf16),
        jax.ShapeDtypeStruct((depth, length), bf16),
        jax.ShapeDtypeStruct((1, length), f32),
        jax.ShapeDtypeStruct((8, length), f32),
        jax.ShapeDtypeStruct((depth, width), bf16),
        jax.ShapeDtypeStruct((depth, forward_shard.shape[1]), bf16),
    ]
    dma = lambda *shape: [pltpu.SemaphoreType.DMA(shape)] * 2
    return pl.pallas_call(
        partial(entry_kernel, heads=heads, groups=groups),
        grid=(2 * half,),
        in_specs=[
            pl.BlockSpec(memory_space=pl.ANY),
            pl.BlockSpec(
                (1, tile, depth),
                lambda i: (lax.axis_index("context"), jnp.minimum(i, half - 1), 0),
            ),
            pl.BlockSpec(memory_space=pl.ANY),
            pl.BlockSpec(forward_shard.shape, whole),
            pl.BlockSpec((depth, 1), whole),
            pl.BlockSpec((depth, 1), whole),
            pl.BlockSpec((HALF, tile), lanes),
            pl.BlockSpec((HALF, tile), lanes),
            pl.BlockSpec((1, tile), lanes),
        ],
        out_specs=[
            pl.BlockSpec((heads, WIDE, tile), heads_lanes),
            pl.BlockSpec((heads, tile, WIDE), heads_rows),
            pl.BlockSpec((heads, WIDE, tile), heads_lanes),
            pl.BlockSpec((heads, WIDE, tile), heads_lanes),
            pl.BlockSpec((depth, tile), lanes),
            pl.BlockSpec((1, tile), lanes),
            pl.BlockSpec((8, tile), lanes),
            pl.BlockSpec((depth, width), whole),
            pl.BlockSpec(memory_space=pl.ANY),
        ],
        out_shape=shapes,
        scratch_shapes=[
            pltpu.VMEM((groups, shard_rows, width), bf16),
            pltpu.VMEM((width, depth), bf16),
            pltpu.VMEM((tile, depth), bf16),
            pltpu.VMEM((4, tile, depth), bf16),
            *dma(groups - 1),
            pltpu.SemaphoreType.DMA,
            *dma(chunks),
            *dma(chunks),
            *dma(chunks),
            *dma(chunks),
            pltpu.SemaphoreType.DMA((2, groups)),
            pltpu.SemaphoreType.DMA((groups,)),
            pltpu.SemaphoreType.DMA,
        ],
        compiler_params=pltpu.CompilerParams(
            vmem_limit_bytes=VMEM, collective_id=1, has_side_effects=True
        ),
        cost_estimate=cost(4 * tokens.shape[1] * depth * width, tokens, *shapes),
        name="entry",
    )(tokens, tokens, shard, forward_shard, gain, shift, cosine, sine, segment)


def attend_kernel(
    range_ref, query_ref, key_ref, value_ref, norm_ref, out_ref, told_ref, total_ref, top_ref, safe_ref, *, block
):
    step = pl.program_id(0)
    first, count = range_ref[0, step], range_ref[1, step]
    heads = query_ref.shape[0]
    total_ref[...] = jnp.zeros_like(total_ref)

    @pl.when(step == 0)
    def _():
        largest = 0.0
        for head in range(heads):
            queries, keys = norm_ref[2 * head : 2 * head + 1], norm_ref[2 * head + 1 : 2 * head + 2]
            largest = jnp.maximum(largest, jnp.max(queries) * jnp.max(keys))
        safe_ref[0] = (largest <= SAFE_EXPONENT**2).astype(jnp.int32)

    def scores(head, at):
        return product(key_ref[head, pl.ds(at, block), :], query_ref[head])

    def mix(head, at, weights):
        return product(value_ref[head, :, pl.ds(at, block)], weights)

    @pl.when(safe_ref[0] == 1)
    def _():
        top_ref[...] = jnp.zeros_like(top_ref)

        def body(number, carry):
            at = pl.multiple_of(first + number * block, WIDE)
            raw = [scores(head, at) for head in range(heads)]
            weights = [jnp.exp2(one).astype(bf16) for one in raw]
            for head in range(heads):
                total_ref[head] += mix(head, at, weights[head])
            return carry

        lax.fori_loop(0, count, body, 0)

    @pl.when(safe_ref[0] != 1)
    def _():
        top_ref[...] = jnp.full_like(top_ref, -3e38)

        def body(number, carry):
            at = pl.multiple_of(first + number * block, WIDE)
            for head in range(heads):
                raw = scores(head, at)
                before = top_ref[head]
                top = jnp.maximum(before, jnp.max(raw, axis=0, keepdims=True))
                weights = jnp.exp2(raw - top).astype(bf16)
                total_ref[head] = total_ref[head] * jnp.exp2(before - top) + mix(head, at, weights)
                top_ref[head] = top
            return carry

        lax.fori_loop(0, count, body, 0)

    tile = query_ref.shape[2]
    number = lax.broadcasted_iota(jnp.int32, (16, tile), 0)
    for head in range(heads):
        total = total_ref[head]
        mass = total[HDIM : HDIM + 1]
        out_ref[0, pl.ds(head * HDIM, HDIM), :] = (total[:HDIM] * (1.0 / mass)).astype(bf16)
        rows = split_rows(-(top_ref[head] + jnp.log2(mass)), number, SEGMENTS)
        told_ref[head, :HDIM, :] = query_ref[head, :HDIM, :]
        told_ref[head, HDIM : HDIM + 16, :] = jnp.where(
            number < SEGMENTS, query_ref[head, HDIM : HDIM + 16, :].astype(f32), rows
        ).astype(bf16)
        told_ref[head, HDIM + 16 :, :] = query_ref[head, HDIM + 16 :, :]


def split_rows(values, number, first):
    high = values.astype(bf16).astype(f32)
    rest = values - high
    middle = rest.astype(bf16).astype(f32)
    low = rest - middle
    return jnp.where(
        number == first,
        high,
        jnp.where(number == first + 1, middle, jnp.where(number == first + 2, low, 0.0)),
    )


def attend_call(ranges, queries, keys, values_t, norms, tile, block):
    heads, _, length = queries.shape
    rows = HDIM + 16
    return pl.pallas_call(
        partial(attend_kernel, block=block),
        grid_spec=pltpu.PrefetchScalarGridSpec(
            num_scalar_prefetch=1,
            grid=(length // tile,),
            in_specs=[
                pl.BlockSpec((heads, WIDE, tile), lambda i, r: (0, 0, i)),
                pl.BlockSpec((heads, length, WIDE), lambda i, r: (0, 0, 0)),
                pl.BlockSpec((heads, rows, length), lambda i, r: (0, 0, 0)),
                pl.BlockSpec(norms.shape, lambda i, r: (0, 0)),
            ],
            out_specs=[
                pl.BlockSpec((1, heads * HDIM, tile), lambda i, r: (i, 0, 0)),
                pl.BlockSpec((heads, WIDE, tile), lambda i, r: (0, 0, i)),
            ],
            scratch_shapes=[
                pltpu.VMEM((heads, rows, tile), f32),
                pltpu.VMEM((heads, 1, tile), f32),
                pltpu.SMEM((1,), jnp.int32),
            ],
        ),
        out_shape=[
            jax.ShapeDtypeStruct((length // tile, heads * HDIM, tile), bf16),
            jax.ShapeDtypeStruct((heads, WIDE, length), bf16),
        ],
        compiler_params=pltpu.CompilerParams(vmem_limit_bytes=VMEM),
        cost_estimate=cost(4 * heads * length * length * WIDE, queries, keys, values_t),
        name="attend",
    )(ranges, queries, keys, values_t, norms)


def attend_back_kernel(
    range_ref,
    query_ref,
    key_ref,
    value_ref,
    mixture_ref,
    grad_ref,
    cosine_ref,
    sine_ref,
    grad_query_ref,
    grad_key_ref,
    grad_value_ref,
    wide_ref,
    query_rows,
    grad_rows,
    query_total,
    key_total,
    value_total,
    *,
    block,
):
    step = pl.program_id(0)
    first, count = range_ref[0, step], range_ref[1, step]
    heads, _, tile = query_ref.shape

    @pl.when(step == 0)
    def _():
        wide_ref[...] = jnp.zeros_like(wide_ref)
        key_total[...] = jnp.zeros_like(key_total)
        value_total[...] = jnp.zeros_like(value_total)

    number = lax.broadcasted_iota(jnp.int32, (16, tile), 0)
    query_total[...] = jnp.zeros_like(query_total)
    for head in range(heads):
        at = pl.ds(head * HDIM, HDIM)
        grad = grad_ref[0, at, :]
        delta = jnp.sum(grad.astype(f32) * mixture_ref[0, at, :].astype(f32), axis=0, keepdims=True)
        wide_ref[head, :HDIM, :] = grad
        wide_ref[head, HDIM : HDIM + 16, :] = split_rows(-delta, number, 0).astype(bf16)
        query_rows[head] = query_ref[head].T
        grad_rows[head] = wide_ref[head].T

    def body(number, carry):
        at = pl.ds(pl.multiple_of(first + number * block, WIDE), block)
        raw = [product(query_rows[head], key_ref[head, :, at]) for head in range(heads)]
        slope = [product(grad_rows[head], value_ref[head, :, at]) for head in range(heads)]
        for head in range(heads):
            weights = jnp.exp2(raw[head])
            grad_scores = (weights * slope[head]).astype(bf16)
            value_total[head, :, at] += product(wide_ref[head, :HDIM, :], weights.astype(bf16))
            key_total[head, :, at] += product(query_ref[head, :HDIM, :], grad_scores)
            query_total[head] += against(key_ref[head, :HDIM, at], grad_scores)
        return carry

    lax.fori_loop(0, count, body, 0)

    def turned_back(grads, cosine, sine):
        front, back = grads[:HALF], grads[HALF:]
        return jnp.concatenate([front * cosine + back * sine, back * cosine - front * sine], axis=0)

    own = pl.ds(pl.multiple_of(step * tile, tile), tile)
    for head in range(heads):
        at = pl.ds(head * HDIM, HDIM)
        grad_query_ref[at, :] = turned_back(
            query_total[head] * 0.125, cosine_ref[:, own], sine_ref[:, own]
        ).astype(bf16)

    @pl.when(step == pl.num_programs(0) - 1)
    def _():
        for head in range(heads):
            at = pl.ds(head * HDIM, HDIM)
            grad_key_ref[at, :] = turned_back(
                key_total[head] * (1.0 / LOG2E), cosine_ref[...], sine_ref[...]
            ).astype(bf16)
            grad_value_ref[at, :] = value_total[head].astype(bf16)


def attend_back_call(
    ranges, queries, keys_t, values_t, mixture, grad_mixture, cosine, sine, tile, block
):
    heads, _, length = queries.shape
    group = heads * HDIM
    whole2 = lambda i, r: (0, 0)
    whole3 = lambda i, r: (0, 0, 0)
    return pl.pallas_call(
        partial(attend_back_kernel, block=block),
        grid_spec=pltpu.PrefetchScalarGridSpec(
            num_scalar_prefetch=1,
            grid=(length // tile,),
            in_specs=[
                pl.BlockSpec((heads, WIDE, tile), lambda i, r: (0, 0, i)),
                pl.BlockSpec((heads, WIDE, length), whole3),
                pl.BlockSpec((heads, WIDE, length), whole3),
                pl.BlockSpec((1, group, tile), lambda i, r: (i, 0, 0)),
                pl.BlockSpec((1, group, tile), lambda i, r: (i, 0, 0)),
                pl.BlockSpec((HALF, length), whole2),
                pl.BlockSpec((HALF, length), whole2),
            ],
            out_specs=[
                pl.BlockSpec((group, tile), lambda i, r: (0, i)),
                pl.BlockSpec((group, length), whole2),
                pl.BlockSpec((group, length), whole2),
            ],
            scratch_shapes=[
                pltpu.VMEM((heads, WIDE, tile), bf16),
                pltpu.VMEM((heads, tile, WIDE), bf16),
                pltpu.VMEM((heads, tile, WIDE), bf16),
                pltpu.VMEM((heads, HDIM, tile), f32),
                pltpu.VMEM((heads, HDIM, length), f32),
                pltpu.VMEM((heads, HDIM, length), f32),
            ],
        ),
        out_shape=[jax.ShapeDtypeStruct((group, length), bf16)] * 3,
        compiler_params=pltpu.CompilerParams(vmem_limit_bytes=VMEM),
        cost_estimate=cost(10 * heads * length * length * WIDE, queries, keys_t, values_t),
        name="attend_back",
    )(ranges, queries, keys_t, values_t, mixture, grad_mixture, cosine, sine)


def middle_kernel(
    mixture_ref,
    rows_ref,
    cotangent_ref,
    valid_ref,
    mod_ref,
    up_bias_ref,
    down_bias_ref,
    out_blocks_ref,
    own_ref,
    other_ref,
    across_ref,
    result_ref,
    grad_mixture_ref,
    grad_middle_ref,
    grad_out_blocks_ref,
    sums_ref,
    bias_sums_ref,
    up_keep_ref,
    up_send_ref,
    down_keep_ref,
    down_send_ref,
    own_mixture,
    out_weight_ref,
    grad_out_ref,
    entry_rows,
    entry_columns,
    grad_output_rows,
    grad_output_columns,
    attended_rows,
    output_rows,
    grad_entry_rows,
    active,
    grad_hidden,
    grad_staged,
    forward_ref,
    landed,
    home_grads,
    to_sibling,
    from_sibling,
    staged_up,
    staged_down,
    sent_mixture,
    got_mixture,
    own_copied,
    sent_grad,
    got_grad,
    grad_copied,
    sent_part,
    got_part,
    kept,
    sent_next,
    got_next,
    loaded,
    sent_other,
    got_other,
    sent_last,
    got_last,
    *,
    tile,
    tiles,
    parts,
    groups,
):
    step = pl.program_id(0)
    context, tensor = lax.axis_index("context"), lax.axis_index("tensor")
    ranks = 4
    everyone = 2 * ranks
    place = context * ranks + tensor
    core = lax.rem(tensor, 2)
    sibling = tensor + 1 - 2 * core
    depth = rows_ref.shape[2]
    group = depth // ranks
    per_sequence = tiles // 2
    part_tiles = tiles // PART_TILES
    per_part = part_tiles + 1
    back_from = tiles + parts * per_part - 1
    last_step = back_from + tiles
    root = math.sqrt(2.0 / math.pi)

    def member(away):
        other = lax.rem(place + away, everyone)
        return other, {"context": other // ranks, "tensor": lax.rem(other, ranks)}

    def mixture_copy(away):
        other, device = member(away)
        return copy_to(
            mixture_ref.at[other],
            own_mixture.at[place],
            sent_mixture.at[away - 1],
            got_mixture.at[lax.rem(place + everyone, everyone)],
            **device,
        )

    def mixture_arrival(source):
        return pltpu.make_async_remote_copy(
            src_ref=mixture_ref.at[source],
            dst_ref=own_mixture.at[source],
            send_sem=sent_mixture.at[0],
            recv_sem=got_mixture.at[source],
            device_id={"tensor": sibling},
            device_id_type=pl.DeviceIdType.MESH,
        )

    def own_copy():
        return pltpu.make_async_copy(mixture_ref.at[place], own_mixture.at[place], own_copied)

    def part_copy(slot):
        return copy_to(
            to_sibling, from_sibling.at[slot], sent_part.at[slot], got_part.at[slot], tensor=sibling
        )

    across = lax.rem(tensor + 2, ranks)
    height = depth // groups

    def rows_of(number):
        return pl.ds(number * height, height)

    def next_copy(kind):
        return copy_to(
            forward_ref.at[kind],
            landed.at[0, kind],
            sent_next.at[kind],
            got_next.at[kind],
            tensor=sibling,
        )

    def out_blocks():
        for rank in range(ranks):
            for number in range(groups):
                rows = slice(rank * group, (rank + 1) * group)
                yield rank * groups + number, (rows, slice(number * height, (number + 1) * height))

    def weight_loads():
        return [
            pltpu.make_async_copy(own_ref, forward_ref.at[context], loaded.at[0]),
            pltpu.make_async_copy(other_ref, forward_ref.at[1 - context], loaded.at[1]),
            pltpu.make_async_copy(across_ref, landed.at[1, context], loaded.at[2]),
        ]

    def other_copy(kind, number):
        place = landed.at[1, kind, rows_of(number), :]
        return copy_to(place, place, sent_other.at[number], got_other.at[number], context=1 - context)

    def last_copy(kind, number):
        return copy_to(
            landed.at[1, kind, rows_of(number), :],
            landed.at[2, kind, rows_of(number), :],
            sent_last.at[kind, number],
            got_last.at[kind, number],
            tensor=sibling,
        )

    def take_other(numbers):
        for number in numbers:
            other_copy(1 - context, number).wait_recv()
            last_copy(1 - context, number).start()

    def gradient_lanes(at):
        return pl.ds(pl.multiple_of(lax.rem(at, per_sequence) * tile, tile), tile)

    def sequence_of(at):
        return lax.rem(at // per_sequence + context, 2)

    def gradient_copy(at, rank):
        return copy_to(
            grad_staged.at[at, rank],
            grad_mixture_ref.at[place, :, gradient_lanes(at)],
            sent_grad.at[at, rank],
            got_grad.at[place, lax.rem(at, per_sequence)],
            context=sequence_of(at),
            tensor=rank,
        )

    def gradient_own(at):
        return pltpu.make_async_copy(
            grad_staged.at[at, tensor],
            grad_mixture_ref.at[place, :, gradient_lanes(at)],
            grad_copied.at[lax.rem(at, per_sequence)],
        )

    def gradient_arrival(source, number):
        return pltpu.make_async_remote_copy(
            src_ref=grad_staged.at[0, 0],
            dst_ref=grad_mixture_ref.at[source, :, pl.ds(number * tile, tile)],
            send_sem=sent_grad.at[0, 0],
            recv_sem=got_grad.at[source, number],
            device_id={"tensor": sibling},
            device_id_type=pl.DeviceIdType.MESH,
        )

    def kept_copies(slot):
        if slot == 1:
            return [
                pltpu.make_async_copy(staged_up, up_send_ref, kept.at[0]),
                pltpu.make_async_copy(staged_down.at[0], down_keep_ref.at[0], kept.at[1]),
                pltpu.make_async_copy(staged_down.at[1], down_send_ref.at[0], kept.at[2]),
            ]
        return [
            pltpu.make_async_copy(staged_up, up_keep_ref, kept.at[3]),
            pltpu.make_async_copy(staged_down.at[0], down_keep_ref.at[1], kept.at[4]),
            pltpu.make_async_copy(staged_down.at[1], down_send_ref.at[1], kept.at[5]),
        ]

    def tile_of(at):
        sequence = sequence_of(at)
        rows = pl.ds(pl.multiple_of(at * tile, tile), tile)
        mods = mod_ref[sequence]
        lanes = gradient_lanes(at)
        mixture_t = jnp.concatenate(
            [own_mixture[sequence * ranks + rank, :, lanes] for rank in range(ranks)], axis=0
        )
        return rows, mixture_t, tuple(mods[k : k + 1] for k in range(4))

    def normal(attended, gate_one):
        middle = rows_ref[0].astype(f32) + gate_one * attended
        center = middle - jnp.mean(middle, axis=-1, keepdims=True)
        scaling = lax.rsqrt(jnp.mean(center * center, axis=-1, keepdims=True) + EPSILON)
        return middle, center * scaling, scaling

    @pl.when(step == 0)
    def _():
        own_copy().start()
        for one in weight_loads():
            one.start()
        greet([member(away)[1] for away in range(1, everyone)])
        for near in (True, False):
            for away in range(1, everyone):

                @pl.when((member(away)[0] // ranks == context) == near)
                def _():
                    mixture_copy(away).start()

        for block, at in out_blocks():
            out_weight_ref[at] = out_blocks_ref[block]
        sums_ref[...] = jnp.zeros_like(sums_ref)
        bias_sums_ref[...] = jnp.zeros_like(bias_sums_ref)
        grad_out_ref[...] = jnp.zeros_like(grad_out_ref)

    for sequence in range(2):

        @pl.when(step == lax.rem(sequence + context, 2) * per_sequence)
        def _():
            for rank in range(ranks):
                source = sequence * ranks + rank

                @pl.when(place == source)
                def _():
                    own_copy().wait()

                @pl.when(place != source)
                def _():
                    mixture_arrival(source).wait_recv()

    @pl.when(step == per_sequence)
    def _():
        for one in weight_loads():
            one.wait()
        for kind in range(2):
            next_copy(kind).start()
        for number in range(groups):
            other_copy(context, number).start()
            last_copy(context, number).start()

    @pl.when(step == tiles + per_part)
    def _():
        for kind in range(2):
            next_copy(kind).wait_recv()

    @pl.when(step == tiles + 2 * per_part - 1)
    def _():
        take_other(range(groups // 2))

    @pl.when(step == tiles + 2 * per_part)
    def _():
        take_other(range(groups // 2, groups))

    @pl.when(step == tiles + 2 * per_part)
    def _():
        for kind in range(2):
            for number in range(groups):
                last_copy(kind, number).wait_recv()

    @pl.when(step < tiles)
    def _():
        rows, mixture_t, (gate_one, shift_two, gain_two, gate_two) = tile_of(step)
        attended = product(mixture_t.T, out_weight_ref[...])
        attended_rows[rows, :] = attended
        _, hat, _ = normal(attended, gate_one)
        entry = (hat * gain_two + shift_two).astype(bf16)
        grad_output = (gate_two * (cotangent_ref[0].astype(f32) * valid_ref[...])).astype(bf16)
        entry_rows[rows, :] = entry
        entry_columns[:, rows] = entry.T
        grad_output_rows[rows, :] = grad_output
        grad_output_columns[:, rows] = grad_output.T
        output_rows[rows, :] = jnp.broadcast_to(down_bias_ref[...], (tile, depth))
        grad_entry_rows[rows, :] = jnp.zeros((tile, depth), f32)

    inner = lax.rem(step - tiles, per_part)
    position = (step - tiles) // per_part
    in_parts = (step >= tiles) & (step < back_from)

    def part_tile(up, down):
        number = part_at(position, tensor)
        size = tile * PART_TILES // PART_CUTS
        for sub in range(PART_CUTS):
            rows = pl.ds(pl.multiple_of((inner * PART_CUTS + sub) * size, size), size)
            hidden = product(entry_rows[rows, :], up[...]) + up_bias_ref[0]
            square = hidden * hidden
            bent = jnp.tanh(root * hidden * (1.0 + 0.044715 * square))
            half = 0.5 * (1.0 + bent)
            activated = (hidden * half).astype(bf16)
            slope = half + (0.5 * root) * hidden * (1.0 - bent * bent) * (1.0 + 0.134145 * square)
            grads = (product(grad_output_rows[rows, :], down[...]) * slope).astype(bf16)
            output_rows[rows, :] += against(activated, down[...])
            grad_entry_rows[rows, :] += against(grads, up[...])
            active[rows, :] = activated
            grad_hidden[rows, :] = grads
            bias_sums_ref[number] += jnp.sum(grads.astype(f32), axis=0, keepdims=True)

    @pl.when(in_parts & (inner < part_tiles) & (position == 0))
    def _():
        part_tile(forward_ref.at[0], forward_ref.at[1])

    @pl.when(in_parts & (inner < part_tiles) & (position > 0))
    def _():
        place = lax.rem((position - 1) * 2, 3)
        part_tile(landed.at[place, 0], landed.at[place, 1])

    def products():
        both = [product(entry_columns[...], grad_hidden[...]), product(grad_output_columns[...], active[...])]
        return lambda other: [one[other * height : (other + 1) * height] for one in both]

    def kept_terms():
        return lambda other: [home_grads[kind, rows_of(other), :].astype(f32) for kind in range(2)]

    def gather_home(slot, own):
        part_copy(slot).wait_recv()
        if slot:
            for one in kept_copies(0):
                one.wait()
        terms = own()
        for other in range(groups):
            for kind, (staged, term) in enumerate(zip((staged_up, staged_down), terms(other))):
                total = (term + from_sibling[slot, kind, rows_of(other), :].astype(f32)).astype(bf16)
                staged[context, other] = total[: height // 2]
                staged[1 - context, other] = total[height // 2 :]
        for one in kept_copies(slot):
            one.start()

    for turn in range(parts):

        @pl.when(step == (tiles + turn * per_part + part_tiles if turn < parts - 1 else last_step))
        def _():
            if turn == 2:
                gather_home(0, kept_terms)
                part_copy(0).wait_send()
            if turn == 3:
                gather_home(1, products)
                return
            target = home_grads if turn == 0 else to_sibling
            terms = products()
            for other in range(groups):
                for kind, term in enumerate(terms(other)):
                    target[kind, rows_of(other), :] = term.astype(bf16)
            if turn:
                part_copy(turn - 1).start()

    @pl.when((step >= back_from) & (step < last_step))
    def _():
        at = lax.rem(step - back_from + per_sequence, tiles)
        sequence = sequence_of(at)
        rows, mixture_t, (gate_one, _, gain_two, gate_two) = tile_of(at)
        attended = attended_rows[rows, :]
        middle, hat, scaling = normal(attended, gate_one)
        output = output_rows[rows, :]
        grad_entry = grad_entry_rows[rows, :]
        grad_result = cotangent_ref[0].astype(f32) * valid_ref[...]
        result_ref[...] = (middle + gate_two * output).astype(bf16)
        grad_lifted = grad_entry * gain_two
        grad_middle = grad_result + scaling * (
            grad_lifted
            - jnp.mean(grad_lifted, axis=-1, keepdims=True)
            - hat * jnp.mean(grad_lifted * hat, axis=-1, keepdims=True)
        )
        grad_attended = (gate_one * grad_middle).astype(bf16)
        grad_mixture = against(out_weight_ref[...], grad_attended).astype(bf16)
        for rank in range(ranks):
            grad_staged[at, rank] = grad_mixture[rank * group : (rank + 1) * group]
        for rank in range(ranks):
            own = (sequence == context) & (tensor == rank)

            @pl.when(own)
            def _():
                gradient_own(at).start()

            @pl.when(jnp.logical_not(own))
            def _():
                gradient_copy(at, rank).start()

        grad_middle_ref[0] = grad_middle.T.astype(bf16)
        grad_out_ref[...] += product(mixture_t, grad_attended)
        lines = [
            jnp.sum(grad_middle * attended, axis=0, keepdims=True),
            jnp.sum(grad_entry, axis=0, keepdims=True),
            jnp.sum(grad_entry * hat, axis=0, keepdims=True),
            jnp.sum(grad_result * output, axis=0, keepdims=True),
            jnp.sum(grad_output_rows[rows, :].astype(f32), axis=0, keepdims=True),
        ]
        lines += [jnp.zeros_like(lines[0])] * (sums_ref.shape[1] - len(lines))
        sums_ref[sequence] += jnp.concatenate(lines, axis=0)

    @pl.when(step == last_step)
    def _():
        for block, at in out_blocks():
            grad_out_blocks_ref[block] = grad_out_ref[at].astype(bf16)
        for source in range(everyone):
            for number in range(per_sequence):

                @pl.when(place != source)
                def _():
                    gradient_arrival(source, number).wait_recv()

        for at in range(tiles):
            for rank in range(ranks):
                own = (sequence_of(at) == context) & (tensor == rank)

                @pl.when(own)
                def _():
                    gradient_own(at).wait()

                @pl.when(jnp.logical_not(own))
                def _():
                    gradient_copy(at, rank).wait_send()

        for away in range(1, everyone):
            mixture_copy(away).wait_send()
        for kind in range(2):
            next_copy(kind).wait_send()
        for number in range(groups):
            other_copy(context, number).wait_send()
            for kind in range(2):
                last_copy(kind, number).wait_send()
        part_copy(1).wait_send()
        for one in kept_copies(1):
            one.wait()


def part_at(position, tensor):
    return quarter_at(jnp.where(position < 2, position, 5 - position), tensor)


def middle_call(
    mixture, rows, cotangent, valid, mods, up_bias, down_bias, out_blocks, own_weight, other_weight, across, groups, tile
):
    pieces, group, own = mixture.shape
    depth = rows.shape[2]
    tokens = rows.shape[0] * own
    parts, _, part_width = up_bias.shape
    tiles = tokens // tile
    per_sequence = tiles // 2
    per_part = tiles // PART_TILES + 1
    back_from = tiles + parts * per_part - 1
    half = depth // groups // 2

    def in_order(at):
        sequence = lax.rem(at // per_sequence + lax.axis_index("context"), 2)
        return sequence, lax.rem(at, per_sequence)

    def back_number(i):
        return lax.rem(jnp.clip(i - back_from, 0, tiles - 1) + per_sequence, tiles)

    def token_place(i):
        return in_order(jnp.where(i < tiles, i, back_number(i)))

    def token_tile(i):
        sequence, number = token_place(i)
        return sequence, lax.axis_index("tensor") * per_sequence + number, 0

    def valid_tile(i):
        sequence, number = token_place(i)
        return sequence * per_sequence + number, 0

    def part_block(i):
        position = jnp.clip((i - tiles) // per_part, 0, parts - 1)
        return part_at(position, lax.axis_index("tensor")), 0, 0

    def back_tile(i):
        return in_order(back_number(i))

    whole2 = lambda i: (0, 0)
    whole3 = lambda i: (0, 0, 0)
    once = pl.Buffered(1)
    hbm = pl.BlockSpec(memory_space=pl.ANY)
    kept = jax.ShapeDtypeStruct((2, groups, half, part_width), bf16)
    wide = (tokens, depth)
    return pl.pallas_call(
        partial(middle_kernel, tile=tile, tiles=tiles, parts=parts, groups=groups),
        grid=(back_from + tiles + 1,),
        in_specs=[
            hbm,
            pl.BlockSpec((1, tile, depth), token_tile),
            pl.BlockSpec((1, tile, depth), token_tile),
            pl.BlockSpec((tile, 1), valid_tile),
            pl.BlockSpec(mods.shape, whole3, pipeline_mode=once),
            pl.BlockSpec((1, 1, part_width), part_block),
            pl.BlockSpec((1, depth), whole2, pipeline_mode=once),
            pl.BlockSpec(out_blocks.shape, whole3, pipeline_mode=once),
            hbm,
            hbm,
            hbm,
        ],
        out_specs=[
            pl.BlockSpec(
                (tile, depth), lambda i: (back_tile(i)[0] * per_sequence + back_tile(i)[1], 0)
            ),
            hbm,
            pl.BlockSpec(
                (1, depth, tile),
                lambda i: (back_tile(i)[0], 0, back_tile(i)[1]),
            ),
            pl.BlockSpec(out_blocks.shape, whole3),
            pl.BlockSpec((2, 8, depth), whole3),
            pl.BlockSpec((parts, 1, part_width), whole3),
            hbm,
            hbm,
            hbm,
            hbm,
        ],
        out_shape=[
            jax.ShapeDtypeStruct((tokens, depth), bf16),
            jax.ShapeDtypeStruct(mixture.shape, bf16),
            jax.ShapeDtypeStruct((2, depth, own), bf16),
            jax.ShapeDtypeStruct(out_blocks.shape, bf16),
            jax.ShapeDtypeStruct((2, 8, depth), f32),
            jax.ShapeDtypeStruct((parts, 1, part_width), f32),
            kept,
            kept,
            kept,
            kept,
        ],
        scratch_shapes=[
            pltpu.VMEM(mixture.shape, bf16),
            pltpu.VMEM((depth, depth), bf16),
            pltpu.VMEM((depth, depth), f32),
            pltpu.VMEM(wide, bf16),
            pltpu.VMEM((depth, tokens), bf16),
            pltpu.VMEM(wide, bf16),
            pltpu.VMEM((depth, tokens), bf16),
            pltpu.VMEM(wide, f32),
            pltpu.VMEM(wide, f32),
            pltpu.VMEM(wide, f32),
            pltpu.VMEM((tokens, part_width), bf16),
            pltpu.VMEM((tokens, part_width), bf16),
            pltpu.VMEM((tiles, 4, group, tile), bf16),
            pltpu.VMEM((2, depth, part_width), bf16),
            pltpu.VMEM((3, 2, depth, part_width), bf16),
            pltpu.VMEM((2, depth, part_width), bf16),
            pltpu.VMEM((2, depth, part_width), bf16),
            pltpu.VMEM((2, 2, depth, part_width), bf16),
            pltpu.VMEM((2, groups, half, part_width), bf16),
            pltpu.VMEM((2, groups, half, part_width), bf16),
            pltpu.SemaphoreType.DMA((pieces - 1,)),
            pltpu.SemaphoreType.DMA((pieces,)),
            pltpu.SemaphoreType.DMA,
            pltpu.SemaphoreType.DMA((tiles, 4)),
            pltpu.SemaphoreType.DMA((pieces, per_sequence)),
            pltpu.SemaphoreType.DMA((per_sequence,)),
            pltpu.SemaphoreType.DMA((2,)),
            pltpu.SemaphoreType.DMA((2,)),
            pltpu.SemaphoreType.DMA((6,)),
            *[pltpu.SemaphoreType.DMA((2,))] * 2,
            pltpu.SemaphoreType.DMA((3,)),
            *[pltpu.SemaphoreType.DMA((groups,))] * 2,
            *[pltpu.SemaphoreType.DMA((2, groups))] * 2,
        ],
        compiler_params=pltpu.CompilerParams(
            vmem_limit_bytes=VMEM_MOST, collective_id=2, has_side_effects=True
        ),
        cost_estimate=cost(6 * tokens * depth * (depth + 3 * parts * part_width), rows, rows, rows),
        name="middle",
    )(mixture, rows, cotangent, valid, mods, up_bias, down_bias, out_blocks, own_weight, other_weight, across)


class Relay:
    def __init__(self, own, out, arrived, sent, got, fsdp, groups):
        self.own, self.out, self.arrived, self.sent, self.got = own, out, arrived, sent, got
        self.fsdp, self.groups = fsdp, groups

    def copy(self, side, target):
        return copy_to(
            self.out.at[side, target],
            self.arrived.at[side, target],
            self.sent.at[side, target],
            self.got.at[side, target],
            fsdp=self.fsdp - 1 if side else self.fsdp + 1,
        )

    def begin(self, target):
        for side, end in ((0, 0), (1, self.groups - 1)):
            if target != end:

                @pl.when(self.fsdp == end)
                def _():
                    self.out[side, target] = self.own[target]
                    self.copy(side, target).start()

    def turn(self, number):
        last = self.groups - 1
        for side in range(2):
            behind = last - self.fsdp if side else self.fsdp

            @pl.when((behind >= 1) & (behind <= number))
            def _():
                target = self.fsdp + (number - last if side else last - number)
                self.copy(side, target).wait_recv()
                if number < last:
                    total = self.own[target].astype(f32) + self.arrived[side, target].astype(f32)
                    self.out[side, target] = total.astype(bf16)
                    self.copy(side, target).start()

    def total(self, sum_ref):
        sum_ref[...] = self.own[self.fsdp].astype(f32)
        for side, end in ((0, 0), (1, self.groups - 1)):

            @pl.when(self.fsdp != end)
            def _():
                sum_ref[...] += self.arrived[side, self.fsdp].astype(f32)

    def finish(self):
        for target in range(self.groups):
            for side, sends in ((0, self.fsdp < target), (1, self.fsdp > target)):

                @pl.when(sends)
                def _():
                    self.copy(side, target).wait_send()


def entry_back_kernel(
    grad_query_ref,
    grad_key_ref,
    grad_value_ref,
    hat_ref,
    scale_ref,
    gain_ref,
    shift_ref,
    weight_ref,
    middle_ref,
    middle_in_ref,
    small_ref,
    up_ref,
    down_ref,
    grad_out_ref,
    result_ref,
    result_in_ref,
    out_ref,
    grad_weight_ref,
    lines_ref,
    embedded_ref,
    vectors_ref,
    pieces_ref,
    grad_out_sum_ref,
    block_ref,
    up_own,
    up_in,
    down_own,
    down_in,
    slices,
    slices_out,
    slices_in,
    slice_sum,
    context_slice,
    context_in,
    all_sums_ref,
    all_small_ref,
    small_part,
    small_in,
    small_sum,
    small_groups,
    out_in,
    loaded,
    sent_up,
    got_up,
    sent_down,
    got_down,
    sent_slice,
    got_slice,
    sent_context,
    got_context,
    sent_small,
    got_small,
    sent_sum,
    got_sum,
    sent_out,
    got_out,
    sent_result,
    got_result,
    moved,
    taken,
    held,
    weight_total,
    sums,
    part,
    part_in,
    pair,
    pair_in,
    chip,
    chip_in,
    piece,
    piece_out,
    piece_in,
    piece_sum,
    block_piece,
    block_in,
    rank_sums,
    rank_in,
    group_sums,
    group_in,
    sent_part,
    got_part,
    sent_pair,
    got_pair,
    sent_chip,
    got_chip,
    sent_piece,
    got_piece,
    sent_block,
    got_block,
    sent_rank,
    got_rank,
    sent_group,
    got_group,
    *,
    tiles,
    groups,
):
    step = pl.program_id(0)
    fsdp, context, tensor = (lax.axis_index(name) for name in ("fsdp", "context", "tensor"))
    ranks = 4
    half = tiles // 2
    core = lax.rem(tensor, 2)
    chip_x = tensor // 2
    sibling = tensor + 1 - 2 * core
    across = lax.rem(tensor + 2, ranks)
    place = fsdp * 2 + context
    depth = hat_ref.shape[0]
    slice_rows = depth // ranks
    weight_rows = depth // groups
    def up_copy(other):
        return copy_to(
            up_ref.at[1, other], up_in.at[other], sent_up.at[other], got_up.at[other], context=1 - context
        )

    def down_copy(other):
        return copy_to(
            down_ref.at[0, other], down_in.at[other], sent_down.at[other], got_down.at[other], tensor=across
        )

    def loads():
        return [
            pltpu.make_async_copy(up_ref.at[0], up_own, loaded.at[0]),
            pltpu.make_async_copy(down_ref.at[1], down_own, loaded.at[1]),
        ]

    far_first = [groups - 1, 0] + list(range(groups - 2, 0, -1))
    slice_relay = Relay(slices, slices_out, slices_in, sent_slice, got_slice, fsdp, groups)
    piece_relay = Relay(piece, piece_out, piece_in, sent_piece, got_piece, fsdp, groups)

    def context_copy():
        return copy_to(context_slice, context_in, sent_context, got_context, context=1 - context)

    rounds = [{"tensor": sibling}, {"tensor": across}, {"context": 1 - context}]

    def small_copy(number):
        return copy_to(
            small_part.at[number], small_in.at[number], sent_small.at[number], got_small.at[number], **rounds[number]
        )

    def sum_copy(away):
        return copy_to(
            small_sum,
            small_groups.at[away - 1],
            sent_sum.at[away - 1],
            got_sum.at[away - 1],
            fsdp=lax.rem(fsdp + away, groups),
        )

    def out_copy():
        return copy_to(grad_out_ref, out_in, sent_out, got_out, context=1 - context)

    quarter = result_ref.shape[1]

    def result_places():
        for number, (source, rank) in enumerate([(result_ref, tensor), (result_in_ref, across)]):
            rows = pl.ds(pl.multiple_of(rank * quarter, quarter), quarter)
            for sequence in range(2):
                yield number * 2 + sequence, source.at[sequence], block_ref.at[sequence, rows, :]

    def result_copies():
        return [
            copy_to(held.at[k], target, sent_result.at[k], got_result.at[k], tensor=sibling)
            for k, source, target in result_places()
        ]

    def result_loads():
        return [
            pltpu.make_async_copy(source, held.at[k], taken.at[k])
            for k, source, target in result_places()
        ]

    def result_moves():
        return [
            pltpu.make_async_copy(held.at[k], target, moved.at[k]) for k, source, target in result_places()
        ]

    def part_copy(tile):
        return copy_to(
            part.at[tile, 1 - core], part_in.at[tile], sent_part.at[tile], got_part.at[tile], tensor=sibling
        )

    def pair_copy(tile):
        return copy_to(
            pair.at[tile, 1 - chip_x], pair_in.at[tile], sent_pair.at[tile], got_pair.at[tile], tensor=across
        )

    def chip_copy(tile):
        return copy_to(
            chip.at[tile], chip_in.at[tile], sent_chip.at[tile], got_chip.at[tile], context=1 - context
        )

    def block_copy():
        return copy_to(block_piece, block_in, sent_block, got_block, context=1 - context)

    def rank_copy(number):
        return copy_to(
            rank_sums.at[number], rank_in.at[number], sent_rank.at[number], got_rank.at[number], **rounds[number]
        )

    def group_copy(away):
        return copy_to(
            group_sums,
            group_in.at[away - 1],
            sent_group.at[away - 1],
            got_group.at[away - 1],
            fsdp=lax.rem(fsdp + away, groups),
        )

    @pl.when(step == 0)
    def _():
        greet(
            rounds + [{"fsdp": lax.rem(fsdp + away, groups)} for away in range(1, groups)]
        )
        for other in far_first:
            up_copy(other).start()
            down_copy(other).start()
        out_copy().start()
        small_part[0] = small_ref[...]
        small_copy(0).start()
        for one in result_loads() + loads():
            one.start()
        weight_total[...] = jnp.zeros_like(weight_total)
        sums[...] = jnp.zeros_like(sums)

    @pl.when(step == 2)
    def _():
        for one in result_loads():
            one.wait()
        for one in result_copies() + result_moves():
            one.start()

    def grads():
        return jnp.concatenate([grad_query_ref[...], grad_key_ref[...], grad_value_ref[...]], axis=0)

    @pl.when(step < tiles)
    def _():
        tile = step
        columns = grads()
        grad_entry = product(weight_ref[...], columns)
        hat = hat_ref[...].astype(f32)
        lifted = hat * gain_ref[...]
        weight_total[...] += against((lifted + shift_ref[...]).astype(bf16), columns)
        grad_lifted = grad_entry * gain_ref[...]
        term = scale_ref[...] * (
            grad_lifted
            - jnp.mean(grad_lifted, axis=0, keepdims=True)
            - hat * jnp.mean(grad_lifted * hat, axis=0, keepdims=True)
        )
        extra = jnp.where(tile < half, middle_in_ref[...], middle_ref[0]).astype(f32)
        term = (term + jnp.where(lax.rem(tile, half) == tensor, extra, 0.0)).astype(bf16)
        for rank in range(ranks):
            part[tile, rank % 2, rank // 2] = term[rank * slice_rows : (rank + 1) * slice_rows]
        part_copy(tile).start()
        weighted = grad_entry * hat
        for lane in range(0, grad_entry.shape[1], WIDE):
            sums[0] += grad_entry[:, lane : lane + WIDE]
            sums[1] += weighted[:, lane : lane + WIDE]

    @pl.when(step == tiles - 1)
    def _():
        for other in range(groups):
            piece[other] = weight_total[other * weight_rows : (other + 1) * weight_rows].astype(bf16)
        for target in far_first:
            piece_relay.begin(target)

    @pl.when((step >= 1) & (step < tiles + 1))
    def _():
        tile = step - 1
        part_copy(tile).wait_recv()
        pair[tile] = (part[tile, core].astype(f32) + part_in[tile].astype(f32)).astype(bf16)
        pair_copy(tile).start()

    @pl.when((step >= 5) & (step < tiles + 5))
    def _():
        tile = step - 5
        pair_copy(tile).wait_recv()
        total = (pair[tile, chip_x].astype(f32) + pair_in[tile].astype(f32)).astype(bf16)

        @pl.when(tile < half)
        def _():
            chip[tile] = total
            chip_copy(tile).start()

        @pl.when(tile >= half)
        def _():
            out_ref[context, tile - half] = total

    @pl.when((step >= tiles + 1) & (step < tiles + 1 + half))
    def _():
        tile = step - tiles - 1
        chip_copy(tile).wait_recv()
        out_ref[1 - context, tile] = chip_in[tile]

    for number in range(3):

        @pl.when(step == (2, 5, 7)[number])
        def _():
            small_copy(number).wait_recv()
            total = small_part[number] + small_in[number]
            if number < 2:
                small_part[number + 1] = total
                small_copy(number + 1).start()
            else:
                small_sum[...] = total
                for away in range(1, groups):
                    sum_copy(away).start()

    for number, other in enumerate(far_first):

        @pl.when(step == 1 + number)
        def _():
            if number == 0:
                for one in loads():
                    one.wait()
            up_copy(other).wait_recv()
            down_copy(other).wait_recv()
            slices[other, 0] = (up_own[other].astype(f32) + up_in[other].astype(f32)).astype(bf16)
            slices[other, 1] = (down_own[other].astype(f32) + down_in[other].astype(f32)).astype(bf16)
            slice_relay.begin(other)

    for number in range(1, groups):

        @pl.when(step == tiles - 2 * (groups - 1 - number))
        def _():
            slice_relay.turn(number)

    @pl.when(step == tiles)
    def _():
        slice_relay.total(slice_sum)
        context_slice[...] = slice_sum[...].astype(bf16)
        context_copy().start()

    for number in range(1, groups):

        @pl.when(step == tiles + number - 1)
        def _():
            piece_relay.turn(number)

    @pl.when(step == tiles + 2)
    def _():
        piece_relay.total(piece_sum)
        block_piece[...] = piece_sum[...].astype(bf16)
        block_copy().start()

    @pl.when(step == tiles + 4)
    def _():
        block_copy().wait_recv()
        grad_weight_ref[...] = block_piece[...].astype(f32) + block_in[...].astype(f32)

    @pl.when(step == tiles - 1)
    def _():
        rows = [jnp.sum(sums[kind].T, axis=0, keepdims=True) for kind in range(2)]
        rank_sums[0] = jnp.concatenate(rows + [jnp.zeros((6, depth), f32)], axis=0)
        rank_copy(0).start()

    @pl.when(step == tiles)
    def _():
        rank_copy(0).wait_recv()
        rank_sums[1] = rank_sums[0] + rank_in[0]
        rank_copy(1).start()

    @pl.when(step == tiles + 3)
    def _():
        rank_copy(1).wait_recv()
        rank_sums[2] = rank_sums[1] + rank_in[1]
        rank_copy(2).start()

    @pl.when(step == tiles + 4)
    def _():
        rank_copy(2).wait_recv()
        group_sums[context] = rank_sums[2]
        group_sums[1 - context] = rank_in[2]
        for away in range(1, groups):
            group_copy(away).start()

    @pl.when(step == tiles + 4)
    def _():
        all_small_ref[fsdp] = small_sum[...]
        for away in range(1, groups):
            sum_copy(away).wait_recv()
            all_small_ref[lax.rem(fsdp + groups - away, groups)] = small_groups[away - 1]
            sum_copy(away).wait_send()
        context_copy().wait()
        pieces_ref[context] = context_slice[...]
        pieces_ref[1 - context] = context_in[...]
        out_copy().wait()
        grad_out_sum_ref[...] = grad_out_ref[...].astype(f32) + out_in[...].astype(f32)
        for other in range(groups):
            up_copy(other).wait_send()
            down_copy(other).wait_send()
        for number in range(3):
            small_copy(number).wait_send()
            rank_copy(number).wait_send()
        for one in result_copies() + result_moves():
            one.wait()
        for number in range(2):
            all_sums_ref[2 * fsdp + number] = group_sums[number]
        for away in range(1, groups):
            group_copy(away).wait_recv()
            for number in range(2):
                source = lax.rem(fsdp + groups - away, groups)
                all_sums_ref[2 * source + number] = group_in[away - 1, number]
            group_copy(away).wait_send()
        for source in range(2 * groups):
            line = slice(source, source + 1)
            first = source % 2 * 5
            terms = [all_sums_ref[source, kind : kind + 1] for kind in range(2)]
            terms += [all_small_ref[source // 2, first + kind : first + kind + 1] for kind in range(4)]
            for kind, term in enumerate(terms):
                lines_ref[line, kind * depth : (kind + 1) * depth] = term
            last = 10 + ranks + source % 2
            embedded_ref[line] = all_small_ref[source // 2, last : last + 1]
        vectors_ref[...] = jnp.zeros_like(vectors_ref)
        for source in range(groups):
            vectors_ref[0:ranks] += all_small_ref[source, 10 : 10 + ranks]
            vectors_ref[ranks : ranks + 1] += all_small_ref[source, 4:5] + all_small_ref[source, 9:10]
        for tile in range(tiles):
            part_copy(tile).wait_send()
            pair_copy(tile).wait_send()
        for tile in range(half):
            chip_copy(tile).wait_send()
        slice_relay.finish()
        piece_relay.finish()
        block_copy().wait_send()


def entry_back_call(
    grad_query,
    grad_key,
    grad_value,
    hat_t,
    scaling,
    gain,
    shift,
    weight,
    grad_middle,
    middle_in,
    small,
    up,
    down,
    grad_out,
    result,
    result_in,
    groups,
    tile,
):
    group, length = grad_query.shape
    depth = hat_t.shape[0]
    tiles = length // tile
    half = tiles // 2
    rows = depth // 4
    weight_rows = depth // groups

    def lanes(step):
        first = (1 - lax.axis_index("context")) * half
        return 0, lax.rem(first + jnp.minimum(step, tiles - 1), tiles)

    whole = lambda step: (0, 0)
    whole3 = lambda step: (0, 0, 0)
    whole4 = lambda step: (0, 0, 0, 0)
    dma = lambda *shape: [pltpu.SemaphoreType.DMA(shape)] * 2
    hbm = pl.BlockSpec(memory_space=pl.ANY)
    piece = up.shape[1:]
    return pl.pallas_call(
        partial(entry_back_kernel, tiles=tiles, groups=groups),
        grid=(tiles + 5,),
        in_specs=[
            pl.BlockSpec((group, tile), lanes),
            pl.BlockSpec((group, tile), lanes),
            pl.BlockSpec((group, tile), lanes),
            pl.BlockSpec((depth, tile), lanes),
            pl.BlockSpec((1, tile), lanes),
            pl.BlockSpec((depth, 1), whole),
            pl.BlockSpec((depth, 1), whole),
            pl.BlockSpec((depth, 3 * group), whole),
            pl.BlockSpec((1, depth, tile), lambda step: (lax.axis_index("context"), 0, 0)),
            pl.BlockSpec((depth, tile), whole),
            pl.BlockSpec(small.shape, whole),
            hbm,
            hbm,
            pl.BlockSpec(grad_out.shape, whole),
            hbm,
            hbm,
        ],
        out_specs=[
            pl.BlockSpec((2, half, rows, tile), whole4),
            pl.BlockSpec((weight_rows, 3 * group), whole),
            pl.BlockSpec((2 * groups, 6 * depth), whole),
            pl.BlockSpec((2 * groups, depth), whole),
            pl.BlockSpec((8, depth), whole),
            pl.BlockSpec((2, 2, *piece[1:]), whole4),
            pl.BlockSpec(grad_out.shape, whole),
            hbm,
        ],
        out_shape=[
            jax.ShapeDtypeStruct((2, half, rows, tile), bf16),
            jax.ShapeDtypeStruct((weight_rows, 3 * group), f32),
            jax.ShapeDtypeStruct((2 * groups, 6 * depth), f32),
            jax.ShapeDtypeStruct((2 * groups, depth), f32),
            jax.ShapeDtypeStruct((8, depth), f32),
            jax.ShapeDtypeStruct((2, 2, *piece[1:]), bf16),
            jax.ShapeDtypeStruct(grad_out.shape, f32),
            jax.ShapeDtypeStruct((2, 4 * result.shape[1], depth), bf16),
        ],
        scratch_shapes=[
            *[pltpu.VMEM(piece, bf16)] * 4,
            pltpu.VMEM((groups, 2, *piece[1:]), bf16),
            *[pltpu.VMEM((2, groups, 2, *piece[1:]), bf16)] * 2,
            pltpu.VMEM((2, *piece[1:]), f32),
            pltpu.VMEM((2, *piece[1:]), bf16),
            pltpu.VMEM((2, *piece[1:]), bf16),
            pltpu.VMEM((2 * groups, 8, depth), f32),
            pltpu.VMEM((groups, *small.shape), f32),
            *[pltpu.VMEM((3, *small.shape), f32)] * 2,
            pltpu.VMEM(small.shape, f32),
            pltpu.VMEM((groups - 1, *small.shape), f32),
            pltpu.VMEM(grad_out.shape, bf16),
            pltpu.SemaphoreType.DMA((2,)),
            *dma(groups),
            *dma(groups),
            *dma(2, groups),
            *[pltpu.SemaphoreType.DMA] * 2,
            *dma(3),
            *dma(groups - 1),
            *[pltpu.SemaphoreType.DMA] * 2,
            *dma(4),
            pltpu.SemaphoreType.DMA((4,)),
            pltpu.SemaphoreType.DMA((4,)),
            pltpu.VMEM((4, *result.shape[1:]), bf16),
            pltpu.VMEM((depth, 3 * group), f32),
            pltpu.VMEM((2, depth, WIDE), f32),
            pltpu.VMEM((tiles, 2, 2, rows, tile), bf16),
            pltpu.VMEM((tiles, 2, rows, tile), bf16),
            pltpu.VMEM((tiles, 2, rows, tile), bf16),
            pltpu.VMEM((tiles, rows, tile), bf16),
            pltpu.VMEM((half, rows, tile), bf16),
            pltpu.VMEM((half, rows, tile), bf16),
            pltpu.VMEM((groups, weight_rows, 3 * group), bf16),
            *[pltpu.VMEM((2, groups, weight_rows, 3 * group), bf16)] * 2,
            pltpu.VMEM((weight_rows, 3 * group), f32),
            pltpu.VMEM((weight_rows, 3 * group), bf16),
            pltpu.VMEM((weight_rows, 3 * group), bf16),
            *[pltpu.VMEM((3, 8, depth), f32)] * 2,
            pltpu.VMEM((2, 8, depth), f32),
            pltpu.VMEM((groups - 1, 2, 8, depth), f32),
            *dma(tiles),
            *dma(tiles),
            *dma(half),
            *dma(2, groups),
            *[pltpu.SemaphoreType.DMA] * 2,
            *dma(3),
            *dma(groups - 1),
        ],
        compiler_params=pltpu.CompilerParams(
            vmem_limit_bytes=VMEM, collective_id=3, has_side_effects=True
        ),
        cost_estimate=cost(12 * length * depth * group, grad_query, hat_t, hat_t),
        name="entry_back",
    )(
        grad_query,
        grad_key,
        grad_value,
        hat_t,
        scaling,
        gain,
        shift,
        weight,
        grad_middle,
        middle_in,
        small,
        up,
        down,
        grad_out,
        result,
        result_in,
    )


def add(left_side, right_side):
    return (left_side.astype(f32) + right_side.astype(f32)).astype(bf16)


def by_sequence(
    tokens,
    cotangent,
    segments,
    steps,
    table,
    ada_w,
    ada_b,
    gain_one,
    w_qkv,
    w_out,
    gain_two,
    w_up,
    b_up,
    w_down,
    b_down,
):
    fsdp, tensor = lax.axis_size("fsdp"), lax.axis_size("tensor")
    context = lax.axis_size("context")
    tensor_rank = lax.axis_index("tensor")
    context_rank = lax.axis_index("context")
    fsdp_rank = lax.axis_index("fsdp")
    sequences, own_rows, depth = tokens.shape
    length = segments.shape[1]
    group = w_out.shape[0]
    part_width = w_up.shape[1]
    heads = group // HDIM
    quarter = own_rows // tensor

    partner = [(k, (k + 1) % context) for k in range(context)]

    by_kind = w_qkv.reshape(-1, heads, 3, HDIM).transpose(0, 2, 1, 3).reshape(-1, 3 * group)
    both = ("tensor", "fsdp")
    out_blocks = lax.all_gather(w_out, both, axis=0, tiled=False)

    numbers = jnp.arange(table.shape[0], dtype=jnp.int32)
    ada_full = ada_w.astype(f32)
    raw = exact_product((steps[:, None] == numbers[None, :]).astype(f32), table.astype(f32))
    local_mods = exact_product(jax.nn.silu(raw), ada_full) + ada_b.astype(f32)
    local_mods = local_mods.reshape(sequences, 6, depth)
    gain_first, gain_second = gain_one.astype(f32), gain_two.astype(f32)
    own_mods = lax.dynamic_index_in_dim(local_mods, context_rank, 0, keepdims=False)
    gain_column = (gain_first * (1.0 + own_mods[1]))[:, None]
    shift_column = own_mods[0][:, None]
    mods = jnp.stack(
        [
            local_mods[:, 2],
            local_mods[:, 3],
            gain_second * (1.0 + local_mods[:, 4]),
            local_mods[:, 5],
        ]
        + [jnp.zeros((sequences, depth), f32)] * 4,
        axis=1,
    )

    segment = lax.dynamic_index_in_dim(segments, context_rank, 0, keepdims=False)
    same, starts, ends = document_bounds(segment)
    offsets = jnp.arange(length, dtype=jnp.int32) - jnp.sum(jnp.where(same, starts[:, None], 0), axis=0)
    angles = frequencies()[:, None] * offsets.astype(f32)[None, :]
    cosine, sine = jnp.cos(angles), jnp.sin(angles)
    tile = length // (context * tensor)
    block = tile
    first_key = jnp.sum(jnp.where(same, starts[:, None], 0), axis=0)[::tile]
    last_key = jnp.sum(jnp.where(same, ends[:, None], 0), axis=0)[tile - 1 :: tile]

    low_key = first_key // WIDE * WIDE
    high_key = (last_key + WIDE - 1) // WIDE * WIDE

    def ranges_of(size):
        count = (high_key - low_key + size - 1) // size
        return jnp.stack([jnp.maximum(high_key - count * size, 0), count]).astype(jnp.int32)

    back_block = block // 2
    ranges, back_ranges = ranges_of(block), ranges_of(back_block)

    queries, keys, keys_t, values_t, hat_t, scaling, norms, qkv, forward = entry_call(
        tokens,
        by_kind,
        jnp.where(context_rank == 0, w_up, w_down.T),
        gain_column,
        shift_column,
        cosine,
        sine,
        segment[None, :],
        groups=fsdp,
        tile=tile,
    )
    across = [(k, (k + 2) % tensor) for k in range(tensor)]
    across_weight = lax.ppermute(forward, "tensor", across)
    other_weight = lax.ppermute(forward, "context", partner)
    mixture, told = attend_call(ranges, queries, keys, values_t, norms, tile, block)

    own_segments = lax.dynamic_slice_in_dim(
        segments, context_rank * own_rows + tensor_rank * quarter, quarter, axis=1
    )
    (
        result,
        grad_mixture,
        grad_middle,
        grad_out,
        sums,
        bias_sums,
        up_keep,
        up_send,
        down_keep,
        down_send,
    ) = middle_call(
        mixture,
        tokens,
        cotangent,
        (own_segments != 0).astype(f32).reshape(-1, 1),
        mods,
        b_up.astype(f32).reshape(tensor, 1, part_width),
        b_down.astype(f32)[None, :],
        out_blocks,
        forward,
        other_weight,
        across_weight,
        fsdp,
        tile=min(tile, 256),
    )
    result = result.reshape(sequences, quarter, depth)
    result_in = lax.ppermute(result, "tensor", across)
    middle_in = lax.ppermute(
        lax.dynamic_index_in_dim(grad_middle, 1 - context_rank, 0, keepdims=False), "context", partner
    )
    small = jnp.concatenate(
        [
            sums[:, :5].reshape(-1, depth),
            bias_sums.reshape(-1, depth),
        ]
    )
    small_rows = small.shape[0]
    cond = raw.shape[1]
    leads = (context_rank == 0) & (tensor_rank == 0)
    embedded = jnp.concatenate([raw, steps.astype(f32)[:, None]], axis=1)
    embedded = jnp.pad(jnp.where(leads, embedded, 0.0), ((0, 0), (0, depth - cond - 1)))
    small = jnp.concatenate([small, embedded])
    small = jnp.pad(small, ((0, -small.shape[0] % 8), (0, 0)))

    up_sum = add(up_keep, lax.ppermute(up_send, "tensor", across))
    down_sum = add(down_keep, lax.ppermute(down_send, "context", partner))
    grad_out = lax.psum_scatter(grad_out, both, scatter_dimension=0, tiled=True)[0]

    grad_query, grad_key, grad_value = attend_back_call(
        back_ranges, told, keys_t, values_t, mixture, grad_mixture, cosine, sine, tile, back_block
    )
    (grad_query, up_sum, down_sum, result_in, middle_in, grad_out) = lax.optimization_barrier(
        (grad_query, up_sum, down_sum, result_in, middle_in, grad_out)
    )
    part, grad_qkv, lines, embedded, vectors, pieces, grad_out, block_out = entry_back_call(
        grad_query,
        grad_key,
        grad_value,
        hat_t,
        scaling,
        gain_column,
        shift_column,
        qkv,
        grad_middle,
        middle_in,
        small,
        up_sum,
        down_sum,
        grad_out,
        result,
        result_in,
        groups=fsdp,
        tile=tile,
    )
    pieces = pieces.transpose(1, 0, 2, 3)
    pieces = pieces.reshape(2, depth // fsdp, part_width).astype(f32)
    grad_w_up = pieces[0]
    grad_w_down = pieces[1].T
    grad_w_out = grad_out
    choose = (embedded[:, cond].astype(jnp.int32)[:, None] == numbers[None, :]).astype(f32)
    embedding, silu_back = jax.vjp(jax.nn.silu, embedded[:, :cond])
    scale_columns = [slice(k * depth, (k + 1) * depth) for k in (1, 4)]
    scales_one, scales_two = (
        exact_product(embedding, ada_full[:, columns]) + ada_b[columns].astype(f32)
        for columns in scale_columns
    )
    grad_b_up = vectors[:tensor].reshape(-1)
    grad_b_down = vectors[tensor]
    grad_gain_one = jnp.sum(lines[:, scale_columns[0]] * (1.0 + scales_one), axis=0)
    grad_gain_two = jnp.sum(lines[:, scale_columns[1]] * (1.0 + scales_two), axis=0)
    part = part.transpose(0, 1, 3, 2).reshape(sequences, own_rows, depth // tensor)
    grad_tokens = part.astype(f32)
    grad_w_qkv = (
        grad_qkv.reshape(-1, 3, heads, HDIM).transpose(0, 2, 1, 3).reshape(-1, 3 * group)
    )
    ones = jnp.ones((depth,), f32)
    grad_mod = lines * jnp.concatenate([ones, gain_first, ones, ones, gain_second, ones])[None, :]
    grad_ada_b = jnp.sum(grad_mod, axis=0)
    grad_ada_w = exact_transposed(embedding, grad_mod)
    grad_before = silu_back(exact_against(grad_mod, ada_full))[0]
    grad_table = exact_transposed(choose, grad_before)
    return (
        block_out,
        grad_tokens,
        grad_table,
        grad_ada_w,
        grad_ada_b,
        grad_gain_one,
        grad_w_qkv,
        grad_w_out,
        grad_gain_two,
        grad_w_up,
        grad_b_up,
        grad_w_down,
        grad_b_down,
    )


def normalize(operand):
    center = operand - jnp.mean(operand, axis=-1, keepdims=True)
    scaling = lax.rsqrt(jnp.mean(center * center, axis=-1, keepdims=True) + 1e-05)
    return (center * scaling, scaling)


def norm_back(grad_hat, hatted, scaling):
    return scaling * (
        grad_hat
        - jnp.mean(grad_hat, axis=-1, keepdims=True)
        - hatted * jnp.mean(grad_hat * hatted, axis=-1, keepdims=True)
    )


def angles_of(offsets, half_width):
    frequency = 10000.0 ** (-jnp.arange(half_width, dtype=jnp.float32) / half_width)
    angles = offsets.astype(jnp.float32)[:, None] * frequency[None, :]
    return (jnp.cos(angles)[:, None, :], jnp.sin(angles)[:, None, :])


def rotate(operand, cosine, sine_part, direction):
    half_width = operand.shape[-1] // 2
    front_half = operand[..., :half_width]
    second = operand[..., half_width:]
    return jnp.concatenate(
        [
            front_half * cosine - direction * second * sine_part,
            direction * front_half * sine_part + second * cosine,
        ],
        axis=-1,
    )


def scores_of(queries, key_rows, allowed):
    raw_scores = (
        jnp.einsum("qhd,khd->hqk", queries, key_rows, preferred_element_type=jnp.float32) * 0.125
    )
    return jnp.where(allowed[None], raw_scores, -1e30)


def attend(queries, key_rows, values, allowed):
    scores = scores_of(queries, key_rows, allowed)
    row_max = jnp.max(scores, axis=-1, keepdims=True)
    weights_raw = jnp.exp(scores - row_max)
    row_total = jnp.sum(weights_raw, axis=-1, keepdims=True)
    weights_low = (weights_raw / row_total).astype(jnp.bfloat16)
    mixture = jnp.einsum("hqk,khd->qhd", weights_low, values, preferred_element_type=jnp.float32)
    return (mixture, row_max + jnp.log(row_total))


def attend_back(queries, key_rows, values, grad_mixture, logsum, allowed, row_delta):
    scores = scores_of(queries, key_rows, allowed)
    chances = jnp.exp(scores - logsum)
    grad_chances = jnp.einsum(
        "qhd,khd->hqk", grad_mixture, values, preferred_element_type=jnp.float32
    )
    row_delta = jnp.sum(chances * grad_chances, axis=-1, keepdims=True)
    grad_scores = (chances * (grad_chances - row_delta)).astype(jnp.bfloat16)
    return (chances.astype(jnp.bfloat16), grad_scores, row_delta)


def by_block(
    tokens,
    cotangent,
    segments,
    steps,
    table,
    ada_w,
    ada_b,
    gain_one,
    w_qkv,
    w_out,
    gain_two,
    w_up,
    b_up,
    w_down,
    b_down,
):
    w_qkv, w_up, w_out, w_down = (
        lax.all_gather(w_qkv, "fsdp", axis=0, tiled=True),
        lax.all_gather(w_up, "fsdp", axis=0, tiled=True),
        lax.all_gather(w_out, "fsdp", axis=1, tiled=True),
        lax.all_gather(w_down, "fsdp", axis=1, tiled=True),
    )
    tensor_rank = lax.axis_index("tensor")
    context_rank = lax.axis_index("context")
    sequences, own_rows, model_width = tokens.shape
    length = segments.shape[1]
    local_heads = w_out.shape[0] // HDIM
    hidden_width = w_up.shape[1]
    up_bias = lax.dynamic_slice_in_dim(b_up, tensor_rank * hidden_width, hidden_width).astype(
        jnp.float32
    )
    down_bias = b_down.astype(jnp.float32)
    gain_first = gain_one.astype(jnp.float32)
    gain_second = gain_two.astype(jnp.float32)
    leader = (tensor_rank == 0).astype(jnp.float32)
    ada_full = ada_w.astype(jnp.float32)
    choose = (steps[:, None] == jnp.arange(table.shape[0], dtype=jnp.int32)[None, :]).astype(
        jnp.float32
    )
    before = exact_product(choose, table.astype(jnp.float32))
    embedding, silu_back = jax.vjp(jax.nn.silu, before)
    modulation = exact_product(embedding, ada_full) + ada_b.astype(jnp.float32)
    grad_qkv = jnp.zeros(w_qkv.shape, jnp.float32)
    grad_out_w = jnp.zeros(w_out.shape, jnp.float32)
    grad_up = jnp.zeros(w_up.shape, jnp.float32)
    grad_down = jnp.zeros(w_down.shape, jnp.float32)
    grad_bias_up = jnp.zeros((hidden_width,), jnp.float32)
    grad_bias_down = jnp.zeros((model_width,), jnp.float32)
    grad_gain_first = jnp.zeros((model_width,), jnp.float32)
    grad_gain_second = jnp.zeros((model_width,), jnp.float32)
    results = []
    partial_inputs = []
    carried = []
    grad_mods = []
    for number in range(sequences):
        shift_one, scale_one, gate_one, shift_two, scale_two, gate_two = jnp.split(
            modulation[number], 6
        )
        segment = segments[number]
        offsets = positions(segment)
        own_segment = lax.dynamic_slice_in_dim(segment, context_rank * own_rows, own_rows)
        own_offsets = lax.dynamic_slice_in_dim(offsets, context_rank * own_rows, own_rows)
        cosine, sine_part = angles_of(own_offsets, HDIM // 2)
        allowed = own_segment[:, None] == segment[None, :]
        inputs_row = tokens[number].astype(jnp.float32)
        hat_one, scaling_one = normalize(inputs_row)
        lifted_one = hat_one * gain_first
        entry_one = (lifted_one * (1.0 + scale_one) + shift_one).astype(jnp.bfloat16)
        projected = product(entry_one, w_qkv).reshape(own_rows, local_heads, 3, HDIM)
        queries = rotate(projected[:, :, 0], cosine, sine_part, 1.0).astype(jnp.bfloat16)
        key_rows = rotate(projected[:, :, 1], cosine, sine_part, 1.0).astype(jnp.bfloat16)
        values = projected[:, :, 2].astype(jnp.bfloat16)
        key_value = jnp.stack([key_rows, values], axis=1).reshape(own_rows, 2 * local_heads * HDIM)
        gathered = lax.all_gather(key_value, "context", axis=0, tiled=True).reshape(
            length, 2, local_heads, HDIM
        )
        all_keys = gathered[:, 0]
        all_values = gathered[:, 1]
        mixture, logsum = attend(queries, all_keys, all_values, allowed)
        mixture_low = mixture.reshape(own_rows, local_heads * HDIM).astype(jnp.bfloat16)
        attended = lax.psum(product(mixture_low, w_out).astype(jnp.bfloat16), "tensor").astype(
            jnp.float32
        )
        middle = inputs_row + gate_one * attended
        hat_two, scaling_two = normalize(middle)
        lifted_two = hat_two * gain_second
        entry_two = (lifted_two * (1.0 + scale_two) + shift_two).astype(jnp.bfloat16)
        hidden = product(entry_two, w_up) + up_bias
        activated, gelu_back = jax.vjp(partial(jax.nn.gelu, approximate=True), hidden)
        activated_low = activated.astype(jnp.bfloat16)
        output = (
            lax.psum(product(activated_low, w_down).astype(jnp.bfloat16), "tensor").astype(
                jnp.float32
            )
            + down_bias
        )
        results.append((middle + gate_two * output).astype(jnp.bfloat16))
        valid = (own_segment != 0).astype(jnp.float32)[:, None]
        grad_result = cotangent[number].astype(jnp.float32) * valid
        grad_output = (gate_two * grad_result).astype(jnp.bfloat16)
        grad_gate_two = jnp.sum(grad_result * output, axis=0)
        grad_bias_down = grad_bias_down + jnp.sum(grad_output.astype(jnp.float32), axis=0)
        grad_down = grad_down + transposed(activated_low, grad_output)
        grad_active = against(grad_output, w_down)
        grad_hidden = gelu_back(grad_active)[0].astype(jnp.bfloat16)
        grad_bias_up = grad_bias_up + jnp.sum(grad_hidden.astype(jnp.float32), axis=0)
        grad_up = grad_up + transposed(entry_two, grad_hidden)
        grad_entry_two = against(grad_hidden, w_up)
        grad_shift_two = jnp.sum(grad_entry_two, axis=0)
        grad_scale_two = jnp.sum(grad_entry_two * lifted_two, axis=0)
        grad_lifted_two = grad_entry_two * (1.0 + scale_two)
        grad_gain_second = grad_gain_second + jnp.sum(grad_lifted_two * hat_two, axis=0)
        part_two = norm_back(grad_lifted_two * gain_second, hat_two, scaling_two)
        grad_middle = grad_result + lax.psum(part_two.astype(jnp.bfloat16), "tensor").astype(
            jnp.float32
        )
        grad_attended = (gate_one * grad_middle).astype(jnp.bfloat16)
        grad_gate_one = jnp.sum(grad_middle * attended, axis=0)
        grad_out_w = grad_out_w + transposed(mixture_low, grad_attended)
        grad_mixture = (
            against(grad_attended, w_out).astype(jnp.bfloat16).reshape(own_rows, local_heads, HDIM)
        )
        chances_low, grad_scores, row_delta = attend_back(
            queries, all_keys, all_values, grad_mixture, logsum, allowed, None
        )
        grad_queries = (
            jnp.einsum("hqk,khd->qhd", grad_scores, all_keys, preferred_element_type=jnp.float32)
            * 0.125
        )
        grad_all_keys = (
            jnp.einsum("hqk,qhd->khd", grad_scores, queries, preferred_element_type=jnp.float32)
            * 0.125
        )
        grad_all_values = jnp.einsum(
            "hqk,qhd->khd", chances_low, grad_mixture, preferred_element_type=jnp.float32
        )
        both_grads = jnp.stack([grad_all_keys, grad_all_values], axis=1).reshape(
            length, 2 * local_heads * HDIM
        )
        own_grads = (
            lax.psum_scatter(
                both_grads.astype(jnp.bfloat16), "context", scatter_dimension=0, tiled=True
            )
            .astype(jnp.float32)
            .reshape(own_rows, 2, local_heads, HDIM)
        )
        grad_keys = own_grads[:, 0]
        grad_values = own_grads[:, 1]
        grad_queries = rotate(grad_queries, cosine, sine_part, -1.0)
        grad_keys = rotate(grad_keys, cosine, sine_part, -1.0)
        grad_projected = (
            jnp.stack([grad_queries, grad_keys, grad_values], axis=2)
            .reshape(own_rows, local_heads * 3 * HDIM)
            .astype(jnp.bfloat16)
        )
        grad_qkv = grad_qkv + transposed(entry_one, grad_projected)
        grad_entry_one = against(grad_projected, w_qkv)
        grad_shift_one = jnp.sum(grad_entry_one, axis=0)
        grad_scale_one = jnp.sum(grad_entry_one * lifted_one, axis=0)
        grad_lifted_one = grad_entry_one * (1.0 + scale_one)
        grad_gain_first = grad_gain_first + jnp.sum(grad_lifted_one * hat_one, axis=0)
        partial_inputs.append(norm_back(grad_lifted_one * gain_first, hat_one, scaling_one))
        carried.append(grad_middle)
        grad_mods.append(
            jnp.concatenate(
                [
                    grad_shift_one,
                    grad_scale_one,
                    grad_gate_one * leader,
                    grad_shift_two,
                    grad_scale_two,
                    grad_gate_two * leader,
                ]
            )
        )
    summed_inputs = lax.psum_scatter(
        jnp.stack(partial_inputs).astype(jnp.bfloat16), "tensor", scatter_dimension=2, tiled=True
    ).astype(jnp.float32)
    slice_width = model_width // lax.axis_size("tensor")
    own_middle = lax.dynamic_slice_in_dim(
        jnp.stack(carried), tensor_rank * slice_width, slice_width, axis=2
    )
    grad_tokens = summed_inputs + own_middle
    grad_mod = jnp.stack(grad_mods)
    bias_up_full = lax.dynamic_update_slice_in_dim(
        jnp.zeros((b_up.shape[0],), jnp.float32), grad_bias_up, tensor_rank * hidden_width, 0
    )
    grad_qkv, grad_up, grad_out_w, grad_down = (
        lax.psum_scatter(
            grad_qkv.astype(jnp.bfloat16), "fsdp", scatter_dimension=0, tiled=True
        ).astype(jnp.float32),
        lax.psum_scatter(
            grad_up.astype(jnp.bfloat16), "fsdp", scatter_dimension=0, tiled=True
        ).astype(jnp.float32),
        lax.psum_scatter(
            grad_out_w.astype(jnp.bfloat16), "fsdp", scatter_dimension=1, tiled=True
        ).astype(jnp.float32),
        lax.psum_scatter(
            grad_down.astype(jnp.bfloat16), "fsdp", scatter_dimension=1, tiled=True
        ).astype(jnp.float32),
    )
    grad_qkv, grad_up, grad_out_w, grad_down = (
        lax.psum(grad_qkv.astype(jnp.bfloat16), "context").astype(jnp.float32),
        lax.psum(grad_up.astype(jnp.bfloat16), "context").astype(jnp.float32),
        lax.psum(grad_out_w.astype(jnp.bfloat16), "context").astype(jnp.float32),
        lax.psum(grad_down.astype(jnp.bfloat16), "context").astype(jnp.float32),
    )
    grad_ada_b = jnp.sum(grad_mod, axis=0)
    grad_ada_w = exact_transposed(embedding, grad_mod)
    grad_embedding = exact_against(grad_mod, ada_full)
    grad_before = silu_back(grad_embedding)[0]
    grad_table = exact_transposed(choose, grad_before)
    (
        grad_table,
        grad_ada_w,
        grad_ada_b,
        grad_gain_first,
        grad_gain_second,
        bias_up_full,
        grad_bias_down,
    ) = lax.psum(
        (
            grad_table,
            grad_ada_w,
            grad_ada_b,
            grad_gain_first,
            grad_gain_second,
            bias_up_full,
            grad_bias_down * leader,
        ),
        ("fsdp", "context", "tensor"),
    )
    return (
        jnp.stack(results),
        grad_tokens,
        grad_table,
        grad_ada_w,
        grad_ada_b,
        grad_gain_first,
        grad_qkv,
        grad_out_w,
        grad_gain_second,
        grad_up,
        bias_up_full,
        grad_down,
        grad_bias_down,
    )


def solution(mesh):
    axes = dict(zip(mesh.axis_names, mesh.devices.shape))

    def whole(tokens, *others):
        sequences = tokens.shape[0] // axes["fsdp"]
        local = by_sequence if sequences == axes["context"] == 2 and axes["tensor"] == 4 else by_block
        return mapped(local, mesh)(tokens, *others)

    return whole


def mapped(local, mesh):
    return jax.shard_map(
        local,
        mesh=mesh,
        in_specs=(
            P("fsdp", "context", None),
            P("fsdp", "context", None),
            P("fsdp", None),
            P("fsdp"),
            P(),
            P(),
            P(),
            P(),
            P("fsdp", "tensor"),
            P("tensor", "fsdp"),
            P(),
            P("fsdp", "tensor"),
            P(),
            P("tensor", "fsdp"),
            P(),
        ),
        out_specs=(
            P("fsdp", "context", None),
            P("fsdp", "context", "tensor"),
            P(),
            P(),
            P(),
            P(),
            P("fsdp", "tensor"),
            P("tensor", "fsdp"),
            P(),
            P("fsdp", "tensor"),
            P(),
            P("tensor", "fsdp"),
            P(),
        ),
        check_vma=False,
    )
```
